32 devices in a mesh: dp: 8 (over y, x, core), expert: 4 (over z).
Axes of the slice: x: 2, y: 2, z: 4, core: 2. Of those that a mesh axis runs over, the one named last changes fastest.
Arguments:
- tokens: bfloat16 [2, 8, 512, 1024], P(None, 'dp', 'expert'), may hold values from -6 to 6
- lengths: int32 [2, 8], P(None, 'dp'), may hold values from 128 to 512, as said below
- routes: int32 [2, 8, 512, 8], P(None, 'dp'), may hold values from 0 to 15, all different within a row; in each aligned block of 128 rows (0 to 127, 128 to 255, ..., all dimensions but the last counted through in order) at most 80 rows name the same one
- attn_gain: float32 [1024], replicated, may hold values from 0.5 to 1.5
- w_query: bfloat16 [1024, 1024], replicated, may hold values from -0.75 to 0.75
- w_keyval: bfloat16 [1024, 1024], replicated, may hold values from -0.75 to 0.75
- w_out: bfloat16 [1024, 1024], replicated, may hold values from -0.1875 to 0.1875
- ffn_gain: float32 [1024], replicated, may hold values from 0.5 to 1.5
- w_router: bfloat16 [1024, 16], replicated, may hold values from -0.09375 to 0.09375
- expert_gate_up: bfloat16 [16, 1024, 1024], P('expert'), may hold values from -0.1875 to 0.1875
- expert_down: bfloat16 [16, 512, 1024], P('expert'), may hold values from -1.5 to 1.5
- cotangent: bfloat16 [2, 8, 512, 1024], P(None, 'dp', 'expert'), may hold values from -6 to 6
Outputs:
- output: bfloat16 [2, 8, 512, 1024], P(None, 'dp', 'expert')
- input_grad: float32 [2, 8, 512, 1024], P(None, 'dp', 'expert')
- grad_attn_gain: float32 [1024], P(('dp', 'expert'))
- grad_query: float32 [1024, 1024], P(('dp', 'expert'))
- grad_keyval: float32 [1024, 1024], P(('dp', 'expert'))
- grad_out: float32 [1024, 1024], P(('dp', 'expert'))
- grad_ffn_gain: float32 [1024], P(('dp', 'expert'))
- grad_router: float32 [1024, 16], P(('dp', 'expert'))
- grad_gate_up: float32 [16, 1024, 1024], P('expert', 'dp')
- grad_down: float32 [16, 512, 1024], P('expert', 'dp')
The draws below stay inside these ranges and needn't reach their ends.
Inputs may be any that keep to these rules, and one draw needn't show every extreme that they name: `lengths`: in every micro-batch one sequence has length 512; the others have 512 // 4 to 512. `routes`: each position names 8 different experts; in each aligned block of 128 positions (the positions of one device) no expert is named more than 80 times.
All inputs are finite; a program needn't handle non-finite values.
Results may differ from the reference program's by a relative error of at most 0.017.
The reference program's roundings to bfloat16 on the way count: a program that leaves them out, or rounds other values in their place, can miss the bound.
Values may be sent and summed in bfloat16 or wider, within the bound.
A program may use at most 192 MiB of HBM per device.

```python
import math
import jax
import jax.numpy as jnp
import numpy as np
from jax import lax

D = 1024
HEADS = 16
KV_HEADS = 8
HEAD_DIM = 64
FF = 512
EXPERTS = 16
TOP = 8
TOK_DEV = 128
MICRO = 2
CAP = 80
GROUPS = 8
SEQ = 512


def draw_lengths(key, part):
    key = jax.random.fold_in(key, 11)
    first_key, second_key = jax.random.split(key)
    draw_len = jax.random.randint(first_key, (MICRO, GROUPS), SEQ // 4, SEQ + 1)
    longest = jax.random.randint(second_key, (MICRO, 1), 0, GROUPS)
    column = jnp.arange(GROUPS, dtype=jnp.int32)[None, :]
    return jnp.where(column == longest, SEQ, draw_len).astype(jnp.int32)


def steps_of(stream_key, extent, shards, smallest, top_value):
    def one(dim, shards_of):
        draws = jax.random.uniform(jax.random.fold_in(jax.random.fold_in(stream_key, 6), dim), (shards_of,), jnp.float32, smallest / len(shards), top_value / len(shards))
        return jnp.repeat(jnp.exp(draws), extent[dim] // shards_of).reshape((-1,) + (1,) * (len(extent) - dim - 1))

    gain = one(*shards[0])
    for cut in shards[1:]:
        gain = gain * one(*cut)
    return gain


def deal_out(own_key, own, number, rows, amount, top, bound, skew):
    sequence = jax.random.permutation(own_key, amount)
    crowded, common = load_shares(amount, rows * top, bound, skew, True), load_shares(amount, rows * top, bound, skew, False)
    places = jnp.arange(amount)

    def named(sizes, rotation):
        used = int((sizes > 0).sum())
        fixed = max(1, used // 4)
        passed = fixed + (places - fixed + rotation * (used - fixed)) % max(1, amount - fixed)
        return jnp.zeros((amount,), jnp.int32).at[sequence[jnp.where(places < fixed, places, passed)]].set(jnp.asarray(sizes, jnp.int32))

    sizes = jnp.where(number % 4 == 0, named(crowded, number // 4), named(common, number - number // 4 - 1))
    mixed = jax.random.permutation(jax.random.fold_in(own, 3), amount)
    source_of, taker = mixed[0:amount // 2 * 2:2], mixed[1:amount // 2 * 2:2]
    slack = jnp.minimum(sizes[source_of] - 1, bound - sizes[taker]) // 2
    slack = jnp.where((source_of == sequence[0]) | (taker == sequence[0]) | (sizes[taker] == 0), 0, jnp.maximum(slack, 0))
    passed = jax.random.randint(jax.random.fold_in(own, 4), (amount // 2,), 0, 1 << 20) % (slack + 1)
    sizes = sizes.at[source_of].add(-passed).at[taker].add(passed)
    labels = jnp.searchsorted(jnp.cumsum(sizes), jnp.arange(rows * top), side="right").astype(jnp.int32)
    grid = labels.reshape(top, rows).T
    grid = grid[jax.random.permutation(jax.random.fold_in(own, 1), rows)]
    rotation = jax.random.randint(jax.random.fold_in(own, 2), (rows, 1), 0, top)
    return jnp.take_along_axis(grid, (jnp.arange(top)[None, :] + rotation) % top, axis=1)


def load_shares(count, total, most, slope, full):
    portions = [(1 << 20) // math.isqrt(grade ** slope) + 1 for grade in range(1, count + 1)]
    largest = most if full else min(most, max(-(-total // count), total * portions[0] // sum(portions)))
    least = 1 if total - largest >= count - 1 else 0
    given, rest = [largest] + [least] * (count - 1), total - largest - least * (count - 1)
    while rest > 0:
        candidates = [i for i in range(1, count) if given[i] < largest] or [i for i in range(1, count) if given[i] < most]
        whole, remaining = sum([portions[i] for i in candidates]), rest
        for i in candidates:
            more = min(most - given[i], max(1, remaining * portions[i] // whole), rest)
            given[i] = given[i] + more
            rest = rest - more
    return np.array(given)


def normal_values(own_key, extent, deviation, reach, pieces=(), kind=jnp.bfloat16):
    values = deviation * jax.random.normal(own_key, extent, jnp.float32)
    if pieces:
        values = values * steps_of(own_key, extent, pieces, -0.22, 0.18)
    return jnp.clip(values, -reach, reach).astype(kind)


def setup_inputs(seed: int = 0) -> dict:
    arg_keys = jax.random.split(jax.random.key(seed), 13)
    tokens = normal_values(arg_keys[0], (MICRO, GROUPS, SEQ, D), 1.0, 6.0, ((1, 8), (2, 4)))
    lengths = draw_lengths(jax.random.fold_in(arg_keys[12], 71), 0)
    routes_keys = jax.random.split(jax.random.fold_in(arg_keys[2], 1), MICRO * GROUPS * SEQ // TOK_DEV)
    routes_turns = jax.random.permutation(jax.random.fold_in(arg_keys[2], 3), MICRO * GROUPS * SEQ // TOK_DEV)
    routes = jax.vmap(lambda own, number: deal_out(jax.random.fold_in(arg_keys[2], 2), own, number, TOK_DEV, EXPERTS, TOP, CAP, 1))(routes_keys, routes_turns).reshape((MICRO, GROUPS, SEQ, TOP))
    attn_gain = jnp.clip(1.0 + 0.1 * jax.random.normal(arg_keys[3], (D,), jnp.float32), 0.5, 1.5)
    w_query = normal_values(arg_keys[4], (D, HEADS * HEAD_DIM), HEAD_DIM ** -0.5, 0.75)
    w_keyval = normal_values(arg_keys[5], (D, 2 * KV_HEADS * HEAD_DIM), HEAD_DIM ** -0.5, 0.75)
    w_out = normal_values(arg_keys[6], (HEADS * HEAD_DIM, D), (HEADS * HEAD_DIM) ** -0.5, 0.1875)
    ffn_gain = jnp.clip(1.0 + 0.1 * jax.random.normal(arg_keys[7], (D,), jnp.float32), 0.5, 1.5)
    w_router = normal_values(arg_keys[8], (D, EXPERTS), (4 * D) ** -0.5, 0.09375)
    expert_gate_up = normal_values(arg_keys[9], (EXPERTS, D, 2 * FF), D ** -0.5, 0.1875, ((0, 4),))
    expert_down = normal_values(arg_keys[10], (EXPERTS, FF, D), (FF // 32) ** -0.5, 1.5, ((0, 4),))
    cotangent = normal_values(arg_keys[11], (MICRO, GROUPS, SEQ, D), 1.0, 6.0, ((1, 8), (2, 4)))
    return dict(tokens=tokens, lengths=lengths, routes=routes, attn_gain=attn_gain, w_query=w_query, w_keyval=w_keyval, w_out=w_out, ffn_gain=ffn_gain, w_router=w_router, expert_gate_up=expert_gate_up, expert_down=expert_down, cotangent=cotangent)


@jax.custom_vjp
def low(v):
    return lax.optimization_barrier(v.astype(jnp.bfloat16)).astype(jnp.float32)

@jax.custom_vjp
def low_back(v):
    return v

def low_keep(v):
    return (low(v), None)

def low_pass(kept, grad):
    return (grad,)

def back_keep(v):
    return (v, None)

def back_low(kept, grad):
    return (low(grad),)
low.defvjp(low_keep, low_pass)
low_back.defvjp(back_keep, back_low)
EPS = 1e-06
ATTENTION_SCALE = 0.015625
ROPE_BASE = 10000.0
HIGH_PRECISION = lax.Precision.HIGHEST

def wide_dot(left_side, right_side):
    return jnp.dot(left_side, right_side, precision=HIGH_PRECISION, preferred_element_type=jnp.float32)

def normalize(operand, gain_vec):
    return operand * lax.rsqrt(lax.optimization_barrier(jnp.mean(operand * operand, -1, keepdims=True)) + EPS) * gain_vec

def rope_tables(positions, head_dim):
    half_dim = head_dim // 2
    frequency = jnp.exp(jnp.arange(half_dim, dtype=jnp.float32) * (-2.0 * math.log(ROPE_BASE) / head_dim))
    angles = positions.astype(jnp.float32)[:, None] * frequency[None, :]
    return (jnp.cos(angles)[:, None, :], jnp.sin(angles)[:, None, :])

def rotate(operand, cos_table, sine_table):
    half_dim = operand.shape[-1] // 2
    front_half = operand[..., :half_dim]
    back_half = operand[..., half_dim:]
    return jnp.concatenate([front_half * cos_table - back_half * sine_table, back_half * cos_table + front_half * sine_table], -1)

def layer_forward(params, tokens, route_ids, seq_length):
    attn_gain, w_query, w_keyval, w_out, ffn_gain, w_router, gate_up, down_proj = params
    seq_len = tokens.shape[0]
    kv_width = KV_HEADS * HEAD_DIM
    position = jnp.arange(seq_len, dtype=jnp.int32)
    is_live = position < seq_length
    keep_mask = is_live.astype(jnp.float32)[:, None]
    cos_table, sine_table = rope_tables(position, HEAD_DIM)
    normed = low(normalize(tokens, attn_gain))
    query_pre = low_back(wide_dot(normed, w_query))
    keyval_pre = low_back(wide_dot(normed, w_keyval))
    queries = low(rotate(query_pre.reshape(seq_len, HEADS, HEAD_DIM), cos_table, sine_table))
    rotary_keys = low(rotate(keyval_pre[:, :kv_width].reshape(seq_len, KV_HEADS, HEAD_DIM), cos_table, sine_table))
    value_rows = low(keyval_pre[:, kv_width:].reshape(seq_len, KV_HEADS, HEAD_DIM))
    block_rows = min(512, seq_len)
    query_blocks = queries.reshape(seq_len // block_rows, block_rows, KV_HEADS, HEADS // KV_HEADS, HEAD_DIM)
    row_blocks = position.reshape(seq_len // block_rows, block_rows)

    @jax.checkpoint
    def attend(element):
        block_query_rows, row_ids = element
        score_matrix = jnp.einsum('jclb,vcb->cljv', block_query_rows, rotary_keys, precision=HIGH_PRECISION) * ATTENTION_SCALE
        score_matrix = low_back(score_matrix)
        allowed = (position[None, :] <= row_ids[:, None]) & is_live[None, :]
        score_matrix = jnp.where(allowed, score_matrix, -1e+30)
        attention_probs = jax.nn.softmax(score_matrix, axis=-1)
        attention_mixture = jnp.einsum('apzm,mau->zapu', low(attention_probs), value_rows, precision=HIGH_PRECISION)
        return attention_mixture.reshape(row_ids.shape[0], HEADS * HEAD_DIM)
    attended = lax.map(attend, (query_blocks, row_blocks)).reshape(seq_len, HEADS * HEAD_DIM)
    attn_out = low_back(wide_dot(low(low_back(attended)), w_out))
    hidden = tokens + keep_mask * attn_out
    normed2 = low(normalize(hidden, ffn_gain))
    logits = low_back(wide_dot(normed2, w_router))
    chosen = jnp.take_along_axis(logits, route_ids, axis=1)
    weights = jax.nn.softmax(chosen, axis=-1)
    slot_count = seq_len // TOK_DEV * CAP
    padded_rows = jnp.concatenate([normed2, jnp.zeros((1, normed2.shape[1]), jnp.float32)], 0)
    expert_ids = jnp.arange(EXPERTS, dtype=jnp.int32)

    @jax.checkpoint
    def expert_step(running, element):
        expert_id, w_gate_up, w_down = element
        is_named = route_ids == expert_id
        is_hit = jnp.any(is_named, axis=1) & is_live
        slot_rank = jnp.cumsum(is_hit.astype(jnp.int32)) - 1
        target = jnp.where(is_hit, slot_rank, slot_count)
        slot_index = jnp.full((slot_count + 1,), seq_len, jnp.int32).at[target].set(position)[:slot_count]
        gate_value = lax.optimization_barrier(jnp.sum(weights * is_named.astype(jnp.float32), axis=1))
        gate_value = jnp.concatenate([gate_value, jnp.zeros((1,), jnp.float32)])[slot_index]
        row_values = padded_rows[slot_index]
        projected = low_back(wide_dot(row_values, w_gate_up))
        activated = low(jax.nn.silu(projected[:, :FF]) * projected[:, FF:] * gate_value[:, None])
        expert_out = wide_dot(activated, w_down)
        return (running.at[slot_index].add(expert_out), None)
    expert_sum, _ = lax.scan(expert_step, jnp.zeros((seq_len + 1, normed2.shape[1]), jnp.float32), (expert_ids, gate_up, down_proj))
    expert_sum = low_back(expert_sum[:seq_len])
    return hidden + expert_sum

def reference(tokens, lengths, routes, attn_gain, w_query, w_keyval, w_out, ffn_gain, w_router, expert_gate_up, expert_down, cotangent):
    params = tuple((p.astype(jnp.float32) for p in (attn_gain, w_query, w_keyval, w_out, ffn_gain, w_router, expert_gate_up, expert_down)))
    seq_count = MICRO * GROUPS
    flat_tokens = tokens.reshape(seq_count, SEQ, D)
    flat_cot = cotangent.reshape(seq_count, SEQ, D)
    flat_routes = routes.reshape(seq_count, SEQ, TOP)
    flat_lengths = lengths.reshape(seq_count)

    def one_sequence(running, element):
        seq_tokens, seq_cot, seq_routes, seq_length = element
        result, pullback = jax.vjp(lambda p, v: layer_forward(p, v, seq_routes, seq_length), params, seq_tokens.astype(jnp.float32))
        gradients, token_grad = pullback(seq_cot.astype(jnp.float32))
        running = tuple((a + b for a, b in zip(running, gradients)))
        return (running, (result.astype(jnp.bfloat16), token_grad))
    initial = tuple((jnp.zeros(p.shape, jnp.float32) for p in params))
    totals, (outputs, token_grads) = lax.scan(one_sequence, initial, (flat_tokens, flat_cot, flat_routes, flat_lengths))
    return (outputs.reshape(tokens.shape), token_grads.reshape(tokens.shape), totals[0], totals[1], totals[2], totals[3], totals[4], totals[5], totals[6], totals[7])
```

```python
import functools
import math

import jax
import jax.numpy as jnp
import numpy as np
from jax import lax
from jax.experimental import pallas as pl
from jax.experimental.pallas import tpu as pltpu
from jax.sharding import PartitionSpec as P

HEAD_DIM = 64
EPS = 1e-06
ATTENTION_SCALE = 0.015625
ROPE_BASE = 10000.0
NEG_FILL = -1e30
LANES = 128
STRIP = 16
BF = jnp.bfloat16
F32 = jnp.float32
VMEM_LIMIT = 62 * 2**20


def dot_of(left, right, left_dim, right_dim):
    return lax.dot_general(
        left, right, (((left_dim,), (right_dim,)), ((), ())), preferred_element_type=F32
    )


def nn(left, right):
    return dot_of(left, right, 1, 0)


def nt(left, right):
    return dot_of(left, right, 1, 1)


def tn(left, right):
    return dot_of(left, right, 0, 0)


def rope_constants(seq_len):
    half = HEAD_DIM // 2
    frequency = np.exp(
        np.arange(half, dtype=np.float32) * np.float32(-2.0 * math.log(ROPE_BASE) / HEAD_DIM)
    ).astype(np.float32)
    angles = np.arange(seq_len, dtype=np.float32)[:, None] * frequency[None, :]
    cos, sin = np.cos(angles).astype(np.float32), np.sin(angles).astype(np.float32)
    heads = LANES // HEAD_DIM
    return np.tile(np.concatenate([cos, cos], 1), (1, heads)), np.tile(
        np.concatenate([-sin, sin], 1), (1, heads)
    )


def lane_ids(rows):
    return lax.broadcasted_iota(jnp.int32, (rows, LANES), 1)


def swap_halves(chunk):
    half = HEAD_DIM // 2
    first = lax.rem(lane_ids(chunk.shape[0]), HEAD_DIM) < half
    return jnp.where(
        first, pltpu.roll(chunk, LANES - half, 1), pltpu.roll(chunk, half, 1)
    )


def rope(chunk, cos, sin):
    return chunk * cos + swap_halves(chunk) * sin


def rms_scale(rows):
    return lax.rsqrt(jnp.mean(rows * rows, -1, keepdims=True) + EPS)


def stack_heads(first, second):
    low = lane_ids(first.shape[0]) < HEAD_DIM
    zero = jnp.zeros_like(first)
    return [
        jnp.where(low, first, zero),
        jnp.where(low, pltpu.roll(first, HEAD_DIM, 1), zero),
        jnp.where(low, zero, pltpu.roll(second, HEAD_DIM, 1)),
        jnp.where(low, zero, second),
    ]


def unstack_heads(stacked, rows):
    low = lane_ids(rows) < HEAD_DIM
    parts = [stacked[k * rows : (k + 1) * rows] for k in range(4)]
    first = jnp.where(low, parts[0], pltpu.roll(parts[1], HEAD_DIM, 1))
    second = jnp.where(low, pltpu.roll(parts[2], HEAD_DIM, 1), parts[3])
    return first, second


def rows_at(index, rows):
    return pl.ds(pl.multiple_of(index * rows, rows), rows)


class Gather:
    def __init__(self, buffer, micro, rows, count, sems, up=True, down=True):
        self.buffer, self.micro, self.rows, self.count, self.sems = buffer, micro, rows, count, sems
        self.ways = [w for w, on in ((0, up), (1, down)) if on]

    def copy(self, way, step, block):
        z = lax.axis_index("expert")
        target = z + 1 if way == 0 else z - 1
        view = self.buffer.at[self.micro, rows_at(block, self.rows), :]
        return pltpu.make_async_remote_copy(
            src_ref=view,
            dst_ref=view,
            send_sem=self.sems.at[0, way, step],
            recv_sem=self.sems.at[1, way, step],
            device_id={"expert": target},
            device_id_type=pl.DeviceIdType.MESH,
        )

    def sends(self, way, step):
        z = lax.axis_index("expert")
        if way == 0:
            return z - step, jnp.logical_and(z < self.count - 1, z - step >= 0)
        return z + step, jnp.logical_and(z > 0, z + step <= self.count - 1)

    def receives(self, way, step):
        z = lax.axis_index("expert")
        if way == 0:
            return z - 1 - step, z - 1 - step >= 0
        return z + 1 + step, z + 1 + step <= self.count - 1

    def start(self, step):
        for way in self.ways:
            block, on = self.sends(way, step)

            @pl.when(on)
            def _(way=way, block=block):
                self.copy(way, step, block).start()

    def wait(self, step):
        for way in self.ways:
            block, on = self.receives(way, step)

            @pl.when(on)
            def _(way=way, block=block):
                self.copy(way, step, block).wait_recv()

    def hop(self, step):
        self.wait(step)
        if step + 1 < self.count - 1:
            self.start(step + 1)

    def finish(self):
        for step in range(self.count - 1):
            for way in self.ways:
                block, on = self.sends(way, step)

                @pl.when(on)
                def _(way=way, step=step, block=block):
                    self.copy(way, step, block).wait_send()


class Reduce:
    def __init__(self, parts, landing, rows, count, sems, up=True, down=True):
        self.parts, self.landing = parts, landing
        self.rows, self.count, self.sems = rows, count, sems
        self.ways = [w for w, on in ((0, up), (1, down)) if on]

    def block(self, way, slot):
        z = lax.axis_index("expert")
        if way == 0:
            return z + self.count - 1 - slot, slot >= z
        return z - (self.count - 1) + slot, slot >= self.count - 1 - z

    def place(self, way, slot, z):
        if way == 0:
            return slot - (z - 1)
        return self.count - (slot - (self.count - 2 - z))

    def copy(self, way, slot, block):
        z = lax.axis_index("expert")
        target = z + 1 if way == 0 else z - 1
        return pltpu.make_async_remote_copy(
            src_ref=self.parts.at[rows_at(block, self.rows), :],
            dst_ref=self.landing.at[self.place(way, slot, target)],
            send_sem=self.sems.at[0, way, slot],
            recv_sem=self.sems.at[1, way, slot],
            device_id={"expert": target},
            device_id_type=pl.DeviceIdType.MESH,
        )

    def arrival(self, way, slot, block):
        z = lax.axis_index("expert")
        source = z - 1 if way == 0 else z + 1
        return pltpu.make_async_remote_copy(
            src_ref=self.parts.at[rows_at(block, self.rows), :],
            dst_ref=self.landing.at[self.place(way, slot, z)],
            send_sem=self.sems.at[0, way, slot],
            recv_sem=self.sems.at[1, way, slot],
            device_id={"expert": source},
            device_id_type=pl.DeviceIdType.MESH,
        )

    def inner(self, way):
        z = lax.axis_index("expert")
        return z >= 1 if way == 0 else z <= self.count - 2

    def slot(self, slot):
        z = lax.axis_index("expert")
        for way in self.ways:
            block, on = self.block(way, slot)
            if slot >= 1:

                @pl.when(jnp.logical_and(on, self.inner(way)))
                def _(way=way, block=block):
                    self.arrival(way, slot - 1, block).wait_recv()
                    if slot < self.count - 1:
                        where = rows_at(block, self.rows)
                        total = self.parts[where, :].astype(F32) + self.landing[
                            self.place(way, slot - 1, z)
                        ].astype(F32)
                        self.parts[where, :] = total.astype(self.parts.dtype)

            if slot < self.count - 1:

                @pl.when(on)
                def _(way=way, block=block):
                    self.copy(way, slot, block).start()

    def total(self, out):
        z = lax.axis_index("expert")
        out[...] = self.parts[rows_at(z, self.rows), :].astype(F32)
        for way in self.ways:

            @pl.when(self.inner(way))
            def _(way=way):
                out[...] += self.landing[self.place(way, self.count - 2, z)].astype(F32)

    def finish(self):
        for slot in range(self.count - 1):
            for way in self.ways:
                block, on = self.block(way, slot)

                @pl.when(on)
                def _(way=way, slot=slot, block=block):
                    self.copy(way, slot, block).wait_send()


def line_barrier(count):
    z = lax.axis_index("expert")
    barrier = pltpu.get_barrier_semaphore()
    for target, on in ((z + 1, z < count - 1), (z - 1, z > 0)):

        @pl.when(on)
        def _(target=target):
            pl.semaphore_signal(
                barrier, inc=1, device_id={"expert": target}, device_id_type=pl.DeviceIdType.MESH
            )

    pl.semaphore_wait(barrier, (z > 0).astype(jnp.int32) + (z < count - 1).astype(jnp.int32))


def masked_scores(scores_ref, strip, rows, seq_len, row_base, length):
    where = rows_at(strip, STRIP)
    shape = (STRIP, seq_len)
    first = row_base + lax.rem(strip * STRIP, rows)
    query_pos = first + lax.broadcasted_iota(jnp.int32, shape, 0)
    key_pos = lax.broadcasted_iota(jnp.int32, shape, 1)
    allowed = jnp.logical_and(key_pos <= query_pos, key_pos < length)
    return jnp.where(allowed, scores_ref[where, :] * ATTENTION_SCALE, NEG_FILL)


def softmax_rows(scores):
    top = jnp.max(scores, -1, keepdims=True)
    raised = jnp.exp(scores - top)
    return raised / jnp.sum(raised, -1, keepdims=True)


def forward_kernel(
    dims,
    lengths,
    tokens,
    cot,
    routes,
    gain_one,
    gain_two,
    cos_ref,
    sin_ref,
    router,
    query_hbm,
    keyval_hbm,
    out_hbm,
    gate_up_hbm,
    down_hbm,
    y_out,
    hidden_out,
    moe_out,
    queries_out,
    keyval_out,
    mixture_out,
    grad_gu_out,
    grad_dn_out,
    wide,
    narrow,
    normed,
    queries,
    keyval,
    mixture,
    hidden,
    named,
    gates,
    router_pad,
    rows_all,
    cot_all,
    acts,
    d_proj,
    w_out,
    w_gu,
    w_dn,
    out_parts,
    out_land,
    in_parts,
    in_land,
    own_sum,
    moe_sum,
    kv_sems,
    rows_sems,
    cot_sems,
    out_sems,
    in_sems,
    load_sems,
    store_sems,
):
    micros, rows, count, local, ff, model = dims
    seq_len = count * rows
    kv = keyval.shape[2] // 2
    chunks = kv // LANES
    z = lax.axis_index("expert")
    row_base = z * rows
    split = -(-model // seq_len)
    piece = model // split
    back = wide
    scores = wide.at[0 : 4 * rows, 0:seq_len]
    probs = d_proj.at[micros * local - 1, 0 : 4 * rows, 0:seq_len]
    tile = 512

    loads = []

    def load(src, dst):
        copy = pltpu.make_async_copy(src, dst, load_sems.at[len(loads)])
        copy.start()
        loads.append(copy)
        return copy

    early = []
    for index, weight in enumerate((query_hbm, keyval_hbm)):
        early.append(
            [
                load(
                    weight.at[pl.ds(k * piece, piece), :],
                    d_proj.at[index * split + k, pl.ds(0, piece), :],
                )
                for k in range(split)
            ]
        )
    load_out = load(out_hbm, w_out)
    load_gu = load(gate_up_hbm, w_gu)
    load_dn = load(down_hbm, w_dn)

    line_barrier(count)

    gather_kv = [
        Gather(keyval, m, rows, count, kv_sems.at[m], down=False) for m in range(micros)
    ]
    gather_rows = [Gather(rows_all, m, rows, count, rows_sems.at[m]) for m in range(micros)]
    gather_cot = [Gather(cot_all, m, rows, count, cot_sems.at[m]) for m in range(micros)]
    reduce_out = [
        Reduce(out_parts, out_land, rows, count, out_sems.at[m]) for m in range(micros)
    ]
    reduce_in = [Reduce(in_parts, in_land, rows, count, in_sems.at[m]) for m in range(micros)]

    for m in range(micros):
        cot_all[m, rows_at(z, rows), :] = cot[m, 0]
    gather_cot[0].start(0)

    for m in range(micros):
        x_rows = tokens[m, 0].astype(F32)
        normed[m * rows : (m + 1) * rows, :] = (
            x_rows * rms_scale(x_rows) * gain_one[...]
        ).astype(BF)
    cos = cos_ref[rows_at(z, rows), :]
    sin = sin_ref[rows_at(z, rows), :]
    both = micros * rows

    def project(index):
        for copy in early[index]:
            copy.wait()
        total = None
        for k in range(split):
            part = nn(
                normed[:, k * piece : (k + 1) * piece], d_proj[index * split + k, 0:piece, :]
            )
            total = part if total is None else total + part
        wide[0:both, :] = total

    project(1)
    for m in range(micros):
        span = slice(m * rows, (m + 1) * rows)
        for c in range(chunks):
            lanes = slice(c * LANES, (c + 1) * LANES)
            keyval[m, rows_at(z, rows), lanes] = rope(wide[span, lanes], cos, sin).astype(BF)
        keyval[m, rows_at(z, rows), kv:] = wide[span, kv:].astype(BF)
        gather_kv[m].start(0)
        for b in range(count):

            @pl.when(b > z)
            def _(m=m, b=b):
                keyval[m, b * rows : (b + 1) * rows, :] = jnp.zeros((rows, 2 * kv), BF)

    project(0)
    for m in range(micros):
        span = slice(m * rows, (m + 1) * rows)
        for i in range(chunks):
            pair = [
                rope(wide[span, c * LANES : (c + 1) * LANES], cos, sin)
                for c in (2 * i, 2 * i + 1)
            ]
            for k, block in enumerate(stack_heads(*pair)):
                queries[m, i, k * rows : (k + 1) * rows, :] = block.astype(BF)

    for m in range(micros):
        lane = lane_ids(seq_len)
        hit = jnp.zeros((seq_len, LANES), F32)
        for k in range(routes.shape[3]):
            hit = hit + (routes[m, 0][:, k : k + 1] == lane).astype(F32)
        live = lax.broadcasted_iota(jnp.int32, (seq_len, LANES), 0) < lengths[m, 0]
        named[m] = jnp.where(live, hit, 0.0)
    router_pad[...] = jnp.zeros(router_pad.shape, BF)
    router_pad[:, 0 : router.shape[1]] = router[...]

    def attend(m):
        length = lengths[m, 0]
        for i in range(chunks):
            lanes = slice(i * LANES, (i + 1) * LANES)
            scores[...] = nt(queries[m, i], keyval[m, :, lanes])

            def strip_step(strip, carry):
                probs[rows_at(strip, STRIP), :] = softmax_rows(
                    masked_scores(scores, strip, rows, seq_len, row_base, length)
                ).astype(BF)
                return carry

            lax.fori_loop(0, 4 * rows // STRIP, strip_step, 0)
            mixed = nn(probs[...], keyval[m, :, kv + i * LANES : kv + (i + 1) * LANES])
            first, second = unstack_heads(mixed, rows)
            mixture[m, :, 2 * i * LANES : (2 * i + 1) * LANES] = first.astype(BF)
            mixture[m, :, (2 * i + 1) * LANES : (2 * i + 2) * LANES] = second.astype(BF)
        if m == 0:
            load_out.wait()
        live = (row_base + lax.broadcasted_iota(jnp.int32, (rows, 1), 0)) < length
        rows_hidden = tokens[m, 0].astype(F32) + jnp.where(
            live, nn(mixture[m], w_out[...]), 0.0
        )
        hidden[m] = rows_hidden
        rows_all[m, rows_at(z, rows), :] = (
            rows_hidden * rms_scale(rows_hidden) * gain_two[...]
        ).astype(BF)
        gather_rows[m].start(0)

    def gate_rows(m):
        logits = nn(rows_all[m], router_pad[...])
        on = named[m] > 0.0
        masked = jnp.where(on, logits, NEG_FILL)
        raised = jnp.where(on, jnp.exp(masked - jnp.max(masked, -1, keepdims=True)), 0.0)
        total = jnp.sum(raised, -1, keepdims=True)
        gates[...] = raised / jnp.where(total > 0.0, total, 1.0)

    def column(block, expert):
        return jnp.sum(
            jnp.where(lane_ids(block.shape[0]) == expert, block, 0.0), -1, keepdims=True
        )

    def expert_forward(m, j):
        expert = z * local + j
        wide[...] = nn(rows_all[m], w_gu[j])

        def strip_step(strip, carry):
            where = rows_at(strip, STRIP)
            gate = column(gates[where, :], expert)
            front, up = wide[where, 0:ff], wide[where, ff:]
            silu = front / (1.0 + jnp.exp(-front))
            acts[m, where, j * ff : (j + 1) * ff] = (silu * up * gate).astype(BF)
            d_proj[m * local + j, where, :] = wide[where, :].astype(BF)
            return carry

        lax.fori_loop(0, seq_len // STRIP, strip_step, 0)

    def expert_backward(m, j):
        expert = z * local + j
        narrow[...] = nt(cot_all[m], w_dn[j * ff : (j + 1) * ff, :])

        def strip_step(strip, carry):
            where = rows_at(strip, STRIP)
            gate = column(gates[where, :], expert)
            front = d_proj[m * local + j, where, 0:ff].astype(F32)
            up = d_proj[m * local + j, where, ff:].astype(F32)
            d_act = narrow[where, :]
            sigmoid = 1.0 / (1.0 + jnp.exp(-front))
            silu = front * sigmoid
            d_gate = jnp.sum(d_act * silu * up, -1, keepdims=True)
            d_prod = d_act * gate
            d_proj[m * local + j, where, 0:ff] = (
                d_prod * up * sigmoid * (1.0 + front * (1.0 - sigmoid))
            ).astype(BF)
            d_proj[m * local + j, where, ff:] = (d_prod * silu).astype(BF)
            lane = lane_ids(STRIP)
            mine = jnp.where(lane == expert, d_gate, 0.0) * named[m, where, :]
            if j == 0:
                in_parts[where, model:] = mine.astype(BF)
            else:
                in_parts[where, model:] = (
                    in_parts[where, model:].astype(F32) + mine
                ).astype(BF)
            return carry

        lax.fori_loop(0, seq_len // STRIP, strip_step, 0)
        for r in range(0, seq_len, tile):
            span = slice(r, r + tile)
            part = nt(d_proj[m * local + j, span, :], w_gu[j])
            if j == 0:
                back[span, :] = part
            elif j < local - 1:
                back[span, :] += part
            else:
                in_parts[span, 0:model] = (back[span, :] + part).astype(BF)

    def weight_grads(j):
        for part_of in range(4):
            lanes = slice(part_of * ff // 2, (part_of + 1) * ff // 2)
            total = None
            for m in range(micros):
                part = tn(rows_all[m], d_proj[m * local + j, :, lanes])
                total = part if total is None else total + part
            w_gu[j, :, lanes] = total.astype(BF)
        total = None
        for m in range(micros):
            part = tn(acts[m, :, j * ff : (j + 1) * ff], cot_all[m])
            total = part if total is None else total + part
        w_dn[j * ff : (j + 1) * ff, :] = total.astype(BF)

    steps = count - 1

    def run(*todo):
        for item in todo:
            item()

    def hops(gather, first=0, last=steps):
        for step in range(first, last):
            gather.hop(step)

    gather_kv[0].hop(0)
    gather_cot[0].hop(0)
    hops(gather_kv[0], 1)
    gather_kv[1].hop(0)
    attend(0)
    hops(gather_cot[0], 1)
    hops(gather_kv[1], 1)
    gather_rows[0].hop(0)
    attend(1)
    gather_cot[1].start(0)
    hops(gather_rows[0], 1)
    gather_rows[1].hop(0)

    load_gu.wait()
    load_dn.wait()
    queue = []

    def advance(amount=1):
        for _ in range(amount):
            if queue:
                queue.pop(0)()

    def finish_out(m):
        reduce_out[m].total(own_sum)
        y_out[m, 0] = (hidden[m] + own_sum[...]).astype(BF)
        reduce_out[m].finish()

    def finish_in(m):
        reduce_in[m].total(moe_sum.at[m])
        reduce_in[m].finish()

    def slots(reduce):
        return [functools.partial(reduce.slot, t) for t in range(count)]

    queue += [functools.partial(gather_cot[1].hop, 0)]
    for step in range(1, steps):
        queue += [functools.partial(gather_rows[1].hop, step)]
        queue += [functools.partial(gather_cot[1].hop, step)]
    for m in range(micros):
        if m == 1:
            while queue:
                advance()
            queue += slots(reduce_in[0]) + [functools.partial(finish_in, 0)]
        gate_rows(m)
        for j in range(local):
            expert_forward(m, j)
            advance()
        while queue:
            advance()
        for r in range(0, seq_len, tile):
            out_parts[r : r + tile, :] = nn(acts[m, r : r + tile, :], w_dn[...]).astype(BF)
        queue += slots(reduce_out[m]) + [functools.partial(finish_out, m)]
        for j in range(local):
            expert_backward(m, j)
            advance()
    while queue:
        advance()
    queue += slots(reduce_in[1]) + [functools.partial(finish_in, 1)]
    stores = []

    def store(src, dst):
        copy = pltpu.make_async_copy(src, dst, store_sems.at[len(stores)])
        copy.start()
        stores.append(copy)

    advance()
    for j in range(local):
        weight_grads(j)
        advance()
        store(w_gu.at[j], grad_gu_out.at[j])
        store(w_dn.at[pl.ds(j * ff, ff), :], grad_dn_out.at[pl.ds(j * ff, ff), :])
    while queue:
        advance()
    store(hidden, hidden_out)
    store(moe_sum, moe_out)
    store(queries, queries_out)
    store(keyval, keyval_out)
    store(mixture, mixture_out)
    for item in gather_kv + gather_rows + gather_cot:
        item.finish()
    for copy in stores:
        copy.wait()


def forward_call(
    count, tokens, lengths, routes, gain_one, w_query, w_keyval, w_out, gain_two, w_router,
    gate_up, down, cot,
):
    micros, _, rows, model = tokens.shape
    local, ff = gate_up.shape[0], down.shape[1]
    seq_len = routes.shape[2]
    kv = w_keyval.shape[1] // 2
    chunks = kv // LANES
    heads = w_query.shape[1]
    steps = count - 1
    split = -(-model // seq_len)
    cos, sin = rope_constants(seq_len)
    vmem = pl.BlockSpec(memory_space=pltpu.VMEM)
    smem = pl.BlockSpec(memory_space=pltpu.SMEM)
    hbm = pl.BlockSpec(memory_space=pl.ANY)
    dma = pltpu.SemaphoreType.DMA
    wide_in = model + LANES
    out_shape = (
        jax.ShapeDtypeStruct((micros, 1, rows, model), BF),
        jax.ShapeDtypeStruct((micros, rows, model), F32),
        jax.ShapeDtypeStruct((micros, rows, wide_in), F32),
        jax.ShapeDtypeStruct((micros, chunks, 4 * rows, LANES), BF),
        jax.ShapeDtypeStruct((micros, seq_len, 2 * kv), BF),
        jax.ShapeDtypeStruct((micros, rows, heads), BF),
        jax.ShapeDtypeStruct((local, model, 2 * ff), BF),
        jax.ShapeDtypeStruct((local * ff, model), BF),
    )
    scratch = [
        pltpu.VMEM((seq_len, model), F32),
        pltpu.VMEM((seq_len, ff), F32),
        pltpu.VMEM((micros * rows, model), BF),
        pltpu.VMEM((micros, chunks, 4 * rows, LANES), BF),
        pltpu.VMEM((micros, seq_len, 2 * kv), BF),
        pltpu.VMEM((micros, rows, heads), BF),
        pltpu.VMEM((micros, rows, model), F32),
        pltpu.VMEM((micros, seq_len, LANES), F32),
        pltpu.VMEM((seq_len, LANES), F32),
        pltpu.VMEM((model, LANES), BF),
        pltpu.VMEM((micros, seq_len, model), BF),
        pltpu.VMEM((micros, seq_len, model), BF),
        pltpu.VMEM((micros, seq_len, local * ff), BF),
        pltpu.VMEM((micros * local, seq_len, 2 * ff), BF),
        pltpu.VMEM(w_out.shape, BF),
        pltpu.VMEM((local, model, 2 * ff), BF),
        pltpu.VMEM((local * ff, model), BF),
        pltpu.VMEM((seq_len, model), BF),
        pltpu.VMEM((count + 1, rows, model), BF),
        pltpu.VMEM((seq_len, wide_in), BF),
        pltpu.VMEM((count + 1, rows, wide_in), BF),
        pltpu.VMEM((rows, model), F32),
        pltpu.VMEM((micros, rows, wide_in), F32),
    ] + [dma((micros, 2, 2, steps))] * 5 + [dma((2 * split + 3,)), dma((2 * local + 5,))]
    dims = (micros, rows, count, local, ff, model)
    return pl.pallas_call(
        functools.partial(forward_kernel, dims),
        out_shape=out_shape,
        in_specs=[smem] + [vmem] * 8 + [hbm] * 5,
        out_specs=(vmem,) + (hbm,) * 7,
        scratch_shapes=scratch,
        name="layer_forward",
        compiler_params=pltpu.CompilerParams(
            collective_id=0, has_side_effects=True, vmem_limit_bytes=VMEM_LIMIT
        ),
    )(
        lengths, tokens, cot, routes, gain_one.reshape(1, -1), gain_two.reshape(1, -1),
        jnp.asarray(cos), jnp.asarray(sin), w_router, w_query, w_keyval, w_out, gate_up,
        down.reshape(local * ff, model),
    )


def norm_backward(grad_normed, inputs, scale_rows, gain_vec):
    scaled = grad_normed * gain_vec
    gain_grad = jnp.sum(grad_normed * inputs * scale_rows, 0)
    input_part = scale_rows * (
        scaled - inputs * scale_rows * scale_rows * jnp.mean(scaled * inputs, -1, keepdims=True)
    )
    return (input_part, gain_grad)


def plain_rope(rows, cos, sin):
    width = rows.shape[1]
    cos, sin = jnp.tile(cos, (1, width // LANES)), jnp.tile(sin, (1, width // LANES))
    grouped = rows.reshape(rows.shape[0], -1, 2, HEAD_DIM // 2)
    return rows * cos + grouped[:, :, ::-1].reshape(rows.shape) * sin


def on_device(
    tokens, lengths, routes, attn_gain, w_query, w_keyval, w_out, ffn_gain, w_router,
    expert_gate_up, expert_down, cotangent,
):
    count = lax.axis_size("expert")
    z = lax.axis_index("expert")
    micros, _, rows, model = tokens.shape
    seq_len = routes.shape[2]
    experts = w_router.shape[1]
    local, ff = expert_gate_up.shape[0], expert_down.shape[1]
    kv = w_keyval.shape[1] // 2
    chunks = kv // LANES
    y, hidden, moe, queries, keyval, mixture, grad_gu, grad_dn = forward_call(
        count, tokens, lengths, routes, attn_gain, w_query, w_keyval, w_out, ffn_gain, w_router,
        expert_gate_up, expert_down, cotangent,
    )
    cos, sin = rope_constants(seq_len)
    cos = lax.dynamic_slice_in_dim(jnp.asarray(cos), z * rows, rows, 0)
    sin = lax.dynamic_slice_in_dim(jnp.asarray(sin), z * rows, rows, 0)
    local_pos = z * rows + jnp.arange(rows, dtype=jnp.int32)
    all_pos = jnp.arange(seq_len, dtype=jnp.int32)
    low = jnp.arange(LANES) < HEAD_DIM
    roll = lambda v: jnp.roll(v, HEAD_DIM, -1)
    sums = [0.0] * 6
    input_grads = []
    for m in range(micros):
        length = lengths[m, 0]
        live = (local_pos < length)[:, None]
        x_rows = tokens[m, 0].astype(F32)
        scale_one = rms_scale(x_rows)
        normed = (x_rows * scale_one * attn_gain).astype(BF)
        scale_two = rms_scale(hidden[m])
        normed2 = (hidden[m] * scale_two * ffn_gain).astype(BF)
        logits = nn(normed2, w_router)
        ids = lax.dynamic_slice_in_dim(routes[m, 0], z * rows, rows, 0)
        named = (ids[:, :, None] == jnp.arange(experts)).any(1) & live
        masked = jnp.where(named, logits, NEG_FILL)
        raised = jnp.where(named, jnp.exp(masked - masked.max(-1, keepdims=True)), 0.0)
        total = raised.sum(-1, keepdims=True)
        gate = raised / jnp.where(total > 0, total, 1.0)
        d_gate = moe[m, :, model : model + experts]
        d_logits = (gate * (d_gate - jnp.sum(gate * d_gate, -1, keepdims=True))).astype(BF)
        d_normed2 = moe[m, :, :model] + nt(d_logits, w_router)
        part, gain_two = norm_backward(d_normed2, hidden[m], scale_two, ffn_gain)
        d_hidden = cotangent[m, 0].astype(F32) + part
        d_attn = jnp.where(live, d_hidden, 0.0).astype(BF)
        d_mix = nt(d_attn, w_out).astype(BF)
        d_query, d_key, d_value = [], [], []
        for i in range(chunks):
            lanes = slice(i * LANES, (i + 1) * LANES)
            key, value = keyval[m, :, lanes], keyval[m, :, kv + i * LANES : kv + (i + 1) * LANES]
            first, second = (
                d_mix[:, c * LANES : (c + 1) * LANES] for c in (2 * i, 2 * i + 1)
            )
            d_stack = jnp.concatenate(
                [
                    jnp.where(low, first, 0), jnp.where(low, roll(first), 0),
                    jnp.where(low, 0, roll(second)), jnp.where(low, 0, second),
                ]
            ).astype(BF)
            s = nt(queries[m, i], key) * ATTENTION_SCALE
            ok = (all_pos[None, :] <= jnp.tile(local_pos, 4)[:, None]) & (all_pos < length)[None, :]
            prob = jax.nn.softmax(jnp.where(ok, s, NEG_FILL), axis=-1)
            d_prob = nt(d_stack, value)
            d_scores = (prob * (d_prob - jnp.sum(prob * d_prob, -1, keepdims=True))).astype(BF)
            dq = nn(d_scores, key) * ATTENTION_SCALE
            d_key.append(tn(d_scores, queries[m, i]) * ATTENTION_SCALE)
            d_value.append(tn(prob.astype(BF), d_stack))
            q = [dq[k * rows : (k + 1) * rows] for k in range(4)]
            d_query += [jnp.where(low, q[0], roll(q[1])), jnp.where(low, roll(q[2]), q[3])]
        d_query = plain_rope(jnp.concatenate(d_query, 1), cos, -sin).astype(BF)
        d_kv = lax.psum_scatter(
            jnp.concatenate(d_key + d_value, 1).astype(BF), "expert", scatter_dimension=0, tiled=True
        ).astype(F32)
        d_kv = jnp.concatenate([plain_rope(d_kv[:, :kv], cos, -sin), d_kv[:, kv:]], 1).astype(BF)
        d_normed = nt(d_query, w_query) + nt(d_kv, w_keyval)
        part, gain_one = norm_backward(d_normed, x_rows, scale_one, attn_gain)
        input_grads.append(d_hidden + part)
        terms = (
            gain_one, tn(normed, d_query), tn(normed, d_kv), tn(mixture[m], d_attn), gain_two,
            tn(normed2, d_logits),
        )
        sums = [a + b for a, b in zip(sums, terms)]
    both = ("dp", "expert")
    scatter = lambda v: lax.psum_scatter(v, both, scatter_dimension=0, tiled=True)
    dense = [
        scatter(v if k in (0, 4, 5) else v.astype(BF)).astype(F32) for k, v in enumerate(sums)
    ]
    spread = lambda v: lax.psum_scatter(v, "dp", scatter_dimension=1, tiled=True).astype(F32)
    return (
        y, jnp.stack(input_grads)[:, None], *dense, spread(grad_gu),
        spread(grad_dn.reshape(local, ff, model)),
    )


def solution(mesh):
    placed = (
        P(None, "dp", "expert", None), P(None, "dp"), P(None, "dp", None, None), P(), P(), P(), P(),
        P(), P(), P("expert", None, None), P("expert", None, None), P(None, "dp", "expert", None),
    )
    return jax.shard_map(
        on_device,
        mesh=mesh,
        in_specs=placed,
        out_specs=(
            P(None, "dp", "expert", None), P(None, "dp", "expert", None), P(("dp", "expert")),
            P(("dp", "expert"), None), P(("dp", "expert"), None), P(("dp", "expert"), None),
            P(("dp", "expert")), P(("dp", "expert"), None), P("expert", "dp", None),
            P("expert", "dp", None),
        ),
        check_vma=False,
    )
```

```python
import functools
import math

import jax
import jax.numpy as jnp
import numpy as np
from jax import lax
from jax.experimental import pallas as pl
from jax.experimental.pallas import tpu as pltpu
from jax.sharding import PartitionSpec as P

HEAD_DIM = 64
EPS = 1e-06
ATTENTION_SCALE = 0.015625
ROPE_BASE = 10000.0
NEG_FILL = -1e30
LANES = 128
STRIP = 16
BF = jnp.bfloat16
F32 = jnp.float32
VMEM_LIMIT = 63 * 2**20


def dot_of(left, right, left_dim, right_dim):
    return lax.dot_general(
        left, right, (((left_dim,), (right_dim,)), ((), ())), preferred_element_type=F32
    )


def nn(left, right):
    return dot_of(left, right, 1, 0)


def nt(left, right):
    return dot_of(left, right, 1, 1)


def tn(left, right):
    return dot_of(left, right, 0, 0)


def rope_constants(seq_len):
    half = HEAD_DIM // 2
    frequency = np.exp(
        np.arange(half, dtype=np.float32) * np.float32(-2.0 * math.log(ROPE_BASE) / HEAD_DIM)
    ).astype(np.float32)
    angles = np.arange(seq_len, dtype=np.float32)[:, None] * frequency[None, :]
    cos, sin = np.cos(angles).astype(np.float32), np.sin(angles).astype(np.float32)
    heads = LANES // HEAD_DIM
    return np.tile(np.concatenate([cos, cos], 1), (1, heads)), np.tile(
        np.concatenate([-sin, sin], 1), (1, heads)
    )


def lane_ids(rows):
    return lax.broadcasted_iota(jnp.int32, (rows, LANES), 1)


def swap_halves(chunk):
    half = HEAD_DIM // 2
    first = lax.rem(lane_ids(chunk.shape[0]), HEAD_DIM) < half
    return jnp.where(
        first, pltpu.roll(chunk, LANES - half, 1), pltpu.roll(chunk, half, 1)
    )


def rope(chunk, cos, sin):
    return chunk * cos + swap_halves(chunk) * sin


def rms_scale(rows):
    return lax.rsqrt(jnp.mean(rows * rows, -1, keepdims=True) + EPS)


def stack_heads(first, second):
    low = lane_ids(first.shape[0]) < HEAD_DIM
    zero = jnp.zeros_like(first)
    return [
        jnp.where(low, first, zero),
        jnp.where(low, pltpu.roll(first, HEAD_DIM, 1), zero),
        jnp.where(low, zero, pltpu.roll(second, HEAD_DIM, 1)),
        jnp.where(low, zero, second),
    ]


def unstack_heads(stacked, rows):
    low = lane_ids(rows) < HEAD_DIM
    parts = [stacked[k * rows : (k + 1) * rows] for k in range(4)]
    first = jnp.where(low, parts[0], pltpu.roll(parts[1], HEAD_DIM, 1))
    second = jnp.where(low, pltpu.roll(parts[2], HEAD_DIM, 1), parts[3])
    return first, second


def rows_at(index, rows):
    return pl.ds(pl.multiple_of(index * rows, rows), rows)


class Gather:
    def __init__(self, buffer, micro, rows, count, sems, up=True, down=True):
        self.buffer, self.micro, self.rows, self.count, self.sems = buffer, micro, rows, count, sems
        self.ways = [w for w, on in ((0, up), (1, down)) if on]

    def copy(self, way, step, block):
        z = lax.axis_index("expert")
        target = z + 1 if way == 0 else z - 1
        view = self.buffer.at[self.micro, rows_at(block, self.rows), :]
        return pltpu.make_async_remote_copy(
            src_ref=view,
            dst_ref=view,
            send_sem=self.sems.at[0, way, step],
            recv_sem=self.sems.at[1, way, step],
            device_id={"expert": target},
            device_id_type=pl.DeviceIdType.MESH,
        )

    def sends(self, way, step):
        z = lax.axis_index("expert")
        if way == 0:
            return z - step, jnp.logical_and(z < self.count - 1, z - step >= 0)
        return z + step, jnp.logical_and(z > 0, z + step <= self.count - 1)

    def receives(self, way, step):
        z = lax.axis_index("expert")
        if way == 0:
            return z - 1 - step, z - 1 - step >= 0
        return z + 1 + step, z + 1 + step <= self.count - 1

    def start(self, step):
        for way in self.ways:
            block, on = self.sends(way, step)

            @pl.when(on)
            def _(way=way, block=block):
                self.copy(way, step, block).start()

    def wait(self, step):
        for way in self.ways:
            block, on = self.receives(way, step)

            @pl.when(on)
            def _(way=way, block=block):
                self.copy(way, step, block).wait_recv()

    def hop(self, step):
        self.wait(step)
        if step + 1 < self.count - 1:
            self.start(step + 1)

    def finish(self):
        for step in range(self.count - 1):
            for way in self.ways:
                block, on = self.sends(way, step)

                @pl.when(on)
                def _(way=way, step=step, block=block):
                    self.copy(way, step, block).wait_send()


class Reduce:
    def __init__(self, parts, landing, rows, count, sems, up=True, down=True):
        self.parts, self.landing = parts, landing
        self.rows, self.count, self.sems = rows, count, sems
        self.ways = [w for w, on in ((0, up), (1, down)) if on]

    def block(self, way, slot):
        z = lax.axis_index("expert")
        if way == 0:
            return z + self.count - 1 - slot, slot >= z
        return z - (self.count - 1) + slot, slot >= self.count - 1 - z

    def place(self, way, slot, z):
        if way == 0:
            return slot - (z - 1)
        return self.count - (slot - (self.count - 2 - z)) - (2 if self.ways == [1] else 0)

    def copy(self, way, slot, block):
        z = lax.axis_index("expert")
        target = z + 1 if way == 0 else z - 1
        return pltpu.make_async_remote_copy(
            src_ref=self.parts.at[rows_at(block, self.rows), :],
            dst_ref=self.landing.at[self.place(way, slot, target)],
            send_sem=self.sems.at[0, way, slot],
            recv_sem=self.sems.at[1, way, slot],
            device_id={"expert": target},
            device_id_type=pl.DeviceIdType.MESH,
        )

    def arrival(self, way, slot, block):
        z = lax.axis_index("expert")
        source = z - 1 if way == 0 else z + 1
        return pltpu.make_async_remote_copy(
            src_ref=self.parts.at[rows_at(block, self.rows), :],
            dst_ref=self.landing.at[self.place(way, slot, z)],
            send_sem=self.sems.at[0, way, slot],
            recv_sem=self.sems.at[1, way, slot],
            device_id={"expert": source},
            device_id_type=pl.DeviceIdType.MESH,
        )

    def inner(self, way):
        z = lax.axis_index("expert")
        return z >= 1 if way == 0 else z <= self.count - 2

    def slot(self, slot):
        z = lax.axis_index("expert")
        for way in self.ways:
            block, on = self.block(way, slot)
            if slot >= 1:

                @pl.when(jnp.logical_and(on, self.inner(way)))
                def _(way=way, block=block):
                    self.arrival(way, slot - 1, block).wait_recv()
                    if slot < self.count - 1:
                        where = rows_at(block, self.rows)
                        total = self.parts[where, :].astype(F32) + self.landing[
                            self.place(way, slot - 1, z)
                        ].astype(F32)
                        self.parts[where, :] = total.astype(self.parts.dtype)

            if slot < self.count - 1:

                @pl.when(on)
                def _(way=way, block=block):
                    self.copy(way, slot, block).start()

    def total(self, out):
        z = lax.axis_index("expert")
        out[...] = self.parts[rows_at(z, self.rows), :].astype(F32)
        for way in self.ways:

            @pl.when(self.inner(way))
            def _(way=way):
                out[...] += self.landing[self.place(way, self.count - 2, z)].astype(F32)

    def finish(self):
        for slot in range(self.count - 1):
            for way in self.ways:
                block, on = self.block(way, slot)

                @pl.when(on)
                def _(way=way, slot=slot, block=block):
                    self.copy(way, slot, block).wait_send()


def line_barrier(count):
    z = lax.axis_index("expert")
    barrier = pltpu.get_barrier_semaphore()
    for target, on in ((z + 1, z < count - 1), (z - 1, z > 0)):

        @pl.when(on)
        def _(target=target):
            pl.semaphore_signal(
                barrier, inc=1, device_id={"expert": target}, device_id_type=pl.DeviceIdType.MESH
            )

    pl.semaphore_wait(barrier, (z > 0).astype(jnp.int32) + (z < count - 1).astype(jnp.int32))


def masked_scores(scores_ref, strip, rows, seq_len, row_base, length):
    where = rows_at(strip, STRIP)
    shape = (STRIP, seq_len)
    first = row_base + lax.rem(strip * STRIP, rows)
    query_pos = first + lax.broadcasted_iota(jnp.int32, shape, 0)
    key_pos = lax.broadcasted_iota(jnp.int32, shape, 1)
    allowed = jnp.logical_and(key_pos <= query_pos, key_pos < length)
    return jnp.where(allowed, scores_ref[where, :] * ATTENTION_SCALE, NEG_FILL)


def softmax_rows(scores):
    top = jnp.max(scores, -1, keepdims=True)
    raised = jnp.exp(scores - top)
    return raised / jnp.sum(raised, -1, keepdims=True)


def forward_kernel(
    dims,
    lengths,
    tokens,
    cot,
    routes,
    gain_one,
    gain_two,
    cos_ref,
    sin_ref,
    router,
    query_hbm,
    keyval_hbm,
    out_hbm,
    gate_up_hbm,
    down_hbm,
    y_out,
    hidden_out,
    moe_out,
    queries_out,
    keyval_out,
    mixture_out,
    grad_gu_out,
    grad_dn_out,
    wide,
    narrow,
    normed,
    queries,
    keyval,
    mixture,
    hidden,
    named,
    gates,
    router_pad,
    rows_all,
    cot_all,
    acts,
    d_proj,
    w_out,
    w_gu,
    w_dn,
    out_parts,
    out_land,
    in_parts,
    in_land,
    own_sum,
    moe_sum,
    kv_sems,
    rows_sems,
    cot_sems,
    out_sems,
    in_sems,
    load_sems,
    store_sems,
):
    micros, rows, count, local, ff, model = dims
    seq_len = count * rows
    kv = keyval.shape[2] // 2
    chunks = kv // LANES
    z = lax.axis_index("expert")
    row_base = z * rows
    split = -(-model // seq_len)
    piece = model // split
    back = wide
    scores = wide.at[0 : 4 * rows, 0:seq_len]
    probs = d_proj.at[micros * local - 1, 0 : 4 * rows, 0:seq_len]
    tile = 512

    loads = []

    def load(src, dst):
        copy = pltpu.make_async_copy(src, dst, load_sems.at[len(loads)])
        copy.start()
        loads.append(copy)
        return copy

    early = []
    for index, weight in enumerate((query_hbm, keyval_hbm)):
        early.append(
            [
                load(
                    weight.at[pl.ds(k * piece, piece), :],
                    d_proj.at[index * split + k, pl.ds(0, piece), :],
                )
                for k in range(split)
            ]
        )
    load_out = load(out_hbm, w_out)
    load_gu = load(gate_up_hbm, w_gu)
    load_dn = load(down_hbm, w_dn)

    line_barrier(count)

    gather_kv = [
        Gather(keyval, m, rows, count, kv_sems.at[m], down=False) for m in range(micros)
    ]
    gather_rows = [Gather(rows_all, m, rows, count, rows_sems.at[m]) for m in range(micros)]
    gather_cot = [Gather(cot_all, m, rows, count, cot_sems.at[m]) for m in range(micros)]
    reduce_out = [
        Reduce(out_parts, out_land, rows, count, out_sems.at[m]) for m in range(micros)
    ]
    reduce_in = [Reduce(in_parts, in_land, rows, count, in_sems.at[m]) for m in range(micros)]

    for m in range(micros):
        cot_all[m, rows_at(z, rows), :] = cot[m, 0]
    gather_cot[0].start(0)

    for m in range(micros):
        x_rows = tokens[m, 0].astype(F32)
        normed[m * rows : (m + 1) * rows, :] = (
            x_rows * rms_scale(x_rows) * gain_one[...]
        ).astype(BF)
    cos = cos_ref[rows_at(z, rows), :]
    sin = sin_ref[rows_at(z, rows), :]
    both = micros * rows

    def project(index):
        for copy in early[index]:
            copy.wait()
        total = None
        for k in range(split):
            part = nn(
                normed[:, k * piece : (k + 1) * piece], d_proj[index * split + k, 0:piece, :]
            )
            total = part if total is None else total + part
        wide[0:both, :] = total

    project(1)
    for m in range(micros):
        span = slice(m * rows, (m + 1) * rows)
        for c in range(chunks):
            lanes = slice(c * LANES, (c + 1) * LANES)
            keyval[m, rows_at(z, rows), lanes] = rope(wide[span, lanes], cos, sin).astype(BF)
        keyval[m, rows_at(z, rows), kv:] = wide[span, kv:].astype(BF)
        gather_kv[m].start(0)
        for b in range(count):

            @pl.when(b > z)
            def _(m=m, b=b):
                keyval[m, b * rows : (b + 1) * rows, :] = jnp.zeros((rows, 2 * kv), BF)

    project(0)
    for m in range(micros):
        span = slice(m * rows, (m + 1) * rows)
        for i in range(chunks):
            pair = [
                rope(wide[span, c * LANES : (c + 1) * LANES], cos, sin)
                for c in (2 * i, 2 * i + 1)
            ]
            for k, block in enumerate(stack_heads(*pair)):
                queries[m, i, k * rows : (k + 1) * rows, :] = block.astype(BF)

    for m in range(micros):
        lane = lane_ids(seq_len)
        hit = jnp.zeros((seq_len, LANES), F32)
        for k in range(routes.shape[3]):
            hit = hit + (routes[m, 0][:, k : k + 1] == lane).astype(F32)
        live = lax.broadcasted_iota(jnp.int32, (seq_len, LANES), 0) < lengths[m, 0]
        named[m] = jnp.where(live, hit, 0.0)
    router_pad[...] = jnp.zeros(router_pad.shape, BF)
    router_pad[:, 0 : router.shape[1]] = router[...]

    def attend(m):
        length = lengths[m, 0]
        for i in range(chunks):
            lanes = slice(i * LANES, (i + 1) * LANES)
            scores[...] = nt(queries[m, i], keyval[m, :, lanes])

            def strip_step(strip, carry):
                probs[rows_at(strip, STRIP), :] = softmax_rows(
                    masked_scores(scores, strip, rows, seq_len, row_base, length)
                ).astype(BF)
                return carry

            lax.fori_loop(0, 4 * rows // STRIP, strip_step, 0)
            mixed = nn(probs[...], keyval[m, :, kv + i * LANES : kv + (i + 1) * LANES])
            first, second = unstack_heads(mixed, rows)
            mixture[m, :, 2 * i * LANES : (2 * i + 1) * LANES] = first.astype(BF)
            mixture[m, :, (2 * i + 1) * LANES : (2 * i + 2) * LANES] = second.astype(BF)
        if m == 0:
            load_out.wait()
        live = (row_base + lax.broadcasted_iota(jnp.int32, (rows, 1), 0)) < length
        rows_hidden = tokens[m, 0].astype(F32) + jnp.where(
            live, nn(mixture[m], w_out[...]), 0.0
        )
        hidden[m] = rows_hidden
        rows_all[m, rows_at(z, rows), :] = (
            rows_hidden * rms_scale(rows_hidden) * gain_two[...]
        ).astype(BF)
        gather_rows[m].start(0)

    def gate_rows(m):
        logits = nn(rows_all[m], router_pad[...])
        on = named[m] > 0.0
        masked = jnp.where(on, logits, NEG_FILL)
        raised = jnp.where(on, jnp.exp(masked - jnp.max(masked, -1, keepdims=True)), 0.0)
        total = jnp.sum(raised, -1, keepdims=True)
        gates[...] = raised / jnp.where(total > 0.0, total, 1.0)

    def column(block, expert):
        return jnp.sum(
            jnp.where(lane_ids(block.shape[0]) == expert, block, 0.0), -1, keepdims=True
        )

    def expert_forward(m, j):
        expert = z * local + j
        wide[...] = nn(rows_all[m], w_gu[j])

        def strip_step(strip, carry):
            where = rows_at(strip, STRIP)
            gate = column(gates[where, :], expert)
            front, up = wide[where, 0:ff], wide[where, ff:]
            silu = front / (1.0 + jnp.exp(-front))
            acts[m, where, j * ff : (j + 1) * ff] = (silu * up * gate).astype(BF)
            d_proj[m * local + j, where, :] = wide[where, :].astype(BF)
            return carry

        lax.fori_loop(0, seq_len // STRIP, strip_step, 0)

    def expert_backward(m, j):
        expert = z * local + j
        narrow[...] = nt(cot_all[m], w_dn[j * ff : (j + 1) * ff, :])

        def strip_step(strip, carry):
            where = rows_at(strip, STRIP)
            gate = column(gates[where, :], expert)
            front = d_proj[m * local + j, where, 0:ff].astype(F32)
            up = d_proj[m * local + j, where, ff:].astype(F32)
            d_act = narrow[where, :]
            sigmoid = 1.0 / (1.0 + jnp.exp(-front))
            silu = front * sigmoid
            d_gate = jnp.sum(d_act * silu * up, -1, keepdims=True)
            d_prod = d_act * gate
            d_proj[m * local + j, where, 0:ff] = (
                d_prod * up * sigmoid * (1.0 + front * (1.0 - sigmoid))
            ).astype(BF)
            d_proj[m * local + j, where, ff:] = (d_prod * silu).astype(BF)
            lane = lane_ids(STRIP)
            mine = jnp.where(lane == expert, d_gate, 0.0) * named[m, where, :]
            if j == 0:
                in_parts[where, model:] = mine.astype(BF)
            else:
                in_parts[where, model:] = (
                    in_parts[where, model:].astype(F32) + mine
                ).astype(BF)
            return carry

        lax.fori_loop(0, seq_len // STRIP, strip_step, 0)
        for r in range(0, seq_len, tile):
            span = slice(r, r + tile)
            part = nt(d_proj[m * local + j, span, :], w_gu[j])
            if j == 0:
                back[span, :] = part
            elif j < local - 1:
                back[span, :] += part
            else:
                in_parts[span, 0:model] = (back[span, :] + part).astype(BF)

    def weight_grads(j):
        for part_of in range(4):
            lanes = slice(part_of * ff // 2, (part_of + 1) * ff // 2)
            total = None
            for m in range(micros):
                part = tn(rows_all[m], d_proj[m * local + j, :, lanes])
                total = part if total is None else total + part
            w_gu[j, :, lanes] = total.astype(BF)
        total = None
        for m in range(micros):
            part = tn(acts[m, :, j * ff : (j + 1) * ff], cot_all[m])
            total = part if total is None else total + part
        w_dn[j * ff : (j + 1) * ff, :] = total.astype(BF)

    steps = count - 1

    def run(*todo):
        for item in todo:
            item()

    def hops(gather, first=0, last=steps):
        for step in range(first, last):
            gather.hop(step)

    gather_kv[0].hop(0)
    gather_cot[0].hop(0)
    hops(gather_kv[0], 1)
    gather_kv[1].hop(0)
    attend(0)
    hops(gather_cot[0], 1)
    hops(gather_kv[1], 1)
    gather_rows[0].hop(0)
    attend(1)
    gather_cot[1].start(0)
    hops(gather_rows[0], 1)
    gather_rows[1].hop(0)

    load_gu.wait()
    load_dn.wait()
    queue = []

    def advance(amount=1):
        for _ in range(amount):
            if queue:
                queue.pop(0)()

    def finish_out(m):
        reduce_out[m].total(own_sum)
        y_out[m, 0] = (hidden[m] + own_sum[...]).astype(BF)
        reduce_out[m].finish()

    def finish_in(m):
        reduce_in[m].total(moe_sum.at[m])
        reduce_in[m].finish()

    def slots(reduce):
        return [functools.partial(reduce.slot, t) for t in range(count)]

    queue += [functools.partial(gather_cot[1].hop, 0)]
    for step in range(1, steps):
        queue += [functools.partial(gather_rows[1].hop, step)]
        queue += [functools.partial(gather_cot[1].hop, step)]
    for m in range(micros):
        if m == 1:
            while queue:
                advance()
            queue += slots(reduce_in[0]) + [functools.partial(finish_in, 0)]
        gate_rows(m)
        for j in range(local):
            expert_forward(m, j)
            advance()
        while queue:
            advance()
        for r in range(0, seq_len, tile):
            out_parts[r : r + tile, :] = nn(acts[m, r : r + tile, :], w_dn[...]).astype(BF)
        queue += slots(reduce_out[m]) + [functools.partial(finish_out, m)]
        for j in range(local):
            expert_backward(m, j)
            advance()
    while queue:
        advance()
    queue += slots(reduce_in[1]) + [functools.partial(finish_in, 1)]
    stores = []

    def store(src, dst):
        copy = pltpu.make_async_copy(src, dst, store_sems.at[len(stores)])
        copy.start()
        stores.append(copy)

    advance()
    for j in range(local):
        weight_grads(j)
        advance()
        store(w_gu.at[j], grad_gu_out.at[j])
        store(w_dn.at[pl.ds(j * ff, ff), :], grad_dn_out.at[pl.ds(j * ff, ff), :])
    while queue:
        advance()
    store(hidden, hidden_out)
    store(moe_sum, moe_out)
    store(queries, queries_out)
    store(keyval, keyval_out)
    store(mixture, mixture_out)
    for item in gather_kv + gather_rows + gather_cot:
        item.finish()
    for copy in stores:
        copy.wait()


def forward_call(
    count, tokens, lengths, routes, gain_one, w_query, w_keyval, w_out, gain_two, w_router,
    gate_up, down, cot,
):
    micros, _, rows, model = tokens.shape
    local, ff = gate_up.shape[0], down.shape[1]
    seq_len = routes.shape[2]
    kv = w_keyval.shape[1] // 2
    chunks = kv // LANES
    heads = w_query.shape[1]
    steps = count - 1
    split = -(-model // seq_len)
    cos, sin = rope_constants(seq_len)
    vmem = pl.BlockSpec(memory_space=pltpu.VMEM)
    smem = pl.BlockSpec(memory_space=pltpu.SMEM)
    hbm = pl.BlockSpec(memory_space=pl.ANY)
    dma = pltpu.SemaphoreType.DMA
    wide_in = model + LANES
    out_shape = (
        jax.ShapeDtypeStruct((micros, 1, rows, model), BF),
        jax.ShapeDtypeStruct((micros, rows, model), F32),
        jax.ShapeDtypeStruct((micros, rows, wide_in), F32),
        jax.ShapeDtypeStruct((micros, chunks, 4 * rows, LANES), BF),
        jax.ShapeDtypeStruct((micros, seq_len, 2 * kv), BF),
        jax.ShapeDtypeStruct((micros, rows, heads), BF),
        jax.ShapeDtypeStruct((local, model, 2 * ff), BF),
        jax.ShapeDtypeStruct((local * ff, model), BF),
    )
    scratch = [
        pltpu.VMEM((seq_len, model), F32),
        pltpu.VMEM((seq_len, ff), F32),
        pltpu.VMEM((micros * rows, model), BF),
        pltpu.VMEM((micros, chunks, 4 * rows, LANES), BF),
        pltpu.VMEM((micros, seq_len, 2 * kv), BF),
        pltpu.VMEM((micros, rows, heads), BF),
        pltpu.VMEM((micros, rows, model), F32),
        pltpu.VMEM((micros, seq_len, LANES), F32),
        pltpu.VMEM((seq_len, LANES), F32),
        pltpu.VMEM((model, LANES), BF),
        pltpu.VMEM((micros, seq_len, model), BF),
        pltpu.VMEM((micros, seq_len, model), BF),
        pltpu.VMEM((micros, seq_len, local * ff), BF),
        pltpu.VMEM((micros * local, seq_len, 2 * ff), BF),
        pltpu.VMEM(w_out.shape, BF),
        pltpu.VMEM((local, model, 2 * ff), BF),
        pltpu.VMEM((local * ff, model), BF),
        pltpu.VMEM((seq_len, model), BF),
        pltpu.VMEM((count + 1, rows, model), BF),
        pltpu.VMEM((seq_len, wide_in), BF),
        pltpu.VMEM((count + 1, rows, wide_in), BF),
        pltpu.VMEM((rows, model), F32),
        pltpu.VMEM((micros, rows, wide_in), F32),
    ] + [dma((micros, 2, 2, steps))] * 5 + [dma((2 * split + 3,)), dma((2 * local + 5,))]
    dims = (micros, rows, count, local, ff, model)
    return pl.pallas_call(
        functools.partial(forward_kernel, dims),
        out_shape=out_shape,
        in_specs=[smem] + [vmem] * 8 + [hbm] * 5,
        out_specs=(vmem,) + (hbm,) * 7,
        scratch_shapes=scratch,
        name="layer_forward",
        compiler_params=pltpu.CompilerParams(
            collective_id=0, has_side_effects=True, vmem_limit_bytes=VMEM_LIMIT
        ),
    )(
        lengths, tokens, cot, routes, gain_one.reshape(1, -1), gain_two.reshape(1, -1),
        jnp.asarray(cos), jnp.asarray(sin), w_router, w_query, w_keyval, w_out, gate_up,
        down.reshape(local * ff, model),
    )


def plane_of(devices):
    side = math.isqrt(devices // 2)
    return side, side


def device_at(plane, y, x, core):
    return {"dp": (y * plane[1] + x) * 2 + core}


class PlaneReduce:
    def __init__(self, plane, source, own, total, first_land, second_land, x_first, sems, local=None):
        self.plane, self.source, self.own, self.total = plane, source, own, total
        self.lands, self.x_first, self.sems, self.local = (first_land, second_land), x_first, sems, local
        index = lax.axis_index("dp")
        self.core = lax.rem(index, 2)
        chip = index // 2
        self.y, self.x = chip // plane[1], lax.rem(chip, plane[1])

    def remote(self, src, dst, number, where):
        return pltpu.make_async_remote_copy(
            src_ref=src,
            dst_ref=dst,
            send_sem=self.sems.at[0, number],
            recv_sem=self.sems.at[1, number],
            device_id=device_at(self.plane, *where),
            device_id_type=pl.DeviceIdType.MESH,
        )

    def sibling(self):
        return self.remote(
            self.source.at[:, :, 1 - self.core], self.total, 0, (self.y, self.x, 1 - self.core)
        )

    def start(self):
        self.sibling().start()

    def along(self, stage):
        return self.x_first == (stage == 0)

    def hops(self, stage):
        along_x = self.along(stage)
        size = self.plane[1] if along_x else self.plane[0]
        base = 1 if stage == 0 else self.plane[1] if self.x_first else self.plane[0]
        for k in range(1, size):
            if along_x:
                place = lax.rem(self.x + k, size)
                where = (self.y, place, self.core)
                view = (
                    self.total.at[:, place] if stage == 0 else self.total.at[self.y, place]
                )
            else:
                place = lax.rem(self.y + k, size)
                where = (place, self.x, self.core)
                view = self.total.at[place] if stage == 0 else self.total.at[place, self.x]
            yield k, self.remote(view, self.lands[stage].at[k - 1], base + k - 1, where)

    def send(self, stage):
        for _, copy in self.hops(stage):
            copy.start()

    def pair_sum(self):
        if self.local is not None:
            self.local.wait()
        self.sibling().wait_recv()
        count = self.plane[0] * self.plane[1]
        for b in range(count):
            y, x = b // self.plane[1], b % self.plane[1]
            own = self.own[y, x] if self.local is not None else self.source[y, x, self.core]
            self.total[y, x] = (self.total[y, x].astype(F32) + own.astype(F32)).astype(BF)

    def take(self, stage):
        land = self.lands[stage]
        for k, copy in self.hops(stage):
            copy.wait_recv()
        if stage == 0:
            for other in range(self.plane[0] if self.x_first else self.plane[1]):
                where = (other, self.x) if self.x_first else (self.y, other)
                summed = self.total[where].astype(F32)
                for k in range(land.shape[0]):
                    summed = summed + land[k, other].astype(F32)
                self.total[where] = summed.astype(BF)
            return None
        summed = self.total[self.y, self.x].astype(F32)
        for k in range(land.shape[0]):
            summed = summed + land[k].astype(F32)
        return summed

    def finish(self):
        self.sibling().wait_send()
        for stage in range(2):
            for _, copy in self.hops(stage):
                copy.wait_send()


class LineReduce:
    def __init__(self, parts, land, rows, count, sems):
        self.parts, self.land, self.rows, self.count, self.sems = parts, land, rows, count, sems
        self.group = max(rows, STRIP)

    def span(self, z):
        if self.group == self.rows:
            return rows_at(z, self.rows)
        return pl.ds(pl.multiple_of(z * self.rows // self.group * self.group, self.group), self.group)

    def hops(self):
        z = lax.axis_index("expert")
        for k in range(1, self.count):
            target = lax.rem(z + k, self.count)
            yield k, pltpu.make_async_remote_copy(
                src_ref=self.parts.at[self.span(target), :],
                dst_ref=self.land.at[k - 1],
                send_sem=self.sems.at[0, k - 1],
                recv_sem=self.sems.at[1, k - 1],
                device_id={"expert": target},
                device_id_type=pl.DeviceIdType.MESH,
            )

    def start(self):
        for _, copy in self.hops():
            copy.start()

    def total(self):
        for _, copy in self.hops():
            copy.wait_recv()
        summed = self.parts[self.span(lax.axis_index("expert")), :].astype(F32)
        for k in range(self.count - 1):
            summed = summed + self.land[k].astype(F32)
        return summed

    def finish(self):
        for _, copy in self.hops():
            copy.wait_send()


def full_barrier(plane, count):
    index = lax.axis_index("dp")
    z = lax.axis_index("expert")
    core, chip = lax.rem(index, 2), index // 2
    y, x = chip // plane[1], lax.rem(chip, plane[1])
    barrier = pltpu.get_barrier_semaphore()
    greeted = [device_at(plane, y, x, 1 - core)]
    greeted += [device_at(plane, y, lax.rem(x + k, plane[1]), core) for k in range(1, plane[1])]
    greeted += [device_at(plane, lax.rem(y + k, plane[0]), x, core) for k in range(1, plane[0])]
    greeted += [{"expert": lax.rem(z + k, count)} for k in range(1, count)]
    for device in greeted:
        pl.semaphore_signal(barrier, inc=1, device_id=device, device_id_type=pl.DeviceIdType.MESH)
    pl.semaphore_wait(barrier, len(greeted))


def backward_kernel(
    dims,
    plane,
    lengths,
    tokens,
    cot,
    routes,
    gain_one,
    gain_two,
    cos_ref,
    sin_ref,
    router,
    hidden,
    moe,
    queries,
    keyval,
    mixture,
    query_hbm,
    keyval_hbm,
    out_hbm,
    grad_gu,
    grad_dn,
    input_grad,
    gu_out,
    dn_out,
    dense_out,
    small_out,
    w_query,
    w_keyval,
    w_out,
    router_pad,
    normed,
    normed2,
    d_attn,
    d_mix,
    d_query,
    d_keyval,
    d_logits,
    wide,
    d_hidden,
    gains,
    scores,
    d_probs,
    probs,
    d_scores,
    stacked,
    kv_parts,
    kv_land,
    kv_own,
    gu_own,
    gu_sum,
    gu_land_a,
    gu_land_b,
    dn_own,
    dn_sum,
    dn_land_a,
    dn_land_b,
    grads,
    grads_sum,
    grads_land_a,
    grads_land_b,
    grads_line,
    grads_line_land,
    small,
    small_sum,
    small_land_a,
    small_land_b,
    small_line,
    small_line_land,
    gu_sems,
    dn_sems,
    grads_sems,
    small_sems,
    line_sems,
    kv_sems,
    load_sems,
    own_sems,
):
    micros, rows, count, local, ff, model = dims
    seq_len = count * rows
    kv = keyval.shape[2] // 2
    chunks = kv // LANES
    both = micros * rows
    z = lax.axis_index("expert")
    row_base = z * rows
    block = small_line.shape[0] // count
    core = lax.rem(lax.axis_index("dp"), 2)

    loads = []
    for number, (src, dst) in enumerate(
        ((out_hbm, w_out), (query_hbm, w_query), (keyval_hbm, w_keyval))
    ):
        loads.append(pltpu.make_async_copy(src, dst, load_sems.at[number]))
        loads[-1].start()
    full_barrier(plane, count)

    experts = []
    for j in range(local):
        for kind, (source, own, total, land_a, land_b, sems) in enumerate(
            (
                (grad_gu, gu_own, gu_sum, gu_land_a, gu_land_b, gu_sems),
                (grad_dn, dn_own, dn_sum, dn_land_a, dn_land_b, dn_sems),
            )
        ):
            load = pltpu.make_async_copy(
                source.at[j, :, :, core], own.at[j % 2], own_sems.at[2 * j + kind]
            )
            item = PlaneReduce(
                plane, source.at[j], own.at[j % 2], total.at[j], land_a.at[j], land_b.at[j],
                j % 2 == 0, sems.at[j], load,
            )
            item.start()
            if j < 2:
                load.start()
            experts.append(item)
    dense = [
        PlaneReduce(
            plane, grads.at[k], None, grads_sum.at[k], grads_land_a.at[k], grads_land_b.at[k],
            k % 2 == 0, grads_sems.at[k],
        )
        for k in range(6)
    ]
    dense.append(
        PlaneReduce(
            plane, small, None, small_sum, small_land_a, small_land_b, True, small_sems
        )
    )
    lines = [
        LineReduce(grads_line.at[k], grads_line_land.at[k], block, count, line_sems.at[k])
        for k in range(6)
    ] + [LineReduce(small_line, small_line_land, block, count, line_sems.at[6])]
    reduce_kv = [
        Reduce(kv_parts.at[m], kv_land.at[m], rows, count, kv_sems.at[m], up=False)
        for m in range(micros)
    ]

    queue = []

    def advance(amount=1):
        for _ in range(amount):
            if queue:
                queue.pop(0)()

    def paired(item):
        item.pair_sum()
        item.send(0)

    def crossed(item):
        item.take(0)
        item.send(1)

    def expert_done(number):
        out = gu_out if number % 2 == 0 else dn_out
        out[number // 2] = experts[number].take(1)

    def dense_done(number):
        ref = grads_line.at[number] if number < 6 else small_line
        ref[...] = dense[number].take(1).astype(BF)
        lines[number].start()

    def line_done(number):
        if number < 6:
            half = model // 2
            dense_out[number // 2, :, (number % 2) * half : (number % 2 + 1) * half] = lines[
                number
            ].total()
        else:
            small_out[...] = lines[number].total()

    def put_grads(number, left, right):
        half = model // 2
        shape = grads.shape[1:]
        for k in range(2):
            value = tn(left, right[:, k * half : (k + 1) * half])
            grads[2 * number + k] = value.astype(BF).reshape(shape)
            dense[2 * number + k].start()

    def part(function, *values):
        return functools.partial(function, *values)

    def expert_paired(number):
        paired(experts[number])
        if number + 4 < len(experts):
            experts[number + 4].local.start()

    queue += [part(expert_paired, number) for number in range(len(experts))]

    router_pad[...] = jnp.zeros(router_pad.shape, BF)
    router_pad[:, 0 : router.shape[1]] = router[...]
    gains[...] = jnp.zeros(gains.shape, F32)

    def norm_back(d_rows, inputs, scale, gain, row):
        scaled = d_rows * gain
        gains[row : row + 1, :] += jnp.sum(d_rows * inputs * scale, 0, keepdims=True)
        return scale * (
            scaled - inputs * scale * scale * jnp.mean(scaled * inputs, -1, keepdims=True)
        )

    def live_rows(m):
        return (row_base + lax.broadcasted_iota(jnp.int32, (rows, 1), 0)) < lengths[m, 0]

    router_lanes = router.shape[1]
    for m in range(micros):
        span = slice(m * rows, (m + 1) * rows)
        x_rows = tokens[m, 0].astype(F32)
        normed[span, :] = (x_rows * rms_scale(x_rows) * gain_one[...]).astype(BF)
        v = hidden[m]
        scale = rms_scale(v)
        normed2[span, :] = (v * scale * gain_two[...]).astype(BF)
        logits = nn(normed2[span, :], router_pad[...])
        lane = lane_ids(rows)
        ids = routes[m, 0, rows_at(z, rows), :]
        hit = jnp.zeros((rows, LANES), F32)
        for k in range(routes.shape[3]):
            hit = hit + (ids[:, k : k + 1] == lane).astype(F32)
        live = live_rows(m)
        on = jnp.where(live, hit, 0.0) > 0.0
        masked = jnp.where(on, logits, NEG_FILL)
        raised = jnp.where(on, jnp.exp(masked - jnp.max(masked, -1, keepdims=True)), 0.0)
        total = jnp.sum(raised, -1, keepdims=True)
        gate = raised / jnp.where(total > 0.0, total, 1.0)
        d_gate = moe[m, :, model:]
        d_logits[span, :] = (
            gate * (d_gate - jnp.sum(gate * d_gate, -1, keepdims=True))
        ).astype(BF)
        d_rows = moe[m, :, 0:model] + nt(d_logits[span, :], router_pad[...])
        grown = cot[m, 0].astype(F32) + norm_back(
            d_rows, v, scale, gain_two[...], router_lanes + 1
        )
        d_hidden[span, :] = grown
        d_attn[span, :] = jnp.where(live, grown, 0.0).astype(BF)

    loads[0].wait()
    d_mix[...] = nt(d_attn[...], w_out[...]).astype(BF)
    put_grads(2, mixture[...].reshape(both, mixture.shape[2]), d_attn[...])
    advance(2)
    cos = cos_ref[rows_at(z, rows), :]
    sin = sin_ref[rows_at(z, rows), :]

    def attend_back(m):
        length = lengths[m, 0]
        span = slice(m * rows, (m + 1) * rows)
        for i in range(chunks):
            lanes = slice(i * LANES, (i + 1) * LANES)
            value_lanes = slice(kv + i * LANES, kv + (i + 1) * LANES)
            pair = [
                d_mix[span, c * LANES : (c + 1) * LANES].astype(F32) for c in (2 * i, 2 * i + 1)
            ]
            for k, rows_of in enumerate(stack_heads(*pair)):
                stacked[k * rows : (k + 1) * rows, :] = rows_of.astype(BF)
            scores[...] = nt(queries[m, i], keyval[m, :, lanes])
            d_probs[...] = nt(stacked[...], keyval[m, :, value_lanes])

            def strip_step(strip, carry):
                where = rows_at(strip, STRIP)
                prob = softmax_rows(
                    masked_scores(scores, strip, rows, seq_len, row_base, length)
                )
                d_prob = d_probs[where, :]
                delta = jnp.sum(prob * d_prob, -1, keepdims=True)
                d_scores[where, :] = (prob * (d_prob - delta)).astype(BF)
                probs[where, :] = prob.astype(BF)
                return carry

            lax.fori_loop(0, 4 * rows // STRIP, strip_step, 0)
            turned = nn(d_scores[...], keyval[m, :, lanes]) * ATTENTION_SCALE
            first, second = unstack_heads(turned, rows)
            for c, chunk in ((2 * i, first), (2 * i + 1, second)):
                d_query[span, c * LANES : (c + 1) * LANES] = rope(chunk, cos, -sin).astype(BF)
            kv_parts[m, :, lanes] = (
                tn(d_scores[...], queries[m, i]) * ATTENTION_SCALE
            ).astype(BF)
            kv_parts[m, :, value_lanes] = tn(probs[...], stacked[...]).astype(BF)
            if i % 2 == 1:
                advance()

    slots = []
    for m in range(micros):
        attend_back(m)
        reduce_kv[m].slot(0)
    while queue:
        advance()
    for k in (4, 5):
        paired(dense[k])
    loads[1].wait()
    put_grads(0, normed[...], d_query[...])
    wide[...] = nt(d_query[...], w_query[...])
    for slot in range(1, count):
        for m in range(micros):
            queue.append(part(reduce_kv[m].slot, slot))
    first_wave = [part(crossed, item) for item in experts]
    for k, item in enumerate(first_wave):
        item()
        advance()
        if k == 1:
            for number in (0, 1):
                paired(dense[number])
    while queue:
        advance()
    loads[2].wait()
    for m in range(micros):
        span = slice(m * rows, (m + 1) * rows)
        reduce_kv[m].total(kv_own)
        for c in range(chunks):
            lanes = slice(c * LANES, (c + 1) * LANES)
            d_keyval[span, lanes] = rope(kv_own[:, lanes], cos, -sin).astype(BF)
        d_keyval[span, kv:] = kv_own[:, kv:].astype(BF)
    put_grads(1, normed[...], d_keyval[...])
    wide[...] += nt(d_keyval[...], w_keyval[...])
    for m in range(micros):
        span = slice(m * rows, (m + 1) * rows)
        x_rows = tokens[m, 0].astype(F32)
        input_grad[m, 0] = d_hidden[span, :] + norm_back(
            wide[span, :], x_rows, rms_scale(x_rows), gain_one[...], router_lanes
        )
    small_value = tn(normed2[...], d_logits[...]) + gains[...].T
    small[...] = small_value.astype(BF).reshape(small.shape)
    dense[6].start()
    for k in (2, 3, 6):
        paired(dense[k])
    for k in (4, 5, 0, 1):
        crossed(dense[k])
    for number in range(len(experts)):
        expert_done(number)
    for k in (4, 5, 0, 1):
        dense_done(k)
    for k in (2, 3, 6):
        crossed(dense[k])
    for k in (2, 3, 6):
        dense_done(k)
    for k in range(7):
        line_done(k)
    for item in experts + dense + lines + reduce_kv:
        item.finish()


def backward_call(
    count, devices, tokens, lengths, routes, gain_one, w_query, w_keyval, w_out, gain_two,
    w_router, cot, local, ff, hidden, moe, queries, keyval, mixture, grad_gu, grad_dn,
):
    micros, _, rows, model = tokens.shape
    seq_len = routes.shape[2]
    kv = w_keyval.shape[1] // 2
    heads = w_query.shape[1]
    plane = plane_of(devices)
    block = model // devices // count
    group = max(block, STRIP)
    line = count * block
    half = model // 2
    both = micros * rows
    cos, sin = rope_constants(seq_len)
    gu_rows, dn_rows = model // devices, ff // devices
    vmem = pl.BlockSpec(memory_space=pltpu.VMEM)
    smem = pl.BlockSpec(memory_space=pltpu.SMEM)
    hbm = pl.BlockSpec(memory_space=pl.ANY)
    dma = pltpu.SemaphoreType.DMA
    hops = plane[0] + plane[1] - 1

    def reduce_scratch(lead, block_rows, width):
        lead = tuple(lead)
        return [
            pltpu.VMEM(lead + plane + (block_rows, width), BF),
            pltpu.VMEM(lead + (plane[1] - 1, plane[0], block_rows, width), BF),
            pltpu.VMEM(lead + (plane[0] - 1, block_rows, width), BF),
        ]

    wide_bf = pltpu.VMEM((both, model), BF)
    out_shape = (
        jax.ShapeDtypeStruct((micros, 1, rows, model), F32),
        jax.ShapeDtypeStruct((local, gu_rows, 2 * ff), F32),
        jax.ShapeDtypeStruct((local, dn_rows, model), F32),
        jax.ShapeDtypeStruct((3, group, model), F32),
        jax.ShapeDtypeStruct((group, LANES), F32),
    )
    scratch = (
        [pltpu.VMEM(w.shape, BF) for w in (w_query, w_keyval, w_out)]
        + [pltpu.VMEM((model, LANES), BF)]
        + [wide_bf, wide_bf, wide_bf, pltpu.VMEM((both, heads), BF), pltpu.VMEM((both, heads), BF)]
        + [pltpu.VMEM((both, 2 * kv), BF), pltpu.VMEM((both, LANES), BF)]
        + [pltpu.VMEM((both, model), F32)]
        + [pltpu.VMEM((both, model), F32), pltpu.VMEM((LANES, model), F32)]
        + [pltpu.VMEM((4 * rows, seq_len), F32)] * 2
        + [pltpu.VMEM((4 * rows, seq_len), BF)] * 2
        + [pltpu.VMEM((4 * rows, LANES), BF)]
        + [pltpu.VMEM((micros, seq_len, 2 * kv), BF)]
        + [pltpu.VMEM((micros, count - 1, rows, 2 * kv), BF), pltpu.VMEM((rows, 2 * kv), F32)]
        + [pltpu.VMEM((2,) + plane + (gu_rows, 2 * ff), BF)]
        + reduce_scratch((local,), gu_rows, 2 * ff)
        + [pltpu.VMEM((2,) + plane + (dn_rows, model), BF)]
        + reduce_scratch((local,), dn_rows, model)
        + [pltpu.VMEM((6,) + plane + (2, line, half), BF)]
        + reduce_scratch((6,), line, half)
        + [pltpu.VMEM((6, line, half), BF), pltpu.VMEM((6, count - 1, group, half), BF)]
        + [pltpu.VMEM(plane + (2, line, LANES), BF)]
        + reduce_scratch((), line, LANES)
        + [pltpu.VMEM((line, LANES), BF), pltpu.VMEM((count - 1, group, LANES), BF)]
        + [dma((local, 2, hops)), dma((local, 2, hops)), dma((6, 2, hops)), dma((2, hops))]
        + [dma((7, 2, count - 1)), dma((micros, 2, 2, count - 1)), dma((3,)), dma((2 * local,))]
    )
    dims = (micros, rows, count, local, ff, model)
    return pl.pallas_call(
        functools.partial(backward_kernel, dims, plane),
        out_shape=out_shape,
        in_specs=[smem] + [vmem] * 13 + [hbm] * 5,
        out_specs=(vmem,) * 5,
        scratch_shapes=scratch,
        name="layer_backward",
        compiler_params=pltpu.CompilerParams(
            collective_id=1, has_side_effects=True, vmem_limit_bytes=VMEM_LIMIT
        ),
    )(
        lengths, tokens, cot, routes, gain_one.reshape(1, -1), gain_two.reshape(1, -1),
        jnp.asarray(cos), jnp.asarray(sin), w_router, hidden, moe, queries, keyval, mixture,
        w_query, w_keyval, w_out,
        grad_gu.reshape((local,) + plane + (2, gu_rows, 2 * ff)),
        grad_dn.reshape((local,) + plane + (2, dn_rows, model)),
    )


def on_device(
    tokens, lengths, routes, attn_gain, w_query, w_keyval, w_out, ffn_gain, w_router,
    expert_gate_up, expert_down, cotangent,
):
    count = lax.axis_size("expert")
    devices = lax.axis_size("dp")
    model = tokens.shape[3]
    experts = w_router.shape[1]
    local, ff = expert_gate_up.shape[0], expert_down.shape[1]
    y, hidden, moe, queries, keyval, mixture, grad_gu, grad_dn = forward_call(
        count, tokens, lengths, routes, attn_gain, w_query, w_keyval, w_out, ffn_gain, w_router,
        expert_gate_up, expert_down, cotangent,
    )
    input_grad, gu, dn, dense, small = backward_call(
        count, devices, tokens, lengths, routes, attn_gain, w_query, w_keyval, w_out, ffn_gain,
        w_router, cotangent, local, ff, hidden, moe, queries, keyval, mixture, grad_gu, grad_dn,
    )
    block = model // devices // count
    if dense.shape[1] != block:
        first = lax.rem(lax.axis_index("expert") * block, dense.shape[1])
        dense = lax.dynamic_slice_in_dim(dense, first, block, 1)
        small = lax.dynamic_slice_in_dim(small, first, block, 0)
    return (
        y, input_grad, small[:, experts], dense[0], dense[1], dense[2], small[:, experts + 1],
        small[:, :experts], gu, dn,
    )


def solution(mesh):
    placed = (
        P(None, "dp", "expert", None), P(None, "dp"), P(None, "dp", None, None), P(), P(), P(), P(),
        P(), P(), P("expert", None, None), P("expert", None, None), P(None, "dp", "expert", None),
    )
    return jax.shard_map(
        on_device,
        mesh=mesh,
        in_specs=placed,
        out_specs=(
            P(None, "dp", "expert", None), P(None, "dp", "expert", None), P(("dp", "expert")),
            P(("dp", "expert"), None), P(("dp", "expert"), None), P(("dp", "expert"), None),
            P(("dp", "expert")), P(("dp", "expert"), None), P("expert", "dp", None),
            P("expert", "dp", None),
        ),
        check_vma=False,
    )
```

```python
import functools
import math

import jax
import jax.numpy as jnp
import numpy as np
from jax import lax
from jax.experimental import pallas as pl
from jax.experimental.pallas import tpu as pltpu
from jax.sharding import PartitionSpec as P

HEAD_DIM = 64
EPS = 1e-06
ATTENTION_SCALE = 0.015625
ROPE_BASE = 10000.0
NEG_FILL = -1e30
LANES = 128
GROUP = 16
STRIP = 64
BF = jnp.bfloat16
F32 = jnp.float32
VMEM_LIMIT = 63 * 2**20


def dot_of(left, right, left_dim, right_dim):
    return lax.dot_general(
        left, right, (((left_dim,), (right_dim,)), ((), ())), preferred_element_type=F32
    )


def nn(left, right):
    return dot_of(left, right, 1, 0)


def nt(left, right):
    return dot_of(left, right, 1, 1)


def tn(left, right):
    return dot_of(left, right, 0, 0)


def rope_constants(seq_len):
    half = HEAD_DIM // 2
    frequency = np.exp(
        np.arange(half, dtype=np.float32) * np.float32(-2.0 * math.log(ROPE_BASE) / HEAD_DIM)
    ).astype(np.float32)
    angles = np.arange(seq_len, dtype=np.float32)[:, None] * frequency[None, :]
    cos, sin = np.cos(angles).astype(np.float32), np.sin(angles).astype(np.float32)
    heads = LANES // HEAD_DIM
    return np.tile(np.concatenate([cos, cos], 1), (1, heads)), np.tile(
        np.concatenate([-sin, sin], 1), (1, heads)
    )


def lane_ids(rows):
    return lax.broadcasted_iota(jnp.int32, (rows, LANES), 1)


def swap_halves(chunk):
    half = HEAD_DIM // 2
    first = lax.rem(lane_ids(chunk.shape[0]), HEAD_DIM) < half
    return jnp.where(
        first, pltpu.roll(chunk, LANES - half, 1), pltpu.roll(chunk, half, 1)
    )


def rope(chunk, cos, sin):
    return chunk * cos + swap_halves(chunk) * sin


def rms_scale(rows):
    return lax.rsqrt(jnp.mean(rows * rows, -1, keepdims=True) + EPS)


def stack_heads(first, second):
    low = lane_ids(first.shape[0]) < HEAD_DIM
    zero = jnp.zeros_like(first)
    return [
        jnp.where(low, first, zero),
        jnp.where(low, pltpu.roll(first, HEAD_DIM, 1), zero),
        jnp.where(low, zero, pltpu.roll(second, HEAD_DIM, 1)),
        jnp.where(low, zero, second),
    ]


def unstack_heads(stacked, rows):
    low = lane_ids(rows) < HEAD_DIM
    parts = [stacked[k * rows : (k + 1) * rows] for k in range(4)]
    first = jnp.where(low, parts[0], pltpu.roll(parts[1], HEAD_DIM, 1))
    second = jnp.where(low, pltpu.roll(parts[2], HEAD_DIM, 1), parts[3])
    return first, second


def rows_at(index, rows):
    return pl.ds(pl.multiple_of(index * rows, rows), rows)


class Gather:
    def __init__(self, buffer, micro, rows, count, sems, up=True, down=True):
        self.buffer, self.micro, self.rows, self.count, self.sems = buffer, micro, rows, count, sems
        self.ways = [w for w, on in ((0, up), (1, down)) if on]

    def copy(self, way, step, block):
        z = lax.axis_index("expert")
        target = z + 1 if way == 0 else z - 1
        view = self.buffer.at[self.micro, rows_at(block, self.rows), :]
        return pltpu.make_async_remote_copy(
            src_ref=view,
            dst_ref=view,
            send_sem=self.sems.at[0, way, step],
            recv_sem=self.sems.at[1, way, step],
            device_id={"expert": target},
            device_id_type=pl.DeviceIdType.MESH,
        )

    def sends(self, way, step):
        z = lax.axis_index("expert")
        if way == 0:
            return z - step, jnp.logical_and(z < self.count - 1, z - step >= 0)
        return z + step, jnp.logical_and(z > 0, z + step <= self.count - 1)

    def receives(self, way, step):
        z = lax.axis_index("expert")
        if way == 0:
            return z - 1 - step, z - 1 - step >= 0
        return z + 1 + step, z + 1 + step <= self.count - 1

    def start(self, step):
        for way in self.ways:
            block, on = self.sends(way, step)

            @pl.when(on)
            def _(way=way, block=block):
                self.copy(way, step, block).start()

    def wait(self, step):
        for way in self.ways:
            block, on = self.receives(way, step)

            @pl.when(on)
            def _(way=way, block=block):
                self.copy(way, step, block).wait_recv()

    def hop(self, step):
        self.wait(step)
        if step + 1 < self.count - 1:
            self.start(step + 1)

    def finish(self):
        for step in range(self.count - 1):
            for way in self.ways:
                block, on = self.sends(way, step)

                @pl.when(on)
                def _(way=way, step=step, block=block):
                    self.copy(way, step, block).wait_send()


class Reduce:
    def __init__(self, parts, landing, rows, count, sems, up=True, down=True):
        self.parts, self.landing = parts, landing
        self.rows, self.count, self.sems = rows, count, sems
        self.ways = [w for w, on in ((0, up), (1, down)) if on]

    def block(self, way, slot):
        z = lax.axis_index("expert")
        if way == 0:
            return z + self.count - 1 - slot, slot >= z
        return z - (self.count - 1) + slot, slot >= self.count - 1 - z

    def place(self, way, slot, z):
        if way == 0:
            return slot - (z - 1)
        return self.count - (slot - (self.count - 2 - z)) - (2 if self.ways == [1] else 0)

    def copy(self, way, slot, block):
        z = lax.axis_index("expert")
        target = z + 1 if way == 0 else z - 1
        return pltpu.make_async_remote_copy(
            src_ref=self.parts.at[rows_at(block, self.rows), :],
            dst_ref=self.landing.at[self.place(way, slot, target)],
            send_sem=self.sems.at[0, way, slot],
            recv_sem=self.sems.at[1, way, slot],
            device_id={"expert": target},
            device_id_type=pl.DeviceIdType.MESH,
        )

    def arrival(self, way, slot, block):
        z = lax.axis_index("expert")
        source = z - 1 if way == 0 else z + 1
        return pltpu.make_async_remote_copy(
            src_ref=self.parts.at[rows_at(block, self.rows), :],
            dst_ref=self.landing.at[self.place(way, slot, z)],
            send_sem=self.sems.at[0, way, slot],
            recv_sem=self.sems.at[1, way, slot],
            device_id={"expert": source},
            device_id_type=pl.DeviceIdType.MESH,
        )

    def inner(self, way):
        z = lax.axis_index("expert")
        return z >= 1 if way == 0 else z <= self.count - 2

    def slot(self, slot):
        z = lax.axis_index("expert")
        for way in self.ways:
            block, on = self.block(way, slot)
            if slot >= 1:

                @pl.when(jnp.logical_and(on, self.inner(way)))
                def _(way=way, block=block):
                    self.arrival(way, slot - 1, block).wait_recv()
                    if slot < self.count - 1:
                        where = rows_at(block, self.rows)
                        total = self.parts[where, :].astype(F32) + self.landing[
                            self.place(way, slot - 1, z)
                        ].astype(F32)
                        self.parts[where, :] = total.astype(self.parts.dtype)

            if slot < self.count - 1:

                @pl.when(on)
                def _(way=way, block=block):
                    self.copy(way, slot, block).start()

    def total(self, out, lanes=slice(None)):
        z = lax.axis_index("expert")
        out[...] = self.parts[rows_at(z, self.rows), lanes].astype(F32)
        for way in self.ways:

            @pl.when(self.inner(way))
            def _(way=way):
                place = self.place(way, self.count - 2, z)
                out[...] += self.landing[place, :, lanes].astype(F32)

    def finish(self):
        for slot in range(self.count - 1):
            for way in self.ways:
                block, on = self.block(way, slot)

                @pl.when(on)
                def _(way=way, slot=slot, block=block):
                    self.copy(way, slot, block).wait_send()


def line_barrier(count):
    z = lax.axis_index("expert")
    barrier = pltpu.get_barrier_semaphore()
    for target, on in ((z + 1, z < count - 1), (z - 1, z > 0)):

        @pl.when(on)
        def _(target=target):
            pl.semaphore_signal(
                barrier, inc=1, device_id={"expert": target}, device_id_type=pl.DeviceIdType.MESH
            )

    pl.semaphore_wait(barrier, (z > 0).astype(jnp.int32) + (z < count - 1).astype(jnp.int32))


def score_bias(bias, row_base, length):
    key_pos = lax.broadcasted_iota(jnp.int32, bias.shape, 0)
    query_pos = row_base + lax.broadcasted_iota(jnp.int32, bias.shape, 1)
    allowed = jnp.logical_and(key_pos <= query_pos, key_pos < length)
    bias[...] = jnp.where(allowed, 0.0, NEG_FILL)


def softmax_columns(scores):
    raised = jnp.exp(scores - jnp.max(scores, 0, keepdims=True))
    return raised * (1.0 / jnp.sum(raised, 0, keepdims=True))


def sigmoid(v):
    return 0.5 * jnp.tanh(0.5 * v) + 0.5


def forward_kernel(
    dims,
    lengths,
    tokens,
    cot,
    routes,
    gain_one,
    gain_two,
    cos_ref,
    sin_ref,
    router,
    query_hbm,
    keyval_hbm,
    out_hbm,
    gate_up_hbm,
    down_hbm,
    y_out,
    hidden_out,
    moe_out,
    queries_out,
    keyval_out,
    mixture_out,
    grad_gu_out,
    grad_dn_out,
    wide,
    narrow,
    normed,
    queries,
    keyval,
    mixture,
    hidden,
    named,
    gates,
    gate_lanes,
    gate_terms,
    router_pad,
    rows_all,
    cot_all,
    acts,
    d_proj,
    w_out,
    w_gu,
    w_dn,
    out_parts,
    out_land,
    in_parts,
    in_land,
    own_sum,
    moe_sum,
    kv_sems,
    rows_sems,
    cot_sems,
    out_sems,
    in_sems,
    load_sems,
    store_sems,
):
    micros, rows, count, local, ff, model = dims
    seq_len = count * rows
    kv = keyval.shape[2] // 2
    chunks = kv // LANES
    z = lax.axis_index("expert")
    row_base = z * rows
    split = -(-model // seq_len)
    piece = model // split
    back = wide
    bias = gate_terms.at[:, 0:rows]
    scores = wide.at[:, 0 : 4 * rows]
    probs = d_proj.at[micros * local - 1, :, 0 : 4 * rows]
    tile = 512

    loads = []

    def load(src, dst):
        copy = pltpu.make_async_copy(src, dst, load_sems.at[len(loads)])
        copy.start()
        loads.append(copy)
        return copy

    early = []
    for index, weight in enumerate((query_hbm, keyval_hbm)):
        early.append(
            [
                load(
                    weight.at[pl.ds(k * piece, piece), :],
                    d_proj.at[index * split + k, pl.ds(0, piece), :],
                )
                for k in range(split)
            ]
        )
    load_out = load(out_hbm, w_out)
    load_gu = load(gate_up_hbm, w_gu)
    load_dn = load(down_hbm, w_dn)

    line_barrier(count)

    gather_kv = [
        Gather(keyval, m, rows, count, kv_sems.at[m], down=False) for m in range(micros)
    ]
    gather_rows = [Gather(rows_all, m, rows, count, rows_sems.at[m]) for m in range(micros)]
    gather_cot = [Gather(cot_all, m, rows, count, cot_sems.at[m]) for m in range(micros)]
    reduce_out = [
        Reduce(out_parts, out_land, rows, count, out_sems.at[m]) for m in range(micros)
    ]
    reduce_in = [Reduce(in_parts, in_land, rows, count, in_sems.at[m]) for m in range(micros)]

    for m in range(micros):
        cot_all[m, rows_at(z, rows), :] = cot[m, 0]
    gather_cot[0].start(0)

    for m in range(micros):
        x_rows = tokens[m, 0].astype(F32)
        normed[m * rows : (m + 1) * rows, :] = (
            x_rows * rms_scale(x_rows) * gain_one[...]
        ).astype(BF)
    cos = cos_ref[rows_at(z, rows), :]
    sin = sin_ref[rows_at(z, rows), :]
    both = micros * rows

    def project(index):
        for copy in early[index]:
            copy.wait()
        total = None
        for k in range(split):
            part = nn(
                normed[:, k * piece : (k + 1) * piece], d_proj[index * split + k, 0:piece, :]
            )
            total = part if total is None else total + part
        wide[0:both, :] = total

    project(1)
    for m in range(micros):
        span = slice(m * rows, (m + 1) * rows)
        for c in range(chunks):
            lanes = slice(c * LANES, (c + 1) * LANES)
            keyval[m, rows_at(z, rows), lanes] = rope(wide[span, lanes], cos, sin).astype(BF)
        keyval[m, rows_at(z, rows), kv:] = wide[span, kv:].astype(BF)
        gather_kv[m].start(0)
        for b in range(count):

            @pl.when(b > z)
            def _(m=m, b=b):
                keyval[m, b * rows : (b + 1) * rows, :] = jnp.zeros((rows, 2 * kv), BF)

    project(0)
    for m in range(micros):
        span = slice(m * rows, (m + 1) * rows)
        for i in range(chunks):
            pair = [
                rope(wide[span, c * LANES : (c + 1) * LANES], cos, sin)
                for c in (2 * i, 2 * i + 1)
            ]
            for k, block in enumerate(stack_heads(*pair)):
                queries[m, i, k * rows : (k + 1) * rows, :] = (
                    block.astype(BF) * ATTENTION_SCALE
                ).astype(BF)

    for m in range(micros):
        lane = lane_ids(seq_len)
        hit = jnp.zeros((seq_len, LANES), F32)
        for k in range(routes.shape[3]):
            hit = hit + (routes[m, 0][:, k : k + 1] == lane).astype(F32)
        live = lax.broadcasted_iota(jnp.int32, (seq_len, LANES), 0) < lengths[m, 0]
        named[m] = jnp.where(live, hit, 0.0)
    router_pad[...] = jnp.zeros(router_pad.shape, BF)
    router_pad[:, 0 : router.shape[1]] = router[...]

    def attend(m):
        length = lengths[m, 0]
        score_bias(bias, row_base, length)
        for i in range(chunks):
            lanes = slice(i * LANES, (i + 1) * LANES)
            scores[...] = nt(keyval[m, :, lanes], queries[m, i])
            for k in range(4):
                span = slice(k * rows, (k + 1) * rows)
                probs[:, span] = softmax_columns(scores[:, span] + bias[...]).astype(BF)
            mixed = tn(probs[...], keyval[m, :, kv + i * LANES : kv + (i + 1) * LANES])
            first, second = unstack_heads(mixed, rows)
            mixture[m, :, 2 * i * LANES : (2 * i + 1) * LANES] = first.astype(BF)
            mixture[m, :, (2 * i + 1) * LANES : (2 * i + 2) * LANES] = second.astype(BF)
        if m == 0:
            load_out.wait()
        live = (row_base + lax.broadcasted_iota(jnp.int32, (rows, 1), 0)) < length
        rows_hidden = tokens[m, 0].astype(F32) + jnp.where(
            live, nn(mixture[m], w_out[...]), 0.0
        )
        hidden[m] = rows_hidden
        rows_all[m, rows_at(z, rows), :] = (
            rows_hidden * rms_scale(rows_hidden) * gain_two[...]
        ).astype(BF)
        gather_rows[m].start(0)

    def gate_rows(m):
        logits = nn(rows_all[m], router_pad[...])
        on = named[m] > 0.0
        masked = jnp.where(on, logits, NEG_FILL)
        raised = jnp.where(on, jnp.exp(masked - jnp.max(masked, -1, keepdims=True)), 0.0)
        total = jnp.sum(raised, -1, keepdims=True)
        gate = raised / jnp.where(total > 0.0, total, 1.0)
        for j in range(local):
            gate_lanes[j] = jnp.broadcast_to(column(gate, z * local + j), gate.shape)

    def column(block, expert):
        return jnp.sum(
            jnp.where(lane_ids(block.shape[0]) == expert, block, 0.0), -1, keepdims=True
        )

    blocks = [slice(c, c + LANES) for c in range(0, ff, LANES)]

    def expert_forward(m, j):
        wide[...] = nn(rows_all[m], w_gu[j])

        def strip_step(strip, carry):
            where = rows_at(strip, STRIP)
            gate = gate_lanes[j, where, :]
            for c, lanes in enumerate(blocks):
                front, up = wide[where, lanes], wide[where, ff + c * LANES : ff + (c + 1) * LANES]
                value = front * sigmoid(front) * up * gate
                acts[m, where, j * ff + c * LANES : j * ff + (c + 1) * LANES] = value.astype(BF)
            d_proj[m * local + j, where, :] = wide[where, :].astype(BF)
            return carry

        lax.fori_loop(0, seq_len // STRIP, strip_step, 0)

    def expert_backward(m, j):
        expert = z * local + j
        narrow[...] = nt(cot_all[m], w_dn[j * ff : (j + 1) * ff, :])

        def strip_step(strip, carry):
            where = rows_at(strip, STRIP)
            gate = gate_lanes[j, where, :]
            terms = None
            for c, lanes in enumerate(blocks):
                up_lanes = slice(ff + c * LANES, ff + (c + 1) * LANES)
                front = d_proj[m * local + j, where, lanes].astype(F32)
                up = d_proj[m * local + j, where, up_lanes].astype(F32)
                d_act = narrow[where, lanes]
                sig = sigmoid(front)
                silu = front * sig
                term = d_act * silu
                terms = term * up if terms is None else terms + term * up
                d_proj[m * local + j, where, up_lanes] = (term * gate).astype(BF)
                d_proj[m * local + j, where, lanes] = (
                    d_act * gate * up * (sig + silu * (1.0 - sig))
                ).astype(BF)
            gate_terms[where, :] = terms
            return carry

        lax.fori_loop(0, seq_len // STRIP, strip_step, 0)
        d_gate = jnp.sum(gate_terms[...], -1, keepdims=True)
        mine = lane_ids(seq_len) == expert
        if j == 0:
            gates[...] = jnp.where(mine, d_gate, 0.0)
        else:
            gates[...] = jnp.where(mine, d_gate, gates[...])
        if j == local - 1:
            in_parts[:, model:] = (gates[...] * named[m]).astype(BF)
        for r in range(0, seq_len, tile):
            span = slice(r, r + tile)
            part = nt(d_proj[m * local + j, span, :], w_gu[j])
            if j == 0:
                back[span, :] = part
            elif j < local - 1:
                back[span, :] += part
            else:
                in_parts[span, 0:model] = (back[span, :] + part).astype(BF)

    def weight_grads(j):
        for part_of in range(4):
            lanes = slice(part_of * ff // 2, (part_of + 1) * ff // 2)
            total = None
            for m in range(micros):
                part = tn(rows_all[m], d_proj[m * local + j, :, lanes])
                total = part if total is None else total + part
            w_gu[j, :, lanes] = total.astype(BF)
        total = None
        for m in range(micros):
            part = tn(acts[m, :, j * ff : (j + 1) * ff], cot_all[m])
            total = part if total is None else total + part
        w_dn[j * ff : (j + 1) * ff, :] = total.astype(BF)

    steps = count - 1

    def run(*todo):
        for item in todo:
            item()

    def hops(gather, first=0, last=steps):
        for step in range(first, last):
            gather.hop(step)

    gather_kv[0].hop(0)
    gather_cot[0].hop(0)
    hops(gather_kv[0], 1)
    gather_kv[1].hop(0)
    attend(0)
    hops(gather_cot[0], 1)
    hops(gather_kv[1], 1)
    gather_rows[0].hop(0)
    attend(1)
    gather_cot[1].start(0)
    hops(gather_rows[0], 1)
    gather_rows[1].hop(0)

    load_gu.wait()
    load_dn.wait()
    queue = []

    def advance(amount=1):
        for _ in range(amount):
            if queue:
                queue.pop(0)()

    def finish_out(m):
        reduce_out[m].total(own_sum)
        y_out[m, 0] = (hidden[m] + own_sum[...]).astype(BF)
        reduce_out[m].finish()

    def finish_in(m):
        reduce_in[m].total(moe_sum.at[m])
        reduce_in[m].finish()

    def slots(reduce):
        return [functools.partial(reduce.slot, t) for t in range(count)]

    queue += [functools.partial(gather_cot[1].hop, 0)]
    for step in range(1, steps):
        queue += [functools.partial(gather_rows[1].hop, step)]
        queue += [functools.partial(gather_cot[1].hop, step)]
    for m in range(micros):
        if m == 1:
            while queue:
                advance()
            queue += slots(reduce_in[0]) + [functools.partial(finish_in, 0)]
        gate_rows(m)
        for j in range(local):
            expert_forward(m, j)
            advance()
        while queue:
            advance()
        for r in range(0, seq_len, tile):
            out_parts[r : r + tile, :] = nn(acts[m, r : r + tile, :], w_dn[...]).astype(BF)
        queue += slots(reduce_out[m]) + [functools.partial(finish_out, m)]
        for j in range(local):
            expert_backward(m, j)
            advance()
    while queue:
        advance()
    queue += slots(reduce_in[1]) + [functools.partial(finish_in, 1)]
    stores = []

    def store(src, dst):
        copy = pltpu.make_async_copy(src, dst, store_sems.at[len(stores)])
        copy.start()
        stores.append(copy)

    advance()
    for j in range(local):
        weight_grads(j)
        advance()
        store(w_gu.at[j], grad_gu_out.at[j])
        store(w_dn.at[pl.ds(j * ff, ff), :], grad_dn_out.at[pl.ds(j * ff, ff), :])
    while queue:
        advance()
    store(hidden, hidden_out)
    store(moe_sum, moe_out)
    store(queries, queries_out)
    store(keyval, keyval_out)
    store(mixture, mixture_out)
    for item in gather_kv + gather_rows + gather_cot:
        item.finish()
    for copy in stores:
        copy.wait()


def forward_call(
    count, tokens, lengths, routes, gain_one, w_query, w_keyval, w_out, gain_two, w_router,
    gate_up, down, cot,
):
    micros, _, rows, model = tokens.shape
    local, ff = gate_up.shape[0], down.shape[1]
    seq_len = routes.shape[2]
    kv = w_keyval.shape[1] // 2
    chunks = kv // LANES
    heads = w_query.shape[1]
    steps = count - 1
    split = -(-model // seq_len)
    cos, sin = rope_constants(seq_len)
    vmem = pl.BlockSpec(memory_space=pltpu.VMEM)
    smem = pl.BlockSpec(memory_space=pltpu.SMEM)
    hbm = pl.BlockSpec(memory_space=pl.ANY)
    dma = pltpu.SemaphoreType.DMA
    wide_in = model + LANES
    out_shape = (
        jax.ShapeDtypeStruct((micros, 1, rows, model), BF),
        jax.ShapeDtypeStruct((micros, rows, model), F32),
        jax.ShapeDtypeStruct((micros, rows, wide_in), F32),
        jax.ShapeDtypeStruct((micros, chunks, 4 * rows, LANES), BF),
        jax.ShapeDtypeStruct((micros, seq_len, 2 * kv), BF),
        jax.ShapeDtypeStruct((micros, rows, heads), BF),
        jax.ShapeDtypeStruct((local, model, 2 * ff), BF),
        jax.ShapeDtypeStruct((local * ff, model), BF),
    )
    scratch = [
        pltpu.VMEM((seq_len, model), F32),
        pltpu.VMEM((seq_len, ff), F32),
        pltpu.VMEM((micros * rows, model), BF),
        pltpu.VMEM((micros, chunks, 4 * rows, LANES), BF),
        pltpu.VMEM((micros, seq_len, 2 * kv), BF),
        pltpu.VMEM((micros, rows, heads), BF),
        pltpu.VMEM((micros, rows, model), F32),
        pltpu.VMEM((micros, seq_len, LANES), F32),
        pltpu.VMEM((seq_len, LANES), F32),
        pltpu.VMEM((local, seq_len, LANES), F32),
        pltpu.VMEM((seq_len, LANES), F32),
        pltpu.VMEM((model, LANES), BF),
        pltpu.VMEM((micros, seq_len, model), BF),
        pltpu.VMEM((micros, seq_len, model), BF),
        pltpu.VMEM((micros, seq_len, local * ff), BF),
        pltpu.VMEM((micros * local, seq_len, 2 * ff), BF),
        pltpu.VMEM(w_out.shape, BF),
        pltpu.VMEM((local, model, 2 * ff), BF),
        pltpu.VMEM((local * ff, model), BF),
        pltpu.VMEM((seq_len, model), BF),
        pltpu.VMEM((count + 1, rows, model), BF),
        pltpu.VMEM((seq_len, wide_in), BF),
        pltpu.VMEM((count + 1, rows, wide_in), BF),
        pltpu.VMEM((rows, model), F32),
        pltpu.VMEM((micros, rows, wide_in), F32),
    ] + [dma((micros, 2, 2, steps))] * 5 + [dma((2 * split + 3,)), dma((2 * local + 5,))]
    dims = (micros, rows, count, local, ff, model)
    return pl.pallas_call(
        functools.partial(forward_kernel, dims),
        out_shape=out_shape,
        in_specs=[smem] + [vmem] * 8 + [hbm] * 5,
        out_specs=(vmem,) + (hbm,) * 7,
        scratch_shapes=scratch,
        name="layer_forward",
        compiler_params=pltpu.CompilerParams(
            collective_id=0, has_side_effects=True, vmem_limit_bytes=VMEM_LIMIT
        ),
    )(
        lengths, tokens, cot, routes, gain_one.reshape(1, -1), gain_two.reshape(1, -1),
        jnp.asarray(cos), jnp.asarray(sin), w_router, w_query, w_keyval, w_out, gate_up,
        down.reshape(local * ff, model),
    )


def plane_of(devices):
    side = math.isqrt(devices // 2)
    return side, side


def device_at(plane, y, x, core):
    return {"dp": (y * plane[1] + x) * 2 + core}


class PlaneReduce:
    def __init__(self, plane, source, own, total, first_land, second_land, x_first, sems, local=None):
        self.plane, self.source, self.own, self.total = plane, source, own, total
        self.lands, self.x_first, self.sems, self.local = (first_land, second_land), x_first, sems, local
        index = lax.axis_index("dp")
        self.core = lax.rem(index, 2)
        chip = index // 2
        self.y, self.x = chip // plane[1], lax.rem(chip, plane[1])

    def remote(self, src, dst, number, where):
        return pltpu.make_async_remote_copy(
            src_ref=src,
            dst_ref=dst,
            send_sem=self.sems.at[0, number],
            recv_sem=self.sems.at[1, number],
            device_id=device_at(self.plane, *where),
            device_id_type=pl.DeviceIdType.MESH,
        )

    def sibling(self):
        return self.remote(
            self.source.at[:, :, 1 - self.core], self.total, 0, (self.y, self.x, 1 - self.core)
        )

    def start(self):
        self.sibling().start()

    def along(self, stage):
        return self.x_first == (stage == 0)

    def hops(self, stage):
        along_x = self.along(stage)
        size = self.plane[1] if along_x else self.plane[0]
        base = 1 if stage == 0 else self.plane[1] if self.x_first else self.plane[0]
        for k in range(1, size):
            if along_x:
                place = lax.rem(self.x + k, size)
                where = (self.y, place, self.core)
                view = (
                    self.total.at[:, place] if stage == 0 else self.total.at[self.y, place]
                )
            else:
                place = lax.rem(self.y + k, size)
                where = (place, self.x, self.core)
                view = self.total.at[place] if stage == 0 else self.total.at[place, self.x]
            yield k, self.remote(view, self.lands[stage].at[k - 1], base + k - 1, where)

    def send(self, stage):
        for _, copy in self.hops(stage):
            copy.start()

    def pair_sum(self):
        if self.local is not None:
            self.local.wait()
        self.sibling().wait_recv()
        count = self.plane[0] * self.plane[1]
        for b in range(count):
            y, x = b // self.plane[1], b % self.plane[1]
            own = self.own[y, x] if self.local is not None else self.source[y, x, self.core]
            self.total[y, x] = (self.total[y, x].astype(F32) + own.astype(F32)).astype(BF)

    def take(self, stage):
        land = self.lands[stage]
        for k, copy in self.hops(stage):
            copy.wait_recv()
        if stage == 0:
            for other in range(self.plane[0] if self.x_first else self.plane[1]):
                where = (other, self.x) if self.x_first else (self.y, other)
                summed = self.total[where].astype(F32)
                for k in range(land.shape[0]):
                    summed = summed + land[k, other].astype(F32)
                self.total[where] = summed.astype(BF)
            return None
        summed = self.total[self.y, self.x].astype(F32)
        for k in range(land.shape[0]):
            summed = summed + land[k].astype(F32)
        return summed

    def finish(self):
        self.sibling().wait_send()
        for stage in range(2):
            for _, copy in self.hops(stage):
                copy.wait_send()


class LineReduce:
    def __init__(self, parts, land, rows, count, sems):
        self.parts, self.land, self.rows, self.count, self.sems = parts, land, rows, count, sems
        self.group = max(rows, GROUP)

    def span(self, z):
        if self.group == self.rows:
            return rows_at(z, self.rows)
        return pl.ds(pl.multiple_of(z * self.rows // self.group * self.group, self.group), self.group)

    def hops(self):
        z = lax.axis_index("expert")
        for k in range(1, self.count):
            target = lax.rem(z + k, self.count)
            yield k, pltpu.make_async_remote_copy(
                src_ref=self.parts.at[self.span(target), :],
                dst_ref=self.land.at[k - 1],
                send_sem=self.sems.at[0, k - 1],
                recv_sem=self.sems.at[1, k - 1],
                device_id={"expert": target},
                device_id_type=pl.DeviceIdType.MESH,
            )

    def start(self):
        for _, copy in self.hops():
            copy.start()

    def total(self):
        for _, copy in self.hops():
            copy.wait_recv()
        summed = self.parts[self.span(lax.axis_index("expert")), :].astype(F32)
        for k in range(self.count - 1):
            summed = summed + self.land[k].astype(F32)
        return summed

    def finish(self):
        for _, copy in self.hops():
            copy.wait_send()


def full_barrier(plane, count):
    index = lax.axis_index("dp")
    z = lax.axis_index("expert")
    core, chip = lax.rem(index, 2), index // 2
    y, x = chip // plane[1], lax.rem(chip, plane[1])
    barrier = pltpu.get_barrier_semaphore()
    greeted = [device_at(plane, y, x, 1 - core)]
    greeted += [device_at(plane, y, lax.rem(x + k, plane[1]), core) for k in range(1, plane[1])]
    greeted += [device_at(plane, lax.rem(y + k, plane[0]), x, core) for k in range(1, plane[0])]
    greeted += [{"expert": lax.rem(z + k, count)} for k in range(1, count)]
    for device in greeted:
        pl.semaphore_signal(barrier, inc=1, device_id=device, device_id_type=pl.DeviceIdType.MESH)
    pl.semaphore_wait(barrier, len(greeted))


def backward_kernel(
    dims,
    plane,
    lengths,
    tokens,
    cot,
    routes,
    gain_one,
    gain_two,
    cos_ref,
    sin_ref,
    router,
    hidden,
    moe,
    queries,
    keyval,
    mixture,
    query_hbm,
    keyval_hbm,
    out_hbm,
    grad_gu,
    grad_dn,
    input_grad,
    gu_out,
    dn_out,
    dense_out,
    small_out,
    w_query,
    w_keyval,
    w_out,
    router_pad,
    normed,
    normed2,
    d_attn,
    d_mix,
    d_keyval,
    d_logits,
    wide,
    gains,
    bias,
    scores,
    d_probs,
    probs,
    d_scores,
    stacked,
    kv_parts,
    kv_land,
    gu_own,
    gu_sum,
    gu_land_a,
    gu_land_b,
    dn_own,
    dn_sum,
    dn_land_a,
    dn_land_b,
    grads,
    grads_sum,
    grads_land_a,
    grads_land_b,
    grads_line,
    grads_line_land,
    small,
    small_sum,
    small_land_a,
    small_land_b,
    small_line,
    small_line_land,
    gu_sems,
    dn_sems,
    grads_sems,
    small_sems,
    line_sems,
    kv_sems,
    load_sems,
    own_sems,
):
    micros, rows, count, local, ff, model = dims
    seq_len = count * rows
    kv = keyval.shape[2] // 2
    chunks = kv // LANES
    both = micros * rows
    d_query = d_mix
    z = lax.axis_index("expert")
    row_base = z * rows
    block = small_line.shape[0] // count
    core = lax.rem(lax.axis_index("dp"), 2)

    loads = []
    for number, (src, dst) in enumerate(
        ((out_hbm, w_out), (query_hbm, w_query), (keyval_hbm, w_keyval))
    ):
        loads.append(pltpu.make_async_copy(src, dst, load_sems.at[number]))
        loads[-1].start()
    full_barrier(plane, count)

    experts = []
    for j in range(local):
        for kind, (source, own, total, land_a, land_b, sems) in enumerate(
            (
                (grad_gu, gu_own, gu_sum, gu_land_a, gu_land_b, gu_sems),
                (grad_dn, dn_own, dn_sum, dn_land_a, dn_land_b, dn_sems),
            )
        ):
            load = pltpu.make_async_copy(
                source.at[j, :, :, core], own.at[j % 2], own_sems.at[2 * j + kind]
            )
            item = PlaneReduce(
                plane, source.at[j], own.at[j % 2], total.at[j], land_a.at[j], land_b.at[j],
                j % 2 == 0, sems.at[j], load,
            )
            item.start()
            if j < 2:
                load.start()
            experts.append(item)
    dense = [
        PlaneReduce(
            plane, grads.at[k], None, grads_sum.at[k], grads_land_a.at[k], grads_land_b.at[k],
            k % 2 == 0, grads_sems.at[k],
        )
        for k in range(6)
    ]
    dense.append(
        PlaneReduce(
            plane, small, None, small_sum, small_land_a, small_land_b, True, small_sems
        )
    )
    lines = [
        LineReduce(grads_line.at[k], grads_line_land.at[k], block, count, line_sems.at[k])
        for k in range(6)
    ] + [LineReduce(small_line, small_line_land, block, count, line_sems.at[6])]
    reduce_kv = [
        Reduce(kv_parts.at[m], kv_land.at[m], rows, count, kv_sems.at[m], up=False)
        for m in range(micros)
    ]

    queue = []

    def advance(amount=1):
        for _ in range(amount):
            if queue:
                queue.pop(0)()

    def paired(item):
        item.pair_sum()
        item.send(0)

    def crossed(item):
        item.take(0)
        item.send(1)

    def expert_done(number):
        out = gu_out if number % 2 == 0 else dn_out
        out[number // 2] = experts[number].take(1)

    def dense_done(number):
        ref = grads_line.at[number] if number < 6 else small_line
        ref[...] = dense[number].take(1).astype(BF)
        lines[number].start()

    def line_done(number):
        if number < 6:
            half = model // 2
            dense_out[number // 2, :, (number % 2) * half : (number % 2 + 1) * half] = lines[
                number
            ].total()
        else:
            small_out[...] = lines[number].total()

    def put_grads(number, left, right):
        half = model // 2
        shape = grads.shape[1:]
        for k in range(2):
            value = tn(left, right[:, k * half : (k + 1) * half])
            grads[2 * number + k] = value.astype(BF).reshape(shape)
            dense[2 * number + k].start()

    def part(function, *values):
        return functools.partial(function, *values)

    def expert_paired(number):
        paired(experts[number])
        if number + 4 < len(experts):
            experts[number + 4].local.start()

    queue += [part(expert_paired, number) for number in range(len(experts))]

    router_pad[...] = jnp.zeros(router_pad.shape, BF)
    router_pad[:, 0 : router.shape[1]] = router[...]
    gains[...] = jnp.zeros(gains.shape, F32)

    def norm_back(d_rows, inputs, scale, gain, row):
        scaled = d_rows * gain
        gains[row : row + 1, :] += jnp.sum(d_rows * inputs * scale, 0, keepdims=True)
        return scale * (
            scaled - inputs * scale * scale * jnp.mean(scaled * inputs, -1, keepdims=True)
        )

    def live_rows(m):
        return (row_base + lax.broadcasted_iota(jnp.int32, (rows, 1), 0)) < lengths[m, 0]

    router_lanes = router.shape[1]
    for m in range(micros):
        span = slice(m * rows, (m + 1) * rows)
        x_rows = tokens[m, 0].astype(F32)
        normed[span, :] = (x_rows * rms_scale(x_rows) * gain_one[...]).astype(BF)
        v = hidden[m]
        scale = rms_scale(v)
        normed2[span, :] = (v * scale * gain_two[...]).astype(BF)
        logits = nn(normed2[span, :], router_pad[...])
        lane = lane_ids(rows)
        ids = routes[m, 0, rows_at(z, rows), :]
        hit = jnp.zeros((rows, LANES), F32)
        for k in range(routes.shape[3]):
            hit = hit + (ids[:, k : k + 1] == lane).astype(F32)
        live = live_rows(m)
        on = jnp.where(live, hit, 0.0) > 0.0
        masked = jnp.where(on, logits, NEG_FILL)
        raised = jnp.where(on, jnp.exp(masked - jnp.max(masked, -1, keepdims=True)), 0.0)
        total = jnp.sum(raised, -1, keepdims=True)
        gate = raised / jnp.where(total > 0.0, total, 1.0)
        d_gate = moe[m, :, model:]
        d_logits[span, :] = (
            gate * (d_gate - jnp.sum(gate * d_gate, -1, keepdims=True))
        ).astype(BF)
        d_rows = moe[m, :, 0:model] + nt(d_logits[span, :], router_pad[...])
        grown = cot[m, 0].astype(F32) + norm_back(
            d_rows, v, scale, gain_two[...], router_lanes + 1
        )
        input_grad[m, 0] = grown
        d_attn[span, :] = jnp.where(live, grown, 0.0).astype(BF)

    loads[0].wait()
    d_mix[...] = nt(d_attn[...], w_out[...]).astype(BF)
    put_grads(2, mixture[...].reshape(both, mixture.shape[2]), d_attn[...])
    advance(2)
    cos = cos_ref[rows_at(z, rows), :]
    sin = sin_ref[rows_at(z, rows), :]

    def attend_back(m):
        score_bias(bias, row_base, lengths[m, 0])
        span = slice(m * rows, (m + 1) * rows)
        for i in range(chunks):
            lanes = slice(i * LANES, (i + 1) * LANES)
            value_lanes = slice(kv + i * LANES, kv + (i + 1) * LANES)
            pair = [
                d_mix[span, c * LANES : (c + 1) * LANES].astype(F32) for c in (2 * i, 2 * i + 1)
            ]
            for k, rows_of in enumerate(stack_heads(*pair)):
                stacked[k * rows : (k + 1) * rows, :] = rows_of.astype(BF)
            scores[...] = nt(keyval[m, :, lanes], queries[m, i])
            d_probs[...] = nt(keyval[m, :, value_lanes], stacked[...])
            for k in range(4):
                where = slice(k * rows, (k + 1) * rows)
                prob = softmax_columns(scores[:, where] + bias[...])
                d_prob = d_probs[:, where]
                delta = jnp.sum(prob * d_prob, 0, keepdims=True)
                d_scores[:, where] = (prob * (d_prob - delta)).astype(BF)
                probs[:, where] = prob.astype(BF)
            turned = tn(d_scores[...], keyval[m, :, lanes]) * ATTENTION_SCALE
            first, second = unstack_heads(turned, rows)
            for c, chunk in ((2 * i, first), (2 * i + 1, second)):
                d_query[span, c * LANES : (c + 1) * LANES] = rope(chunk, cos, -sin).astype(BF)
            kv_parts[m, :, lanes] = nn(d_scores[...], queries[m, i]).astype(BF)
            kv_parts[m, :, value_lanes] = nn(probs[...], stacked[...]).astype(BF)
            if i % 2 == 1:
                advance()

    slots = []
    for m in range(micros):
        attend_back(m)
        reduce_kv[m].slot(0)
    while queue:
        advance()
    for k in (4, 5):
        paired(dense[k])
    loads[1].wait()
    put_grads(0, normed[...], d_query[...])
    wide[...] = nt(d_query[...], w_query[...])
    for slot in range(1, count):
        for m in range(micros):
            queue.append(part(reduce_kv[m].slot, slot))
    first_wave = [part(crossed, item) for item in experts]
    for k, item in enumerate(first_wave):
        item()
        advance()
        if k == 1:
            for number in (0, 1):
                paired(dense[number])
    while queue:
        advance()
    loads[2].wait()
    for m in range(micros):
        span = slice(m * rows, (m + 1) * rows)
        key_own = d_probs.at[0:rows, 0:kv]
        value_own = d_probs.at[rows : 2 * rows, 0:kv]
        reduce_kv[m].total(key_own, slice(0, kv))
        reduce_kv[m].total(value_own, slice(kv, 2 * kv))
        for c in range(chunks):
            lanes = slice(c * LANES, (c + 1) * LANES)
            d_keyval[span, lanes] = rope(key_own[:, lanes], cos, -sin).astype(BF)
        d_keyval[span, kv:] = value_own[...].astype(BF)
    put_grads(1, normed[...], d_keyval[...])
    wide[...] += nt(d_keyval[...], w_keyval[...])
    for m in range(micros):
        span = slice(m * rows, (m + 1) * rows)
        x_rows = tokens[m, 0].astype(F32)
        input_grad[m, 0] += norm_back(
            wide[span, :], x_rows, rms_scale(x_rows), gain_one[...], router_lanes
        )
    small_value = tn(normed2[...], d_logits[...]) + gains[...].T
    small[...] = small_value.astype(BF).reshape(small.shape)
    dense[6].start()
    for k in (2, 3, 6):
        paired(dense[k])
    for k in (4, 5, 0, 1):
        crossed(dense[k])
    for number in range(len(experts)):
        expert_done(number)
    for k in (4, 5, 0, 1):
        dense_done(k)
    for k in (2, 3, 6):
        crossed(dense[k])
    for k in (2, 3, 6):
        dense_done(k)
    for k in range(7):
        line_done(k)
    for item in experts + dense + lines + reduce_kv:
        item.finish()


def backward_call(
    count, devices, tokens, lengths, routes, gain_one, w_query, w_keyval, w_out, gain_two,
    w_router, cot, local, ff, hidden, moe, queries, keyval, mixture, grad_gu, grad_dn,
):
    micros, _, rows, model = tokens.shape
    seq_len = routes.shape[2]
    kv = w_keyval.shape[1] // 2
    heads = w_query.shape[1]
    plane = plane_of(devices)
    block = model // devices // count
    group = max(block, GROUP)
    line = count * block
    half = model // 2
    both = micros * rows
    cos, sin = rope_constants(seq_len)
    gu_rows, dn_rows = model // devices, ff // devices
    vmem = pl.BlockSpec(memory_space=pltpu.VMEM)
    smem = pl.BlockSpec(memory_space=pltpu.SMEM)
    hbm = pl.BlockSpec(memory_space=pl.ANY)
    dma = pltpu.SemaphoreType.DMA
    hops = plane[0] + plane[1] - 1

    def reduce_scratch(lead, block_rows, width):
        lead = tuple(lead)
        return [
            pltpu.VMEM(lead + plane + (block_rows, width), BF),
            pltpu.VMEM(lead + (plane[1] - 1, plane[0], block_rows, width), BF),
            pltpu.VMEM(lead + (plane[0] - 1, block_rows, width), BF),
        ]

    wide_bf = pltpu.VMEM((both, model), BF)
    out_shape = (
        jax.ShapeDtypeStruct((micros, 1, rows, model), F32),
        jax.ShapeDtypeStruct((local, gu_rows, 2 * ff), F32),
        jax.ShapeDtypeStruct((local, dn_rows, model), F32),
        jax.ShapeDtypeStruct((3, group, model), F32),
        jax.ShapeDtypeStruct((group, LANES), F32),
    )
    scratch = (
        [pltpu.VMEM(w.shape, BF) for w in (w_query, w_keyval, w_out)]
        + [pltpu.VMEM((model, LANES), BF)]
        + [wide_bf, wide_bf, wide_bf, pltpu.VMEM((both, heads), BF)]
        + [pltpu.VMEM((both, 2 * kv), BF), pltpu.VMEM((both, LANES), BF)]
        + [pltpu.VMEM((both, model), F32)]
        + [pltpu.VMEM((LANES, model), F32)]
        + [pltpu.VMEM((seq_len, rows), F32)]
        + [pltpu.VMEM((seq_len, 4 * rows), F32)] * 2
        + [pltpu.VMEM((seq_len, 4 * rows), BF)] * 2
        + [pltpu.VMEM((4 * rows, LANES), BF)]
        + [pltpu.VMEM((micros, seq_len, 2 * kv), BF)]
        + [pltpu.VMEM((micros, count - 1, rows, 2 * kv), BF)]
        + [pltpu.VMEM((2,) + plane + (gu_rows, 2 * ff), BF)]
        + reduce_scratch((local,), gu_rows, 2 * ff)
        + [pltpu.VMEM((2,) + plane + (dn_rows, model), BF)]
        + reduce_scratch((local,), dn_rows, model)
        + [pltpu.VMEM((6,) + plane + (2, line, half), BF)]
        + reduce_scratch((6,), line, half)
        + [pltpu.VMEM((6, line, half), BF), pltpu.VMEM((6, count - 1, group, half), BF)]
        + [pltpu.VMEM(plane + (2, line, LANES), BF)]
        + reduce_scratch((), line, LANES)
        + [pltpu.VMEM((line, LANES), BF), pltpu.VMEM((count - 1, group, LANES), BF)]
        + [dma((local, 2, hops)), dma((local, 2, hops)), dma((6, 2, hops)), dma((2, hops))]
        + [dma((7, 2, count - 1)), dma((micros, 2, 2, count - 1)), dma((3,)), dma((2 * local,))]
    )
    dims = (micros, rows, count, local, ff, model)
    return pl.pallas_call(
        functools.partial(backward_kernel, dims, plane),
        out_shape=out_shape,
        in_specs=[smem] + [vmem] * 13 + [hbm] * 5,
        out_specs=(vmem,) * 5,
        scratch_shapes=scratch,
        name="layer_backward",
        compiler_params=pltpu.CompilerParams(
            collective_id=1, has_side_effects=True, vmem_limit_bytes=VMEM_LIMIT
        ),
    )(
        lengths, tokens, cot, routes, gain_one.reshape(1, -1), gain_two.reshape(1, -1),
        jnp.asarray(cos), jnp.asarray(sin), w_router, hidden, moe, queries, keyval, mixture,
        w_query, w_keyval, w_out,
        grad_gu.reshape((local,) + plane + (2, gu_rows, 2 * ff)),
        grad_dn.reshape((local,) + plane + (2, dn_rows, model)),
    )


def on_device(
    tokens, lengths, routes, attn_gain, w_query, w_keyval, w_out, ffn_gain, w_router,
    expert_gate_up, expert_down, cotangent,
):
    count = lax.axis_size("expert")
    devices = lax.axis_size("dp")
    model = tokens.shape[3]
    experts = w_router.shape[1]
    local, ff = expert_gate_up.shape[0], expert_down.shape[1]
    y, hidden, moe, queries, keyval, mixture, grad_gu, grad_dn = forward_call(
        count, tokens, lengths, routes, attn_gain, w_query, w_keyval, w_out, ffn_gain, w_router,
        expert_gate_up, expert_down, cotangent,
    )
    input_grad, gu, dn, dense, small = backward_call(
        count, devices, tokens, lengths, routes, attn_gain, w_query, w_keyval, w_out, ffn_gain,
        w_router, cotangent, local, ff, hidden, moe, queries, keyval, mixture, grad_gu, grad_dn,
    )
    block = model // devices // count
    if dense.shape[1] != block:
        first = lax.rem(lax.axis_index("expert") * block, dense.shape[1])
        dense = lax.dynamic_slice_in_dim(dense, first, block, 1)
        small = lax.dynamic_slice_in_dim(small, first, block, 0)
    return (
        y, input_grad, small[:, experts], dense[0], dense[1], dense[2], small[:, experts + 1],
        small[:, :experts], gu, dn,
    )


def solution(mesh):
    placed = (
        P(None, "dp", "expert", None), P(None, "dp"), P(None, "dp", None, None), P(), P(), P(), P(),
        P(), P(), P("expert", None, None), P("expert", None, None), P(None, "dp", "expert", None),
    )
    return jax.shard_map(
        on_device,
        mesh=mesh,
        in_specs=placed,
        out_specs=(
            P(None, "dp", "expert", None), P(None, "dp", "expert", None), P(("dp", "expert")),
            P(("dp", "expert"), None), P(("dp", "expert"), None), P(("dp", "expert"), None),
            P(("dp", "expert")), P(("dp", "expert"), None), P("expert", "dp", None),
            P("expert", "dp", None),
        ),
        check_vma=False,
    )
```

```python
import functools
import math

import jax
import jax.numpy as jnp
import numpy as np
from jax import lax
from jax.experimental import pallas as pl
from jax.experimental.pallas import tpu as pltpu
from jax.sharding import PartitionSpec as P

HEAD_DIM = 64
EPS = 1e-06
ATTENTION_SCALE = 0.015625
ROPE_BASE = 10000.0
NEG_FILL = -1e30
LANES = 128
GROUP = 16
STRIP = 64
BF = jnp.bfloat16
F32 = jnp.float32
VMEM_LIMIT = 63 * 2**20
(
    DO_NORM, DO_KV, DO_QUERY, DO_ATTEND, DO_GATE, DO_FWD, DO_OUT, DO_BWD, DO_GRAD, DO_ROUTER,
    DO_MIXTURE, DO_GRAD_OUT, DO_GRAD_QUERY, DO_TOTAL, DO_GRAD_KEYVAL, DO_KEYVAL, DO_INPUT,
    DO_SMALL, ON_S, ON_H, ON_L, ON_K, ON_N, ON_C, ON_O, ON_D, ON_E, ON_G, ON_P, ON_X, ON_Z,
) = range(31)
FORWARD_ORDER = (
    (ON_S, ON_C, 0, 0), (ON_S, ON_C, 0, 1), (DO_NORM,), (DO_KV,), (ON_S, ON_K, 0, 0), (ON_S, ON_C, 1, 1),
    (DO_QUERY,), (ON_S, ON_K, 1, 0), (ON_H, ON_K, 0, 0, 0), (ON_H, ON_K, 1, 0, 0), (ON_H, ON_K, 0, 0, 1),
    (ON_H, ON_K, 0, 0, 2), (DO_ATTEND, 0), (ON_H, ON_C, 1, 1, 0), (ON_S, ON_N, 0, 0),
    (ON_H, ON_K, 1, 0, 1), (ON_H, ON_C, 0, 1, 0), (ON_S, ON_N, 0, 1), (ON_H, ON_C, 0, 0, 0),
    (ON_H, ON_N, 0, 0, 0), (ON_H, ON_C, 1, 1, 1), (ON_H, ON_K, 1, 0, 2), (ON_H, ON_N, 0, 1, 0),
    (ON_H, ON_N, 0, 0, 1), (DO_ATTEND, 1), (ON_S, ON_N, 1, 0), (ON_H, ON_N, 0, 1, 1),
    (ON_H, ON_C, 0, 1, 1), (ON_S, ON_N, 1, 1), (ON_H, ON_N, 0, 1, 2), (ON_H, ON_N, 0, 0, 2), (DO_GATE, 0),
    (DO_FWD, 0, 0), (DO_FWD, 0, 1), (DO_FWD, 0, 2), (ON_H, ON_C, 0, 0, 1), (ON_H, ON_N, 1, 0, 0),
    (DO_FWD, 0, 3), (ON_S, ON_C, 1, 0), (DO_OUT, 0), (ON_H, ON_C, 0, 0, 2), (ON_L, ON_O, 0, 1, 0),
    (ON_H, ON_C, 0, 1, 2), (DO_BWD, 0, 0), (ON_L, ON_O, 0, 0, 0), (DO_BWD, 0, 1), (ON_H, ON_N, 1, 1, 0),
    (ON_L, ON_O, 0, 1, 1), (ON_L, ON_O, 0, 0, 1), (ON_H, ON_N, 1, 1, 1), (ON_H, ON_N, 1, 0, 1),
    (DO_BWD, 0, 2), (DO_BWD, 0, 3), (ON_L, ON_D, 0, 1, 0), (ON_L, ON_O, 0, 1, 2), (ON_L, ON_D, 0, 0, 0),
    (ON_H, ON_C, 1, 0, 0), (ON_H, ON_N, 1, 1, 2), (ON_H, ON_N, 1, 0, 2), (ON_L, ON_O, 0, 0, 2),
    (DO_GATE, 1), (ON_L, ON_D, 0, 1, 1), (DO_FWD, 1, 0), (DO_FWD, 1, 1), (ON_H, ON_C, 1, 0, 1),
    (DO_FWD, 1, 2), (ON_L, ON_D, 0, 0, 1), (DO_FWD, 1, 3), (ON_L, ON_O, 0, 1, 3), (ON_L, ON_O, 0, 0, 3),
    (ON_H, ON_C, 1, 1, 2), (DO_OUT, 1), (ON_L, ON_D, 0, 1, 2), (ON_L, ON_D, 0, 0, 2),
    (ON_H, ON_C, 1, 0, 2), (DO_BWD, 1, 0), (DO_BWD, 1, 1), (DO_BWD, 1, 2), (ON_L, ON_D, 0, 0, 3),
    (ON_L, ON_D, 0, 1, 3), (DO_BWD, 1, 3), (ON_L, ON_D, 1, 1, 0), (ON_L, ON_D, 1, 0, 0),
    (ON_L, ON_D, 1, 0, 1), (DO_GRAD, 0), (ON_L, ON_D, 1, 1, 1), (ON_L, ON_D, 1, 0, 2), (DO_GRAD, 1),
    (ON_L, ON_D, 1, 1, 2), (DO_GRAD, 2), (DO_GRAD, 3), (ON_L, ON_D, 1, 0, 3), (ON_L, ON_D, 1, 1, 3),
)
BACKWARD_ORDER = (
    (ON_P, ON_E, 0), (DO_ROUTER,), (ON_L, ON_O, 1, 0), (ON_P, ON_E, 2), (DO_MIXTURE,), (DO_GRAD_OUT,),
    (DO_ATTEND, 0, 0), (DO_ATTEND, 0, 1), (ON_P, ON_E, 1), (DO_ATTEND, 0, 2), (DO_ATTEND, 0, 3),
    (ON_L, ON_K, 0, 1, 0), (DO_ATTEND, 1, 0), (ON_P, ON_G, 5), (DO_ATTEND, 1, 1), (ON_P, ON_G, 4),
    (ON_L, ON_K, 0, 1, 1), (DO_ATTEND, 1, 2), (ON_P, ON_E, 3), (ON_P, ON_E, 5), (DO_ATTEND, 1, 3),
    (ON_L, ON_K, 1, 1, 0), (ON_L, ON_O, 0, 0), (DO_GRAD_QUERY,), (ON_X, ON_G, 4), (ON_X, ON_G, 5),
    (ON_P, ON_G, 1), (ON_L, ON_K, 1, 1, 1), (ON_P, ON_G, 0), (ON_X, ON_E, 1), (ON_D, ON_G, 5),
    (ON_L, ON_K, 0, 1, 2), (ON_X, ON_G, 1), (ON_P, ON_E, 6), (ON_P, ON_E, 4), (ON_X, ON_G, 0),
    (ON_P, ON_E, 7), (DO_QUERY,), (ON_X, ON_E, 3), (ON_L, ON_K, 1, 1, 2), (ON_L, ON_K, 1, 1, 3),
    (ON_L, ON_O, 0, 1), (ON_L, ON_K, 0, 1, 3), (DO_TOTAL,), (DO_GRAD_KEYVAL,), (ON_L, ON_O, 1, 1),
    (DO_KEYVAL,), (DO_INPUT,), (DO_SMALL,), (ON_P, ON_G, 2), (ON_L, ON_O, 0, 2), (ON_P, ON_G, 6),
    (ON_D, ON_E, 1), (ON_P, ON_G, 3), (ON_X, ON_E, 7), (ON_X, ON_G, 6), (ON_X, ON_G, 2), (ON_X, ON_E, 0),
    (ON_D, ON_G, 0), (ON_X, ON_G, 3), (ON_L, ON_O, 1, 2), (ON_D, ON_E, 7), (ON_D, ON_G, 1), (ON_X, ON_E, 2),
    (ON_D, ON_E, 3), (ON_D, ON_G, 6), (ON_D, ON_G, 3), (ON_X, ON_E, 6), (ON_Z, ON_G, 5), (ON_Z, ON_G, 1),
    (ON_X, ON_E, 4), (ON_D, ON_G, 2), (ON_L, ON_O, 0, 3), (ON_D, ON_G, 4), (ON_D, ON_E, 0), (ON_Z, ON_G, 0),
    (ON_L, ON_O, 1, 3), (ON_X, ON_E, 5), (ON_D, ON_E, 2), (ON_Z, ON_G, 4), (ON_D, ON_E, 4), (ON_Z, ON_G, 2),
    (ON_Z, ON_G, 6), (ON_Z, ON_G, 3), (ON_D, ON_E, 6), (ON_D, ON_E, 5),
)


def dot_of(left, right, left_dim, right_dim):
    return lax.dot_general(
        left, right, (((left_dim,), (right_dim,)), ((), ())), preferred_element_type=F32
    )


def nn(left, right):
    return dot_of(left, right, 1, 0)


def nt(left, right):
    return dot_of(left, right, 1, 1)


def tn(left, right):
    return dot_of(left, right, 0, 0)


def rope_constants(seq_len):
    half = HEAD_DIM // 2
    frequency = np.exp(
        np.arange(half, dtype=np.float32) * np.float32(-2.0 * math.log(ROPE_BASE) / HEAD_DIM)
    ).astype(np.float32)
    angles = np.arange(seq_len, dtype=np.float32)[:, None] * frequency[None, :]
    cos, sin = np.cos(angles).astype(np.float32), np.sin(angles).astype(np.float32)
    heads = LANES // HEAD_DIM
    return np.tile(np.concatenate([cos, cos], 1), (1, heads)), np.tile(
        np.concatenate([-sin, sin], 1), (1, heads)
    )


def lane_ids(rows):
    return lax.broadcasted_iota(jnp.int32, (rows, LANES), 1)


def swap_halves(chunk):
    half = HEAD_DIM // 2
    first = lax.rem(lane_ids(chunk.shape[0]), HEAD_DIM) < half
    return jnp.where(
        first, pltpu.roll(chunk, LANES - half, 1), pltpu.roll(chunk, half, 1)
    )


def rope(chunk, cos, sin):
    return chunk * cos + swap_halves(chunk) * sin


def rms_scale(rows):
    return lax.rsqrt(jnp.mean(rows * rows, -1, keepdims=True) + EPS)


def stack_heads(first, second):
    low = lane_ids(first.shape[0]) < HEAD_DIM
    zero = jnp.zeros_like(first)
    return [
        jnp.where(low, first, zero),
        jnp.where(low, pltpu.roll(first, HEAD_DIM, 1), zero),
        jnp.where(low, zero, pltpu.roll(second, HEAD_DIM, 1)),
        jnp.where(low, zero, second),
    ]


def unstack_heads(stacked, rows):
    low = lane_ids(rows) < HEAD_DIM
    parts = [stacked[k * rows : (k + 1) * rows] for k in range(4)]
    first = jnp.where(low, parts[0], pltpu.roll(parts[1], HEAD_DIM, 1))
    second = jnp.where(low, pltpu.roll(parts[2], HEAD_DIM, 1), parts[3])
    return first, second


def rows_at(index, rows):
    return pl.ds(pl.multiple_of(index * rows, rows), rows)


def natural_order(chain, services, before):
    order, placed = [], set()

    def place(item):
        if item not in placed:
            placed.add(item)
            for first, then in before:
                if then == item:
                    place(first)
            order.append(item)

    for item in chain + services:
        place(item)
    return order


def chained(*items):
    return list(zip(items, items[1:]))


def named_lanes(ids):
    lane = lax.broadcasted_iota(jnp.int32, (LANES, ids.shape[1]), 0)
    hit = jnp.zeros(lane.shape, F32)
    for k in range(ids.shape[0]):
        hit = hit + (ids[k : k + 1, :] == lane).astype(F32)
    return hit.T


class Gather:
    def __init__(self, buffer, micro, rows, count, sems, up=True, down=True):
        self.buffer, self.micro, self.rows, self.count, self.sems = buffer, micro, rows, count, sems
        self.ways = [w for w, on in ((0, up), (1, down)) if on]

    def copy(self, way, step, block):
        z = lax.axis_index("expert")
        target = z + 1 if way == 0 else z - 1
        view = self.buffer.at[self.micro, rows_at(block, self.rows), :]
        return pltpu.make_async_remote_copy(
            src_ref=view,
            dst_ref=view,
            send_sem=self.sems.at[0, way, step],
            recv_sem=self.sems.at[1, way, step],
            device_id={"expert": target},
            device_id_type=pl.DeviceIdType.MESH,
        )

    def sends(self, way, step):
        z = lax.axis_index("expert")
        if way == 0:
            return z - step, jnp.logical_and(z < self.count - 1, z - step >= 0)
        return z + step, jnp.logical_and(z > 0, z + step <= self.count - 1)

    def receives(self, way, step):
        z = lax.axis_index("expert")
        if way == 0:
            return z - 1 - step, z - 1 - step >= 0
        return z + 1 + step, z + 1 + step <= self.count - 1

    def start(self, way, step):
        block, on = self.sends(way, step)

        @pl.when(on)
        def _():
            self.copy(way, step, block).start()

    def hop(self, way, step):
        block, on = self.receives(way, step)

        @pl.when(on)
        def _():
            self.copy(way, step, block).wait_recv()

        if step + 1 < self.count - 1:
            self.start(way, step + 1)

    def finish(self):
        for step in range(self.count - 1):
            for way in self.ways:
                block, on = self.sends(way, step)

                @pl.when(on)
                def _(way=way, step=step, block=block):
                    self.copy(way, step, block).wait_send()


class Reduce:
    def __init__(self, parts, landing, rows, count, sems, up=True, down=True):
        self.parts, self.landing = parts, landing
        self.rows, self.count, self.sems = rows, count, sems
        self.ways = [w for w, on in ((0, up), (1, down)) if on]

    def block(self, way, slot):
        z = lax.axis_index("expert")
        if way == 0:
            return z + self.count - 1 - slot, slot >= z
        return z - (self.count - 1) + slot, slot >= self.count - 1 - z

    def place(self, way, slot, z):
        if way == 0:
            return slot - (z - 1)
        return self.count - (slot - (self.count - 2 - z)) - (2 if self.ways == [1] else 0)

    def copy(self, way, slot, block):
        z = lax.axis_index("expert")
        target = z + 1 if way == 0 else z - 1
        return pltpu.make_async_remote_copy(
            src_ref=self.parts.at[rows_at(block, self.rows), :],
            dst_ref=self.landing.at[self.place(way, slot, target)],
            send_sem=self.sems.at[0, way, slot],
            recv_sem=self.sems.at[1, way, slot],
            device_id={"expert": target},
            device_id_type=pl.DeviceIdType.MESH,
        )

    def arrival(self, way, slot, block):
        z = lax.axis_index("expert")
        source = z - 1 if way == 0 else z + 1
        return pltpu.make_async_remote_copy(
            src_ref=self.parts.at[rows_at(block, self.rows), :],
            dst_ref=self.landing.at[self.place(way, slot, z)],
            send_sem=self.sems.at[0, way, slot],
            recv_sem=self.sems.at[1, way, slot],
            device_id={"expert": source},
            device_id_type=pl.DeviceIdType.MESH,
        )

    def inner(self, way):
        z = lax.axis_index("expert")
        return z >= 1 if way == 0 else z <= self.count - 2

    def slot(self, way, slot):
        z = lax.axis_index("expert")
        block, on = self.block(way, slot)
        if slot >= 1:

            @pl.when(jnp.logical_and(on, self.inner(way)))
            def _():
                self.arrival(way, slot - 1, block).wait_recv()
                if slot < self.count - 1:
                    where = rows_at(block, self.rows)
                    total = self.parts[where, :].astype(F32) + self.landing[
                        self.place(way, slot - 1, z)
                    ].astype(F32)
                    self.parts[where, :] = total.astype(self.parts.dtype)

        if slot < self.count - 1:

            @pl.when(on)
            def _():
                self.copy(way, slot, block).start()

    def total(self, out, lanes=slice(None)):
        z = lax.axis_index("expert")
        out[...] = self.parts[rows_at(z, self.rows), lanes].astype(F32)
        for way in self.ways:

            @pl.when(self.inner(way))
            def _(way=way):
                place = self.place(way, self.count - 2, z)
                out[...] += self.landing[place, :, lanes].astype(F32)

    def finish(self):
        for slot in range(self.count - 1):
            for way in self.ways:
                block, on = self.block(way, slot)

                @pl.when(on)
                def _(way=way, slot=slot, block=block):
                    self.copy(way, slot, block).wait_send()


def line_barrier(count):
    z = lax.axis_index("expert")
    barrier = pltpu.get_barrier_semaphore()
    for target, on in ((z + 1, z < count - 1), (z - 1, z > 0)):

        @pl.when(on)
        def _(target=target):
            pl.semaphore_signal(
                barrier, inc=1, device_id={"expert": target}, device_id_type=pl.DeviceIdType.MESH
            )

    pl.semaphore_wait(barrier, (z > 0).astype(jnp.int32) + (z < count - 1).astype(jnp.int32))


def score_bias(bias, row_base, length):
    key_pos = lax.broadcasted_iota(jnp.int32, bias.shape, 0)
    query_pos = row_base + lax.broadcasted_iota(jnp.int32, bias.shape, 1)
    allowed = jnp.logical_and(key_pos <= query_pos, key_pos < length)
    bias[...] = jnp.where(allowed, 0.0, NEG_FILL)


def softmax_columns(scores):
    raised = jnp.exp(scores - jnp.max(scores, 0, keepdims=True))
    return raised * (1.0 / jnp.sum(raised, 0, keepdims=True))


def sigmoid(v):
    return 0.5 * jnp.tanh(0.5 * v) + 0.5


def late_sums(count):
    return count <= 4


def forward_kernel(
    dims,
    lengths,
    tokens,
    cot,
    routes,
    gain_one,
    gain_two,
    cos_ref,
    sin_ref,
    router,
    query_hbm,
    keyval_hbm,
    out_hbm,
    gate_up_hbm,
    down_hbm,
    y_out,
    hidden_out,
    moe_out,
    queries_out,
    keyval_out,
    mixture_out,
    grad_gu_out,
    grad_dn_out,
    late_out,
    wide,
    narrow,
    normed,
    queries,
    keyval,
    mixture,
    hidden,
    named,
    gates,
    gate_lanes,
    gate_terms,
    router_pad,
    rows_all,
    cot_all,
    acts,
    d_proj,
    w_out,
    w_gu,
    w_dn,
    out_parts,
    out_land,
    in_parts,
    in_land,
    own_sum,
    moe_sum,
    kv_sems,
    rows_sems,
    cot_sems,
    out_sems,
    in_sems,
    load_sems,
    store_sems,
    free_sems,
):
    micros, rows, count, local, ff, model, late = dims
    seq_len = count * rows
    kv = keyval.shape[2] // 2
    chunks = kv // LANES
    z = lax.axis_index("expert")
    row_base = z * rows
    split = -(-model // seq_len)
    piece = model // split
    back = wide
    bias = gate_terms.at[:, 0:rows]
    scores = wide.at[:, 0 : 4 * rows]
    probs = d_proj.at[micros * local - 1, :, 0 : 4 * rows]
    tile = 512

    loads = []

    def load(src, dst):
        copy = pltpu.make_async_copy(src, dst, load_sems.at[len(loads)])
        copy.start()
        loads.append(copy)
        return copy

    early = []
    for index, weight in enumerate((query_hbm, keyval_hbm)):
        early.append(
            [
                load(
                    weight.at[pl.ds(k * piece, piece), :],
                    d_proj.at[index * split + k, pl.ds(0, piece), :],
                )
                for k in range(split)
            ]
        )
    load_out = load(out_hbm, w_out)
    load_gu = load(gate_up_hbm, w_gu)
    load_dn = load(down_hbm, w_dn)

    line_barrier(count)

    gather_kv = [
        Gather(keyval, m, rows, count, kv_sems.at[m], down=False) for m in range(micros)
    ]
    gather_rows = [Gather(rows_all, m, rows, count, rows_sems.at[m]) for m in range(micros)]
    gather_cot = [Gather(cot_all, m, rows, count, cot_sems.at[m]) for m in range(micros)]
    reduce_out = [
        Reduce(out_parts, out_land, rows, count, out_sems.at[m]) for m in range(micros)
    ]
    reduce_in = [Reduce(in_parts, in_land, rows, count, in_sems.at[m]) for m in range(micros)]

    for m in range(micros):
        cot_all[m, rows_at(z, rows), :] = cot[m, 0]

    both = micros * rows

    def norm():
        for m in range(micros):
            x_rows = tokens[m, 0].astype(F32)
            normed[m * rows : (m + 1) * rows, :] = (
                x_rows * rms_scale(x_rows) * gain_one[...]
            ).astype(BF)

    cos = cos_ref[rows_at(z, rows), :]
    sin = sin_ref[rows_at(z, rows), :]

    def project(index):
        for copy in early[index]:
            copy.wait()
        total = None
        for k in range(split):
            part = nn(
                normed[:, k * piece : (k + 1) * piece], d_proj[index * split + k, 0:piece, :]
            )
            total = part if total is None else total + part
        wide[0:both, :] = total

    def keys_values():
        project(1)
        for m in range(micros):
            span = slice(m * rows, (m + 1) * rows)
            for c in range(chunks):
                lanes = slice(c * LANES, (c + 1) * LANES)
                keyval[m, rows_at(z, rows), lanes] = rope(wide[span, lanes], cos, sin).astype(BF)
            keyval[m, rows_at(z, rows), kv:] = wide[span, kv:].astype(BF)

    def first_queries():
        project(0)
        for m in range(micros):
            span = slice(m * rows, (m + 1) * rows)
            for i in range(chunks):
                pair = [
                    rope(wide[span, c * LANES : (c + 1) * LANES], cos, sin)
                    for c in (2 * i, 2 * i + 1)
                ]
                for k, block in enumerate(stack_heads(*pair)):
                    queries[m, i, k * rows : (k + 1) * rows, :] = (
                        block.astype(BF) * ATTENTION_SCALE
                    ).astype(BF)
            for b in range(count):

                @pl.when(b > z)
                def _(m=m, b=b):
                    keyval[m, b * rows : (b + 1) * rows, :] = jnp.zeros((rows, 2 * kv), BF)

            live = lax.broadcasted_iota(jnp.int32, (seq_len, LANES), 0) < lengths[0, m]
            named[m] = jnp.where(live, named_lanes(routes[m, 0]), 0.0)
        router_pad[...] = jnp.zeros(router_pad.shape, BF)
        router_pad[0 : router.shape[0], :] = router[...]

    def attend(m):
        length = lengths[0, m]
        score_bias(bias, row_base, length)
        for i in range(chunks):
            lanes = slice(i * LANES, (i + 1) * LANES)
            scores[...] = nt(keyval[m, :, lanes], queries[m, i])
            for k in range(4):
                span = slice(k * rows, (k + 1) * rows)
                probs[:, span] = softmax_columns(scores[:, span] + bias[...]).astype(BF)
            mixed = tn(probs[...], keyval[m, :, kv + i * LANES : kv + (i + 1) * LANES])
            first, second = unstack_heads(mixed, rows)
            mixture[m, :, 2 * i * LANES : (2 * i + 1) * LANES] = first.astype(BF)
            mixture[m, :, (2 * i + 1) * LANES : (2 * i + 2) * LANES] = second.astype(BF)
        if m == 0:
            load_out.wait()
        live = (row_base + lax.broadcasted_iota(jnp.int32, (rows, 1), 0)) < length
        rows_hidden = tokens[m, 0].astype(F32) + jnp.where(
            live, nn(mixture[m], w_out[...]), 0.0
        )
        hidden[m] = rows_hidden
        rows_all[m, rows_at(z, rows), :] = (
            rows_hidden * rms_scale(rows_hidden) * gain_two[...]
        ).astype(BF)

    def gate_rows(m):
        if m == 0:
            load_gu.wait()
            load_dn.wait()
        logits = nt(rows_all[m], router_pad[...])
        on = named[m] > 0.0
        masked = jnp.where(on, logits, NEG_FILL)
        raised = jnp.where(on, jnp.exp(masked - jnp.max(masked, -1, keepdims=True)), 0.0)
        total = jnp.sum(raised, -1, keepdims=True)
        gate = raised / jnp.where(total > 0.0, total, 1.0)
        for j in range(local):
            gate_lanes[j] = jnp.broadcast_to(column(gate, z * local + j), gate.shape)

    def column(block, expert):
        return jnp.sum(
            jnp.where(lane_ids(block.shape[0]) == expert, block, 0.0), -1, keepdims=True
        )

    blocks = [slice(c, c + LANES) for c in range(0, ff, LANES)]

    def expert_forward(m, j):
        wide[...] = nn(rows_all[m], w_gu[j])

        def strip_step(strip, carry):
            where = rows_at(strip, STRIP)
            gate = gate_lanes[j, where, :]
            for c, lanes in enumerate(blocks):
                front, up = wide[where, lanes], wide[where, ff + c * LANES : ff + (c + 1) * LANES]
                value = front * sigmoid(front) * up * gate
                acts[m, where, j * ff + c * LANES : j * ff + (c + 1) * LANES] = value.astype(BF)
            d_proj[m * local + j, where, :] = wide[where, :].astype(BF)
            return carry

        lax.fori_loop(0, seq_len // STRIP, strip_step, 0)

    def expert_backward(m, j):
        expert = z * local + j
        narrow[...] = nt(cot_all[m], w_dn[j * ff : (j + 1) * ff, :])

        def strip_step(strip, carry):
            where = rows_at(strip, STRIP)
            gate = gate_lanes[j, where, :]
            terms = None
            for c, lanes in enumerate(blocks):
                up_lanes = slice(ff + c * LANES, ff + (c + 1) * LANES)
                front = d_proj[m * local + j, where, lanes].astype(F32)
                up = d_proj[m * local + j, where, up_lanes].astype(F32)
                d_act = narrow[where, lanes]
                sig = sigmoid(front)
                silu = front * sig
                term = d_act * silu
                terms = term * up if terms is None else terms + term * up
                d_proj[m * local + j, where, up_lanes] = (term * gate).astype(BF)
                d_proj[m * local + j, where, lanes] = (
                    d_act * gate * up * (sig + silu * (1.0 - sig))
                ).astype(BF)
            gate_terms[where, :] = terms
            return carry

        lax.fori_loop(0, seq_len // STRIP, strip_step, 0)
        d_gate = jnp.sum(gate_terms[...], -1, keepdims=True)
        mine = lane_ids(seq_len) == expert
        if j == 0:
            gates[...] = jnp.where(mine, d_gate, 0.0)
        else:
            gates[...] = jnp.where(mine, d_gate, gates[...])
        if j == local - 1:
            in_parts[:, model:] = (gates[...] * named[m]).astype(BF)
        for r in range(0, seq_len, tile):
            span = slice(r, r + tile)
            part = nt(d_proj[m * local + j, span, :], w_gu[j])
            if j == 0:
                back[span, :] = part
            elif j < local - 1:
                back[span, :] += part
            else:
                in_parts[span, 0:model] = (back[span, :] + part).astype(BF)

    def weight_grads(j):
        for part_of in range(4):
            lanes = slice(part_of * ff // 2, (part_of + 1) * ff // 2)
            total = None
            for m in range(micros):
                part = tn(rows_all[m], d_proj[m * local + j, :, lanes])
                total = part if total is None else total + part
            w_gu[j, :, lanes] = total.astype(BF)
        total = None
        for m in range(micros):
            part = tn(acts[m, :, j * ff : (j + 1) * ff], cot_all[m])
            total = part if total is None else total + part
        w_dn[j * ff : (j + 1) * ff, :] = total.astype(BF)

    def out_rows(m):
        for r in range(0, seq_len, tile):
            out_parts[r : r + tile, :] = nn(acts[m, r : r + tile, :], w_dn[...]).astype(BF)

    stores = []

    def store(src, dst):
        copy = pltpu.make_async_copy(src, dst, store_sems.at[len(stores)])
        copy.start()
        stores.append(copy)

    def grad(j):
        weight_grads(j)
        store(w_gu.at[j], grad_gu_out.at[j])
        store(w_dn.at[pl.ds(j * ff, ff), :], grad_dn_out.at[pl.ds(j * ff, ff), :])

    def finish_out(m):
        reduce_out[m].total(own_sum)
        y_out[m, 0] = (hidden[m] + own_sum[...]).astype(BF)
        reduce_out[m].finish()
        if not late:
            free_landing(0, m)

    def finish_in(m):
        reduce_in[m].total(moe_sum.at[m])
        reduce_in[m].finish()
        free_landing(1, m)

    def free_landing(kind, m):
        if m < micros - 1:
            for way, target, on in ((0, z - 1, z > 0), (1, z + 1, z < count - 1)):

                @pl.when(on)
                def _(way=way, target=target):
                    pl.semaphore_signal(
                        free_sems.at[kind, way], inc=1, device_id={"expert": target},
                        device_id_type=pl.DeviceIdType.MESH,
                    )

    def reduce_slot(kind, m, way, slot):
        if m > 0 and slot == 0:

            @pl.when(z < count - 1 if way == 0 else z > 0)
            def _():
                pl.semaphore_wait(free_sems.at[kind, way], 1)

        (reduce_out, reduce_in)[kind][m].slot(way, slot)

    steps, last = count - 1, local - 1
    work, before, services = {}, [], []
    work[DO_NORM,], work[DO_KV,], work[DO_QUERY,] = norm, keys_values, first_queries
    chain = [(DO_NORM,), (DO_KV,), (DO_QUERY,)]
    for name, function in ((DO_ATTEND, attend),):
        for m in range(micros):
            work[name, m] = functools.partial(function, m)
            chain.append((name, m))
    for m in range(micros):
        work[DO_GATE, m] = functools.partial(gate_rows, m)
        work[DO_OUT, m] = functools.partial(out_rows, m)
        chain.append((DO_GATE, m))
        for name, function in ((DO_FWD, expert_forward), (DO_BWD, expert_backward)):
            for j in range(local):
                work[name, m, j] = functools.partial(function, m, j)
                chain.append((name, m, j))
            if name == DO_FWD:
                chain.append((DO_OUT, m))
    for j in range(local):
        work[DO_GRAD, j] = functools.partial(grad, j)
        chain.append((DO_GRAD, j))
    before += chained(*chain)
    for m in range(micros):
        for name, gather, after, ahead in (
            (ON_K, gather_kv[m], (DO_KV,), (DO_ATTEND, m)),
            (ON_N, gather_rows[m], (DO_ATTEND, m), (DO_GATE, m)),
            (ON_C, gather_cot[m], None, (DO_BWD, m, 0)),
        ):
            for way in gather.ways:
                items = [(ON_S, name, m, way)]
                work[items[0]] = functools.partial(gather.start, way, 0)
                for step in range(steps):
                    items.append((ON_H, name, m, way, step))
                    work[items[-1]] = functools.partial(gather.hop, way, step)
                services += items
                before += chained(*([after] if after else []), *items, ahead)
        for name, after in ((ON_O, (DO_OUT, m)), (ON_D, (DO_BWD, m, last))):
            if name == ON_O and m > 0 and late:
                continue
            for way in range(2):
                items = [(ON_L, name, m, way, t) for t in range(count)]
                for t, item in enumerate(items):
                    work[item] = functools.partial(reduce_slot, int(name == ON_D), m, way, t)
                services += items
                before += chained(after, *items)
                if m < micros - 1:
                    before.append((items[-1], (DO_BWD, m + 1, last) if name == ON_D else (DO_OUT, m + 1)))
    order = [item for item in FORWARD_ORDER if item in work]
    if set(order) != set(work):
        order = natural_order(chain, services, before)
    done = set()
    for item in order:
        work[item]()
        done.add(item)
        if item[0] == ON_L and item[4] == count - 1:
            if item[:3] + (1 - item[3], count - 1) in done:
                (finish_out if item[1] == ON_O else finish_in)(item[2])
        if item == (DO_OUT, micros - 1) and late:
            store(out_parts, late_out)
        if item == (DO_ATTEND, micros - 1):
            for src, dst in (
                (hidden, hidden_out), (queries, queries_out), (keyval, keyval_out),
                (mixture, mixture_out),
            ):
                store(src, dst)
    store(moe_sum, moe_out)
    for item in gather_kv + gather_rows + gather_cot:
        item.finish()
    for copy in stores:
        copy.wait()


def forward_call(
    count, tokens, lengths, routes, gain_one, w_query, w_keyval, w_out, gain_two, w_router,
    gate_up, down, cot,
):
    micros, _, rows, model = tokens.shape
    local, ff = gate_up.shape[0], down.shape[1]
    seq_len = routes.shape[2]
    kv = w_keyval.shape[1] // 2
    chunks = kv // LANES
    heads = w_query.shape[1]
    steps = count - 1
    split = -(-model // seq_len)
    cos, sin = rope_constants(seq_len)
    vmem = pl.BlockSpec(memory_space=pltpu.VMEM)
    smem = pl.BlockSpec(memory_space=pltpu.SMEM)
    hbm = pl.BlockSpec(memory_space=pl.ANY)
    dma = pltpu.SemaphoreType.DMA
    wide_in = model + LANES
    out_shape = (
        jax.ShapeDtypeStruct((micros, 1, rows, model), BF),
        jax.ShapeDtypeStruct((micros, rows, model), F32),
        jax.ShapeDtypeStruct((micros, rows, wide_in), F32),
        jax.ShapeDtypeStruct((micros, chunks, 4 * rows, LANES), BF),
        jax.ShapeDtypeStruct((micros, seq_len, 2 * kv), BF),
        jax.ShapeDtypeStruct((micros, rows, heads), BF),
        jax.ShapeDtypeStruct((local, model, 2 * ff), BF),
        jax.ShapeDtypeStruct((local * ff, model), BF),
        jax.ShapeDtypeStruct((seq_len, model), BF),
    )
    scratch = [
        pltpu.VMEM((seq_len, model), F32),
        pltpu.VMEM((seq_len, ff), F32),
        pltpu.VMEM((micros * rows, model), BF),
        pltpu.VMEM((micros, chunks, 4 * rows, LANES), BF),
        pltpu.VMEM((micros, seq_len, 2 * kv), BF),
        pltpu.VMEM((micros, rows, heads), BF),
        pltpu.VMEM((micros, rows, model), F32),
        pltpu.VMEM((micros, seq_len, LANES), F32),
        pltpu.VMEM((seq_len, LANES), F32),
        pltpu.VMEM((local, seq_len, LANES), F32),
        pltpu.VMEM((seq_len, LANES), F32),
        pltpu.VMEM((LANES, model), BF),
        pltpu.VMEM((micros, seq_len, model), BF),
        pltpu.VMEM((micros, seq_len, model), BF),
        pltpu.VMEM((micros, seq_len, local * ff), BF),
        pltpu.VMEM((micros * local, seq_len, 2 * ff), BF),
        pltpu.VMEM(w_out.shape, BF),
        pltpu.VMEM((local, model, 2 * ff), BF),
        pltpu.VMEM((local * ff, model), BF),
        pltpu.VMEM((seq_len, model), BF),
        pltpu.VMEM((count + 1, rows, model), BF),
        pltpu.VMEM((seq_len, wide_in), BF),
        pltpu.VMEM((count + 1, rows, wide_in), BF),
        pltpu.VMEM((rows, model), F32),
        pltpu.VMEM((micros, rows, wide_in), F32),
    ] + [dma((micros, 2, 2, steps))] * 5 + [dma((2 * split + 3,)), dma((2 * local + 6,))]
    scratch.append(pltpu.SemaphoreType.REGULAR((2, 2)))
    dims = (micros, rows, count, local, ff, model, late_sums(count))
    return pl.pallas_call(
        functools.partial(forward_kernel, dims),
        out_shape=out_shape,
        in_specs=[smem] + [vmem] * 8 + [hbm] * 5,
        out_specs=(vmem,) + (hbm,) * 8,
        scratch_shapes=scratch,
        name="layer_forward",
        compiler_params=pltpu.CompilerParams(
            collective_id=0, has_side_effects=True, vmem_limit_bytes=VMEM_LIMIT
        ),
    )(
        lengths.T, tokens, cot, jnp.swapaxes(routes, 2, 3), gain_one.reshape(1, -1),
        gain_two.reshape(1, -1), jnp.asarray(cos), jnp.asarray(sin), w_router.T, w_query, w_keyval, w_out, gate_up,
        down.reshape(local * ff, model),
    )


def plane_of(devices):
    side = math.isqrt(devices // 2)
    return side, side


def device_at(plane, y, x, core):
    return {"dp": (y * plane[1] + x) * 2 + core}


class PlaneReduce:
    def __init__(self, plane, source, own, total, first_land, second_land, x_first, sems, local=None):
        self.plane, self.source, self.own, self.total = plane, source, own, total
        self.lands, self.x_first, self.sems, self.local = (first_land, second_land), x_first, sems, local
        index = lax.axis_index("dp")
        self.core = lax.rem(index, 2)
        chip = index // 2
        self.y, self.x = chip // plane[1], lax.rem(chip, plane[1])

    def remote(self, src, dst, number, where):
        return pltpu.make_async_remote_copy(
            src_ref=src,
            dst_ref=dst,
            send_sem=self.sems.at[0, number],
            recv_sem=self.sems.at[1, number],
            device_id=device_at(self.plane, *where),
            device_id_type=pl.DeviceIdType.MESH,
        )

    def sibling(self):
        return self.remote(
            self.source.at[:, :, 1 - self.core], self.total, 0, (self.y, self.x, 1 - self.core)
        )

    def start(self):
        self.sibling().start()

    def along(self, stage):
        return self.x_first == (stage == 0)

    def hops(self, stage):
        along_x = self.along(stage)
        size = self.plane[1] if along_x else self.plane[0]
        base = 1 if stage == 0 else self.plane[1] if self.x_first else self.plane[0]
        for k in range(1, size):
            if along_x:
                place = lax.rem(self.x + k, size)
                where = (self.y, place, self.core)
                view = (
                    self.total.at[:, place] if stage == 0 else self.total.at[self.y, place]
                )
            else:
                place = lax.rem(self.y + k, size)
                where = (place, self.x, self.core)
                view = self.total.at[place] if stage == 0 else self.total.at[place, self.x]
            yield k, self.remote(view, self.lands[stage].at[k - 1], base + k - 1, where)

    def send(self, stage):
        for _, copy in self.hops(stage):
            copy.start()

    def pair_sum(self):
        if self.local is not None:
            self.local.wait()
        self.sibling().wait_recv()
        count = self.plane[0] * self.plane[1]
        for b in range(count):
            y, x = b // self.plane[1], b % self.plane[1]
            own = self.own[y, x] if self.local is not None else self.source[y, x, self.core]
            self.total[y, x] = (self.total[y, x].astype(F32) + own.astype(F32)).astype(BF)

    def take(self, stage):
        land = self.lands[stage]
        for k, copy in self.hops(stage):
            copy.wait_recv()
        if stage == 0:
            for other in range(self.plane[0] if self.x_first else self.plane[1]):
                where = (other, self.x) if self.x_first else (self.y, other)
                summed = self.total[where].astype(F32)
                for k in range(land.shape[0]):
                    summed = summed + land[k, other].astype(F32)
                self.total[where] = summed.astype(BF)
            return None
        summed = self.total[self.y, self.x].astype(F32)
        for k in range(land.shape[0]):
            summed = summed + land[k].astype(F32)
        return summed

    def finish(self):
        self.sibling().wait_send()
        for stage in range(2):
            for _, copy in self.hops(stage):
                copy.wait_send()


class LineReduce:
    def __init__(self, parts, land, rows, count, sems):
        self.parts, self.land, self.rows, self.count, self.sems = parts, land, rows, count, sems
        self.group = max(rows, GROUP)

    def span(self, z):
        if self.group == self.rows:
            return rows_at(z, self.rows)
        return pl.ds(pl.multiple_of(z * self.rows // self.group * self.group, self.group), self.group)

    def hops(self):
        z = lax.axis_index("expert")
        for k in range(1, self.count):
            target = lax.rem(z + k, self.count)
            yield k, pltpu.make_async_remote_copy(
                src_ref=self.parts.at[self.span(target), :],
                dst_ref=self.land.at[k - 1],
                send_sem=self.sems.at[0, k - 1],
                recv_sem=self.sems.at[1, k - 1],
                device_id={"expert": target},
                device_id_type=pl.DeviceIdType.MESH,
            )

    def start(self):
        for _, copy in self.hops():
            copy.start()

    def total(self):
        for _, copy in self.hops():
            copy.wait_recv()
        summed = self.parts[self.span(lax.axis_index("expert")), :].astype(F32)
        for k in range(self.count - 1):
            summed = summed + self.land[k].astype(F32)
        return summed

    def finish(self):
        for _, copy in self.hops():
            copy.wait_send()


def full_barrier(plane, count):
    index = lax.axis_index("dp")
    z = lax.axis_index("expert")
    core, chip = lax.rem(index, 2), index // 2
    y, x = chip // plane[1], lax.rem(chip, plane[1])
    barrier = pltpu.get_barrier_semaphore()
    greeted = [device_at(plane, y, x, 1 - core)]
    greeted += [device_at(plane, y, lax.rem(x + k, plane[1]), core) for k in range(1, plane[1])]
    greeted += [device_at(plane, lax.rem(y + k, plane[0]), x, core) for k in range(1, plane[0])]
    greeted += [{"expert": lax.rem(z + k, count)} for k in range(1, count)]
    for device in greeted:
        pl.semaphore_signal(barrier, inc=1, device_id=device, device_id_type=pl.DeviceIdType.MESH)
    pl.semaphore_wait(barrier, len(greeted))


def backward_kernel(
    dims,
    plane,
    lengths,
    tokens,
    cot,
    routes,
    gain_one,
    gain_two,
    cos_ref,
    sin_ref,
    router,
    y_first,
    hidden,
    moe,
    queries,
    keyval,
    mixture,
    query_hbm,
    keyval_hbm,
    out_hbm,
    grad_gu,
    grad_dn,
    late_parts,
    y_out,
    input_grad,
    gu_out,
    dn_out,
    dense_out,
    small_out,
    w_query,
    w_keyval,
    w_out,
    router_pad,
    normed,
    normed2,
    d_attn,
    d_mix,
    d_keyval,
    d_logits,
    wide,
    gains,
    bias,
    scores,
    d_probs,
    probs,
    d_scores,
    stacked,
    kv_parts,
    kv_land,
    gu_own,
    gu_sum,
    gu_land_a,
    gu_land_b,
    dn_own,
    dn_sum,
    dn_land_a,
    dn_land_b,
    grads,
    grads_sum,
    grads_land_a,
    grads_land_b,
    grads_line,
    grads_line_land,
    small,
    small_sum,
    small_land_a,
    small_land_b,
    small_line,
    small_line_land,
    gu_sems,
    dn_sems,
    grads_sems,
    small_sems,
    line_sems,
    kv_sems,
    load_sems,
    own_sems,
    out_sems,
    *late_scratch,
):
    micros, rows, count, local, ff, model, late = dims
    seq_len = count * rows
    kv = keyval.shape[2] // 2
    chunks = kv // LANES
    both = micros * rows
    d_query = d_mix
    z = lax.axis_index("expert")
    row_base = z * rows
    block = small_line.shape[0] // count
    core = lax.rem(lax.axis_index("dp"), 2)

    loads = []
    for number, (src, dst) in enumerate(
        ((out_hbm, w_out), (query_hbm, w_query), (keyval_hbm, w_keyval))
    ):
        loads.append(pltpu.make_async_copy(src, dst, load_sems.at[number]))
        loads[-1].start()
    full_barrier(plane, count)

    experts = []
    for j in range(local):
        for kind, (source, own, total, land_a, land_b, sems) in enumerate(
            (
                (grad_gu, gu_own, gu_sum, gu_land_a, gu_land_b, gu_sems),
                (grad_dn, dn_own, dn_sum, dn_land_a, dn_land_b, dn_sems),
            )
        ):
            load = pltpu.make_async_copy(
                source.at[j, :, :, core], own.at[j % 2], own_sems.at[2 * j + kind]
            )
            item = PlaneReduce(
                plane, source.at[j], own.at[j % 2], total.at[j], land_a.at[j], land_b.at[j],
                j % 2 == 0, sems.at[j], load,
            )
            item.start()
            if j < 2:
                load.start()
            experts.append(item)
    dense = [
        PlaneReduce(
            plane, grads.at[k], None, grads_sum.at[k], grads_land_a.at[k], grads_land_b.at[k],
            k % 2 == 0, grads_sems.at[k],
        )
        for k in range(6)
    ]
    dense.append(
        PlaneReduce(
            plane, small, None, small_sum, small_land_a, small_land_b, True, small_sems
        )
    )
    lines = [
        LineReduce(grads_line.at[k], grads_line_land.at[k], block, count, line_sems.at[k])
        for k in range(6)
    ] + [LineReduce(small_line, small_line_land, block, count, line_sems.at[6])]
    reduce_kv = [
        Reduce(kv_parts.at[m], kv_land.at[m], rows, count, kv_sems.at[m], up=False)
        for m in range(micros)
    ]

    def paired(item):
        item.pair_sum()
        item.send(0)

    def crossed(item):
        item.take(0)
        item.send(1)

    def expert_paired(number):
        paired(experts[number])
        if number + 4 < len(experts):
            experts[number + 4].local.start()

    def expert_done(number):
        out = gu_out if number % 2 == 0 else dn_out
        out[number // 2] = experts[number].take(1)

    def dense_done(number):
        ref = grads_line.at[number] if number < 6 else small_line
        ref[...] = dense[number].take(1).astype(BF)
        lines[number].start()

    def line_done(number):
        if number < 6:
            half = model // 2
            dense_out[number // 2, :, (number % 2) * half : (number % 2 + 1) * half] = lines[
                number
            ].total()
        else:
            small_out[...] = lines[number].total().T[:, 0 : small_out.shape[1]]

    def put_grads(number, left, right):
        half = model // 2
        shape = grads.shape[1:]
        for k in range(2):
            value = tn(left, right[:, k * half : (k + 1) * half])
            grads[2 * number + k] = value.astype(BF).reshape(shape)
            dense[2 * number + k].start()

    router_pad[...] = jnp.zeros(router_pad.shape, BF)
    router_pad[0 : router.shape[0], :] = router[...]
    gains[...] = jnp.zeros(gains.shape, F32)

    def norm_back(d_rows, inputs, scale, gain, row):
        scaled = d_rows * gain
        gains[row : row + 1, :] += jnp.sum(d_rows * inputs * scale, 0, keepdims=True)
        return scale * (
            scaled - inputs * scale * scale * jnp.mean(scaled * inputs, -1, keepdims=True)
        )

    def live_rows(m):
        return (row_base + lax.broadcasted_iota(jnp.int32, (rows, 1), 0)) < lengths[0, m]

    router_lanes = router.shape[0]

    def router_back():
        for m in range(micros):
            span = slice(m * rows, (m + 1) * rows)
            x_rows = tokens[m, 0].astype(F32)
            normed[span, :] = (x_rows * rms_scale(x_rows) * gain_one[...]).astype(BF)
            v = hidden[m]
            scale = rms_scale(v)
            normed2[span, :] = (v * scale * gain_two[...]).astype(BF)
            logits = nt(normed2[span, :], router_pad[...])
            live = live_rows(m)
            on = jnp.where(live, named_lanes(routes[m, 0, :, rows_at(z, rows)]), 0.0) > 0.0
            masked = jnp.where(on, logits, NEG_FILL)
            raised = jnp.where(on, jnp.exp(masked - jnp.max(masked, -1, keepdims=True)), 0.0)
            total = jnp.sum(raised, -1, keepdims=True)
            gate = raised / jnp.where(total > 0.0, total, 1.0)
            d_gate = moe[m, :, model:]
            d_logits[span, :] = (
                gate * (d_gate - jnp.sum(gate * d_gate, -1, keepdims=True))
            ).astype(BF)
            d_rows = moe[m, :, 0:model] + nn(d_logits[span, :], router_pad[...])
            grown = cot[m, 0].astype(F32) + norm_back(
                d_rows, v, scale, gain_two[...], router_lanes + 1
            )
            input_grad[m, 0] = grown
            d_attn[span, :] = jnp.where(live, grown, 0.0).astype(BF)

    def mixture_back():
        loads[0].wait()
        d_mix[...] = nt(d_attn[...], w_out[...]).astype(BF)

    def grad_out():
        put_grads(2, mixture[...].reshape(both, mixture.shape[2]), d_attn[...])

    cos = cos_ref[rows_at(z, rows), :]
    sin = sin_ref[rows_at(z, rows), :]

    def attend_back(m, i):
        span = slice(m * rows, (m + 1) * rows)
        lanes = slice(i * LANES, (i + 1) * LANES)
        value_lanes = slice(kv + i * LANES, kv + (i + 1) * LANES)
        if i == 0:
            score_bias(bias, row_base, lengths[0, m])
        pair = [d_mix[span, c * LANES : (c + 1) * LANES].astype(F32) for c in (2 * i, 2 * i + 1)]
        for k, rows_of in enumerate(stack_heads(*pair)):
            stacked[k * rows : (k + 1) * rows, :] = rows_of.astype(BF)
        scores[...] = nt(keyval[m, :, lanes], queries[m, i])
        d_probs[...] = nt(keyval[m, :, value_lanes], stacked[...])
        for k in range(4):
            where = slice(k * rows, (k + 1) * rows)
            prob = softmax_columns(scores[:, where] + bias[...])
            d_prob = d_probs[:, where]
            delta = jnp.sum(prob * d_prob, 0, keepdims=True)
            d_scores[:, where] = (prob * (d_prob - delta)).astype(BF)
            probs[:, where] = prob.astype(BF)
        turned = tn(d_scores[...], keyval[m, :, lanes]) * ATTENTION_SCALE
        for c, chunk in zip((2 * i, 2 * i + 1), unstack_heads(turned, rows)):
            d_query[span, c * LANES : (c + 1) * LANES] = rope(chunk, cos, -sin).astype(BF)
        kv_parts[m, :, lanes] = nn(d_scores[...], queries[m, i]).astype(BF)
        kv_parts[m, :, value_lanes] = nn(probs[...], stacked[...]).astype(BF)

    def grad_query():
        put_grads(0, normed[...], d_query[...])

    def query_back():
        loads[1].wait()
        wide[...] = nt(d_query[...], w_query[...])

    def keyval_total():
        for m in range(micros):
            span = slice(m * rows, (m + 1) * rows)
            key_own = d_probs.at[0:rows, 0:kv]
            value_own = d_probs.at[rows : 2 * rows, 0:kv]
            reduce_kv[m].total(key_own, slice(0, kv))
            reduce_kv[m].total(value_own, slice(kv, 2 * kv))
            for c in range(chunks):
                lanes = slice(c * LANES, (c + 1) * LANES)
                d_keyval[span, lanes] = rope(key_own[:, lanes], cos, -sin).astype(BF)
            d_keyval[span, kv:] = value_own[...].astype(BF)

    def grad_keyval():
        put_grads(1, normed[...], d_keyval[...])

    def keyval_back():
        loads[2].wait()
        wide[...] += nt(d_keyval[...], w_keyval[...])

    def input_back():
        for m in range(micros):
            span = slice(m * rows, (m + 1) * rows)
            x_rows = tokens[m, 0].astype(F32)
            input_grad[m, 0] += norm_back(
                wide[span, :], x_rows, rms_scale(x_rows), gain_one[...], router_lanes
            )

    def grad_small():
        small_value = tn(normed2[...], d_logits[...]) + gains[...].T
        small[...] = small_value.astype(BF).reshape(small.shape)
        dense[6].start()

    if late:
        out_parts, out_land, out_own = late_scratch
        late_load = pltpu.make_async_copy(late_parts, out_parts, load_sems.at[3])
        late_load.start()
        reduce_out = Reduce(out_parts, out_land, rows, count, out_sems)
    y_out[...] = y_first[...]

    arrived = []

    def out_slot(way, slot):
        if not arrived:
            late_load.wait()
            arrived.append(True)
        reduce_out.slot(way, slot)

    def finish_out():
        reduce_out.total(out_own)
        y_out[micros - 1, 0] = (hidden[micros - 1] + out_own[...]).astype(BF)
        reduce_out.finish()

    work, before, services = {}, [], []
    chain = [(DO_ROUTER,), (DO_MIXTURE,), (DO_GRAD_OUT,)]
    work[DO_ROUTER,], work[DO_MIXTURE,], work[DO_GRAD_OUT,] = router_back, mixture_back, grad_out
    for m in range(micros):
        for i in range(chunks):
            chain.append((DO_ATTEND, m, i))
            work[chain[-1]] = functools.partial(attend_back, m, i)
    for name, function in (
        (DO_GRAD_QUERY, grad_query), (DO_QUERY, query_back), (DO_TOTAL, keyval_total),
        (DO_GRAD_KEYVAL, grad_keyval), (DO_KEYVAL, keyval_back), (DO_INPUT, input_back),
        (DO_SMALL, grad_small),
    ):
        chain.append((name,))
        work[name,] = function
    before += chained(*chain)
    for m in range(micros):
        items = [(ON_L, ON_K, m, 1, t) for t in range(count)]
        for t, item in enumerate(items):
            work[item] = functools.partial(reduce_kv[m].slot, 1, t)
        services += items
        before += chained((DO_ATTEND, m, chunks - 1), *items, (DO_TOTAL,))
    if late:
        for way in range(2):
            items = [(ON_L, ON_O, way, t) for t in range(count)]
            for t, item in enumerate(items):
                work[item] = functools.partial(out_slot, way, t)
            services += items
            before += chained(*items)
    for number in range(len(experts)):
        items = [(stage, ON_E, number) for stage in (ON_P, ON_X, ON_D)]
        work[items[0]] = functools.partial(expert_paired, number)
        work[items[1]] = functools.partial(crossed, experts[number])
        work[items[2]] = functools.partial(expert_done, number)
        services += items
        before += chained(*items)
        if number >= 4:
            before.append(((ON_P, ON_E, number - 4), items[0]))
    for number, source in enumerate(
        (DO_GRAD_QUERY, DO_GRAD_QUERY, DO_GRAD_KEYVAL, DO_GRAD_KEYVAL, DO_GRAD_OUT, DO_GRAD_OUT, DO_SMALL)
    ):
        items = [(stage, ON_G, number) for stage in (ON_P, ON_X, ON_D, ON_Z)]
        work[items[0]] = functools.partial(paired, dense[number])
        work[items[1]] = functools.partial(crossed, dense[number])
        work[items[2]] = functools.partial(dense_done, number)
        work[items[3]] = functools.partial(line_done, number)
        services += items
        before += chained((source,), *items)
    services.sort(key=lambda item: (ON_L, ON_P, ON_X, ON_D, ON_Z).index(item[0]))
    order = [item for item in BACKWARD_ORDER if item in work]
    if set(order) != set(work):
        order = natural_order(chain, services, before)
    done = set()
    for item in order:
        work[item]()
        done.add(item)
        if item[:2] == (ON_L, ON_O) and item[3] == count - 1 and (ON_L, ON_O, 1 - item[2], count - 1) in done:
            finish_out()
    for item in experts + dense + lines + reduce_kv:
        item.finish()


def backward_call(
    count, devices, tokens, lengths, routes, gain_one, w_query, w_keyval, w_out, gain_two,
    w_router, cot, local, ff, y_first, hidden, moe, queries, keyval, mixture, grad_gu, grad_dn, late_parts,
):
    micros, _, rows, model = tokens.shape
    seq_len = routes.shape[2]
    kv = w_keyval.shape[1] // 2
    heads = w_query.shape[1]
    plane = plane_of(devices)
    block = model // devices // count
    group = max(block, GROUP)
    line = count * block
    half = model // 2
    both = micros * rows
    cos, sin = rope_constants(seq_len)
    gu_rows, dn_rows = model // devices, ff // devices
    vmem = pl.BlockSpec(memory_space=pltpu.VMEM)
    smem = pl.BlockSpec(memory_space=pltpu.SMEM)
    hbm = pl.BlockSpec(memory_space=pl.ANY)
    dma = pltpu.SemaphoreType.DMA
    hops = plane[0] + plane[1] - 1

    def reduce_scratch(lead, block_rows, width):
        lead = tuple(lead)
        return [
            pltpu.VMEM(lead + plane + (block_rows, width), BF),
            pltpu.VMEM(lead + (plane[1] - 1, plane[0], block_rows, width), BF),
            pltpu.VMEM(lead + (plane[0] - 1, block_rows, width), BF),
        ]

    wide_bf = pltpu.VMEM((both, model), BF)
    late = late_sums(count)
    out_shape = (
        jax.ShapeDtypeStruct((micros, 1, rows, model), BF),
        jax.ShapeDtypeStruct((micros, 1, rows, model), F32),
        jax.ShapeDtypeStruct((local, gu_rows, 2 * ff), F32),
        jax.ShapeDtypeStruct((local, dn_rows, model), F32),
        jax.ShapeDtypeStruct((3, group, model), F32),
        jax.ShapeDtypeStruct((LANES, group), F32),
    )
    scratch = (
        [pltpu.VMEM(w.shape, BF) for w in (w_query, w_keyval, w_out)]
        + [pltpu.VMEM((LANES, model), BF)]
        + [wide_bf, wide_bf, wide_bf, pltpu.VMEM((both, heads), BF)]
        + [pltpu.VMEM((both, 2 * kv), BF), pltpu.VMEM((both, LANES), BF)]
        + [pltpu.VMEM((both, model), F32)]
        + [pltpu.VMEM((LANES, model), F32)]
        + [pltpu.VMEM((seq_len, rows), F32)]
        + [pltpu.VMEM((seq_len, 4 * rows), F32)] * 2
        + [pltpu.VMEM((seq_len, 4 * rows), BF)] * 2
        + [pltpu.VMEM((4 * rows, LANES), BF)]
        + [pltpu.VMEM((micros, seq_len, 2 * kv), BF)]
        + [pltpu.VMEM((micros, count - 1, rows, 2 * kv), BF)]
        + [pltpu.VMEM((2,) + plane + (gu_rows, 2 * ff), BF)]
        + reduce_scratch((local,), gu_rows, 2 * ff)
        + [pltpu.VMEM((2,) + plane + (dn_rows, model), BF)]
        + reduce_scratch((local,), dn_rows, model)
        + [pltpu.VMEM((6,) + plane + (2, line, half), BF)]
        + reduce_scratch((6,), line, half)
        + [pltpu.VMEM((6, line, half), BF), pltpu.VMEM((6, count - 1, group, half), BF)]
        + [pltpu.VMEM(plane + (2, line, LANES), BF)]
        + reduce_scratch((), line, LANES)
        + [pltpu.VMEM((line, LANES), BF), pltpu.VMEM((count - 1, group, LANES), BF)]
        + [dma((local, 2, hops)), dma((local, 2, hops)), dma((6, 2, hops)), dma((2, hops))]
        + [dma((7, 2, count - 1)), dma((micros, 2, 2, count - 1)), dma((4,)), dma((2 * local,))]
        + [dma((2, 2, count - 1))]
    )
    if late:
        scratch += [
            pltpu.VMEM((seq_len, model), BF),
            pltpu.VMEM((count + 1, rows, model), BF),
            pltpu.VMEM((rows, model), F32),
        ]
    dims = (micros, rows, count, local, ff, model, late)
    return pl.pallas_call(
        functools.partial(backward_kernel, dims, plane),
        out_shape=out_shape,
        in_specs=[smem] + [vmem] * 14 + [hbm] * 6,
        out_specs=(vmem,) * 6,
        scratch_shapes=scratch,
        name="layer_backward",
        compiler_params=pltpu.CompilerParams(
            collective_id=1, has_side_effects=True, vmem_limit_bytes=VMEM_LIMIT
        ),
    )(
        lengths.T, tokens, cot, jnp.swapaxes(routes, 2, 3), gain_one.reshape(1, -1),
        gain_two.reshape(1, -1), jnp.asarray(cos), jnp.asarray(sin), w_router.T, y_first, hidden,
        moe, queries, keyval, mixture,
        w_query, w_keyval, w_out,
        grad_gu.reshape((local,) + plane + (2, gu_rows, 2 * ff)),
        grad_dn.reshape((local,) + plane + (2, dn_rows, model)),
        late_parts,
    )


def finish_kernel(*refs):
    *arrays, dense, small = refs[:6]
    outs, stages, sems = refs[6:16], refs[16:23], refs[23]
    pairs = list(zip(arrays, outs)) + [(dense.at[k], outs[4 + k]) for k in range(3)]
    inward = [
        pltpu.make_async_copy(src, stage, sems.at[0, k])
        for k, ((src, _), stage) in enumerate(zip(pairs, stages))
    ]
    outward = [
        pltpu.make_async_copy(stage, dst, sems.at[1, k])
        for k, ((_, dst), stage) in enumerate(zip(pairs, stages))
    ]
    for copy in inward:
        copy.start()
    router, gain_one, gain_two = outs[7:]
    lanes = router.shape[0]
    router[...] = small[0:lanes, :]
    gain_one[...] = small[lanes : lanes + 1, :]
    gain_two[...] = small[lanes + 1 : lanes + 2, :]
    for arrived, leaving in zip(inward, outward):
        arrived.wait()
        leaving.start()
    for copy in outward:
        copy.wait()


def finish_call(arrays, dense, small, experts):
    hbm = pl.BlockSpec(memory_space=pl.ANY)
    vmem = pl.BlockSpec(memory_space=pltpu.VMEM)
    shapes = [jax.ShapeDtypeStruct(v.shape, v.dtype) for v in arrays]
    shapes += [jax.ShapeDtypeStruct(dense.shape[1:], F32)] * 3
    shapes += [jax.ShapeDtypeStruct((n, small.shape[1]), F32) for n in (experts, 1, 1)]
    return pl.pallas_call(
        finish_kernel,
        out_shape=tuple(shapes),
        in_specs=[hbm] * 5 + [vmem],
        out_specs=(hbm,) * 7 + (vmem,) * 3,
        scratch_shapes=[pltpu.VMEM(v.shape, v.dtype) for v in shapes[:7]]
        + [pltpu.SemaphoreType.DMA((2, 7))],
        name="layer_results",
    )(*arrays, dense, small)


def on_device(
    tokens, lengths, routes, attn_gain, w_query, w_keyval, w_out, ffn_gain, w_router,
    expert_gate_up, expert_down, cotangent,
):
    count = lax.axis_size("expert")
    devices = lax.axis_size("dp")
    model = tokens.shape[3]
    experts = w_router.shape[1]
    local, ff = expert_gate_up.shape[0], expert_down.shape[1]
    y, hidden, moe, queries, keyval, mixture, grad_gu, grad_dn, late_parts = forward_call(
        count, tokens, lengths, routes, attn_gain, w_query, w_keyval, w_out, ffn_gain, w_router,
        expert_gate_up, expert_down, cotangent,
    )
    y, input_grad, gu, dn, dense, small = backward_call(
        count, devices, tokens, lengths, routes, attn_gain, w_query, w_keyval, w_out, ffn_gain,
        w_router, cotangent, local, ff, y, hidden, moe, queries, keyval, mixture, grad_gu,
        grad_dn, late_parts,
    )
    block = model // devices // count
    if dense.shape[1] != block:
        first = lax.rem(lax.axis_index("expert") * block, dense.shape[1])
        dense = lax.dynamic_slice_in_dim(dense, first, block, 1)
        small = lax.dynamic_slice_in_dim(small, first, block, 1)
    *whole, router, gain_one, gain_two = finish_call(
        (y, input_grad, gu, dn), dense, small, experts
    )
    return (
        whole[0], whole[1], gain_one[0], whole[4], whole[5], whole[6], gain_two[0], router.T,
        whole[2], whole[3],
    )


def solution(mesh):
    placed = (
        P(None, "dp", "expert", None), P(None, "dp"), P(None, "dp", None, None), P(), P(), P(), P(),
        P(), P(), P("expert", None, None), P("expert", None, None), P(None, "dp", "expert", None),
    )
    return jax.shard_map(
        on_device,
        mesh=mesh,
        in_specs=placed,
        out_specs=(
            P(None, "dp", "expert", None), P(None, "dp", "expert", None), P(("dp", "expert")),
            P(("dp", "expert"), None), P(("dp", "expert"), None), P(("dp", "expert"), None),
            P(("dp", "expert")), P(("dp", "expert"), None), P("expert", "dp", None),
            P("expert", "dp", None),
        ),
        check_vma=False,
    )
```

```python
import functools
import math

import jax
import jax.numpy as jnp
import numpy as np
from jax import lax
from jax.experimental import pallas as pl
from jax.experimental.pallas import tpu as pltpu
from jax.sharding import PartitionSpec as P

HEAD_DIM = 64
EPS = 1e-06
ATTENTION_SCALE = 0.015625
ROPE_BASE = 10000.0
NEG_FILL = -1e30
LANES = 128
GROUP = 16
STRIP = 64
BF = jnp.bfloat16
F32 = jnp.float32
VMEM_LIMIT = 63 * 2**20
(
    DO_NORM, DO_KV, DO_QUERY, DO_ATTEND, DO_GATE, DO_FWD, DO_OUT, DO_BWD, DO_GRAD, DO_ROUTER,
    DO_MIXTURE, DO_GRAD_OUT, DO_GRAD_QUERY, DO_TOTAL, DO_GRAD_KEYVAL, DO_KEYVAL, DO_INPUT,
    DO_SMALL, ON_S, ON_H, ON_L, ON_K, ON_N, ON_C, ON_O, ON_D, ON_E, ON_G, ON_P, ON_X, ON_Z,
) = range(31)
FORWARD_ORDER = (
    (ON_S, ON_C, 0, 0), (ON_S, ON_C, 1, 1), (DO_NORM,), (DO_KV,), (ON_S, ON_C, 0, 1), (ON_S, ON_K, 0, 0),
    (ON_S, ON_K, 1, 0), (ON_H, ON_K, 0, 0, 0), (DO_QUERY,), (ON_H, ON_K, 1, 0, 0), (ON_H, ON_K, 0, 0, 1),
    (ON_H, ON_K, 0, 0, 2), (ON_H, ON_C, 0, 1, 0), (DO_ATTEND, 0), (ON_H, ON_C, 0, 1, 1),
    (ON_S, ON_N, 0, 1), (ON_S, ON_N, 0, 0), (ON_H, ON_K, 1, 0, 1), (ON_H, ON_K, 1, 0, 2),
    (ON_H, ON_N, 0, 0, 0), (DO_ATTEND, 1), (ON_H, ON_N, 0, 1, 0), (ON_H, ON_N, 0, 1, 1),
    (ON_H, ON_N, 0, 0, 1), (ON_S, ON_N, 1, 1), (ON_H, ON_N, 0, 0, 2), (ON_H, ON_N, 0, 1, 2),
    (ON_H, ON_C, 0, 0, 0), (DO_GATE, 0), (DO_FWD, 0, 0), (DO_FWD, 0, 1), (ON_H, ON_C, 0, 0, 1),
    (ON_H, ON_N, 1, 1, 0), (ON_H, ON_C, 0, 1, 2), (ON_S, ON_N, 1, 0), (ON_S, ON_C, 1, 0), (DO_FWD, 0, 2),
    (DO_FWD, 0, 3), (ON_H, ON_N, 1, 1, 1), (DO_OUT, 0), (ON_L, ON_O, 0, 0, 0), (ON_H, ON_C, 0, 0, 2),
    (ON_L, ON_O, 0, 1, 0), (DO_BWD, 0, 0), (ON_H, ON_N, 1, 0, 0), (ON_H, ON_C, 1, 1, 0), (DO_BWD, 0, 1),
    (ON_L, ON_O, 0, 1, 1), (ON_L, ON_O, 0, 0, 1), (ON_H, ON_C, 1, 1, 1), (DO_BWD, 0, 2), (DO_BWD, 0, 3),
    (ON_H, ON_N, 1, 0, 1), (ON_L, ON_D, 0, 0, 0), (ON_L, ON_D, 0, 1, 0), (ON_H, ON_N, 1, 0, 2),
    (ON_H, ON_C, 1, 0, 0), (ON_L, ON_O, 0, 1, 2), (ON_H, ON_N, 1, 1, 2), (DO_GATE, 1), (DO_FWD, 1, 0),
    (ON_L, ON_D, 0, 1, 1), (ON_L, ON_O, 0, 0, 2), (DO_FWD, 1, 1), (DO_FWD, 1, 2), (DO_FWD, 1, 3),
    (ON_L, ON_D, 0, 0, 1), (ON_H, ON_C, 1, 0, 1), (ON_L, ON_O, 0, 1, 3), (ON_L, ON_O, 0, 0, 3),
    (DO_OUT, 1), (ON_L, ON_D, 0, 1, 2), (ON_H, ON_C, 1, 0, 2), (ON_H, ON_C, 1, 1, 2), (DO_BWD, 1, 0),
    (ON_L, ON_D, 0, 0, 2), (DO_BWD, 1, 1), (DO_BWD, 1, 2), (ON_L, ON_D, 0, 1, 3), (ON_L, ON_D, 0, 0, 3),
    (DO_BWD, 1, 3), (DO_GRAD, 0), (ON_L, ON_D, 1, 1, 0), (DO_GRAD, 1), (ON_L, ON_D, 1, 0, 0),
    (ON_P, ON_E, 0), (DO_GRAD, 2), (ON_P, ON_E, 2), (ON_L, ON_D, 1, 1, 1), (DO_GRAD, 3), (ON_P, ON_E, 1),
    (ON_L, ON_D, 1, 0, 1), (ON_P, ON_E, 3), (ON_L, ON_D, 1, 1, 2), (ON_L, ON_D, 1, 0, 2), (ON_X, ON_E, 1),
    (ON_X, ON_E, 2), (ON_X, ON_E, 0), (ON_L, ON_D, 1, 0, 3), (ON_X, ON_E, 3), (ON_L, ON_D, 1, 1, 3),
)
BACKWARD_ORDER = (
    (ON_X, ON_E, 0), (DO_ROUTER,), (DO_MIXTURE,), (DO_GRAD_OUT,), (DO_ATTEND, 0, 0), (ON_P, ON_E, 5),
    (DO_ATTEND, 0, 1), (DO_ATTEND, 0, 2), (DO_ATTEND, 0, 3), (ON_L, ON_K, 0, 1, 0), (ON_P, ON_E, 7),
    (ON_P, ON_G, 4), (DO_ATTEND, 1, 0), (DO_ATTEND, 1, 1), (DO_ATTEND, 1, 2), (DO_ATTEND, 1, 3),
    (ON_L, ON_K, 1, 1, 0), (ON_L, ON_K, 0, 1, 1), (ON_X, ON_E, 2), (ON_X, ON_E, 1), (ON_L, ON_O, 0, 0),
    (DO_GRAD_QUERY,), (ON_X, ON_G, 4), (ON_P, ON_G, 0), (ON_P, ON_G, 5), (ON_P, ON_G, 1), (ON_P, ON_E, 4),
    (ON_L, ON_K, 1, 1, 1), (ON_X, ON_G, 5), (ON_L, ON_K, 0, 1, 2), (ON_X, ON_E, 7), (ON_X, ON_G, 0),
    (ON_P, ON_E, 6), (ON_L, ON_K, 1, 1, 2), (ON_D, ON_G, 4), (DO_QUERY,), (ON_L, ON_K, 0, 1, 3),
    (ON_X, ON_G, 1), (ON_X, ON_E, 5), (ON_L, ON_O, 0, 1), (ON_D, ON_G, 0), (ON_L, ON_K, 1, 1, 3),
    (DO_TOTAL,), (DO_GRAD_KEYVAL,), (ON_P, ON_G, 2), (ON_D, ON_E, 0), (ON_P, ON_G, 3), (ON_D, ON_G, 5),
    (ON_L, ON_O, 1, 0), (ON_L, ON_O, 1, 1), (ON_D, ON_G, 1), (DO_KEYVAL,), (DO_INPUT,), (ON_X, ON_E, 3),
    (DO_SMALL,), (ON_Z, ON_G, 4), (ON_L, ON_O, 0, 2), (ON_D, ON_E, 1), (ON_X, ON_G, 2), (ON_P, ON_G, 6),
    (ON_X, ON_G, 3), (ON_Z, ON_G, 1), (ON_L, ON_O, 1, 2), (ON_D, ON_E, 3), (ON_D, ON_G, 2), (ON_D, ON_E, 7),
    (ON_X, ON_G, 6), (ON_Z, ON_G, 0), (ON_X, ON_E, 4), (ON_X, ON_E, 6), (ON_D, ON_E, 2), (ON_D, ON_E, 5),
    (ON_D, ON_G, 3), (ON_D, ON_G, 6), (ON_Z, ON_G, 2), (ON_D, ON_E, 4), (ON_L, ON_O, 1, 3), (ON_Z, ON_G, 3),
    (ON_L, ON_O, 0, 3), (ON_D, ON_E, 6), (ON_Z, ON_G, 5), (ON_Z, ON_G, 6),
)


def dot_of(left, right, left_dim, right_dim):
    return lax.dot_general(
        left, right, (((left_dim,), (right_dim,)), ((), ())), preferred_element_type=F32
    )


def nn(left, right):
    return dot_of(left, right, 1, 0)


def nt(left, right):
    return dot_of(left, right, 1, 1)


def tn(left, right):
    return dot_of(left, right, 0, 0)


def rope_constants(seq_len):
    half = HEAD_DIM // 2
    frequency = np.exp(
        np.arange(half, dtype=np.float32) * np.float32(-2.0 * math.log(ROPE_BASE) / HEAD_DIM)
    ).astype(np.float32)
    angles = np.arange(seq_len, dtype=np.float32)[:, None] * frequency[None, :]
    cos, sin = np.cos(angles).astype(np.float32), np.sin(angles).astype(np.float32)
    heads = LANES // HEAD_DIM
    return np.tile(np.concatenate([cos, cos], 1), (1, heads)), np.tile(
        np.concatenate([-sin, sin], 1), (1, heads)
    )


def lane_ids(rows):
    return lax.broadcasted_iota(jnp.int32, (rows, LANES), 1)


def swap_halves(chunk):
    half = HEAD_DIM // 2
    first = lax.rem(lane_ids(chunk.shape[0]), HEAD_DIM) < half
    return jnp.where(
        first, pltpu.roll(chunk, LANES - half, 1), pltpu.roll(chunk, half, 1)
    )


def rope(chunk, cos, sin):
    return chunk * cos + swap_halves(chunk) * sin


def rms_scale(rows):
    return lax.rsqrt(jnp.mean(rows * rows, -1, keepdims=True) + EPS)


def stack_heads(first, second):
    low = lane_ids(first.shape[0]) < HEAD_DIM
    zero = jnp.zeros_like(first)
    return [
        jnp.where(low, first, zero),
        jnp.where(low, pltpu.roll(first, HEAD_DIM, 1), zero),
        jnp.where(low, zero, pltpu.roll(second, HEAD_DIM, 1)),
        jnp.where(low, zero, second),
    ]


def unstack_heads(stacked, rows):
    low = lane_ids(rows) < HEAD_DIM
    parts = [stacked[k * rows : (k + 1) * rows] for k in range(4)]
    first = jnp.where(low, parts[0], pltpu.roll(parts[1], HEAD_DIM, 1))
    second = jnp.where(low, pltpu.roll(parts[2], HEAD_DIM, 1), parts[3])
    return first, second


def rows_at(index, rows):
    return pl.ds(pl.multiple_of(index * rows, rows), rows)


def natural_order(chain, services, before):
    order, placed = [], set()

    def place(item):
        if item not in placed:
            placed.add(item)
            for first, then in before:
                if then == item:
                    place(first)
            order.append(item)

    for item in chain + services:
        place(item)
    return order


def chained(*items):
    return list(zip(items, items[1:]))


def named_lanes(ids):
    lane = lax.broadcasted_iota(jnp.int32, (LANES, ids.shape[1]), 0)
    hit = jnp.zeros(lane.shape, F32)
    for k in range(ids.shape[0]):
        hit = hit + (ids[k : k + 1, :] == lane).astype(F32)
    return hit.T


class Gather:
    def __init__(self, buffer, micro, rows, count, sems, up=True, down=True):
        self.buffer, self.micro, self.rows, self.count, self.sems = buffer, micro, rows, count, sems
        self.ways = [w for w, on in ((0, up), (1, down)) if on]

    def copy(self, way, step, block):
        z = lax.axis_index("expert")
        target = z + 1 if way == 0 else z - 1
        view = self.buffer.at[self.micro, rows_at(block, self.rows), :]
        return pltpu.make_async_remote_copy(
            src_ref=view,
            dst_ref=view,
            send_sem=self.sems.at[0, way, step],
            recv_sem=self.sems.at[1, way, step],
            device_id={"expert": target},
            device_id_type=pl.DeviceIdType.MESH,
        )

    def sends(self, way, step):
        z = lax.axis_index("expert")
        if way == 0:
            return z - step, jnp.logical_and(z < self.count - 1, z - step >= 0)
        return z + step, jnp.logical_and(z > 0, z + step <= self.count - 1)

    def receives(self, way, step):
        z = lax.axis_index("expert")
        if way == 0:
            return z - 1 - step, z - 1 - step >= 0
        return z + 1 + step, z + 1 + step <= self.count - 1

    def start(self, way, step):
        block, on = self.sends(way, step)

        @pl.when(on)
        def _():
            self.copy(way, step, block).start()

    def hop(self, way, step):
        block, on = self.receives(way, step)

        @pl.when(on)
        def _():
            self.copy(way, step, block).wait_recv()

        if step + 1 < self.count - 1:
            self.start(way, step + 1)

    def finish(self):
        for step in range(self.count - 1):
            for way in self.ways:
                block, on = self.sends(way, step)

                @pl.when(on)
                def _(way=way, step=step, block=block):
                    self.copy(way, step, block).wait_send()


class Reduce:
    def __init__(self, parts, landing, rows, count, sems, up=True, down=True):
        self.parts, self.landing = parts, landing
        self.rows, self.count, self.sems = rows, count, sems
        self.ways = [w for w, on in ((0, up), (1, down)) if on]

    def block(self, way, slot):
        z = lax.axis_index("expert")
        if way == 0:
            return z + self.count - 1 - slot, slot >= z
        return z - (self.count - 1) + slot, slot >= self.count - 1 - z

    def place(self, way, slot, z):
        if way == 0:
            return slot - (z - 1)
        return self.count - (slot - (self.count - 2 - z)) - (2 if self.ways == [1] else 0)

    def copy(self, way, slot, block):
        z = lax.axis_index("expert")
        target = z + 1 if way == 0 else z - 1
        return pltpu.make_async_remote_copy(
            src_ref=self.parts.at[rows_at(block, self.rows), :],
            dst_ref=self.landing.at[self.place(way, slot, target)],
            send_sem=self.sems.at[0, way, slot],
            recv_sem=self.sems.at[1, way, slot],
            device_id={"expert": target},
            device_id_type=pl.DeviceIdType.MESH,
        )

    def arrival(self, way, slot, block):
        z = lax.axis_index("expert")
        source = z - 1 if way == 0 else z + 1
        return pltpu.make_async_remote_copy(
            src_ref=self.parts.at[rows_at(block, self.rows), :],
            dst_ref=self.landing.at[self.place(way, slot, z)],
            send_sem=self.sems.at[0, way, slot],
            recv_sem=self.sems.at[1, way, slot],
            device_id={"expert": source},
            device_id_type=pl.DeviceIdType.MESH,
        )

    def inner(self, way):
        z = lax.axis_index("expert")
        return z >= 1 if way == 0 else z <= self.count - 2

    def slot(self, way, slot):
        z = lax.axis_index("expert")
        block, on = self.block(way, slot)
        if slot >= 1:

            @pl.when(jnp.logical_and(on, self.inner(way)))
            def _():
                self.arrival(way, slot - 1, block).wait_recv()
                if slot < self.count - 1:
                    where = rows_at(block, self.rows)
                    total = self.parts[where, :].astype(F32) + self.landing[
                        self.place(way, slot - 1, z)
                    ].astype(F32)
                    self.parts[where, :] = total.astype(self.parts.dtype)

        if slot < self.count - 1:

            @pl.when(on)
            def _():
                self.copy(way, slot, block).start()

    def total(self, out, lanes=slice(None)):
        z = lax.axis_index("expert")
        out[...] = self.parts[rows_at(z, self.rows), lanes].astype(F32)
        for way in self.ways:

            @pl.when(self.inner(way))
            def _(way=way):
                place = self.place(way, self.count - 2, z)
                out[...] += self.landing[place, :, lanes].astype(F32)

    def finish(self):
        for slot in range(self.count - 1):
            for way in self.ways:
                block, on = self.block(way, slot)

                @pl.when(on)
                def _(way=way, slot=slot, block=block):
                    self.copy(way, slot, block).wait_send()


def line_barrier(count, plane=None):
    z = lax.axis_index("expert")
    barrier = pltpu.get_barrier_semaphore()
    mesh = pl.DeviceIdType.MESH
    for target, on in ((z + 1, z < count - 1), (z - 1, z > 0)):

        @pl.when(on)
        def _(target=target):
            pl.semaphore_signal(
                barrier, inc=1, device_id={"expert": target}, device_id_type=mesh
            )

    others = plane_partners(plane) if plane else []
    for device in others:
        pl.semaphore_signal(barrier, inc=1, device_id=device, device_id_type=mesh)
    awaited = (z > 0).astype(jnp.int32) + (z < count - 1).astype(jnp.int32)
    pl.semaphore_wait(barrier, awaited + len(others))


def score_bias(bias, row_base, length):
    key_pos = lax.broadcasted_iota(jnp.int32, bias.shape, 0)
    query_pos = row_base + lax.broadcasted_iota(jnp.int32, bias.shape, 1)
    allowed = jnp.logical_and(key_pos <= query_pos, key_pos < length)
    bias[...] = jnp.where(allowed, 0.0, NEG_FILL)


def softmax_columns(scores):
    raised = jnp.exp(scores - jnp.max(scores, 0, keepdims=True))
    return raised * (1.0 / jnp.sum(raised, 0, keepdims=True))


def sigmoid(v):
    return 0.5 * jnp.tanh(0.5 * v) + 0.5


def plane_of(devices):
    side = math.isqrt(devices // 2)
    return side, side


def device_at(plane, y, x, core):
    return {"dp": (y * plane[1] + x) * 2 + core}


def plane_partners(plane):
    index = lax.axis_index("dp")
    core, chip = lax.rem(index, 2), index // 2
    y, x = chip // plane[1], lax.rem(chip, plane[1])
    partners = [device_at(plane, y, x, 1 - core)]
    partners += [device_at(plane, y, lax.rem(x + k, plane[1]), core) for k in range(1, plane[1])]
    partners += [device_at(plane, lax.rem(y + k, plane[0]), x, core) for k in range(1, plane[0])]
    return partners


class PlaneReduce:
    def __init__(self, plane, source, own, total, first_land, second_land, x_first, sems, local=None):
        self.plane, self.source, self.own, self.total = plane, source, own, total
        self.lands, self.x_first, self.sems, self.local = (first_land, second_land), x_first, sems, local
        index = lax.axis_index("dp")
        self.core = lax.rem(index, 2)
        chip = index // 2
        self.y, self.x = chip // plane[1], lax.rem(chip, plane[1])

    def remote(self, src, dst, number, where):
        return pltpu.make_async_remote_copy(
            src_ref=src,
            dst_ref=dst,
            send_sem=self.sems.at[0, number],
            recv_sem=self.sems.at[1, number],
            device_id=device_at(self.plane, *where),
            device_id_type=pl.DeviceIdType.MESH,
        )

    def sibling(self):
        return self.remote(
            self.source.at[:, :, 1 - self.core], self.total, 0, (self.y, self.x, 1 - self.core)
        )

    def start(self):
        self.sibling().start()

    def along(self, stage):
        return self.x_first == (stage == 0)

    def hops(self, stage):
        along_x = self.along(stage)
        size = self.plane[1] if along_x else self.plane[0]
        base = 1 if stage == 0 else self.plane[1] if self.x_first else self.plane[0]
        for k in range(1, size):
            if along_x:
                place = lax.rem(self.x + k, size)
                where = (self.y, place, self.core)
                view = (
                    self.total.at[:, place] if stage == 0 else self.total.at[self.y, place]
                )
            else:
                place = lax.rem(self.y + k, size)
                where = (place, self.x, self.core)
                view = self.total.at[place] if stage == 0 else self.total.at[place, self.x]
            yield k, self.remote(view, self.lands[stage].at[k - 1], base + k - 1, where)

    def send(self, stage):
        for _, copy in self.hops(stage):
            copy.start()

    def pair_sum(self):
        if self.local is not None:
            self.local.wait()
        self.sibling().wait_recv()
        count = self.plane[0] * self.plane[1]
        for b in range(count):
            y, x = b // self.plane[1], b % self.plane[1]
            own = self.own[y, x] if self.local is not None else self.source[y, x, self.core]
            self.total[y, x] = (self.total[y, x].astype(F32) + own.astype(F32)).astype(BF)

    def take(self, stage):
        land = self.lands[stage]
        for k, copy in self.hops(stage):
            copy.wait_recv()
        if stage == 0:
            for other in range(self.plane[0] if self.x_first else self.plane[1]):
                where = (other, self.x) if self.x_first else (self.y, other)
                summed = self.total[where].astype(F32)
                for k in range(land.shape[0]):
                    summed = summed + land[k, other].astype(F32)
                self.total[where] = summed.astype(BF)
            return None
        summed = self.total[self.y, self.x].astype(F32)
        for k in range(land.shape[0]):
            summed = summed + land[k].astype(F32)
        return summed

    def crossed_view(self):
        return self.total.at[:, self.x] if self.x_first else self.total.at[self.y]

    def finish(self, parts=(0, 1, 2)):
        if 0 in parts:
            self.sibling().wait_send()
        for stage in range(2):
            if stage + 1 in parts:
                for _, copy in self.hops(stage):
                    copy.wait_send()


def early_experts(count, local):
    return 2 if count <= 4 and local >= 4 else 0


def late_sums(count):
    return count <= 4


def forward_kernel(
    dims,
    lengths,
    tokens,
    cot,
    routes,
    gain_one,
    gain_two,
    cos_ref,
    sin_ref,
    router,
    query_hbm,
    keyval_hbm,
    out_hbm,
    gate_up_hbm,
    down_hbm,
    y_out,
    hidden_out,
    moe_out,
    queries_out,
    keyval_out,
    mixture_out,
    grad_gu_out,
    grad_dn_out,
    late_out,
    early_gu_out,
    early_dn_out,
    wide,
    narrow,
    normed,
    queries,
    keyval,
    mixture,
    hidden,
    named,
    gates,
    gate_lanes,
    gate_terms,
    router_pad,
    rows_all,
    cot_all,
    acts,
    d_proj,
    w_out,
    w_gu,
    w_dn,
    out_parts,
    out_land,
    in_parts,
    in_land,
    own_sum,
    moe_sum,
    kv_sems,
    rows_sems,
    cot_sems,
    out_sems,
    in_sems,
    load_sems,
    store_sems,
    free_sems,
    *early_scratch,
):
    micros, rows, count, local, ff, model, late, early_count, plane = dims
    seq_len = count * rows
    kv = keyval.shape[2] // 2
    chunks = kv // LANES
    z = lax.axis_index("expert")
    row_base = z * rows
    split = -(-model // seq_len)
    piece = model // split
    back = wide
    bias = gate_terms.at[:, 0:rows]
    scores = wide.at[:, 0 : 4 * rows]
    probs = d_proj.at[micros * local - 1, :, 0 : 4 * rows]
    tile = 512

    loads = []

    def load(src, dst):
        copy = pltpu.make_async_copy(src, dst, load_sems.at[len(loads)])
        copy.start()
        loads.append(copy)
        return copy

    early = []
    for index, weight in enumerate((query_hbm, keyval_hbm)):
        early.append(
            [
                load(
                    weight.at[pl.ds(k * piece, piece), :],
                    d_proj.at[index * split + k, pl.ds(0, piece), :],
                )
                for k in range(split)
            ]
        )
    load_out = load(out_hbm, w_out)
    load_gu = load(gate_up_hbm, w_gu)
    load_dn = load(down_hbm, w_dn)

    line_barrier(count, plane if early_count else None)

    gather_kv = [
        Gather(keyval, m, rows, count, kv_sems.at[m], down=False) for m in range(micros)
    ]
    gather_rows = [Gather(rows_all, m, rows, count, rows_sems.at[m]) for m in range(micros)]
    gather_cot = [Gather(cot_all, m, rows, count, cot_sems.at[m]) for m in range(micros)]
    reduce_out = [
        Reduce(out_parts, out_land, rows, count, out_sems.at[m]) for m in range(micros)
    ]
    reduce_in = [Reduce(in_parts, in_land, rows, count, in_sems.at[m]) for m in range(micros)]

    for m in range(micros):
        cot_all[m, rows_at(z, rows), :] = cot[m, 0]

    both = micros * rows

    def norm():
        for m in range(micros):
            x_rows = tokens[m, 0].astype(F32)
            normed[m * rows : (m + 1) * rows, :] = (
                x_rows * rms_scale(x_rows) * gain_one[...]
            ).astype(BF)

    cos = cos_ref[rows_at(z, rows), :]
    sin = sin_ref[rows_at(z, rows), :]

    def project(index):
        for copy in early[index]:
            copy.wait()
        total = None
        for k in range(split):
            part = nn(
                normed[:, k * piece : (k + 1) * piece], d_proj[index * split + k, 0:piece, :]
            )
            total = part if total is None else total + part
        wide[0:both, :] = total

    def keys_values():
        project(1)
        for m in range(micros):
            span = slice(m * rows, (m + 1) * rows)
            for c in range(chunks):
                lanes = slice(c * LANES, (c + 1) * LANES)
                keyval[m, rows_at(z, rows), lanes] = rope(wide[span, lanes], cos, sin).astype(BF)
            keyval[m, rows_at(z, rows), kv:] = wide[span, kv:].astype(BF)

    def first_queries():
        project(0)
        for m in range(micros):
            span = slice(m * rows, (m + 1) * rows)
            for i in range(chunks):
                pair = [
                    rope(wide[span, c * LANES : (c + 1) * LANES], cos, sin)
                    for c in (2 * i, 2 * i + 1)
                ]
                for k, block in enumerate(stack_heads(*pair)):
                    queries[m, i, k * rows : (k + 1) * rows, :] = (
                        block.astype(BF) * ATTENTION_SCALE
                    ).astype(BF)
            for b in range(count):

                @pl.when(b > z)
                def _(m=m, b=b):
                    keyval[m, b * rows : (b + 1) * rows, :] = jnp.zeros((rows, 2 * kv), BF)

            live = lax.broadcasted_iota(jnp.int32, (seq_len, LANES), 0) < lengths[0, m]
            named[m] = jnp.where(live, named_lanes(routes[m, 0]), 0.0)
        router_pad[...] = jnp.zeros(router_pad.shape, BF)
        router_pad[0 : router.shape[0], :] = router[...]

    def attend(m):
        length = lengths[0, m]
        score_bias(bias, row_base, length)
        for i in range(chunks):
            lanes = slice(i * LANES, (i + 1) * LANES)
            scores[...] = nt(keyval[m, :, lanes], queries[m, i])
            for k in range(4):
                span = slice(k * rows, (k + 1) * rows)
                probs[:, span] = softmax_columns(scores[:, span] + bias[...]).astype(BF)
            mixed = tn(probs[...], keyval[m, :, kv + i * LANES : kv + (i + 1) * LANES])
            first, second = unstack_heads(mixed, rows)
            mixture[m, :, 2 * i * LANES : (2 * i + 1) * LANES] = first.astype(BF)
            mixture[m, :, (2 * i + 1) * LANES : (2 * i + 2) * LANES] = second.astype(BF)
        if m == 0:
            load_out.wait()
        live = (row_base + lax.broadcasted_iota(jnp.int32, (rows, 1), 0)) < length
        rows_hidden = tokens[m, 0].astype(F32) + jnp.where(
            live, nn(mixture[m], w_out[...]), 0.0
        )
        hidden[m] = rows_hidden
        rows_all[m, rows_at(z, rows), :] = (
            rows_hidden * rms_scale(rows_hidden) * gain_two[...]
        ).astype(BF)

    def gate_rows(m):
        if m == 0:
            load_gu.wait()
            load_dn.wait()
        logits = nt(rows_all[m], router_pad[...])
        on = named[m] > 0.0
        masked = jnp.where(on, logits, NEG_FILL)
        raised = jnp.where(on, jnp.exp(masked - jnp.max(masked, -1, keepdims=True)), 0.0)
        total = jnp.sum(raised, -1, keepdims=True)
        gate = raised / jnp.where(total > 0.0, total, 1.0)
        for j in range(local):
            gate_lanes[j] = jnp.broadcast_to(column(gate, z * local + j), gate.shape)

    def column(block, expert):
        return jnp.sum(
            jnp.where(lane_ids(block.shape[0]) == expert, block, 0.0), -1, keepdims=True
        )

    blocks = [slice(c, c + LANES) for c in range(0, ff, LANES)]

    def expert_forward(m, j):
        wide[...] = nn(rows_all[m], w_gu[j].reshape(model, 2 * ff))

        def strip_step(strip, carry):
            where = rows_at(strip, STRIP)
            gate = gate_lanes[j, where, :]
            for c, lanes in enumerate(blocks):
                front, up = wide[where, lanes], wide[where, ff + c * LANES : ff + (c + 1) * LANES]
                value = front * sigmoid(front) * up * gate
                acts[m, where, j * ff + c * LANES : j * ff + (c + 1) * LANES] = value.astype(BF)
            d_proj[m * local + j, where, :] = wide[where, :].astype(BF)
            return carry

        lax.fori_loop(0, seq_len // STRIP, strip_step, 0)

    def expert_backward(m, j):
        expert = z * local + j
        narrow[...] = nt(cot_all[m], w_dn[j].reshape(ff, model))

        def strip_step(strip, carry):
            where = rows_at(strip, STRIP)
            gate = gate_lanes[j, where, :]
            terms = None
            for c, lanes in enumerate(blocks):
                up_lanes = slice(ff + c * LANES, ff + (c + 1) * LANES)
                front = d_proj[m * local + j, where, lanes].astype(F32)
                up = d_proj[m * local + j, where, up_lanes].astype(F32)
                d_act = narrow[where, lanes]
                sig = sigmoid(front)
                silu = front * sig
                term = d_act * silu
                terms = term * up if terms is None else terms + term * up
                d_proj[m * local + j, where, up_lanes] = (term * gate).astype(BF)
                d_proj[m * local + j, where, lanes] = (
                    d_act * gate * up * (sig + silu * (1.0 - sig))
                ).astype(BF)
            gate_terms[where, :] = terms
            return carry

        lax.fori_loop(0, seq_len // STRIP, strip_step, 0)
        d_gate = jnp.sum(gate_terms[...], -1, keepdims=True)
        mine = lane_ids(seq_len) == expert
        if j == 0:
            gates[...] = jnp.where(mine, d_gate, 0.0)
        else:
            gates[...] = jnp.where(mine, d_gate, gates[...])
        if j == local - 1:
            in_parts[:, model:] = (gates[...] * named[m]).astype(BF)
        for r in range(0, seq_len, tile):
            span = slice(r, r + tile)
            part = nt(d_proj[m * local + j, span, :], w_gu[j].reshape(model, 2 * ff))
            if j == 0:
                back[span, :] = part
            elif j < local - 1:
                back[span, :] += part
            else:
                in_parts[span, 0:model] = (back[span, :] + part).astype(BF)

    def weight_grads(j):
        for part_of in range(4):
            lanes = slice(part_of * ff // 2, (part_of + 1) * ff // 2)
            total = None
            for m in range(micros):
                part = tn(rows_all[m], d_proj[m * local + j, :, lanes])
                total = part if total is None else total + part
            w_gu[j, :, :, :, :, lanes] = total.astype(BF).reshape(
                w_gu.shape[1:5] + (ff // 2,)
            )
        total = None
        for m in range(micros):
            part = tn(acts[m, :, j * ff : (j + 1) * ff], cot_all[m])
            total = part if total is None else total + part
        w_dn[j] = total.astype(BF).reshape(w_dn.shape[1:])

    def out_rows(m):
        for r in range(0, seq_len, tile):
            out_parts[r : r + tile, :] = nn(
                acts[m, r : r + tile, :], w_dn[...].reshape(local * ff, model)
            ).astype(BF)

    stores = []

    def store(src, dst):
        copy = pltpu.make_async_copy(src, dst, store_sems.at[len(stores)])
        copy.start()
        stores.append(copy)

    early_items = []
    if early_count:
        gu_sum, gu_land, dn_sum, dn_land, gu_sems, dn_sems = early_scratch
        for j in range(early_count):
            for source, total, land, sems in (
                (w_gu, gu_sum, gu_land, gu_sems), (w_dn, dn_sum, dn_land, dn_sems)
            ):
                early_items.append(
                    PlaneReduce(
                        plane, source.at[j], None, total.at[j], land.at[j], None, j % 2 == 0,
                        sems.at[j],
                    )
                )

    def grad(j):
        weight_grads(j)
        if j < early_count:
            for item in early_items[2 * j : 2 * j + 2]:
                item.start()
        else:
            store(w_gu.at[j], grad_gu_out.at[j])
            store(w_dn.at[j], grad_dn_out.at[j])

    def early_paired(number):
        early_items[number].pair_sum()
        early_items[number].send(0)

    def early_crossed(number):
        early_items[number].take(0)
        out = early_gu_out if number % 2 == 0 else early_dn_out
        store(early_items[number].crossed_view(), out.at[number // 2])

    def finish_out(m):
        reduce_out[m].total(own_sum)
        y_out[m, 0] = (hidden[m] + own_sum[...]).astype(BF)
        reduce_out[m].finish()
        if not late:
            free_landing(0, m)

    def finish_in(m):
        reduce_in[m].total(moe_sum.at[m])
        reduce_in[m].finish()
        free_landing(1, m)

    def free_landing(kind, m):
        if m < micros - 1:
            for way, target, on in ((0, z - 1, z > 0), (1, z + 1, z < count - 1)):

                @pl.when(on)
                def _(way=way, target=target):
                    pl.semaphore_signal(
                        free_sems.at[kind, way], inc=1, device_id={"expert": target},
                        device_id_type=pl.DeviceIdType.MESH,
                    )

    def reduce_slot(kind, m, way, slot):
        if m > 0 and slot == 0:

            @pl.when(z < count - 1 if way == 0 else z > 0)
            def _():
                pl.semaphore_wait(free_sems.at[kind, way], 1)

        (reduce_out, reduce_in)[kind][m].slot(way, slot)

    steps, last = count - 1, local - 1
    work, before, services = {}, [], []
    work[DO_NORM,], work[DO_KV,], work[DO_QUERY,] = norm, keys_values, first_queries
    chain = [(DO_NORM,), (DO_KV,), (DO_QUERY,)]
    for name, function in ((DO_ATTEND, attend),):
        for m in range(micros):
            work[name, m] = functools.partial(function, m)
            chain.append((name, m))
    for m in range(micros):
        work[DO_GATE, m] = functools.partial(gate_rows, m)
        work[DO_OUT, m] = functools.partial(out_rows, m)
        chain.append((DO_GATE, m))
        for name, function in ((DO_FWD, expert_forward), (DO_BWD, expert_backward)):
            for j in range(local):
                work[name, m, j] = functools.partial(function, m, j)
                chain.append((name, m, j))
            if name == DO_FWD:
                chain.append((DO_OUT, m))
    for j in range(local):
        work[DO_GRAD, j] = functools.partial(grad, j)
        chain.append((DO_GRAD, j))
    before += chained(*chain)
    for m in range(micros):
        for name, gather, after, ahead in (
            (ON_K, gather_kv[m], (DO_KV,), (DO_ATTEND, m)),
            (ON_N, gather_rows[m], (DO_ATTEND, m), (DO_GATE, m)),
            (ON_C, gather_cot[m], None, (DO_BWD, m, 0)),
        ):
            for way in gather.ways:
                items = [(ON_S, name, m, way)]
                work[items[0]] = functools.partial(gather.start, way, 0)
                for step in range(steps):
                    items.append((ON_H, name, m, way, step))
                    work[items[-1]] = functools.partial(gather.hop, way, step)
                services += items
                before += chained(*([after] if after else []), *items, ahead)
        for name, after in ((ON_O, (DO_OUT, m)), (ON_D, (DO_BWD, m, last))):
            if name == ON_O and m > 0 and late:
                continue
            for way in range(2):
                items = [(ON_L, name, m, way, t) for t in range(count)]
                for t, item in enumerate(items):
                    work[item] = functools.partial(reduce_slot, int(name == ON_D), m, way, t)
                services += items
                before += chained(after, *items)
                if m < micros - 1:
                    before.append((items[-1], (DO_BWD, m + 1, last) if name == ON_D else (DO_OUT, m + 1)))
    for number in range(len(early_items)):
        items = [(ON_P, ON_E, number), (ON_X, ON_E, number)]
        work[items[0]] = functools.partial(early_paired, number)
        work[items[1]] = functools.partial(early_crossed, number)
        services += items
        before += chained((DO_GRAD, number // 2), *items)
    order = [item for item in FORWARD_ORDER if item in work]
    if set(order) != set(work):
        order = natural_order(chain, services, before)
    done = set()
    for item in order:
        work[item]()
        done.add(item)
        if item[0] == ON_L and item[4] == count - 1:
            if item[:3] + (1 - item[3], count - 1) in done:
                (finish_out if item[1] == ON_O else finish_in)(item[2])
        if item == (DO_OUT, micros - 1) and late:
            store(out_parts, late_out)
        if item == (DO_ATTEND, micros - 1):
            for src, dst in (
                (hidden, hidden_out), (queries, queries_out), (keyval, keyval_out),
                (mixture, mixture_out),
            ):
                store(src, dst)
    store(moe_sum, moe_out)
    for item in gather_kv + gather_rows + gather_cot:
        item.finish()
    for item in early_items:
        item.finish((0, 1))
    for copy in stores:
        copy.wait()


def forward_call(
    count, devices, tokens, lengths, routes, gain_one, w_query, w_keyval, w_out, gain_two, w_router,
    gate_up, down, cot,
):
    micros, _, rows, model = tokens.shape
    local, ff = gate_up.shape[0], down.shape[1]
    seq_len = routes.shape[2]
    kv = w_keyval.shape[1] // 2
    chunks = kv // LANES
    heads = w_query.shape[1]
    steps = count - 1
    split = -(-model // seq_len)
    cos, sin = rope_constants(seq_len)
    vmem = pl.BlockSpec(memory_space=pltpu.VMEM)
    smem = pl.BlockSpec(memory_space=pltpu.SMEM)
    hbm = pl.BlockSpec(memory_space=pl.ANY)
    dma = pltpu.SemaphoreType.DMA
    wide_in = model + LANES
    plane = plane_of(devices)
    early = early_experts(count, local)
    gu_shape = (local,) + plane + (2, model // devices, 2 * ff)
    dn_shape = (local,) + plane + (2, ff // devices, model)
    out_shape = (
        jax.ShapeDtypeStruct((micros, 1, rows, model), BF),
        jax.ShapeDtypeStruct((micros, rows, model), F32),
        jax.ShapeDtypeStruct((micros, rows, wide_in), F32),
        jax.ShapeDtypeStruct((micros, chunks, 4 * rows, LANES), BF),
        jax.ShapeDtypeStruct((micros, seq_len, 2 * kv), BF),
        jax.ShapeDtypeStruct((micros, rows, heads), BF),
        jax.ShapeDtypeStruct(gu_shape, BF),
        jax.ShapeDtypeStruct(dn_shape, BF),
        jax.ShapeDtypeStruct((seq_len, model), BF),
        jax.ShapeDtypeStruct((max(early, 1), plane[0]) + gu_shape[4:], BF),
        jax.ShapeDtypeStruct((max(early, 1), plane[0]) + dn_shape[4:], BF),
    )
    scratch = [
        pltpu.VMEM((seq_len, model), F32),
        pltpu.VMEM((seq_len, ff), F32),
        pltpu.VMEM((micros * rows, model), BF),
        pltpu.VMEM((micros, chunks, 4 * rows, LANES), BF),
        pltpu.VMEM((micros, seq_len, 2 * kv), BF),
        pltpu.VMEM((micros, rows, heads), BF),
        pltpu.VMEM((micros, rows, model), F32),
        pltpu.VMEM((micros, seq_len, LANES), F32),
        pltpu.VMEM((seq_len, LANES), F32),
        pltpu.VMEM((local, seq_len, LANES), F32),
        pltpu.VMEM((seq_len, LANES), F32),
        pltpu.VMEM((LANES, model), BF),
        pltpu.VMEM((micros, seq_len, model), BF),
        pltpu.VMEM((micros, seq_len, model), BF),
        pltpu.VMEM((micros, seq_len, local * ff), BF),
        pltpu.VMEM((micros * local, seq_len, 2 * ff), BF),
        pltpu.VMEM(w_out.shape, BF),
        pltpu.VMEM(gu_shape, BF),
        pltpu.VMEM(dn_shape, BF),
        pltpu.VMEM((seq_len, model), BF),
        pltpu.VMEM((count + 1, rows, model), BF),
        pltpu.VMEM((seq_len, wide_in), BF),
        pltpu.VMEM((count + 1, rows, wide_in), BF),
        pltpu.VMEM((rows, model), F32),
        pltpu.VMEM((micros, rows, wide_in), F32),
    ] + [dma((micros, 2, 2, steps))] * 5 + [dma((2 * split + 3,)), dma((2 * local + 6,))]
    scratch.append(pltpu.SemaphoreType.REGULAR((2, 2)))
    if early:
        for shape in (gu_shape, dn_shape):
            scratch.append(pltpu.VMEM((early,) + plane + shape[4:], BF))
            scratch.append(pltpu.VMEM((early, plane[1] - 1, plane[0]) + shape[4:], BF))
        scratch += [dma((early, 2, plane[0] + plane[1] - 1))] * 2
    dims = (micros, rows, count, local, ff, model, late_sums(count), early, plane)
    return pl.pallas_call(
        functools.partial(forward_kernel, dims),
        out_shape=out_shape,
        in_specs=[smem] + [vmem] * 8 + [hbm] * 5,
        out_specs=(vmem,) + (hbm,) * 10,
        scratch_shapes=scratch,
        name="layer_forward",
        compiler_params=pltpu.CompilerParams(
            collective_id=0, has_side_effects=True, vmem_limit_bytes=VMEM_LIMIT
        ),
    )(
        lengths.T, tokens, cot, jnp.swapaxes(routes, 2, 3), gain_one.reshape(1, -1),
        gain_two.reshape(1, -1), jnp.asarray(cos), jnp.asarray(sin), w_router.T, w_query, w_keyval, w_out,
        gate_up.reshape(gu_shape), down.reshape(dn_shape),
    )


class LineReduce:
    def __init__(self, parts, land, rows, count, sems):
        self.parts, self.land, self.rows, self.count, self.sems = parts, land, rows, count, sems
        self.group = max(rows, GROUP)

    def span(self, z):
        if self.group == self.rows:
            return rows_at(z, self.rows)
        return pl.ds(pl.multiple_of(z * self.rows // self.group * self.group, self.group), self.group)

    def hops(self):
        z = lax.axis_index("expert")
        for k in range(1, self.count):
            target = lax.rem(z + k, self.count)
            yield k, pltpu.make_async_remote_copy(
                src_ref=self.parts.at[self.span(target), :],
                dst_ref=self.land.at[k - 1],
                send_sem=self.sems.at[0, k - 1],
                recv_sem=self.sems.at[1, k - 1],
                device_id={"expert": target},
                device_id_type=pl.DeviceIdType.MESH,
            )

    def start(self):
        for _, copy in self.hops():
            copy.start()

    def total(self):
        for _, copy in self.hops():
            copy.wait_recv()
        summed = self.parts[self.span(lax.axis_index("expert")), :].astype(F32)
        for k in range(self.count - 1):
            summed = summed + self.land[k].astype(F32)
        return summed

    def finish(self):
        for _, copy in self.hops():
            copy.wait_send()


def full_barrier(plane, count):
    z = lax.axis_index("expert")
    barrier = pltpu.get_barrier_semaphore()
    greeted = plane_partners(plane)
    greeted += [{"expert": lax.rem(z + k, count)} for k in range(1, count)]
    for device in greeted:
        pl.semaphore_signal(barrier, inc=1, device_id=device, device_id_type=pl.DeviceIdType.MESH)
    pl.semaphore_wait(barrier, len(greeted))


def backward_kernel(
    dims,
    plane,
    lengths,
    tokens,
    cot,
    routes,
    gain_one,
    gain_two,
    cos_ref,
    sin_ref,
    router,
    y_first,
    hidden,
    moe,
    queries,
    keyval,
    mixture,
    query_hbm,
    keyval_hbm,
    out_hbm,
    grad_gu,
    grad_dn,
    late_parts,
    early_gu,
    early_dn,
    y_out,
    input_grad,
    gu_out,
    dn_out,
    dense_out,
    small_out,
    w_query,
    w_keyval,
    w_out,
    router_pad,
    normed,
    normed2,
    d_attn,
    d_mix,
    d_keyval,
    d_logits,
    wide,
    gains,
    bias,
    scores,
    d_probs,
    probs,
    d_scores,
    stacked,
    kv_parts,
    kv_land,
    gu_own,
    gu_sum,
    gu_land_a,
    gu_land_b,
    dn_own,
    dn_sum,
    dn_land_a,
    dn_land_b,
    grads,
    grads_sum,
    grads_land_a,
    grads_land_b,
    grads_line,
    grads_line_land,
    small,
    small_sum,
    small_land_a,
    small_land_b,
    small_line,
    small_line_land,
    gu_sems,
    dn_sems,
    grads_sems,
    small_sems,
    line_sems,
    kv_sems,
    load_sems,
    own_sems,
    out_sems,
    *late_scratch,
):
    micros, rows, count, local, ff, model, late, early_count = dims
    seq_len = count * rows
    kv = keyval.shape[2] // 2
    chunks = kv // LANES
    both = micros * rows
    d_query = d_mix
    z = lax.axis_index("expert")
    row_base = z * rows
    block = small_line.shape[0] // count
    core = lax.rem(lax.axis_index("dp"), 2)

    loads = []
    for number, (src, dst) in enumerate(
        ((out_hbm, w_out), (query_hbm, w_query), (keyval_hbm, w_keyval))
    ):
        loads.append(pltpu.make_async_copy(src, dst, load_sems.at[number]))
        loads[-1].start()
    full_barrier(plane, count)

    experts = []
    for j in range(local):
        for kind, (source, early, own, total, land_a, land_b, sems) in enumerate(
            (
                (grad_gu, early_gu, gu_own, gu_sum, gu_land_a, gu_land_b, gu_sems),
                (grad_dn, early_dn, dn_own, dn_sum, dn_land_a, dn_land_b, dn_sems),
            )
        ):
            slot = (j - early_count) % 2
            item = PlaneReduce(
                plane, source.at[j], own.at[slot], total.at[j], land_a.at[j], land_b.at[j],
                j % 2 == 0, sems.at[j],
            )
            if j < early_count:
                view, into = early.at[j], item.crossed_view()
            else:
                view, into = source.at[j, :, :, core], own.at[slot]
                item.start()
            item.local = pltpu.make_async_copy(view, into, own_sems.at[2 * j + kind])
            if j < early_count + 2:
                item.local.start()
            experts.append(item)
    dense = [
        PlaneReduce(
            plane, grads.at[k], None, grads_sum.at[k], grads_land_a.at[k], grads_land_b.at[k],
            k % 2 == 0, grads_sems.at[k],
        )
        for k in range(6)
    ]
    dense.append(
        PlaneReduce(
            plane, small, None, small_sum, small_land_a, small_land_b, True, small_sems
        )
    )
    lines = [
        LineReduce(grads_line.at[k], grads_line_land.at[k], block, count, line_sems.at[k])
        for k in range(6)
    ] + [LineReduce(small_line, small_line_land, block, count, line_sems.at[6])]
    reduce_kv = [
        Reduce(kv_parts.at[m], kv_land.at[m], rows, count, kv_sems.at[m], up=False)
        for m in range(micros)
    ]

    def paired(item):
        item.pair_sum()
        item.send(0)

    def crossed(item):
        item.take(0)
        item.send(1)

    def expert_paired(number):
        paired(experts[number])
        if 2 * early_count + 4 <= number + 4 < len(experts):
            experts[number + 4].local.start()

    def early_crossed(number):
        experts[number].local.wait()
        experts[number].send(1)

    def expert_done(number):
        out = gu_out if number % 2 == 0 else dn_out
        out[number // 2] = experts[number].take(1)

    def dense_done(number):
        ref = grads_line.at[number] if number < 6 else small_line
        ref[...] = dense[number].take(1).astype(BF)
        lines[number].start()

    def line_done(number):
        if number < 6:
            half = model // 2
            dense_out[number // 2, :, (number % 2) * half : (number % 2 + 1) * half] = lines[
                number
            ].total()
        else:
            small_out[...] = lines[number].total().T[:, 0 : small_out.shape[1]]

    def put_grads(number, left, right):
        half = model // 2
        shape = grads.shape[1:]
        for k in range(2):
            value = tn(left, right[:, k * half : (k + 1) * half])
            grads[2 * number + k] = value.astype(BF).reshape(shape)
            dense[2 * number + k].start()

    router_pad[...] = jnp.zeros(router_pad.shape, BF)
    router_pad[0 : router.shape[0], :] = router[...]
    gains[...] = jnp.zeros(gains.shape, F32)

    def norm_back(d_rows, inputs, scale, gain, row):
        scaled = d_rows * gain
        gains[row : row + 1, :] += jnp.sum(d_rows * inputs * scale, 0, keepdims=True)
        return scale * (
            scaled - inputs * scale * scale * jnp.mean(scaled * inputs, -1, keepdims=True)
        )

    def live_rows(m):
        return (row_base + lax.broadcasted_iota(jnp.int32, (rows, 1), 0)) < lengths[0, m]

    router_lanes = router.shape[0]

    def router_back():
        for m in range(micros):
            span = slice(m * rows, (m + 1) * rows)
            x_rows = tokens[m, 0].astype(F32)
            normed[span, :] = (x_rows * rms_scale(x_rows) * gain_one[...]).astype(BF)
            v = hidden[m]
            scale = rms_scale(v)
            normed2[span, :] = (v * scale * gain_two[...]).astype(BF)
            logits = nt(normed2[span, :], router_pad[...])
            live = live_rows(m)
            on = jnp.where(live, named_lanes(routes[m, 0, :, rows_at(z, rows)]), 0.0) > 0.0
            masked = jnp.where(on, logits, NEG_FILL)
            raised = jnp.where(on, jnp.exp(masked - jnp.max(masked, -1, keepdims=True)), 0.0)
            total = jnp.sum(raised, -1, keepdims=True)
            gate = raised / jnp.where(total > 0.0, total, 1.0)
            d_gate = moe[m, :, model:]
            d_logits[span, :] = (
                gate * (d_gate - jnp.sum(gate * d_gate, -1, keepdims=True))
            ).astype(BF)
            d_rows = moe[m, :, 0:model] + nn(d_logits[span, :], router_pad[...])
            grown = cot[m, 0].astype(F32) + norm_back(
                d_rows, v, scale, gain_two[...], router_lanes + 1
            )
            input_grad[m, 0] = grown
            d_attn[span, :] = jnp.where(live, grown, 0.0).astype(BF)

    def mixture_back():
        loads[0].wait()
        d_mix[...] = nt(d_attn[...], w_out[...]).astype(BF)

    def grad_out():
        put_grads(2, mixture[...].reshape(both, mixture.shape[2]), d_attn[...])

    cos = cos_ref[rows_at(z, rows), :]
    sin = sin_ref[rows_at(z, rows), :]

    def attend_back(m, i):
        span = slice(m * rows, (m + 1) * rows)
        lanes = slice(i * LANES, (i + 1) * LANES)
        value_lanes = slice(kv + i * LANES, kv + (i + 1) * LANES)
        if i == 0:
            score_bias(bias, row_base, lengths[0, m])
        pair = [d_mix[span, c * LANES : (c + 1) * LANES].astype(F32) for c in (2 * i, 2 * i + 1)]
        for k, rows_of in enumerate(stack_heads(*pair)):
            stacked[k * rows : (k + 1) * rows, :] = rows_of.astype(BF)
        scores[...] = nt(keyval[m, :, lanes], queries[m, i])
        d_probs[...] = nt(keyval[m, :, value_lanes], stacked[...])
        for k in range(4):
            where = slice(k * rows, (k + 1) * rows)
            prob = softmax_columns(scores[:, where] + bias[...])
            d_prob = d_probs[:, where]
            delta = jnp.sum(prob * d_prob, 0, keepdims=True)
            d_scores[:, where] = (prob * (d_prob - delta)).astype(BF)
            probs[:, where] = prob.astype(BF)
        turned = tn(d_scores[...], keyval[m, :, lanes]) * ATTENTION_SCALE
        for c, chunk in zip((2 * i, 2 * i + 1), unstack_heads(turned, rows)):
            d_query[span, c * LANES : (c + 1) * LANES] = rope(chunk, cos, -sin).astype(BF)
        kv_parts[m, :, lanes] = nn(d_scores[...], queries[m, i]).astype(BF)
        kv_parts[m, :, value_lanes] = nn(probs[...], stacked[...]).astype(BF)

    def grad_query():
        put_grads(0, normed[...], d_query[...])

    def query_back():
        loads[1].wait()
        wide[...] = nt(d_query[...], w_query[...])

    def keyval_total():
        for m in range(micros):
            span = slice(m * rows, (m + 1) * rows)
            key_own = d_probs.at[0:rows, 0:kv]
            value_own = d_probs.at[rows : 2 * rows, 0:kv]
            reduce_kv[m].total(key_own, slice(0, kv))
            reduce_kv[m].total(value_own, slice(kv, 2 * kv))
            for c in range(chunks):
                lanes = slice(c * LANES, (c + 1) * LANES)
                d_keyval[span, lanes] = rope(key_own[:, lanes], cos, -sin).astype(BF)
            d_keyval[span, kv:] = value_own[...].astype(BF)

    def grad_keyval():
        put_grads(1, normed[...], d_keyval[...])

    def keyval_back():
        loads[2].wait()
        wide[...] += nt(d_keyval[...], w_keyval[...])

    def input_back():
        for m in range(micros):
            span = slice(m * rows, (m + 1) * rows)
            x_rows = tokens[m, 0].astype(F32)
            input_grad[m, 0] += norm_back(
                wide[span, :], x_rows, rms_scale(x_rows), gain_one[...], router_lanes
            )

    def grad_small():
        small_value = tn(normed2[...], d_logits[...]) + gains[...].T
        small[...] = small_value.astype(BF).reshape(small.shape)
        dense[6].start()

    if late:
        out_parts, out_land, out_own = late_scratch
        late_load = pltpu.make_async_copy(late_parts, out_parts, load_sems.at[3])
        late_load.start()
        reduce_out = Reduce(out_parts, out_land, rows, count, out_sems)
    y_out[...] = y_first[...]

    arrived = []

    def out_slot(way, slot):
        if not arrived:
            late_load.wait()
            arrived.append(True)
        reduce_out.slot(way, slot)

    def finish_out():
        reduce_out.total(out_own)
        y_out[micros - 1, 0] = (hidden[micros - 1] + out_own[...]).astype(BF)
        reduce_out.finish()

    work, before, services = {}, [], []
    chain = [(DO_ROUTER,), (DO_MIXTURE,), (DO_GRAD_OUT,)]
    work[DO_ROUTER,], work[DO_MIXTURE,], work[DO_GRAD_OUT,] = router_back, mixture_back, grad_out
    for m in range(micros):
        for i in range(chunks):
            chain.append((DO_ATTEND, m, i))
            work[chain[-1]] = functools.partial(attend_back, m, i)
    for name, function in (
        (DO_GRAD_QUERY, grad_query), (DO_QUERY, query_back), (DO_TOTAL, keyval_total),
        (DO_GRAD_KEYVAL, grad_keyval), (DO_KEYVAL, keyval_back), (DO_INPUT, input_back),
        (DO_SMALL, grad_small),
    ):
        chain.append((name,))
        work[name,] = function
    before += chained(*chain)
    for m in range(micros):
        items = [(ON_L, ON_K, m, 1, t) for t in range(count)]
        for t, item in enumerate(items):
            work[item] = functools.partial(reduce_kv[m].slot, 1, t)
        services += items
        before += chained((DO_ATTEND, m, chunks - 1), *items, (DO_TOTAL,))
    if late:
        for way in range(2):
            items = [(ON_L, ON_O, way, t) for t in range(count)]
            for t, item in enumerate(items):
                work[item] = functools.partial(out_slot, way, t)
            services += items
            before += chained(*items)
    for number in range(len(experts)):
        items = [(stage, ON_E, number) for stage in (ON_P, ON_X, ON_D)]
        work[items[1]] = functools.partial(crossed, experts[number])
        work[items[2]] = functools.partial(expert_done, number)
        if number < 2 * early_count:
            items = items[1:]
            work[items[0]] = functools.partial(early_crossed, number)
        else:
            work[items[0]] = functools.partial(expert_paired, number)
            if number >= 2 * early_count + 4:
                before.append(((ON_P, ON_E, number - 4), items[0]))
        services += items
        before += chained(*items)
    for number, source in enumerate(
        (DO_GRAD_QUERY, DO_GRAD_QUERY, DO_GRAD_KEYVAL, DO_GRAD_KEYVAL, DO_GRAD_OUT, DO_GRAD_OUT, DO_SMALL)
    ):
        items = [(stage, ON_G, number) for stage in (ON_P, ON_X, ON_D, ON_Z)]
        work[items[0]] = functools.partial(paired, dense[number])
        work[items[1]] = functools.partial(crossed, dense[number])
        work[items[2]] = functools.partial(dense_done, number)
        work[items[3]] = functools.partial(line_done, number)
        services += items
        before += chained((source,), *items)
    services.sort(key=lambda item: (ON_L, ON_P, ON_X, ON_D, ON_Z).index(item[0]))
    order = [item for item in BACKWARD_ORDER if item in work]
    if set(order) != set(work):
        order = natural_order(chain, services, before)
    done = set()
    for item in order:
        work[item]()
        done.add(item)
        if item[:2] == (ON_L, ON_O) and item[3] == count - 1 and (ON_L, ON_O, 1 - item[2], count - 1) in done:
            finish_out()
    for number, item in enumerate(experts):
        item.finish((2,) if number < 2 * early_count else (0, 1, 2))
    for item in dense + lines + reduce_kv:
        item.finish()


def backward_call(
    count, devices, tokens, lengths, routes, gain_one, w_query, w_keyval, w_out, gain_two,
    w_router, cot, local, ff, y_first, hidden, moe, queries, keyval, mixture, grad_gu, grad_dn, late_parts,
    early_gu, early_dn,
):
    micros, _, rows, model = tokens.shape
    seq_len = routes.shape[2]
    kv = w_keyval.shape[1] // 2
    heads = w_query.shape[1]
    plane = plane_of(devices)
    block = model // devices // count
    group = max(block, GROUP)
    line = count * block
    half = model // 2
    both = micros * rows
    cos, sin = rope_constants(seq_len)
    gu_rows, dn_rows = model // devices, ff // devices
    vmem = pl.BlockSpec(memory_space=pltpu.VMEM)
    smem = pl.BlockSpec(memory_space=pltpu.SMEM)
    hbm = pl.BlockSpec(memory_space=pl.ANY)
    dma = pltpu.SemaphoreType.DMA
    hops = plane[0] + plane[1] - 1

    def reduce_scratch(lead, block_rows, width):
        lead = tuple(lead)
        return [
            pltpu.VMEM(lead + plane + (block_rows, width), BF),
            pltpu.VMEM(lead + (plane[1] - 1, plane[0], block_rows, width), BF),
            pltpu.VMEM(lead + (plane[0] - 1, block_rows, width), BF),
        ]

    wide_bf = pltpu.VMEM((both, model), BF)
    late = late_sums(count)
    out_shape = (
        jax.ShapeDtypeStruct((micros, 1, rows, model), BF),
        jax.ShapeDtypeStruct((micros, 1, rows, model), F32),
        jax.ShapeDtypeStruct((local, gu_rows, 2 * ff), F32),
        jax.ShapeDtypeStruct((local, dn_rows, model), F32),
        jax.ShapeDtypeStruct((3, group, model), F32),
        jax.ShapeDtypeStruct((LANES, group), F32),
    )
    scratch = (
        [pltpu.VMEM(w.shape, BF) for w in (w_query, w_keyval, w_out)]
        + [pltpu.VMEM((LANES, model), BF)]
        + [wide_bf, wide_bf, wide_bf, pltpu.VMEM((both, heads), BF)]
        + [pltpu.VMEM((both, 2 * kv), BF), pltpu.VMEM((both, LANES), BF)]
        + [pltpu.VMEM((both, model), F32)]
        + [pltpu.VMEM((LANES, model), F32)]
        + [pltpu.VMEM((seq_len, rows), F32)]
        + [pltpu.VMEM((seq_len, 4 * rows), F32)] * 2
        + [pltpu.VMEM((seq_len, 4 * rows), BF)] * 2
        + [pltpu.VMEM((4 * rows, LANES), BF)]
        + [pltpu.VMEM((micros, seq_len, 2 * kv), BF)]
        + [pltpu.VMEM((micros, count - 1, rows, 2 * kv), BF)]
        + [pltpu.VMEM((2,) + plane + (gu_rows, 2 * ff), BF)]
        + reduce_scratch((local,), gu_rows, 2 * ff)
        + [pltpu.VMEM((2,) + plane + (dn_rows, model), BF)]
        + reduce_scratch((local,), dn_rows, model)
        + [pltpu.VMEM((6,) + plane + (2, line, half), BF)]
        + reduce_scratch((6,), line, half)
        + [pltpu.VMEM((6, line, half), BF), pltpu.VMEM((6, count - 1, group, half), BF)]
        + [pltpu.VMEM(plane + (2, line, LANES), BF)]
        + reduce_scratch((), line, LANES)
        + [pltpu.VMEM((line, LANES), BF), pltpu.VMEM((count - 1, group, LANES), BF)]
        + [dma((local, 2, hops)), dma((local, 2, hops)), dma((6, 2, hops)), dma((2, hops))]
        + [dma((7, 2, count - 1)), dma((micros, 2, 2, count - 1)), dma((4,)), dma((2 * local,))]
        + [dma((2, 2, count - 1))]
    )
    if late:
        scratch += [
            pltpu.VMEM((seq_len, model), BF),
            pltpu.VMEM((count + 1, rows, model), BF),
            pltpu.VMEM((rows, model), F32),
        ]
    dims = (micros, rows, count, local, ff, model, late, early_experts(count, local))
    return pl.pallas_call(
        functools.partial(backward_kernel, dims, plane),
        out_shape=out_shape,
        in_specs=[smem] + [vmem] * 14 + [hbm] * 8,
        out_specs=(vmem,) * 6,
        scratch_shapes=scratch,
        name="layer_backward",
        compiler_params=pltpu.CompilerParams(
            collective_id=1, has_side_effects=True, vmem_limit_bytes=VMEM_LIMIT
        ),
    )(
        lengths.T, tokens, cot, jnp.swapaxes(routes, 2, 3), gain_one.reshape(1, -1),
        gain_two.reshape(1, -1), jnp.asarray(cos), jnp.asarray(sin), w_router.T, y_first, hidden,
        moe, queries, keyval, mixture,
        w_query, w_keyval, w_out,
        grad_gu.reshape((local,) + plane + (2, gu_rows, 2 * ff)),
        grad_dn.reshape((local,) + plane + (2, dn_rows, model)),
        late_parts,
        early_gu,
        early_dn,
    )


def finish_kernel(*refs):
    *arrays, dense, small = refs[:6]
    outs, stages, sems = refs[6:16], refs[16:23], refs[23]
    pairs = list(zip(arrays, outs)) + [(dense.at[k], outs[4 + k]) for k in range(3)]
    inward = [
        pltpu.make_async_copy(src, stage, sems.at[0, k])
        for k, ((src, _), stage) in enumerate(zip(pairs, stages))
    ]
    outward = [
        pltpu.make_async_copy(stage, dst, sems.at[1, k])
        for k, ((_, dst), stage) in enumerate(zip(pairs, stages))
    ]
    for copy in inward:
        copy.start()
    router, gain_one, gain_two = outs[7:]
    lanes = router.shape[0]
    router[...] = small[0:lanes, :]
    gain_one[...] = small[lanes : lanes + 1, :]
    gain_two[...] = small[lanes + 1 : lanes + 2, :]
    for arrived, leaving in zip(inward, outward):
        arrived.wait()
        leaving.start()
    for copy in outward:
        copy.wait()


def finish_call(arrays, dense, small, experts):
    hbm = pl.BlockSpec(memory_space=pl.ANY)
    vmem = pl.BlockSpec(memory_space=pltpu.VMEM)
    shapes = [jax.ShapeDtypeStruct(v.shape, v.dtype) for v in arrays]
    shapes += [jax.ShapeDtypeStruct(dense.shape[1:], F32)] * 3
    shapes += [jax.ShapeDtypeStruct((n, small.shape[1]), F32) for n in (experts, 1, 1)]
    return pl.pallas_call(
        finish_kernel,
        out_shape=tuple(shapes),
        in_specs=[hbm] * 5 + [vmem],
        out_specs=(hbm,) * 7 + (vmem,) * 3,
        scratch_shapes=[pltpu.VMEM(v.shape, v.dtype) for v in shapes[:7]]
        + [pltpu.SemaphoreType.DMA((2, 7))],
        name="layer_results",
    )(*arrays, dense, small)


def on_device(
    tokens, lengths, routes, attn_gain, w_query, w_keyval, w_out, ffn_gain, w_router,
    expert_gate_up, expert_down, cotangent,
):
    count = lax.axis_size("expert")
    devices = lax.axis_size("dp")
    model = tokens.shape[3]
    experts = w_router.shape[1]
    local, ff = expert_gate_up.shape[0], expert_down.shape[1]
    y, hidden, moe, queries, keyval, mixture, grad_gu, grad_dn, *partial = forward_call(
        count, devices, tokens, lengths, routes, attn_gain, w_query, w_keyval, w_out, ffn_gain, w_router,
        expert_gate_up, expert_down, cotangent,
    )
    y, input_grad, gu, dn, dense, small = backward_call(
        count, devices, tokens, lengths, routes, attn_gain, w_query, w_keyval, w_out, ffn_gain,
        w_router, cotangent, local, ff, y, hidden, moe, queries, keyval, mixture, grad_gu,
        grad_dn, *partial,
    )
    block = model // devices // count
    if dense.shape[1] != block:
        first = lax.rem(lax.axis_index("expert") * block, dense.shape[1])
        dense = lax.dynamic_slice_in_dim(dense, first, block, 1)
        small = lax.dynamic_slice_in_dim(small, first, block, 1)
    *whole, router, gain_one, gain_two = finish_call(
        (y, input_grad, gu, dn), dense, small, experts
    )
    return (
        whole[0], whole[1], gain_one[0], whole[4], whole[5], whole[6], gain_two[0], router.T,
        whole[2], whole[3],
    )


def solution(mesh):
    placed = (
        P(None, "dp", "expert", None), P(None, "dp"), P(None, "dp", None, None), P(), P(), P(), P(),
        P(), P(), P("expert", None, None), P("expert", None, None), P(None, "dp", "expert", None),
    )
    return jax.shard_map(
        on_device,
        mesh=mesh,
        in_specs=placed,
        out_specs=(
            P(None, "dp", "expert", None), P(None, "dp", "expert", None), P(("dp", "expert")),
            P(("dp", "expert"), None), P(("dp", "expert"), None), P(("dp", "expert"), None),
            P(("dp", "expert")), P(("dp", "expert"), None), P("expert", "dp", None),
            P("expert", "dp", None),
        ),
        check_vma=False,
    )
```

```python
import functools
import math

import jax
import jax.numpy as jnp
import numpy as np
from jax import lax
from jax.experimental import pallas as pl
from jax.experimental.pallas import tpu as pltpu
from jax.sharding import PartitionSpec as P

HEAD_DIM = 64
EPS = 1e-06
ATTENTION_SCALE = 0.015625
ROPE_BASE = 10000.0
NEG_FILL = -1e30
LANES = 128
GROUP = 16
STRIP = 64
BF = jnp.bfloat16
F32 = jnp.float32
VMEM_LIMIT = 63 * 2**20
(
    DO_NORM, DO_KV, DO_QUERY, DO_LEND, DO_REST, DO_ATTEND, DO_GATE, DO_FWD, DO_OUT, DO_BWD,
    DO_GRAD, DO_ROUTER, DO_MIXTURE, DO_GRAD_OUT, DO_GRAD_QUERY, DO_TOTAL, DO_GRAD_KEYVAL,
    DO_KEYVAL, DO_INPUT, DO_SMALL, ON_S, ON_H, ON_L, ON_K, ON_N, ON_C, ON_O, ON_D, ON_E, ON_G,
    ON_P, ON_X, ON_Z, ON_T, ON_W,
) = range(35)
FORWARD_ORDER = (
    (ON_S, ON_C, 0, 1), (ON_S, ON_C, 0, 0), (DO_NORM,), (DO_KV,), (ON_S, ON_K, 0, 0),
    (ON_H, ON_C, 0, 1, 0), (ON_T, 1, 0), (ON_H, ON_K, 0, 0, 0), (DO_QUERY,), (ON_H, ON_C, 0, 0, 0),
    (ON_W, 1, 0), (ON_S, ON_K, 1, 0), (ON_H, ON_K, 0, 0, 1), (ON_H, ON_C, 0, 1, 1), (ON_T, 0, 0),
    (ON_W, 0, 0), (DO_LEND, 0), (ON_T, 2, 0), (ON_T, 1, 1), (ON_H, ON_C, 0, 0, 1), (ON_T, 0, 1),
    (DO_ATTEND, 0), (ON_W, 2, 0), (ON_W, 0, 1), (DO_REST, 0), (ON_S, ON_N, 0, 1), (ON_S, ON_N, 0, 0),
    (ON_H, ON_K, 1, 0, 0), (ON_W, 1, 1), (ON_H, ON_N, 0, 1, 0), (ON_H, ON_N, 0, 0, 0),
    (ON_H, ON_K, 1, 0, 1), (DO_LEND, 1), (ON_H, ON_C, 0, 1, 2), (ON_T, 2, 1), (ON_W, 2, 1),
    (DO_ATTEND, 1), (ON_H, ON_N, 0, 1, 1), (ON_H, ON_N, 0, 0, 1), (DO_REST, 1), (ON_S, ON_C, 1, 0),
    (ON_S, ON_N, 1, 1), (ON_S, ON_C, 1, 1), (ON_S, ON_N, 1, 0), (ON_H, ON_C, 0, 0, 2),
    (ON_H, ON_N, 0, 0, 2), (ON_H, ON_N, 0, 1, 2), (DO_GATE, 0), (DO_FWD, 0, 0), (DO_FWD, 0, 1),
    (DO_FWD, 0, 2), (DO_FWD, 0, 3), (DO_OUT, 0), (ON_L, ON_O, 0, 0, 0), (ON_L, ON_O, 0, 1, 0),
    (ON_H, ON_N, 1, 0, 0), (DO_BWD, 0, 0), (ON_H, ON_N, 1, 1, 0), (ON_H, ON_C, 1, 0, 0),
    (ON_L, ON_O, 0, 0, 1), (DO_BWD, 0, 1), (ON_H, ON_N, 1, 0, 1), (ON_L, ON_O, 0, 1, 1),
    (ON_H, ON_N, 1, 1, 1), (DO_BWD, 0, 2), (DO_BWD, 0, 3), (ON_L, ON_D, 0, 1, 0), (ON_H, ON_C, 1, 1, 0),
    (ON_L, ON_D, 0, 0, 0), (ON_H, ON_N, 1, 0, 2), (ON_L, ON_O, 0, 0, 2), (ON_H, ON_N, 1, 1, 2),
    (ON_H, ON_C, 1, 0, 1), (DO_GATE, 1), (ON_L, ON_O, 0, 1, 2), (DO_FWD, 1, 0), (ON_L, ON_D, 0, 0, 1),
    (DO_FWD, 1, 1), (DO_FWD, 1, 2), (ON_H, ON_C, 1, 1, 1), (ON_L, ON_D, 0, 1, 1), (ON_L, ON_O, 0, 0, 3),
    (DO_FWD, 1, 3), (ON_L, ON_D, 0, 0, 2), (ON_T, 3, 0), (ON_L, ON_O, 0, 1, 3), (DO_OUT, 1),
    (ON_H, ON_C, 1, 0, 2), (ON_H, ON_C, 1, 1, 2), (DO_BWD, 1, 0), (ON_L, ON_D, 0, 1, 2), (DO_BWD, 1, 1),
    (ON_L, ON_D, 0, 0, 3), (DO_BWD, 1, 2), (ON_L, ON_D, 0, 1, 3), (DO_BWD, 1, 3), (DO_GRAD, 0),
    (DO_GRAD, 1), (ON_T, 3, 1), (ON_L, ON_D, 1, 1, 0), (ON_L, ON_D, 1, 0, 0), (ON_P, ON_E, 0),
    (ON_P, ON_E, 1), (ON_P, ON_E, 2), (ON_P, ON_E, 3), (ON_L, ON_D, 1, 0, 1), (ON_L, ON_D, 1, 1, 1),
    (DO_GRAD, 2), (ON_L, ON_D, 1, 1, 2), (ON_L, ON_D, 1, 0, 2), (ON_X, ON_E, 2), (ON_X, ON_E, 1),
    (DO_GRAD, 3), (ON_L, ON_D, 1, 1, 3), (ON_X, ON_E, 0), (ON_W, 3, 0), (ON_X, ON_E, 3), (ON_W, 3, 1),
    (ON_L, ON_D, 1, 0, 3),
)
BACKWARD_ORDER = (
    (ON_X, ON_E, 2), (DO_ROUTER, 0), (DO_MIXTURE, 0), (DO_ATTEND, 0, 0), (ON_X, ON_E, 1),
    (DO_ATTEND, 0, 1), (DO_ATTEND, 0, 2), (DO_ATTEND, 0, 3), (ON_L, ON_K, 0, 1, 0), (ON_P, ON_E, 6),
    (ON_P, ON_E, 5), (ON_P, ON_E, 4), (DO_ROUTER, 1), (ON_D, ON_E, 1), (ON_P, ON_E, 7), (DO_MIXTURE, 1),
    (ON_L, ON_K, 0, 1, 1), (DO_ATTEND, 1, 0), (ON_L, ON_O, 0, 0), (DO_ATTEND, 1, 1), (ON_D, ON_E, 2),
    (DO_ATTEND, 1, 2), (DO_ATTEND, 1, 3), (ON_L, ON_K, 1, 1, 0), (DO_GRAD_OUT,), (ON_P, ON_G, 4),
    (ON_L, ON_K, 0, 1, 2), (ON_P, ON_G, 5), (DO_GRAD_QUERY,), (ON_P, ON_G, 0), (ON_L, ON_O, 0, 1),
    (ON_L, ON_K, 1, 1, 1), (ON_P, ON_G, 1), (ON_X, ON_G, 4), (ON_X, ON_E, 0), (ON_L, ON_K, 1, 1, 2),
    (ON_X, ON_G, 1), (DO_QUERY,), (ON_X, ON_G, 5), (ON_X, ON_E, 5), (ON_D, ON_G, 1), (ON_X, ON_E, 6),
    (ON_X, ON_G, 0), (ON_L, ON_K, 0, 1, 3), (ON_L, ON_O, 1, 0), (ON_L, ON_K, 1, 1, 3), (DO_TOTAL,),
    (DO_GRAD_KEYVAL,), (ON_D, ON_G, 5), (ON_D, ON_G, 4), (ON_P, ON_G, 2), (ON_L, ON_O, 1, 1),
    (ON_Z, ON_G, 1), (ON_P, ON_G, 3), (DO_KEYVAL,), (DO_INPUT,), (DO_SMALL,), (ON_X, ON_G, 2),
    (ON_L, ON_O, 0, 2), (ON_P, ON_G, 6), (ON_X, ON_G, 3), (ON_D, ON_G, 0), (ON_D, ON_E, 5), (ON_X, ON_G, 6),
    (ON_X, ON_E, 4), (ON_D, ON_G, 2), (ON_Z, ON_G, 4), (ON_X, ON_E, 3), (ON_D, ON_E, 0), (ON_L, ON_O, 1, 2),
    (ON_X, ON_E, 7), (ON_D, ON_G, 6), (ON_D, ON_G, 3), (ON_Z, ON_G, 6), (ON_L, ON_O, 0, 3), (ON_D, ON_E, 7),
    (ON_D, ON_E, 4), (ON_Z, ON_G, 0), (ON_D, ON_E, 6), (ON_L, ON_O, 1, 3), (ON_D, ON_E, 3), (ON_Z, ON_G, 5),
    (ON_Z, ON_G, 2), (ON_Z, ON_G, 3),
)


def dot_of(left, right, left_dim, right_dim):
    return lax.dot_general(
        left, right, (((left_dim,), (right_dim,)), ((), ())), preferred_element_type=F32
    )


def nn(left, right):
    return dot_of(left, right, 1, 0)


def nt(left, right):
    return dot_of(left, right, 1, 1)


def tn(left, right):
    return dot_of(left, right, 0, 0)


def rope_constants(seq_len):
    half = HEAD_DIM // 2
    frequency = np.exp(
        np.arange(half, dtype=np.float32) * np.float32(-2.0 * math.log(ROPE_BASE) / HEAD_DIM)
    ).astype(np.float32)
    angles = np.arange(seq_len, dtype=np.float32)[:, None] * frequency[None, :]
    cos, sin = np.cos(angles).astype(np.float32), np.sin(angles).astype(np.float32)
    heads = LANES // HEAD_DIM
    return np.tile(np.concatenate([cos, cos], 1), (1, heads)), np.tile(
        np.concatenate([-sin, sin], 1), (1, heads)
    )


def lane_ids(rows):
    return lax.broadcasted_iota(jnp.int32, (rows, LANES), 1)


def swap_halves(chunk):
    half = HEAD_DIM // 2
    first = lax.rem(lane_ids(chunk.shape[0]), HEAD_DIM) < half
    return jnp.where(
        first, pltpu.roll(chunk, LANES - half, 1), pltpu.roll(chunk, half, 1)
    )


def rope(chunk, cos, sin):
    return chunk * cos + swap_halves(chunk) * sin


def rms_scale(rows):
    return lax.rsqrt(jnp.mean(rows * rows, -1, keepdims=True) + EPS)


def stack_heads(first, second):
    low = lane_ids(first.shape[0]) < HEAD_DIM
    zero = jnp.zeros_like(first)
    return [
        jnp.where(low, first, zero),
        jnp.where(low, pltpu.roll(first, HEAD_DIM, 1), zero),
        jnp.where(low, zero, pltpu.roll(second, HEAD_DIM, 1)),
        jnp.where(low, zero, second),
    ]


def unstack_heads(stacked, rows):
    low = lane_ids(rows) < HEAD_DIM
    parts = [stacked[k * rows : (k + 1) * rows] for k in range(4)]
    first = jnp.where(low, parts[0], pltpu.roll(parts[1], HEAD_DIM, 1))
    second = jnp.where(low, pltpu.roll(parts[2], HEAD_DIM, 1), parts[3])
    return first, second


def rows_at(index, rows):
    return pl.ds(pl.multiple_of(index * rows, rows), rows)


def natural_order(chain, services, before):
    order, placed = [], set()

    def place(item):
        if item not in placed:
            placed.add(item)
            for first, then in before:
                if then == item:
                    place(first)
            order.append(item)

    for item in chain + services:
        place(item)
    return order


def chained(*items):
    return list(zip(items, items[1:]))


def named_lanes(ids):
    lane = lax.broadcasted_iota(jnp.int32, (LANES, ids.shape[1]), 0)
    hit = jnp.zeros(lane.shape, F32)
    for k in range(ids.shape[0]):
        hit = hit + (ids[k : k + 1, :] == lane).astype(F32)
    return hit.T


class Gather:
    def __init__(self, buffer, micro, rows, count, sems, up=True, down=True):
        self.buffer, self.micro, self.rows, self.count, self.sems = buffer, micro, rows, count, sems
        self.ways = [w for w, on in ((0, up), (1, down)) if on]

    def copy(self, way, step, block):
        z = lax.axis_index("expert")
        target = z + 1 if way == 0 else z - 1
        view = self.buffer.at[self.micro, rows_at(block, self.rows), :]
        return pltpu.make_async_remote_copy(
            src_ref=view,
            dst_ref=view,
            send_sem=self.sems.at[0, way, step],
            recv_sem=self.sems.at[1, way, step],
            device_id={"expert": target},
            device_id_type=pl.DeviceIdType.MESH,
        )

    def sends(self, way, step):
        z = lax.axis_index("expert")
        if way == 0:
            return z - step, jnp.logical_and(z < self.count - 1, z - step >= 0)
        return z + step, jnp.logical_and(z > 0, z + step <= self.count - 1)

    def receives(self, way, step):
        z = lax.axis_index("expert")
        if way == 0:
            return z - 1 - step, jnp.logical_and(z <= self.count - 1, z - 1 - step >= 0)
        return z + 1 + step, z + 1 + step <= self.count - 1

    def start(self, way, step):
        block, on = self.sends(way, step)

        @pl.when(on)
        def _():
            self.copy(way, step, block).start()

    def hop(self, way, step):
        block, on = self.receives(way, step)

        @pl.when(on)
        def _():
            self.copy(way, step, block).wait_recv()

        if step + 1 < self.count - 1:
            self.start(way, step + 1)

    def finish(self):
        for step in range(self.count - 1):
            for way in self.ways:
                block, on = self.sends(way, step)

                @pl.when(on)
                def _(way=way, step=step, block=block):
                    self.copy(way, step, block).wait_send()


class Reduce:
    def __init__(self, parts, landing, rows, count, sems, up=True, down=True):
        self.parts, self.landing = parts, landing
        self.rows, self.count, self.sems = rows, count, sems
        self.ways = [w for w, on in ((0, up), (1, down)) if on]

    def block(self, way, slot):
        z = lax.axis_index("expert")
        if way == 0:
            return z + self.count - 1 - slot, slot >= z
        return z - (self.count - 1) + slot, slot >= self.count - 1 - z

    def place(self, way, slot, z):
        if way == 0:
            return slot - (z - 1)
        return self.count - (slot - (self.count - 2 - z)) - (2 if self.ways == [1] else 0)

    def copy(self, way, slot, block):
        z = lax.axis_index("expert")
        target = z + 1 if way == 0 else z - 1
        return pltpu.make_async_remote_copy(
            src_ref=self.parts.at[rows_at(block, self.rows), :],
            dst_ref=self.landing.at[self.place(way, slot, target)],
            send_sem=self.sems.at[0, way, slot],
            recv_sem=self.sems.at[1, way, slot],
            device_id={"expert": target},
            device_id_type=pl.DeviceIdType.MESH,
        )

    def arrival(self, way, slot, block):
        z = lax.axis_index("expert")
        source = z - 1 if way == 0 else z + 1
        return pltpu.make_async_remote_copy(
            src_ref=self.parts.at[rows_at(block, self.rows), :],
            dst_ref=self.landing.at[self.place(way, slot, z)],
            send_sem=self.sems.at[0, way, slot],
            recv_sem=self.sems.at[1, way, slot],
            device_id={"expert": source},
            device_id_type=pl.DeviceIdType.MESH,
        )

    def inner(self, way):
        z = lax.axis_index("expert")
        return z >= 1 if way == 0 else z <= self.count - 2

    def slot(self, way, slot):
        z = lax.axis_index("expert")
        block, on = self.block(way, slot)
        if slot >= 1:

            @pl.when(jnp.logical_and(on, self.inner(way)))
            def _():
                self.arrival(way, slot - 1, block).wait_recv()
                if slot < self.count - 1:
                    where = rows_at(block, self.rows)
                    total = self.parts[where, :].astype(F32) + self.landing[
                        self.place(way, slot - 1, z)
                    ].astype(F32)
                    self.parts[where, :] = total.astype(self.parts.dtype)

        if slot < self.count - 1:

            @pl.when(on)
            def _():
                self.copy(way, slot, block).start()

    def total(self, out, lanes=slice(None)):
        z = lax.axis_index("expert")
        out[...] = self.parts[rows_at(z, self.rows), lanes].astype(F32)
        for way in self.ways:

            @pl.when(self.inner(way))
            def _(way=way):
                place = self.place(way, self.count - 2, z)
                out[...] += self.landing[place, :, lanes].astype(F32)

    def finish(self):
        for slot in range(self.count - 1):
            for way in self.ways:
                block, on = self.block(way, slot)

                @pl.when(on)
                def _(way=way, slot=slot, block=block):
                    self.copy(way, slot, block).wait_send()


def line_barrier(count, plane=None):
    z = lax.axis_index("expert")
    barrier = pltpu.get_barrier_semaphore()
    mesh = pl.DeviceIdType.MESH
    for target, on in ((z + 1, z < count - 1), (z - 1, z > 0)):

        @pl.when(on)
        def _(target=target):
            pl.semaphore_signal(
                barrier, inc=1, device_id={"expert": target}, device_id_type=mesh
            )

    others = plane_partners(plane) if plane else []
    for device in others:
        pl.semaphore_signal(barrier, inc=1, device_id=device, device_id_type=mesh)
    awaited = (z > 0).astype(jnp.int32) + (z < count - 1).astype(jnp.int32)
    pl.semaphore_wait(barrier, awaited + len(others))


def score_bias(bias, row_base, length):
    key_pos = lax.broadcasted_iota(jnp.int32, bias.shape, 0)
    query_pos = row_base + lax.broadcasted_iota(jnp.int32, bias.shape, 1)
    allowed = jnp.logical_and(key_pos <= query_pos, key_pos < length)
    bias[...] = jnp.where(allowed, 0.0, NEG_FILL)


def softmax_columns(scores):
    raised = jnp.exp(scores - jnp.max(scores, 0, keepdims=True))
    return raised * (1.0 / jnp.sum(raised, 0, keepdims=True))


def sigmoid(v):
    return 0.5 * jnp.tanh(0.5 * v) + 0.5


def plane_of(devices):
    side = math.isqrt(devices // 2)
    return side, side


def device_at(plane, y, x, core):
    return {"dp": (y * plane[1] + x) * 2 + core}


def plane_partners(plane):
    index = lax.axis_index("dp")
    core, chip = lax.rem(index, 2), index // 2
    y, x = chip // plane[1], lax.rem(chip, plane[1])
    partners = [device_at(plane, y, x, 1 - core)]
    partners += [device_at(plane, y, lax.rem(x + k, plane[1]), core) for k in range(1, plane[1])]
    partners += [device_at(plane, lax.rem(y + k, plane[0]), x, core) for k in range(1, plane[0])]
    return partners


class PlaneReduce:
    def __init__(self, plane, source, own, total, first_land, second_land, x_first, sems, local=None):
        self.plane, self.source, self.own, self.total = plane, source, own, total
        self.lands, self.x_first, self.sems, self.local = (first_land, second_land), x_first, sems, local
        index = lax.axis_index("dp")
        self.core = lax.rem(index, 2)
        chip = index // 2
        self.y, self.x = chip // plane[1], lax.rem(chip, plane[1])

    def remote(self, src, dst, number, where):
        return pltpu.make_async_remote_copy(
            src_ref=src,
            dst_ref=dst,
            send_sem=self.sems.at[0, number],
            recv_sem=self.sems.at[1, number],
            device_id=device_at(self.plane, *where),
            device_id_type=pl.DeviceIdType.MESH,
        )

    def sibling(self):
        return self.remote(
            self.source.at[:, :, 1 - self.core], self.total, 0, (self.y, self.x, 1 - self.core)
        )

    def start(self):
        self.sibling().start()

    def along(self, stage):
        return self.x_first == (stage == 0)

    def hops(self, stage):
        along_x = self.along(stage)
        size = self.plane[1] if along_x else self.plane[0]
        base = 1 if stage == 0 else self.plane[1] if self.x_first else self.plane[0]
        for k in range(1, size):
            if along_x:
                place = lax.rem(self.x + k, size)
                where = (self.y, place, self.core)
                view = (
                    self.total.at[:, place] if stage == 0 else self.total.at[self.y, place]
                )
            else:
                place = lax.rem(self.y + k, size)
                where = (place, self.x, self.core)
                view = self.total.at[place] if stage == 0 else self.total.at[place, self.x]
            yield k, self.remote(view, self.lands[stage].at[k - 1], base + k - 1, where)

    def send(self, stage):
        for _, copy in self.hops(stage):
            copy.start()

    def pair_sum(self):
        if self.local is not None:
            self.local.wait()
        self.sibling().wait_recv()
        count = self.plane[0] * self.plane[1]
        for b in range(count):
            y, x = b // self.plane[1], b % self.plane[1]
            own = self.own[y, x] if self.local is not None else self.source[y, x, self.core]
            self.total[y, x] = (self.total[y, x].astype(F32) + own.astype(F32)).astype(BF)

    def take(self, stage):
        land = self.lands[stage]
        for k, copy in self.hops(stage):
            copy.wait_recv()
        if stage == 0:
            for other in range(self.plane[0] if self.x_first else self.plane[1]):
                where = (other, self.x) if self.x_first else (self.y, other)
                summed = self.total[where].astype(F32)
                for k in range(land.shape[0]):
                    summed = summed + land[k, other].astype(F32)
                self.total[where] = summed.astype(BF)
            return None
        summed = self.total[self.y, self.x].astype(F32)
        for k in range(land.shape[0]):
            summed = summed + land[k].astype(F32)
        return summed

    def crossed_view(self):
        return self.total.at[:, self.x] if self.x_first else self.total.at[self.y]

    def finish(self, parts=(0, 1, 2)):
        if 0 in parts:
            self.sibling().wait_send()
        for stage in range(2):
            if stage + 1 in parts:
                for _, copy in self.hops(stage):
                    copy.wait_send()


def early_experts(count, local):
    return 2 if count <= 4 and local >= 4 else 0


def late_sums(count):
    return count <= 4


def forward_kernel(
    dims,
    lengths,
    tokens,
    cot,
    routes,
    gain_one,
    gain_two,
    cos_ref,
    sin_ref,
    router,
    query_hbm,
    keyval_hbm,
    out_hbm,
    gate_up_hbm,
    down_hbm,
    y_out,
    hidden_out,
    moe_out,
    queries_out,
    keyval_out,
    mixture_out,
    grad_gu_out,
    grad_dn_out,
    late_out,
    early_gu_out,
    early_dn_out,
    wide,
    narrow,
    normed,
    queries,
    keyval,
    mixture,
    hidden,
    named,
    gates,
    gate_lanes,
    gate_terms,
    router_pad,
    rows_all,
    cot_all,
    acts,
    d_proj,
    w_out,
    w_gu,
    w_dn,
    out_parts,
    out_land,
    in_parts,
    in_land,
    own_sum,
    moe_sum,
    kv_sems,
    rows_sems,
    cot_sems,
    out_sems,
    in_sems,
    load_sems,
    store_sems,
    free_sems,
    lent_sems,
    flat_queries,
    lent_queries,
    lent_mixture,
    *early_scratch,
):
    micros, rows, count, local, ff, model, late, early_count, plane = dims
    seq_len = count * rows
    kv = keyval.shape[2] // 2
    chunks = kv // LANES
    z = lax.axis_index("expert")
    row_base = z * rows
    split = -(-model // seq_len)
    piece = model // split
    back = wide
    bias = gate_terms.at[:, 0:rows]
    scores = wide.at[:, 0 : 4 * rows]
    probs = d_proj.at[micros * local - 1, :, 0 : 4 * rows]
    tile = 512

    loads = []

    def load(src, dst):
        copy = pltpu.make_async_copy(src, dst, load_sems.at[len(loads)])
        copy.start()
        loads.append(copy)
        return copy

    early = []
    for index, weight in enumerate((query_hbm, keyval_hbm)):
        early.append(
            [
                load(
                    weight.at[pl.ds(k * piece, piece), :],
                    d_proj.at[index * split + k, pl.ds(0, piece), :],
                )
                for k in range(split)
            ]
        )
    load_out = load(out_hbm, w_out)
    load_gu = load(gate_up_hbm, w_gu)
    load_dn = load(down_hbm, w_dn)

    line_barrier(count, plane if early_count else None)

    lender, last_z = count - 2, count - 1
    gather_kv = [
        Gather(keyval, m, rows, count - 1, kv_sems.at[m], down=False) for m in range(micros)
    ]

    def lent_copy(kind, m):
        own = rows_at(jnp.int32(last_z), rows)
        earlier = pl.ds(0, last_z * rows)
        src, dst, target = (
            (flat_queries.at[m], flat_queries.at[m], lender),
            (keyval.at[m, own, :], keyval.at[m, own, :], lender),
            (lent_mixture.at[m], mixture.at[m], last_z),
            (keyval.at[m, earlier, :], keyval.at[m, earlier, :], last_z),
        )[kind]
        copy = pltpu.make_async_remote_copy(
            src_ref=src,
            dst_ref=dst,
            send_sem=lent_sems.at[0, m, kind],
            recv_sem=lent_sems.at[1, m, kind],
            device_id={"expert": jnp.int32(target)},
            device_id_type=pl.DeviceIdType.MESH,
        )
        return copy, z == (last_z if target == lender else lender), z == target

    def lent_start(kind, m):
        copy, sends, _ = lent_copy(kind, m)

        @pl.when(sends)
        def _():
            copy.start()

    def lent_wait(kind, m):
        copy, _, receives = lent_copy(kind, m)

        @pl.when(receives)
        def _():
            copy.wait_recv()

    def lent_finish(kind, m):
        copy, sends, _ = lent_copy(kind, m)

        @pl.when(sends)
        def _():
            copy.wait_send()
    gather_rows = [Gather(rows_all, m, rows, count, rows_sems.at[m]) for m in range(micros)]
    gather_cot = [Gather(cot_all, m, rows, count, cot_sems.at[m]) for m in range(micros)]
    reduce_out = [
        Reduce(out_parts, out_land, rows, count, out_sems.at[m]) for m in range(micros)
    ]
    reduce_in = [Reduce(in_parts, in_land, rows, count, in_sems.at[m]) for m in range(micros)]

    for m in range(micros):
        cot_all[m, rows_at(z, rows), :] = cot[m, 0]

    both = micros * rows

    def norm():
        for m in range(micros):
            x_rows = tokens[m, 0].astype(F32)
            normed[m * rows : (m + 1) * rows, :] = (
                x_rows * rms_scale(x_rows) * gain_one[...]
            ).astype(BF)

    cos = cos_ref[rows_at(z, rows), :]
    sin = sin_ref[rows_at(z, rows), :]

    def project(index):
        for copy in early[index]:
            copy.wait()
        total = None
        for k in range(split):
            part = nn(
                normed[:, k * piece : (k + 1) * piece], d_proj[index * split + k, 0:piece, :]
            )
            total = part if total is None else total + part
        wide[0:both, :] = total

    def keys_values():
        project(1)
        for m in range(micros):
            span = slice(m * rows, (m + 1) * rows)
            for c in range(chunks):
                lanes = slice(c * LANES, (c + 1) * LANES)
                keyval[m, rows_at(z, rows), lanes] = rope(wide[span, lanes], cos, sin).astype(BF)
            keyval[m, rows_at(z, rows), kv:] = wide[span, kv:].astype(BF)

    def first_queries():
        project(0)
        for m in range(micros):
            span = slice(m * rows, (m + 1) * rows)
            for i in range(chunks):
                pair = [
                    rope(wide[span, c * LANES : (c + 1) * LANES], cos, sin)
                    for c in (2 * i, 2 * i + 1)
                ]
                pair = [(chunk.astype(BF) * ATTENTION_SCALE).astype(BF) for chunk in pair]

                @pl.when(z == last_z)
                def _(m=m, i=i, pair=pair):
                    for c, chunk in zip((2 * i, 2 * i + 1), pair):
                        flat_queries[m, :, c * LANES : (c + 1) * LANES] = chunk

                pair = [chunk.astype(F32) for chunk in pair]
                for k, block in enumerate(stack_heads(*pair)):
                    queries[m, i, k * rows : (k + 1) * rows, :] = block.astype(BF)
            for b in range(count):

                @pl.when(jnp.logical_and(b > z, z < lender))
                def _(m=m, b=b):
                    keyval[m, b * rows : (b + 1) * rows, :] = jnp.zeros((rows, 2 * kv), BF)

            live = lax.broadcasted_iota(jnp.int32, (seq_len, LANES), 0) < lengths[0, m]
            named[m] = jnp.where(live, named_lanes(routes[m, 0]), 0.0)
        router_pad[...] = jnp.zeros(router_pad.shape, BF)
        router_pad[0 : router.shape[0], :] = router[...]

    def attend_rows(m, stacked, mixed_rows, first_row):
        score_bias(bias, first_row, lengths[0, m])

        def chunk_step(i, carry):
            key_lanes = rows_at(i, LANES)
            value_lanes = pl.ds(pl.multiple_of(kv + i * LANES, LANES), LANES)
            scores[...] = nt(keyval[m, :, key_lanes], stacked[i])
            for k in range(4):
                span = slice(k * rows, (k + 1) * rows)
                probs[:, span] = softmax_columns(scores[:, span] + bias[...]).astype(BF)
            mixed = tn(probs[...], keyval[m, :, value_lanes])
            for c, part in enumerate(unstack_heads(mixed, rows)):
                lanes = pl.ds(pl.multiple_of((2 * i + c) * LANES, LANES), LANES)
                mixed_rows[:, lanes] = part.astype(BF)
            return carry

        lax.fori_loop(0, chunks, chunk_step, 0)

    def lend(m):
        @pl.when(z == lender)
        def _():
            for i in range(chunks):
                pair = [
                    flat_queries[m, :, c * LANES : (c + 1) * LANES].astype(F32)
                    for c in (2 * i, 2 * i + 1)
                ]
                for k, block in enumerate(stack_heads(*pair)):
                    lent_queries[i, k * rows : (k + 1) * rows, :] = block.astype(BF)
            attend_rows(m, lent_queries, lent_mixture.at[m], last_z * rows)

    def attend(m):
        @pl.when(z < last_z)
        def _():
            attend_rows(m, queries.at[m], mixture.at[m], row_base)

    def hidden_rows(m):
        if m == 0:
            load_out.wait()
        live = (row_base + lax.broadcasted_iota(jnp.int32, (rows, 1), 0)) < lengths[0, m]
        rows_hidden = tokens[m, 0].astype(F32) + jnp.where(
            live, nn(mixture[m], w_out[...]), 0.0
        )
        hidden[m] = rows_hidden
        rows_all[m, rows_at(z, rows), :] = (
            rows_hidden * rms_scale(rows_hidden) * gain_two[...]
        ).astype(BF)

    def gate_rows(m):
        if m == 0:
            load_gu.wait()
            load_dn.wait()
        logits = nt(rows_all[m], router_pad[...])
        on = named[m] > 0.0
        masked = jnp.where(on, logits, NEG_FILL)
        raised = jnp.where(on, jnp.exp(masked - jnp.max(masked, -1, keepdims=True)), 0.0)
        total = jnp.sum(raised, -1, keepdims=True)
        gate = raised / jnp.where(total > 0.0, total, 1.0)
        for j in range(local):
            gate_lanes[j] = jnp.broadcast_to(column(gate, z * local + j), gate.shape)

    def column(block, expert):
        return jnp.sum(
            jnp.where(lane_ids(block.shape[0]) == expert, block, 0.0), -1, keepdims=True
        )

    blocks = [slice(c, c + LANES) for c in range(0, ff, LANES)]

    def expert_forward(m, j):
        wide[...] = nn(rows_all[m], w_gu[j].reshape(model, 2 * ff))

        def strip_step(strip, carry):
            where = rows_at(strip, STRIP)
            gate = gate_lanes[j, where, :]
            for c, lanes in enumerate(blocks):
                front, up = wide[where, lanes], wide[where, ff + c * LANES : ff + (c + 1) * LANES]
                value = front * sigmoid(front) * up * gate
                acts[m, where, j * ff + c * LANES : j * ff + (c + 1) * LANES] = value.astype(BF)
            d_proj[m * local + j, where, :] = wide[where, :].astype(BF)
            return carry

        lax.fori_loop(0, seq_len // STRIP, strip_step, 0)

    def expert_backward(m, j):
        expert = z * local + j
        narrow[...] = nt(cot_all[m], w_dn[j].reshape(ff, model))

        def strip_step(strip, carry):
            where = rows_at(strip, STRIP)
            gate = gate_lanes[j, where, :]
            terms = None
            for c, lanes in enumerate(blocks):
                up_lanes = slice(ff + c * LANES, ff + (c + 1) * LANES)
                front = d_proj[m * local + j, where, lanes].astype(F32)
                up = d_proj[m * local + j, where, up_lanes].astype(F32)
                d_act = narrow[where, lanes]
                sig = sigmoid(front)
                silu = front * sig
                term = d_act * silu
                terms = term * up if terms is None else terms + term * up
                d_proj[m * local + j, where, up_lanes] = (term * gate).astype(BF)
                d_proj[m * local + j, where, lanes] = (
                    d_act * gate * up * (sig + silu * (1.0 - sig))
                ).astype(BF)
            gate_terms[where, :] = terms
            return carry

        lax.fori_loop(0, seq_len // STRIP, strip_step, 0)
        d_gate = jnp.sum(gate_terms[...], -1, keepdims=True)
        mine = lane_ids(seq_len) == expert
        if j == 0:
            gates[...] = jnp.where(mine, d_gate, 0.0)
        else:
            gates[...] = jnp.where(mine, d_gate, gates[...])
        if j == local - 1:
            in_parts[:, model:] = (gates[...] * named[m]).astype(BF)
        for r in range(0, seq_len, tile):
            span = slice(r, r + tile)
            part = nt(d_proj[m * local + j, span, :], w_gu[j].reshape(model, 2 * ff))
            if j == 0:
                back[span, :] = part
            elif j < local - 1:
                back[span, :] += part
            else:
                in_parts[span, 0:model] = (back[span, :] + part).astype(BF)

    def weight_grads(j):
        for part_of in range(4):
            lanes = slice(part_of * ff // 2, (part_of + 1) * ff // 2)
            total = None
            for m in range(micros):
                part = tn(rows_all[m], d_proj[m * local + j, :, lanes])
                total = part if total is None else total + part
            w_gu[j, :, :, :, :, lanes] = total.astype(BF).reshape(
                w_gu.shape[1:5] + (ff // 2,)
            )
        total = None
        for m in range(micros):
            part = tn(acts[m, :, j * ff : (j + 1) * ff], cot_all[m])
            total = part if total is None else total + part
        w_dn[j] = total.astype(BF).reshape(w_dn.shape[1:])

    def out_rows(m):
        for r in range(0, seq_len, tile):
            out_parts[r : r + tile, :] = nn(
                acts[m, r : r + tile, :], w_dn[...].reshape(local * ff, model)
            ).astype(BF)

    stores = []

    def store(src, dst):
        copy = pltpu.make_async_copy(src, dst, store_sems.at[len(stores)])
        copy.start()
        stores.append(copy)

    early_items = []
    if early_count:
        gu_sum, gu_land, dn_sum, dn_land, gu_sems, dn_sems = early_scratch
        for j in range(early_count):
            for source, total, land, sems in (
                (w_gu, gu_sum, gu_land, gu_sems), (w_dn, dn_sum, dn_land, dn_sems)
            ):
                early_items.append(
                    PlaneReduce(
                        plane, source.at[j], None, total.at[j], land.at[j], None, j % 2 == 0,
                        sems.at[j],
                    )
                )

    def grad(j):
        weight_grads(j)
        if j < early_count:
            for item in early_items[2 * j : 2 * j + 2]:
                item.start()
        else:
            store(w_gu.at[j], grad_gu_out.at[j])
            store(w_dn.at[j], grad_dn_out.at[j])

    def early_paired(number):
        early_items[number].pair_sum()
        early_items[number].send(0)

    def early_crossed(number):
        early_items[number].take(0)
        out = early_gu_out if number % 2 == 0 else early_dn_out
        store(early_items[number].crossed_view(), out.at[number // 2])

    def finish_out(m):
        reduce_out[m].total(own_sum)
        y_out[m, 0] = (hidden[m] + own_sum[...]).astype(BF)
        reduce_out[m].finish()
        if not late:
            free_landing(0, m)

    def finish_in(m):
        reduce_in[m].total(moe_sum.at[m])
        reduce_in[m].finish()
        free_landing(1, m)

    def free_landing(kind, m):
        if m < micros - 1:
            for way, target, on in ((0, z - 1, z > 0), (1, z + 1, z < count - 1)):

                @pl.when(on)
                def _(way=way, target=target):
                    pl.semaphore_signal(
                        free_sems.at[kind, way], inc=1, device_id={"expert": target},
                        device_id_type=pl.DeviceIdType.MESH,
                    )

    def reduce_slot(kind, m, way, slot):
        if m > 0 and slot == 0:

            @pl.when(z < count - 1 if way == 0 else z > 0)
            def _():
                pl.semaphore_wait(free_sems.at[kind, way], 1)

        (reduce_out, reduce_in)[kind][m].slot(way, slot)

    steps, last = count - 1, local - 1
    work, before, services = {}, [], []
    work[DO_NORM,], work[DO_KV,], work[DO_QUERY,] = norm, keys_values, first_queries
    chain = [(DO_NORM,), (DO_KV,), (DO_QUERY,)]
    for m in range(micros):
        for name, function in ((DO_LEND, lend), (DO_ATTEND, attend), (DO_REST, hidden_rows)):
            work[name, m] = functools.partial(function, m)
            chain.append((name, m))
    for m in range(micros):
        work[DO_GATE, m] = functools.partial(gate_rows, m)
        work[DO_OUT, m] = functools.partial(out_rows, m)
        chain.append((DO_GATE, m))
        for name, function in ((DO_FWD, expert_forward), (DO_BWD, expert_backward)):
            for j in range(local):
                work[name, m, j] = functools.partial(function, m, j)
                chain.append((name, m, j))
            if name == DO_FWD:
                chain.append((DO_OUT, m))
    for j in range(local):
        work[DO_GRAD, j] = functools.partial(grad, j)
        chain.append((DO_GRAD, j))
    before += chained(*chain)
    for m in range(micros):
        for name, gather, after, ahead in (
            (ON_K, gather_kv[m], (DO_KV,), (DO_LEND, m)),
            (ON_N, gather_rows[m], (DO_REST, m), (DO_GATE, m)),
            (ON_C, gather_cot[m], None, (DO_BWD, m, 0)),
        ):
            for way in gather.ways:
                items = [(ON_S, name, m, way)]
                work[items[0]] = functools.partial(gather.start, way, 0)
                for step in range(gather.count - 1):
                    items.append((ON_H, name, m, way, step))
                    work[items[-1]] = functools.partial(gather.hop, way, step)
                services += items
                before += chained(*([after] if after else []), *items, ahead)
        for kind, after, ahead in (
            (0, (DO_QUERY,), (DO_LEND, m)),
            (1, (DO_KV,), (DO_LEND, m)),
            (2, (DO_LEND, m), (DO_REST, m)),
            (3, (ON_H, ON_K, m, 0, count - 3), None),
        ):
            items = [(ON_T, kind, m), (ON_W, kind, m)]
            work[items[0]] = functools.partial(lent_start, kind, m)
            work[items[1]] = functools.partial(lent_wait, kind, m)
            services += items
            before += chained(after, *items, *([ahead] if ahead else []))
        for name, after in ((ON_O, (DO_OUT, m)), (ON_D, (DO_BWD, m, last))):
            if name == ON_O and m > 0 and late:
                continue
            for way in range(2):
                items = [(ON_L, name, m, way, t) for t in range(count)]
                for t, item in enumerate(items):
                    work[item] = functools.partial(reduce_slot, int(name == ON_D), m, way, t)
                services += items
                before += chained(after, *items)
                if m < micros - 1:
                    before.append((items[-1], (DO_BWD, m + 1, last) if name == ON_D else (DO_OUT, m + 1)))
    for number in range(len(early_items)):
        items = [(ON_P, ON_E, number), (ON_X, ON_E, number)]
        work[items[0]] = functools.partial(early_paired, number)
        work[items[1]] = functools.partial(early_crossed, number)
        services += items
        before += chained((DO_GRAD, number // 2), *items)
    order = [item for item in FORWARD_ORDER if item in work]
    if set(order) != set(work):
        order = natural_order(chain, services, before)
    done = set()
    for item in order:
        work[item]()
        done.add(item)
        if item[0] == ON_L and item[4] == count - 1:
            if item[:3] + (1 - item[3], count - 1) in done:
                (finish_out if item[1] == ON_O else finish_in)(item[2])
        if item == (DO_OUT, micros - 1) and late:
            store(out_parts, late_out)
        if item == (DO_REST, micros - 1):
            for src, dst in (
                (hidden, hidden_out), (queries, queries_out), (mixture, mixture_out)
            ):
                store(src, dst)
    store(keyval, keyval_out)
    store(moe_sum, moe_out)
    for item in gather_kv + gather_rows + gather_cot:
        item.finish()
    for m in range(micros):
        for kind in range(4):
            lent_finish(kind, m)
    for item in early_items:
        item.finish((0, 1))
    for copy in stores:
        copy.wait()


def forward_call(
    count, devices, tokens, lengths, routes, gain_one, w_query, w_keyval, w_out, gain_two, w_router,
    gate_up, down, cot,
):
    micros, _, rows, model = tokens.shape
    local, ff = gate_up.shape[0], down.shape[1]
    seq_len = routes.shape[2]
    kv = w_keyval.shape[1] // 2
    chunks = kv // LANES
    heads = w_query.shape[1]
    steps = count - 1
    split = -(-model // seq_len)
    cos, sin = rope_constants(seq_len)
    vmem = pl.BlockSpec(memory_space=pltpu.VMEM)
    smem = pl.BlockSpec(memory_space=pltpu.SMEM)
    hbm = pl.BlockSpec(memory_space=pl.ANY)
    dma = pltpu.SemaphoreType.DMA
    wide_in = model + LANES
    plane = plane_of(devices)
    early = early_experts(count, local)
    gu_shape = (local,) + plane + (2, model // devices, 2 * ff)
    dn_shape = (local,) + plane + (2, ff // devices, model)
    out_shape = (
        jax.ShapeDtypeStruct((micros, 1, rows, model), BF),
        jax.ShapeDtypeStruct((micros, rows, model), F32),
        jax.ShapeDtypeStruct((micros, rows, wide_in), F32),
        jax.ShapeDtypeStruct((micros, chunks, 4 * rows, LANES), BF),
        jax.ShapeDtypeStruct((micros, seq_len, 2 * kv), BF),
        jax.ShapeDtypeStruct((micros, rows, heads), BF),
        jax.ShapeDtypeStruct(gu_shape, BF),
        jax.ShapeDtypeStruct(dn_shape, BF),
        jax.ShapeDtypeStruct((seq_len, model), BF),
        jax.ShapeDtypeStruct((max(early, 1), plane[0]) + gu_shape[4:], BF),
        jax.ShapeDtypeStruct((max(early, 1), plane[0]) + dn_shape[4:], BF),
    )
    scratch = [
        pltpu.VMEM((seq_len, model), F32),
        pltpu.VMEM((seq_len, ff), F32),
        pltpu.VMEM((micros * rows, model), BF),
        pltpu.VMEM((micros, chunks, 4 * rows, LANES), BF),
        pltpu.VMEM((micros, seq_len, 2 * kv), BF),
        pltpu.VMEM((micros, rows, heads), BF),
        pltpu.VMEM((micros, rows, model), F32),
        pltpu.VMEM((micros, seq_len, LANES), F32),
        pltpu.VMEM((seq_len, LANES), F32),
        pltpu.VMEM((local, seq_len, LANES), F32),
        pltpu.VMEM((seq_len, LANES), F32),
        pltpu.VMEM((LANES, model), BF),
        pltpu.VMEM((micros, seq_len, model), BF),
        pltpu.VMEM((micros, seq_len, model), BF),
        pltpu.VMEM((micros, seq_len, local * ff), BF),
        pltpu.VMEM((micros * local, seq_len, 2 * ff), BF),
        pltpu.VMEM(w_out.shape, BF),
        pltpu.VMEM(gu_shape, BF),
        pltpu.VMEM(dn_shape, BF),
        pltpu.VMEM((seq_len, model), BF),
        pltpu.VMEM((count + 1, rows, model), BF),
        pltpu.VMEM((seq_len, wide_in), BF),
        pltpu.VMEM((count + 1, rows, wide_in), BF),
        pltpu.VMEM((rows, model), F32),
        pltpu.VMEM((micros, rows, wide_in), F32),
    ] + [dma((micros, 2, 2, steps))] * 5 + [dma((2 * split + 3,)), dma((2 * local + 6,))]
    scratch += [pltpu.SemaphoreType.REGULAR((2, 2)), dma((2, micros, 4))]
    scratch += [
        pltpu.VMEM((micros, rows, heads), BF),
        pltpu.VMEM((chunks, 4 * rows, LANES), BF),
        pltpu.VMEM((micros, rows, heads), BF),
    ]
    if early:
        for shape in (gu_shape, dn_shape):
            scratch.append(pltpu.VMEM((early,) + plane + shape[4:], BF))
            scratch.append(pltpu.VMEM((early, plane[1] - 1, plane[0]) + shape[4:], BF))
        scratch += [dma((early, 2, plane[0] + plane[1] - 1))] * 2
    dims = (micros, rows, count, local, ff, model, late_sums(count), early, plane)
    return pl.pallas_call(
        functools.partial(forward_kernel, dims),
        out_shape=out_shape,
        in_specs=[smem] + [vmem] * 8 + [hbm] * 5,
        out_specs=(vmem,) + (hbm,) * 10,
        scratch_shapes=scratch,
        name="layer_forward",
        compiler_params=pltpu.CompilerParams(
            collective_id=0, has_side_effects=True, vmem_limit_bytes=VMEM_LIMIT
        ),
    )(
        lengths.T, tokens, cot, jnp.swapaxes(routes, 2, 3), gain_one.reshape(1, -1),
        gain_two.reshape(1, -1), jnp.asarray(cos), jnp.asarray(sin), w_router.T, w_query, w_keyval, w_out,
        gate_up.reshape(gu_shape), down.reshape(dn_shape),
    )


class LineReduce:
    def __init__(self, parts, land, rows, count, sems):
        self.parts, self.land, self.rows, self.count, self.sems = parts, land, rows, count, sems
        self.group = max(rows, GROUP)

    def span(self, z):
        if self.group == self.rows:
            return rows_at(z, self.rows)
        return pl.ds(pl.multiple_of(z * self.rows // self.group * self.group, self.group), self.group)

    def hops(self):
        z = lax.axis_index("expert")
        for k in range(1, self.count):
            target = lax.rem(z + k, self.count)
            yield k, pltpu.make_async_remote_copy(
                src_ref=self.parts.at[self.span(target), :],
                dst_ref=self.land.at[k - 1],
                send_sem=self.sems.at[0, k - 1],
                recv_sem=self.sems.at[1, k - 1],
                device_id={"expert": target},
                device_id_type=pl.DeviceIdType.MESH,
            )

    def start(self):
        for _, copy in self.hops():
            copy.start()

    def total(self):
        for _, copy in self.hops():
            copy.wait_recv()
        summed = self.parts[self.span(lax.axis_index("expert")), :].astype(F32)
        for k in range(self.count - 1):
            summed = summed + self.land[k].astype(F32)
        return summed

    def finish(self):
        for _, copy in self.hops():
            copy.wait_send()


def full_barrier(plane, count):
    z = lax.axis_index("expert")
    barrier = pltpu.get_barrier_semaphore()
    greeted = plane_partners(plane)
    greeted += [{"expert": lax.rem(z + k, count)} for k in range(1, count)]
    for device in greeted:
        pl.semaphore_signal(barrier, inc=1, device_id=device, device_id_type=pl.DeviceIdType.MESH)
    pl.semaphore_wait(barrier, len(greeted))


def backward_kernel(
    dims,
    plane,
    lengths,
    tokens,
    cot,
    routes,
    gain_one,
    gain_two,
    cos_ref,
    sin_ref,
    router,
    moe_hbm,
    hidden_hbm,
    queries_hbm,
    keyval_hbm_rows,
    mixture_hbm,
    y_hbm,
    query_hbm,
    keyval_hbm,
    out_hbm,
    grad_gu,
    grad_dn,
    late_parts,
    early_gu,
    early_dn,
    y_result,
    input_result,
    gu_result,
    dn_result,
    dense_out,
    small_out,
    y_out,
    input_grad,
    gu_out,
    dn_out,
    moe,
    hidden,
    queries,
    keyval,
    mixture,
    w_query,
    w_keyval,
    w_out,
    router_pad,
    normed,
    normed2,
    d_attn,
    d_mix,
    d_keyval,
    d_logits,
    wide,
    gains,
    bias,
    scores,
    d_probs,
    probs,
    d_scores,
    stacked,
    kv_parts,
    kv_land,
    gu_own,
    gu_sum,
    gu_land_a,
    gu_land_b,
    dn_own,
    dn_sum,
    dn_land_a,
    dn_land_b,
    grads,
    grads_sum,
    grads_land_a,
    grads_land_b,
    grads_line,
    grads_line_land,
    small,
    small_sum,
    small_land_a,
    small_land_b,
    small_line,
    small_line_land,
    gu_sems,
    dn_sems,
    grads_sems,
    small_sems,
    line_sems,
    kv_sems,
    load_sems,
    own_sems,
    out_sems,
    store_sems,
    *late_scratch,
):
    micros, rows, count, local, ff, model, late, early_count = dims
    seq_len = count * rows
    kv = keyval.shape[2] // 2
    chunks = kv // LANES
    both = micros * rows
    d_query = d_mix
    z = lax.axis_index("expert")
    row_base = z * rows
    block = small_line.shape[0] // count
    core = lax.rem(lax.axis_index("dp"), 2)

    loads = []
    for number, (src, dst) in enumerate(
        (
            (moe_hbm, moe), (hidden_hbm, hidden), (out_hbm, w_out), (queries_hbm, queries),
            (keyval_hbm_rows, keyval), (mixture_hbm, mixture), (query_hbm, w_query),
            (keyval_hbm, w_keyval), (y_hbm, y_out),
        )
    ):
        loads.append(pltpu.make_async_copy(src, dst, load_sems.at[number]))
        loads[-1].start()
    stores = []

    def store(src, dst):
        stores.append(pltpu.make_async_copy(src, dst, store_sems.at[len(stores)]))
        stores[-1].start()

    def loaded(*numbers):
        for number in numbers:
            loads[number].wait()

    full_barrier(plane, count)

    experts = []
    for j in range(local):
        for kind, (source, early, own, total, land_a, land_b, sems) in enumerate(
            (
                (grad_gu, early_gu, gu_own, gu_sum, gu_land_a, gu_land_b, gu_sems),
                (grad_dn, early_dn, dn_own, dn_sum, dn_land_a, dn_land_b, dn_sems),
            )
        ):
            slot = (j - early_count) % 2
            item = PlaneReduce(
                plane, source.at[j], own.at[slot], total.at[j], land_a.at[j], land_b.at[j],
                j % 2 == 0, sems.at[j],
            )
            if j < early_count:
                view, into = early.at[j], item.crossed_view()
            else:
                view, into = source.at[j, :, :, core], own.at[slot]
                item.start()
            item.local = pltpu.make_async_copy(view, into, own_sems.at[2 * j + kind])
            if j < early_count + 2:
                item.local.start()
            experts.append(item)
    dense = [
        PlaneReduce(
            plane, grads.at[k], None, grads_sum.at[k], grads_land_a.at[k], grads_land_b.at[k],
            k % 2 == 0, grads_sems.at[k],
        )
        for k in range(6)
    ]
    dense.append(
        PlaneReduce(
            plane, small, None, small_sum, small_land_a, small_land_b, True, small_sems
        )
    )
    lines = [
        LineReduce(grads_line.at[k], grads_line_land.at[k], block, count, line_sems.at[k])
        for k in range(6)
    ] + [LineReduce(small_line, small_line_land, block, count, line_sems.at[6])]
    reduce_kv = [
        Reduce(kv_parts.at[m], kv_land.at[m], rows, count, kv_sems.at[m], up=False)
        for m in range(micros)
    ]

    def paired(item):
        item.pair_sum()
        item.send(0)

    def crossed(item):
        item.take(0)
        item.send(1)

    def expert_paired(number):
        paired(experts[number])
        if 2 * early_count + 4 <= number + 4 < len(experts):
            experts[number + 4].local.start()

    def early_crossed(number):
        experts[number].local.wait()
        experts[number].send(1)

    def expert_done(number):
        out, result = (gu_out, gu_result) if number % 2 == 0 else (dn_out, dn_result)
        out[number // 2] = experts[number].take(1)
        store(out.at[number // 2], result.at[number // 2])

    def dense_done(number):
        ref = grads_line.at[number] if number < 6 else small_line
        ref[...] = dense[number].take(1).astype(BF)
        lines[number].start()

    def line_done(number):
        if number < 6:
            half = model // 2
            dense_out[number // 2, :, (number % 2) * half : (number % 2 + 1) * half] = lines[
                number
            ].total()
        else:
            small_out[...] = lines[number].total().T[:, 0 : small_out.shape[1]]

    def put_grads(number, left, right):
        half = model // 2
        shape = grads.shape[1:]
        for k in range(2):
            value = tn(left, right[:, k * half : (k + 1) * half])
            grads[2 * number + k] = value.astype(BF).reshape(shape)
            dense[2 * number + k].start()

    router_pad[...] = jnp.zeros(router_pad.shape, BF)
    router_pad[0 : router.shape[0], :] = router[...]
    gains[...] = jnp.zeros(gains.shape, F32)

    def norm_back(d_rows, inputs, scale, gain, row):
        scaled = d_rows * gain
        gains[row : row + 1, :] += jnp.sum(d_rows * inputs * scale, 0, keepdims=True)
        return scale * (
            scaled - inputs * scale * scale * jnp.mean(scaled * inputs, -1, keepdims=True)
        )

    def live_rows(m):
        return (row_base + lax.broadcasted_iota(jnp.int32, (rows, 1), 0)) < lengths[0, m]

    router_lanes = router.shape[0]

    def router_back(m):
        if m == 0:
            loaded(0, 1)
        span = slice(m * rows, (m + 1) * rows)
        x_rows = tokens[m, 0].astype(F32)
        normed[span, :] = (x_rows * rms_scale(x_rows) * gain_one[...]).astype(BF)
        v = hidden[m]
        scale = rms_scale(v)
        normed2[span, :] = (v * scale * gain_two[...]).astype(BF)
        logits = nt(normed2[span, :], router_pad[...])
        live = live_rows(m)
        on = jnp.where(live, named_lanes(routes[m, 0, :, rows_at(z, rows)]), 0.0) > 0.0
        masked = jnp.where(on, logits, NEG_FILL)
        raised = jnp.where(on, jnp.exp(masked - jnp.max(masked, -1, keepdims=True)), 0.0)
        total = jnp.sum(raised, -1, keepdims=True)
        gate = raised / jnp.where(total > 0.0, total, 1.0)
        d_gate = moe[m, :, model:]
        d_logits[span, :] = (
            gate * (d_gate - jnp.sum(gate * d_gate, -1, keepdims=True))
        ).astype(BF)
        d_rows = moe[m, :, 0:model] + nn(d_logits[span, :], router_pad[...])
        grown = cot[m, 0].astype(F32) + norm_back(
            d_rows, v, scale, gain_two[...], router_lanes + 1
        )
        input_grad[m, 0] = grown
        d_attn[span, :] = jnp.where(live, grown, 0.0).astype(BF)

    def mixture_back(m):
        if m == 0:
            loaded(2)
        span = slice(m * rows, (m + 1) * rows)
        d_mix[span, :] = nt(d_attn[span, :], w_out[...]).astype(BF)

    def grad_out():
        loaded(5)
        put_grads(2, mixture[...].reshape(both, mixture.shape[2]), d_attn[...])

    cos = cos_ref[rows_at(z, rows), :]
    sin = sin_ref[rows_at(z, rows), :]

    def attend_back(m, i):
        if m == 0 and i == 0:
            loaded(3, 4)
        span = slice(m * rows, (m + 1) * rows)
        lanes = slice(i * LANES, (i + 1) * LANES)
        value_lanes = slice(kv + i * LANES, kv + (i + 1) * LANES)
        if i == 0:
            score_bias(bias, row_base, lengths[0, m])
        pair = [d_mix[span, c * LANES : (c + 1) * LANES].astype(F32) for c in (2 * i, 2 * i + 1)]
        for k, rows_of in enumerate(stack_heads(*pair)):
            stacked[k * rows : (k + 1) * rows, :] = rows_of.astype(BF)
        scores[...] = nt(keyval[m, :, lanes], queries[m, i])
        d_probs[...] = nt(keyval[m, :, value_lanes], stacked[...])
        for k in range(4):
            where = slice(k * rows, (k + 1) * rows)
            prob = softmax_columns(scores[:, where] + bias[...])
            d_prob = d_probs[:, where]
            delta = jnp.sum(prob * d_prob, 0, keepdims=True)
            d_scores[:, where] = (prob * (d_prob - delta)).astype(BF)
            probs[:, where] = prob.astype(BF)
        turned = tn(d_scores[...], keyval[m, :, lanes]) * ATTENTION_SCALE
        for c, chunk in zip((2 * i, 2 * i + 1), unstack_heads(turned, rows)):
            d_query[span, c * LANES : (c + 1) * LANES] = rope(chunk, cos, -sin).astype(BF)
        kv_parts[m, :, lanes] = nn(d_scores[...], queries[m, i]).astype(BF)
        kv_parts[m, :, value_lanes] = nn(probs[...], stacked[...]).astype(BF)

    def grad_query():
        put_grads(0, normed[...], d_query[...])

    def query_back():
        loaded(6)
        wide[...] = nt(d_query[...], w_query[...])

    def keyval_total():
        for m in range(micros):
            span = slice(m * rows, (m + 1) * rows)
            key_own = d_probs.at[0:rows, 0:kv]
            value_own = d_probs.at[rows : 2 * rows, 0:kv]
            reduce_kv[m].total(key_own, slice(0, kv))
            reduce_kv[m].total(value_own, slice(kv, 2 * kv))
            for c in range(chunks):
                lanes = slice(c * LANES, (c + 1) * LANES)
                d_keyval[span, lanes] = rope(key_own[:, lanes], cos, -sin).astype(BF)
            d_keyval[span, kv:] = value_own[...].astype(BF)

    def grad_keyval():
        put_grads(1, normed[...], d_keyval[...])

    def keyval_back():
        loaded(7)
        wide[...] += nt(d_keyval[...], w_keyval[...])

    def input_back():
        for m in range(micros):
            span = slice(m * rows, (m + 1) * rows)
            x_rows = tokens[m, 0].astype(F32)
            input_grad[m, 0] += norm_back(
                wide[span, :], x_rows, rms_scale(x_rows), gain_one[...], router_lanes
            )
        store(input_grad, input_result)

    def grad_small():
        small_value = tn(normed2[...], d_logits[...]) + gains[...].T
        small[...] = small_value.astype(BF).reshape(small.shape)
        dense[6].start()

    if late:
        out_parts, out_land, out_own = late_scratch
        late_load = pltpu.make_async_copy(late_parts, out_parts, load_sems.at[9])
        late_load.start()
        reduce_out = Reduce(out_parts, out_land, rows, count, out_sems)

    arrived = []

    def out_slot(way, slot):
        if not arrived:
            late_load.wait()
            arrived.append(True)
        reduce_out.slot(way, slot)

    def finish_out():
        reduce_out.total(out_own)
        loaded(8)
        y_out[micros - 1, 0] = (hidden[micros - 1] + out_own[...]).astype(BF)
        reduce_out.finish()

    work, before, services = {}, [], []
    chain = []
    for m in range(micros):
        chain += [(DO_ROUTER, m), (DO_MIXTURE, m)]
        work[DO_ROUTER, m] = functools.partial(router_back, m)
        work[DO_MIXTURE, m] = functools.partial(mixture_back, m)
        for i in range(chunks):
            chain.append((DO_ATTEND, m, i))
            work[chain[-1]] = functools.partial(attend_back, m, i)
    for name, function in (
        (DO_GRAD_OUT, grad_out),
        (DO_GRAD_QUERY, grad_query), (DO_QUERY, query_back), (DO_TOTAL, keyval_total),
        (DO_GRAD_KEYVAL, grad_keyval), (DO_KEYVAL, keyval_back), (DO_INPUT, input_back),
        (DO_SMALL, grad_small),
    ):
        chain.append((name,))
        work[name,] = function
    before += chained(*chain)
    for m in range(micros):
        items = [(ON_L, ON_K, m, 1, t) for t in range(count)]
        for t, item in enumerate(items):
            work[item] = functools.partial(reduce_kv[m].slot, 1, t)
        services += items
        before += chained((DO_ATTEND, m, chunks - 1), *items, (DO_TOTAL,))
    if late:
        for way in range(2):
            items = [(ON_L, ON_O, way, t) for t in range(count)]
            for t, item in enumerate(items):
                work[item] = functools.partial(out_slot, way, t)
            services += items
            before += chained(*items)
    for number in range(len(experts)):
        items = [(stage, ON_E, number) for stage in (ON_P, ON_X, ON_D)]
        work[items[1]] = functools.partial(crossed, experts[number])
        work[items[2]] = functools.partial(expert_done, number)
        if number < 2 * early_count:
            items = items[1:]
            work[items[0]] = functools.partial(early_crossed, number)
        else:
            work[items[0]] = functools.partial(expert_paired, number)
            if number >= 2 * early_count + 4:
                before.append(((ON_P, ON_E, number - 4), items[0]))
        services += items
        before += chained(*items)
    for number, source in enumerate(
        (DO_GRAD_QUERY, DO_GRAD_QUERY, DO_GRAD_KEYVAL, DO_GRAD_KEYVAL, DO_GRAD_OUT, DO_GRAD_OUT, DO_SMALL)
    ):
        items = [(stage, ON_G, number) for stage in (ON_P, ON_X, ON_D, ON_Z)]
        work[items[0]] = functools.partial(paired, dense[number])
        work[items[1]] = functools.partial(crossed, dense[number])
        work[items[2]] = functools.partial(dense_done, number)
        work[items[3]] = functools.partial(line_done, number)
        services += items
        before += chained((source,), *items)
    services.sort(key=lambda item: (ON_L, ON_P, ON_X, ON_D, ON_Z).index(item[0]))
    order = [item for item in BACKWARD_ORDER if item in work]
    if set(order) != set(work):
        order = natural_order(chain, services, before)
    done = set()
    for item in order:
        work[item]()
        done.add(item)
        if item[:2] == (ON_L, ON_O) and item[3] == count - 1 and (ON_L, ON_O, 1 - item[2], count - 1) in done:
            finish_out()
    if not late:
        loaded(8)
    store(y_out, y_result)
    for number, item in enumerate(experts):
        item.finish((2,) if number < 2 * early_count else (0, 1, 2))
    for item in dense + lines + reduce_kv:
        item.finish()
    for copy in stores:
        copy.wait()


def backward_call(
    count, devices, tokens, lengths, routes, gain_one, w_query, w_keyval, w_out, gain_two,
    w_router, cot, local, ff, y_first, hidden, moe, queries, keyval, mixture, grad_gu, grad_dn, late_parts,
    early_gu, early_dn,
):
    micros, _, rows, model = tokens.shape
    seq_len = routes.shape[2]
    kv = w_keyval.shape[1] // 2
    heads = w_query.shape[1]
    plane = plane_of(devices)
    block = model // devices // count
    group = max(block, GROUP)
    line = count * block
    half = model // 2
    both = micros * rows
    cos, sin = rope_constants(seq_len)
    gu_rows, dn_rows = model // devices, ff // devices
    vmem = pl.BlockSpec(memory_space=pltpu.VMEM)
    smem = pl.BlockSpec(memory_space=pltpu.SMEM)
    hbm = pl.BlockSpec(memory_space=pl.ANY)
    dma = pltpu.SemaphoreType.DMA
    hops = plane[0] + plane[1] - 1

    def reduce_scratch(lead, block_rows, width):
        lead = tuple(lead)
        return [
            pltpu.VMEM(lead + plane + (block_rows, width), BF),
            pltpu.VMEM(lead + (plane[1] - 1, plane[0], block_rows, width), BF),
            pltpu.VMEM(lead + (plane[0] - 1, block_rows, width), BF),
        ]

    wide_bf = pltpu.VMEM((both, model), BF)
    late = late_sums(count)
    out_shape = (
        jax.ShapeDtypeStruct((micros, 1, rows, model), BF),
        jax.ShapeDtypeStruct((micros, 1, rows, model), F32),
        jax.ShapeDtypeStruct((local, gu_rows, 2 * ff), F32),
        jax.ShapeDtypeStruct((local, dn_rows, model), F32),
        jax.ShapeDtypeStruct((3, group, model), F32),
        jax.ShapeDtypeStruct((LANES, group), F32),
    )
    scratch = (
        [pltpu.VMEM(v.shape, v.dtype) for v in out_shape[:4]]
        + [pltpu.VMEM(v.shape, v.dtype) for v in (moe, hidden, queries, keyval, mixture)]
        + [pltpu.VMEM(w.shape, BF) for w in (w_query, w_keyval, w_out)]
        + [pltpu.VMEM((LANES, model), BF)]
        + [wide_bf, wide_bf, wide_bf, pltpu.VMEM((both, heads), BF)]
        + [pltpu.VMEM((both, 2 * kv), BF), pltpu.VMEM((both, LANES), BF)]
        + [pltpu.VMEM((both, model), F32)]
        + [pltpu.VMEM((LANES, model), F32)]
        + [pltpu.VMEM((seq_len, rows), F32)]
        + [pltpu.VMEM((seq_len, 4 * rows), F32)] * 2
        + [pltpu.VMEM((seq_len, 4 * rows), BF)] * 2
        + [pltpu.VMEM((4 * rows, LANES), BF)]
        + [pltpu.VMEM((micros, seq_len, 2 * kv), BF)]
        + [pltpu.VMEM((micros, count - 1, rows, 2 * kv), BF)]
        + [pltpu.VMEM((2,) + plane + (gu_rows, 2 * ff), BF)]
        + reduce_scratch((local,), gu_rows, 2 * ff)
        + [pltpu.VMEM((2,) + plane + (dn_rows, model), BF)]
        + reduce_scratch((local,), dn_rows, model)
        + [pltpu.VMEM((6,) + plane + (2, line, half), BF)]
        + reduce_scratch((6,), line, half)
        + [pltpu.VMEM((6, line, half), BF), pltpu.VMEM((6, count - 1, group, half), BF)]
        + [pltpu.VMEM(plane + (2, line, LANES), BF)]
        + reduce_scratch((), line, LANES)
        + [pltpu.VMEM((line, LANES), BF), pltpu.VMEM((count - 1, group, LANES), BF)]
        + [dma((local, 2, hops)), dma((local, 2, hops)), dma((6, 2, hops)), dma((2, hops))]
        + [dma((7, 2, count - 1)), dma((micros, 2, 2, count - 1)), dma((10,)), dma((2 * local,))]
        + [dma((2, 2, count - 1)), dma((2 * local + 2,))]
    )
    if late:
        scratch += [
            pltpu.VMEM((seq_len, model), BF),
            pltpu.VMEM((count + 1, rows, model), BF),
            pltpu.VMEM((rows, model), F32),
        ]
    dims = (micros, rows, count, local, ff, model, late, early_experts(count, local))
    return pl.pallas_call(
        functools.partial(backward_kernel, dims, plane),
        out_shape=out_shape,
        in_specs=[smem] + [vmem] * 8 + [hbm] * 14,
        out_specs=(hbm,) * 4 + (vmem,) * 2,
        scratch_shapes=scratch,
        name="layer_backward",
        compiler_params=pltpu.CompilerParams(
            collective_id=1, has_side_effects=True, vmem_limit_bytes=VMEM_LIMIT
        ),
    )(
        lengths.T, tokens, cot, jnp.swapaxes(routes, 2, 3), gain_one.reshape(1, -1),
        gain_two.reshape(1, -1), jnp.asarray(cos), jnp.asarray(sin), w_router.T, moe, hidden,
        queries, keyval, mixture, y_first,
        w_query, w_keyval, w_out,
        grad_gu.reshape((local,) + plane + (2, gu_rows, 2 * ff)),
        grad_dn.reshape((local,) + plane + (2, dn_rows, model)),
        late_parts,
        early_gu,
        early_dn,
    )


def finish_kernel(*refs):
    *arrays, dense, small = refs[:6]
    outs, stages, sems = refs[6:16], refs[16:23], refs[23]
    pairs = list(zip(arrays, outs)) + [(dense.at[k], outs[4 + k]) for k in range(3)]
    inward = [
        pltpu.make_async_copy(src, stage, sems.at[0, k])
        for k, ((src, _), stage) in enumerate(zip(pairs, stages))
    ]
    outward = [
        pltpu.make_async_copy(stage, dst, sems.at[1, k])
        for k, ((_, dst), stage) in enumerate(zip(pairs, stages))
    ]
    for copy in inward:
        copy.start()
    router, gain_one, gain_two = outs[7:]
    lanes = router.shape[0]
    router[...] = small[0:lanes, :]
    gain_one[...] = small[lanes : lanes + 1, :]
    gain_two[...] = small[lanes + 1 : lanes + 2, :]
    for arrived, leaving in zip(inward, outward):
        arrived.wait()
        leaving.start()
    for copy in outward:
        copy.wait()


def finish_call(arrays, dense, small, experts):
    hbm = pl.BlockSpec(memory_space=pl.ANY)
    vmem = pl.BlockSpec(memory_space=pltpu.VMEM)
    shapes = [jax.ShapeDtypeStruct(v.shape, v.dtype) for v in arrays]
    shapes += [jax.ShapeDtypeStruct(dense.shape[1:], F32)] * 3
    shapes += [jax.ShapeDtypeStruct((n, small.shape[1]), F32) for n in (experts, 1, 1)]
    return pl.pallas_call(
        finish_kernel,
        out_shape=tuple(shapes),
        in_specs=[hbm] * 5 + [vmem],
        out_specs=(hbm,) * 7 + (vmem,) * 3,
        scratch_shapes=[pltpu.VMEM(v.shape, v.dtype) for v in shapes[:7]]
        + [pltpu.SemaphoreType.DMA((2, 7))],
        name="layer_results",
    )(*arrays, dense, small)


def on_device(
    tokens, lengths, routes, attn_gain, w_query, w_keyval, w_out, ffn_gain, w_router,
    expert_gate_up, expert_down, cotangent,
):
    count = lax.axis_size("expert")
    devices = lax.axis_size("dp")
    model = tokens.shape[3]
    experts = w_router.shape[1]
    local, ff = expert_gate_up.shape[0], expert_down.shape[1]
    y, hidden, moe, queries, keyval, mixture, grad_gu, grad_dn, *partial = forward_call(
        count, devices, tokens, lengths, routes, attn_gain, w_query, w_keyval, w_out, ffn_gain, w_router,
        expert_gate_up, expert_down, cotangent,
    )
    y, input_grad, gu, dn, dense, small = backward_call(
        count, devices, tokens, lengths, routes, attn_gain, w_query, w_keyval, w_out, ffn_gain,
        w_router, cotangent, local, ff, y, hidden, moe, queries, keyval, mixture, grad_gu,
        grad_dn, *partial,
    )
    block = model // devices // count
    if dense.shape[1] != block:
        first = lax.rem(lax.axis_index("expert") * block, dense.shape[1])
        dense = lax.dynamic_slice_in_dim(dense, first, block, 1)
        small = lax.dynamic_slice_in_dim(small, first, block, 1)
    *whole, router, gain_one, gain_two = finish_call(
        (y, input_grad, gu, dn), dense, small, experts
    )
    return (
        whole[0], whole[1], gain_one[0], whole[4], whole[5], whole[6], gain_two[0], router.T,
        whole[2], whole[3],
    )


def solution(mesh):
    placed = (
        P(None, "dp", "expert", None), P(None, "dp"), P(None, "dp", None, None), P(), P(), P(), P(),
        P(), P(), P("expert", None, None), P("expert", None, None), P(None, "dp", "expert", None),
    )
    return jax.shard_map(
        on_device,
        mesh=mesh,
        in_specs=placed,
        out_specs=(
            P(None, "dp", "expert", None), P(None, "dp", "expert", None), P(("dp", "expert")),
            P(("dp", "expert"), None), P(("dp", "expert"), None), P(("dp", "expert"), None),
            P(("dp", "expert")), P(("dp", "expert"), None), P("expert", "dp", None),
            P("expert", "dp", None),
        ),
        check_vma=False,
    )
```

```python
import functools
import math

import jax
import jax.numpy as jnp
import numpy as np
from jax import lax
from jax.experimental import pallas as pl
from jax.experimental.pallas import tpu as pltpu
from jax.sharding import PartitionSpec as P

HEAD_DIM = 64
EPS = 1e-06
ATTENTION_SCALE = 0.015625
ROPE_BASE = 10000.0
NEG_FILL = -1e30
LANES = 128
GROUP = 16
PIECES = 2
STRIP = 64
BF = jnp.bfloat16
F32 = jnp.float32
VMEM_LIMIT = 127 * 2**19
(
    DO_NORM, DO_KV, DO_QUERY, DO_LEND, DO_REST, DO_ATTEND, DO_GATE, DO_FWD, DO_OUT, DO_BWD,
    DO_GRAD, DO_ROUTER, DO_MIXTURE, DO_GRAD_OUT, DO_GRAD_QUERY, DO_TOTAL, DO_GRAD_KEYVAL,
    DO_KEYVAL, DO_INPUT, DO_SMALL, ON_S, ON_H, ON_L, ON_K, ON_N, ON_C, ON_O, ON_D, ON_E, ON_G,
    ON_P, ON_X, ON_Z, ON_T, ON_W,
) = range(35)
FORWARD_ORDER = (
    (
        (ON_S, ON_C, 0, 0, 0), (DO_NORM,), (DO_KV,), (ON_S, ON_C, 0, 0, 1), (ON_S, ON_K, 0, 1, 0),
        (ON_S, ON_K, 0, 0, 0), (DO_QUERY,), (ON_H, ON_C, 0, 0, 1, 0), (ON_T, 0, 0), (ON_T, 1, 0),
        (ON_W, 1, 0), (ON_H, ON_K, 0, 1, 0, 0), (ON_H, ON_K, 0, 0, 0, 0), (ON_H, ON_K, 0, 0, 0, 1),
        (ON_S, ON_K, 1, 0, 0), (ON_W, 0, 0), (ON_H, ON_K, 0, 1, 0, 1), (DO_LEND, 0),
        (ON_H, ON_C, 0, 0, 1, 1), (ON_T, 2, 0), (DO_ATTEND, 0), (ON_S, ON_K, 1, 1, 0), (ON_W, 2, 0),
        (ON_T, 1, 1), (DO_REST, 0), (ON_S, ON_N, 0, 0, 0), (ON_S, ON_N, 0, 1, 1), (ON_T, 0, 1),
        (ON_S, ON_C, 1, 0, 1), (ON_H, ON_K, 1, 1, 0, 0), (ON_H, ON_K, 1, 0, 0, 0), (ON_H, ON_K, 1, 0, 0, 1),
        (ON_H, ON_K, 1, 1, 0, 1), (ON_S, ON_N, 0, 1, 0), (ON_W, 1, 1), (ON_S, ON_N, 0, 0, 1), (ON_W, 0, 1),
        (ON_H, ON_C, 0, 0, 0, 0), (DO_LEND, 1), (ON_H, ON_N, 0, 0, 0, 0), (ON_T, 2, 1), (DO_ATTEND, 1),
        (ON_H, ON_N, 0, 1, 0, 0), (ON_W, 2, 1), (DO_REST, 1), (ON_S, ON_N, 1, 0, 0), (ON_S, ON_N, 1, 1, 0),
        (ON_H, ON_C, 0, 0, 0, 1), (ON_H, ON_N, 0, 1, 1, 0), (ON_H, ON_N, 1, 0, 0, 0),
        (ON_H, ON_N, 0, 1, 0, 1), (ON_S, ON_C, 1, 0, 0), (ON_H, ON_N, 1, 1, 0, 0), (ON_H, ON_N, 0, 0, 1, 0),
        (ON_H, ON_N, 0, 0, 0, 1), (ON_H, ON_N, 0, 0, 1, 1), (ON_H, ON_N, 0, 0, 0, 2),
        (ON_H, ON_C, 1, 0, 0, 0), (ON_H, ON_N, 0, 1, 1, 1), (ON_H, ON_N, 0, 1, 1, 2),
        (ON_H, ON_N, 0, 0, 1, 2), (ON_H, ON_C, 0, 0, 0, 2), (ON_H, ON_N, 0, 1, 0, 2), (DO_GATE, 0),
        (ON_S, ON_N, 1, 1, 1), (DO_FWD, 0, 0), (ON_S, ON_N, 1, 0, 1), (DO_FWD, 0, 1), (DO_FWD, 0, 2),
        (ON_H, ON_N, 1, 0, 1, 0), (DO_FWD, 0, 3), (ON_H, ON_C, 1, 0, 1, 0), (DO_OUT, 0),
        (ON_H, ON_N, 1, 0, 0, 1), (ON_L, ON_O, 0, 0, 0, 0), (ON_H, ON_N, 1, 1, 1, 0),
        (ON_H, ON_N, 1, 1, 0, 1), (ON_H, ON_C, 0, 0, 1, 2), (ON_H, ON_N, 1, 0, 1, 1), (DO_BWD, 0, 0),
        (DO_BWD, 0, 1), (ON_L, ON_O, 0, 0, 1, 0), (ON_H, ON_N, 1, 1, 1, 1), (ON_H, ON_N, 1, 1, 0, 2),
        (ON_L, ON_O, 0, 0, 0, 1), (ON_H, ON_C, 1, 0, 0, 1), (DO_BWD, 0, 2), (ON_H, ON_N, 1, 1, 1, 2),
        (ON_L, ON_O, 0, 0, 1, 1), (ON_L, ON_O, 0, 0, 0, 2), (DO_BWD, 0, 3), (ON_H, ON_N, 1, 0, 1, 2),
        (ON_L, ON_D, 0, 0, 1, 0), (ON_L, ON_D, 0, 1, 1, 0), (ON_L, ON_O, 0, 0, 1, 2),
        (ON_H, ON_N, 1, 0, 0, 2), (ON_L, ON_D, 0, 0, 0, 0), (ON_H, ON_C, 1, 0, 0, 2), (DO_GATE, 1),
        (ON_L, ON_D, 0, 0, 1, 1), (DO_FWD, 1, 0), (DO_FWD, 1, 1), (ON_L, ON_D, 0, 1, 0, 0),
        (ON_L, ON_D, 0, 1, 1, 1), (ON_H, ON_C, 1, 0, 1, 1), (DO_FWD, 1, 2), (ON_L, ON_D, 0, 1, 0, 1),
        (ON_L, ON_O, 0, 0, 1, 3), (ON_L, ON_O, 0, 0, 0, 3), (ON_L, ON_D, 0, 0, 0, 1), (DO_FWD, 1, 3),
        (ON_L, ON_D, 0, 1, 0, 2), (DO_OUT, 1), (ON_L, ON_D, 0, 0, 0, 2), (ON_H, ON_C, 1, 0, 1, 2),
        (ON_L, ON_D, 0, 0, 1, 2), (DO_BWD, 1, 0), (ON_L, ON_D, 0, 1, 1, 2), (DO_BWD, 1, 1),
        (ON_L, ON_D, 0, 1, 0, 3), (ON_L, ON_D, 0, 0, 0, 3), (DO_BWD, 1, 2), (ON_L, ON_D, 0, 0, 1, 3),
        (ON_L, ON_D, 0, 1, 1, 3), (DO_BWD, 1, 3), (ON_L, ON_D, 1, 0, 0, 0), (DO_GRAD, 0), (DO_GRAD, 1),
        (ON_L, ON_D, 1, 0, 0, 1), (ON_P, ON_E, 1), (ON_L, ON_D, 1, 0, 1, 0), (ON_L, ON_D, 1, 0, 1, 1),
        (ON_P, ON_E, 2), (ON_T, 3, 0), (ON_L, ON_D, 1, 0, 1, 2), (DO_GRAD, 2), (ON_L, ON_D, 1, 1, 1, 0),
        (ON_L, ON_D, 1, 1, 1, 1), (ON_W, 3, 0), (ON_L, ON_D, 1, 1, 0, 0), (ON_L, ON_D, 1, 1, 1, 2),
        (ON_L, ON_D, 1, 0, 0, 2), (ON_P, ON_E, 0), (ON_P, ON_E, 3), (ON_L, ON_D, 1, 1, 0, 1),
        (ON_L, ON_D, 1, 0, 0, 3), (ON_L, ON_D, 1, 1, 0, 2), (ON_X, ON_E, 1), (ON_L, ON_D, 1, 1, 1, 3),
        (DO_GRAD, 3), (ON_X, ON_E, 2), (ON_L, ON_D, 1, 1, 0, 3), (ON_X, ON_E, 0), (ON_L, ON_D, 1, 0, 1, 3),
        (ON_X, ON_E, 3),
    ),
    (
        (ON_S, ON_C, 0, 0, 0), (ON_S, ON_C, 0, 0, 1), (DO_NORM,), (DO_KV,), (ON_S, ON_K, 0, 1, 0),
        (ON_H, ON_C, 0, 0, 1, 0), (ON_T, 1, 0), (ON_H, ON_C, 0, 0, 0, 0), (ON_S, ON_C, 1, 0, 0), (DO_QUERY,),
        (ON_T, 0, 0), (ON_W, 0, 0), (ON_H, ON_K, 0, 1, 0, 0), (ON_H, ON_K, 0, 1, 0, 1), (ON_T, 0, 1),
        (ON_S, ON_K, 0, 0, 0), (ON_S, ON_K, 1, 0, 0), (ON_S, ON_K, 1, 1, 0), (ON_W, 1, 0),
        (ON_H, ON_K, 0, 0, 0, 0), (ON_H, ON_K, 0, 0, 0, 1), (DO_LEND, 0), (ON_T, 1, 1), (ON_T, 2, 0),
        (ON_H, ON_C, 0, 0, 1, 1), (ON_W, 2, 0), (DO_ATTEND, 0), (DO_REST, 0), (ON_S, ON_N, 0, 1, 1),
        (ON_W, 0, 1), (ON_H, ON_K, 1, 1, 0, 0), (ON_S, ON_N, 0, 0, 0), (ON_S, ON_N, 0, 0, 1),
        (ON_H, ON_N, 0, 0, 0, 0), (ON_H, ON_C, 0, 0, 1, 2), (ON_H, ON_K, 1, 1, 0, 1),
        (ON_H, ON_K, 1, 0, 0, 0), (ON_S, ON_N, 0, 1, 0), (ON_W, 1, 1), (ON_H, ON_K, 1, 0, 0, 1),
        (DO_LEND, 1), (ON_T, 2, 1), (ON_H, ON_N, 0, 0, 1, 0), (ON_H, ON_N, 0, 1, 1, 0),
        (ON_H, ON_N, 0, 1, 1, 1), (ON_H, ON_N, 0, 1, 1, 2), (ON_H, ON_N, 0, 1, 0, 0),
        (ON_H, ON_N, 0, 0, 1, 1), (DO_ATTEND, 1), (ON_H, ON_N, 0, 0, 1, 2), (ON_W, 2, 1), (DO_REST, 1),
        (ON_S, ON_N, 1, 1, 1), (ON_S, ON_N, 1, 0, 1), (ON_H, ON_N, 0, 0, 0, 1), (ON_H, ON_N, 0, 1, 0, 1),
        (ON_S, ON_N, 1, 0, 0), (ON_S, ON_C, 1, 0, 1), (ON_H, ON_N, 0, 0, 0, 2), (ON_H, ON_N, 0, 1, 0, 2),
        (DO_GATE, 0), (DO_FWD, 0, 0), (DO_FWD, 0, 1), (ON_H, ON_N, 1, 0, 1, 0), (DO_FWD, 0, 2),
        (ON_H, ON_C, 0, 0, 0, 1), (DO_FWD, 0, 3), (ON_H, ON_N, 1, 1, 1, 0), (ON_H, ON_N, 1, 1, 1, 1),
        (ON_H, ON_N, 1, 0, 1, 1), (ON_S, ON_N, 1, 1, 0), (DO_OUT, 0), (ON_H, ON_N, 1, 1, 0, 0),
        (ON_H, ON_C, 1, 0, 1, 0), (ON_H, ON_C, 0, 0, 0, 2), (ON_H, ON_N, 1, 1, 1, 2),
        (ON_L, ON_O, 0, 0, 1, 0), (ON_H, ON_N, 1, 0, 0, 0), (DO_BWD, 0, 0), (DO_BWD, 0, 1),
        (ON_H, ON_N, 1, 1, 0, 1), (ON_H, ON_N, 1, 0, 0, 1), (ON_L, ON_O, 0, 0, 1, 1), (DO_BWD, 0, 2),
        (ON_H, ON_C, 1, 0, 0, 0), (DO_BWD, 0, 3), (ON_L, ON_O, 0, 0, 0, 0), (ON_L, ON_O, 0, 0, 0, 1),
        (ON_L, ON_O, 0, 0, 1, 2), (ON_H, ON_N, 1, 0, 1, 2), (ON_H, ON_N, 1, 0, 0, 2),
        (ON_L, ON_D, 0, 1, 0, 0), (ON_H, ON_N, 1, 1, 0, 2), (DO_GATE, 1), (ON_L, ON_O, 0, 0, 0, 2),
        (ON_L, ON_D, 0, 0, 1, 0), (DO_FWD, 1, 0), (ON_H, ON_C, 1, 0, 1, 1), (ON_L, ON_D, 0, 1, 1, 0),
        (DO_FWD, 1, 1), (ON_L, ON_D, 0, 0, 0, 0), (ON_L, ON_D, 0, 0, 0, 1), (ON_H, ON_C, 1, 0, 0, 1),
        (DO_FWD, 1, 2), (ON_L, ON_O, 0, 0, 1, 3), (DO_FWD, 1, 3), (ON_L, ON_O, 0, 0, 0, 3),
        (ON_L, ON_D, 0, 0, 1, 1), (DO_OUT, 1), (ON_L, ON_D, 0, 1, 0, 1), (ON_L, ON_D, 0, 1, 0, 2),
        (ON_L, ON_D, 0, 1, 1, 1), (ON_L, ON_D, 0, 0, 0, 2), (ON_H, ON_C, 1, 0, 1, 2),
        (ON_L, ON_D, 0, 0, 1, 2), (ON_H, ON_C, 1, 0, 0, 2), (DO_BWD, 1, 0), (ON_T, 3, 0),
        (ON_L, ON_D, 0, 1, 1, 2), (DO_BWD, 1, 1), (ON_L, ON_D, 0, 0, 1, 3), (DO_BWD, 1, 2),
        (ON_L, ON_D, 0, 1, 0, 3), (ON_L, ON_D, 0, 0, 0, 3), (ON_L, ON_D, 0, 1, 1, 3), (DO_BWD, 1, 3),
        (ON_L, ON_D, 1, 0, 1, 0), (ON_L, ON_D, 1, 1, 1, 0), (DO_GRAD, 0), (DO_GRAD, 1),
        (ON_L, ON_D, 1, 0, 1, 1), (ON_L, ON_D, 1, 0, 0, 0), (ON_L, ON_D, 1, 1, 1, 1), (ON_P, ON_E, 0),
        (ON_P, ON_E, 1), (ON_P, ON_E, 2), (ON_P, ON_E, 3), (ON_L, ON_D, 1, 0, 0, 1), (ON_L, ON_D, 1, 0, 1, 2),
        (ON_L, ON_D, 1, 1, 1, 2), (DO_GRAD, 2), (ON_L, ON_D, 1, 0, 1, 3), (DO_GRAD, 3),
        (ON_L, ON_D, 1, 1, 0, 0), (ON_L, ON_D, 1, 0, 0, 2), (ON_L, ON_D, 1, 1, 0, 1),
        (ON_L, ON_D, 1, 1, 0, 2), (ON_L, ON_D, 1, 0, 0, 3), (ON_L, ON_D, 1, 1, 1, 3),
        (ON_L, ON_D, 1, 1, 0, 3), (ON_X, ON_E, 1), (ON_X, ON_E, 0), (ON_X, ON_E, 2), (ON_X, ON_E, 3),
        (ON_W, 3, 0),
    ),
)
BACKWARD_ORDER = (
    (ON_T,), (ON_L, ON_O, 1, 0), (DO_ROUTER, 0), (ON_X, ON_E, 2), (DO_MIXTURE, 0), (ON_L, ON_O, 0, 0),
    (DO_ATTEND, 0, 0), (DO_ATTEND, 0, 1), (DO_ATTEND, 0, 2), (DO_ATTEND, 0, 3), (ON_L, ON_K, 0, 1, 0),
    (ON_X, ON_E, 0), (DO_ROUTER, 1), (ON_L, ON_O, 0, 1), (DO_MIXTURE, 1), (ON_X, ON_E, 3), (ON_P, ON_E, 5),
    (ON_P, ON_E, 6), (ON_P, ON_E, 4), (ON_L, ON_K, 0, 1, 1), (ON_W,), (ON_P, ON_E, 7),
    (ON_L, ON_K, 0, 1, 2), (DO_ATTEND, 1, 0), (ON_L, ON_O, 0, 2), (DO_ATTEND, 1, 1), (DO_ATTEND, 1, 2),
    (DO_ATTEND, 1, 3), (ON_L, ON_K, 1, 1, 0), (DO_GRAD_OUT,), (DO_GRAD_QUERY,), (ON_P, ON_G, 4),
    (ON_X, ON_E, 5), (ON_D, ON_E, 0), (ON_L, ON_K, 1, 1, 1), (ON_P, ON_G, 0), (ON_P, ON_G, 1), (DO_QUERY,),
    (ON_X, ON_E, 7), (ON_P, ON_G, 5), (ON_D, ON_E, 3), (ON_D, ON_E, 2), (ON_L, ON_K, 1, 1, 2),
    (ON_X, ON_G, 0), (ON_X, ON_G, 4), (ON_X, ON_G, 1), (ON_L, ON_K, 0, 1, 3), (ON_L, ON_K, 1, 1, 3),
    (DO_TOTAL,), (DO_GRAD_KEYVAL,), (ON_X, ON_G, 5), (DO_KEYVAL,), (DO_INPUT,), (ON_L, ON_O, 1, 1),
    (ON_D, ON_G, 0), (DO_SMALL,), (ON_P, ON_G, 2), (ON_P, ON_G, 3), (ON_D, ON_G, 1), (ON_D, ON_G, 4),
    (ON_X, ON_E, 1), (ON_P, ON_G, 6), (ON_D, ON_G, 5), (ON_X, ON_G, 3), (ON_L, ON_O, 1, 2), (ON_X, ON_G, 6),
    (ON_X, ON_G, 2), (ON_L, ON_O, 0, 3), (ON_X, ON_E, 6), (ON_D, ON_G, 6), (ON_D, ON_G, 3), (ON_X, ON_E, 4),
    (ON_D, ON_G, 2), (ON_D, ON_E, 7), (ON_D, ON_E, 6), (ON_D, ON_E, 5), (ON_Z, ON_G, 4), (ON_Z, ON_G, 3),
    (ON_Z, ON_G, 5), (ON_D, ON_E, 1), (ON_Z, ON_G, 6), (ON_Z, ON_G, 0), (ON_Z, ON_G, 1), (ON_D, ON_E, 4),
    (ON_L, ON_O, 1, 3), (ON_Z, ON_G, 2),
)


def dot_of(left, right, left_dim, right_dim):
    return lax.dot_general(
        left, right, (((left_dim,), (right_dim,)), ((), ())), preferred_element_type=F32
    )


def nn(left, right):
    return dot_of(left, right, 1, 0)


def nt(left, right):
    return dot_of(left, right, 1, 1)


def tn(left, right):
    return dot_of(left, right, 0, 0)


def rope_constants(seq_len):
    half = HEAD_DIM // 2
    frequency = np.exp(
        np.arange(half, dtype=np.float32) * np.float32(-2.0 * math.log(ROPE_BASE) / HEAD_DIM)
    ).astype(np.float32)
    angles = np.arange(seq_len, dtype=np.float32)[:, None] * frequency[None, :]
    cos, sin = np.cos(angles).astype(np.float32), np.sin(angles).astype(np.float32)
    heads = LANES // HEAD_DIM
    return np.tile(np.concatenate([cos, cos], 1), (1, heads)), np.tile(
        np.concatenate([-sin, sin], 1), (1, heads)
    )


def lane_ids(rows):
    return lax.broadcasted_iota(jnp.int32, (rows, LANES), 1)


def swap_halves(chunk):
    half = HEAD_DIM // 2
    first = lax.rem(lane_ids(chunk.shape[0]), HEAD_DIM) < half
    return jnp.where(
        first, pltpu.roll(chunk, LANES - half, 1), pltpu.roll(chunk, half, 1)
    )


def rope(chunk, cos, sin):
    return chunk * cos + swap_halves(chunk) * sin


def rms_scale(rows):
    return lax.rsqrt(jnp.mean(rows * rows, -1, keepdims=True) + EPS)


def stack_heads(first, second):
    low = lane_ids(first.shape[0]) < HEAD_DIM
    zero = jnp.zeros_like(first)
    return [
        jnp.where(low, first, zero),
        jnp.where(low, pltpu.roll(first, HEAD_DIM, 1), zero),
        jnp.where(low, zero, pltpu.roll(second, HEAD_DIM, 1)),
        jnp.where(low, zero, second),
    ]


def unstack_heads(stacked, rows):
    low = lane_ids(rows) < HEAD_DIM
    parts = [stacked[k * rows : (k + 1) * rows] for k in range(4)]
    first = jnp.where(low, parts[0], pltpu.roll(parts[1], HEAD_DIM, 1))
    second = jnp.where(low, pltpu.roll(parts[2], HEAD_DIM, 1), parts[3])
    return first, second


def rows_at(index, rows):
    return pl.ds(pl.multiple_of(index * rows, rows), rows)


def natural_order(chain, services, before):
    order, placed = [], set()

    def place(item):
        if item not in placed:
            placed.add(item)
            for first, then in before:
                if then == item:
                    place(first)
            order.append(item)

    for item in chain + services:
        place(item)
    return order


def chained(*items):
    return list(zip(items, items[1:]))


def named_lanes(ids):
    lane = lax.broadcasted_iota(jnp.int32, (LANES, ids.shape[1]), 0)
    hit = jnp.zeros(lane.shape, F32)
    for k in range(ids.shape[0]):
        hit = hit + (ids[k : k + 1, :] == lane).astype(F32)
    return hit.T


def piece_at(block, rows, piece):
    size = rows // piece[1]
    return pl.ds(pl.multiple_of(block * rows + piece[0] * size, size), size)


class Gather:
    def __init__(self, buffer, micro, rows, count, sems, up=True, down=True, piece=(0, 1)):
        self.buffer, self.micro, self.rows, self.count, self.sems = buffer, micro, rows, count, sems
        self.piece = piece
        self.ways = [w for w, on in ((0, up), (1, down)) if on]

    def copy(self, way, step, block):
        z = lax.axis_index("expert")
        target = z + 1 if way == 0 else z - 1
        view = self.buffer.at[self.micro, piece_at(block, self.rows, self.piece), :]
        return pltpu.make_async_remote_copy(
            src_ref=view,
            dst_ref=view,
            send_sem=self.sems.at[0, way, step],
            recv_sem=self.sems.at[1, way, step],
            device_id={"expert": target},
            device_id_type=pl.DeviceIdType.MESH,
        )

    def sends(self, way, step):
        z = lax.axis_index("expert")
        if way == 0:
            return z - step, jnp.logical_and(z < self.count - 1, z - step >= 0)
        return z + step, jnp.logical_and(z > 0, z + step <= self.count - 1)

    def receives(self, way, step):
        z = lax.axis_index("expert")
        if way == 0:
            return z - 1 - step, jnp.logical_and(z <= self.count - 1, z - 1 - step >= 0)
        return z + 1 + step, z + 1 + step <= self.count - 1

    def start(self, way, step):
        block, on = self.sends(way, step)

        @pl.when(on)
        def _():
            self.copy(way, step, block).start()

    def hop(self, way, step):
        block, on = self.receives(way, step)

        @pl.when(on)
        def _():
            self.copy(way, step, block).wait_recv()

        if step + 1 < self.count - 1:
            self.start(way, step + 1)

    def finish(self):
        for step in range(self.count - 1):
            for way in self.ways:
                block, on = self.sends(way, step)

                @pl.when(on)
                def _(way=way, step=step, block=block):
                    self.copy(way, step, block).wait_send()


class Reduce:
    def __init__(self, parts, landing, rows, count, sems, up=True, down=True, piece=(0, 1)):
        self.parts, self.landing, self.piece = parts, landing, piece
        self.inside = slice(piece[0] * rows // piece[1], (piece[0] + 1) * rows // piece[1])
        self.rows, self.count, self.sems = rows, count, sems
        self.ways = [w for w, on in ((0, up), (1, down)) if on]

    def block(self, way, slot):
        z = lax.axis_index("expert")
        if way == 0:
            return z + self.count - 1 - slot, slot >= z
        return z - (self.count - 1) + slot, slot >= self.count - 1 - z

    def place(self, way, slot, z):
        if way == 0:
            return slot - (z - 1)
        return self.count - (slot - (self.count - 2 - z)) - (2 if self.ways == [1] else 0)

    def copy(self, way, slot, block):
        z = lax.axis_index("expert")
        target = z + 1 if way == 0 else z - 1
        return pltpu.make_async_remote_copy(
            src_ref=self.parts.at[piece_at(block, self.rows, self.piece), :],
            dst_ref=self.landing.at[self.place(way, slot, target), self.inside],
            send_sem=self.sems.at[0, way, slot],
            recv_sem=self.sems.at[1, way, slot],
            device_id={"expert": target},
            device_id_type=pl.DeviceIdType.MESH,
        )

    def arrival(self, way, slot, block):
        z = lax.axis_index("expert")
        source = z - 1 if way == 0 else z + 1
        return pltpu.make_async_remote_copy(
            src_ref=self.parts.at[piece_at(block, self.rows, self.piece), :],
            dst_ref=self.landing.at[self.place(way, slot, z), self.inside],
            send_sem=self.sems.at[0, way, slot],
            recv_sem=self.sems.at[1, way, slot],
            device_id={"expert": source},
            device_id_type=pl.DeviceIdType.MESH,
        )

    def inner(self, way):
        z = lax.axis_index("expert")
        return z >= 1 if way == 0 else z <= self.count - 2

    def slot(self, way, slot):
        z = lax.axis_index("expert")
        block, on = self.block(way, slot)
        if slot >= 1:

            @pl.when(jnp.logical_and(on, self.inner(way)))
            def _():
                self.arrival(way, slot - 1, block).wait_recv()
                if slot < self.count - 1:
                    where = piece_at(block, self.rows, self.piece)
                    total = self.parts[where, :].astype(F32) + self.landing[
                        self.place(way, slot - 1, z), self.inside
                    ].astype(F32)
                    self.parts[where, :] = total.astype(self.parts.dtype)

        if slot < self.count - 1:

            @pl.when(on)
            def _():
                self.copy(way, slot, block).start()

    def total(self, out, lanes=slice(None)):
        z = lax.axis_index("expert")
        out[...] = self.parts[piece_at(z, self.rows, self.piece), lanes].astype(F32)
        for way in self.ways:

            @pl.when(self.inner(way))
            def _(way=way):
                place = self.place(way, self.count - 2, z)
                out[...] += self.landing[place, self.inside, lanes].astype(F32)

    def finish(self):
        for slot in range(self.count - 1):
            for way in self.ways:
                block, on = self.block(way, slot)

                @pl.when(on)
                def _(way=way, slot=slot, block=block):
                    self.copy(way, slot, block).wait_send()


def line_barrier(count, plane=None):
    z = lax.axis_index("expert")
    barrier = pltpu.get_barrier_semaphore()
    mesh = pl.DeviceIdType.MESH
    for target, on in ((z + 1, z < count - 1), (z - 1, z > 0)):

        @pl.when(on)
        def _(target=target):
            pl.semaphore_signal(
                barrier, inc=1, device_id={"expert": target}, device_id_type=mesh
            )

    others = plane_partners(plane) if plane else []
    for device in others:
        pl.semaphore_signal(barrier, inc=1, device_id=device, device_id_type=mesh)
    awaited = (z > 0).astype(jnp.int32) + (z < count - 1).astype(jnp.int32)
    pl.semaphore_wait(barrier, awaited + len(others))


def score_bias(bias, row_base, length):
    key_pos = lax.broadcasted_iota(jnp.int32, bias.shape, 0)
    query_pos = row_base + lax.broadcasted_iota(jnp.int32, bias.shape, 1)
    allowed = jnp.logical_and(key_pos <= query_pos, key_pos < length)
    bias[...] = jnp.where(allowed, 0.0, NEG_FILL)


def softmax_columns(scores):
    raised = jnp.exp(scores - jnp.max(scores, 0, keepdims=True))
    return raised * (1.0 / jnp.sum(raised, 0, keepdims=True))


def sigmoid(v):
    return 0.5 * jnp.tanh(0.5 * v) + 0.5


def plane_of(devices):
    side = math.isqrt(devices // 2)
    return side, side


def device_at(plane, y, x, core):
    return {"dp": (y * plane[1] + x) * 2 + core}


def plane_partners(plane):
    index = lax.axis_index("dp")
    core, chip = lax.rem(index, 2), index // 2
    y, x = chip // plane[1], lax.rem(chip, plane[1])
    partners = [device_at(plane, y, x, 1 - core)]
    partners += [device_at(plane, y, lax.rem(x + k, plane[1]), core) for k in range(1, plane[1])]
    partners += [device_at(plane, lax.rem(y + k, plane[0]), x, core) for k in range(1, plane[0])]
    return partners


class PlaneReduce:
    def __init__(self, plane, source, own, total, first_land, second_land, x_first, sems, local=None):
        self.plane, self.source, self.own, self.total = plane, source, own, total
        self.lands, self.x_first, self.sems, self.local = (first_land, second_land), x_first, sems, local
        index = lax.axis_index("dp")
        self.core = lax.rem(index, 2)
        chip = index // 2
        self.y, self.x = chip // plane[1], lax.rem(chip, plane[1])

    def remote(self, src, dst, number, where):
        return pltpu.make_async_remote_copy(
            src_ref=src,
            dst_ref=dst,
            send_sem=self.sems.at[0, number],
            recv_sem=self.sems.at[1, number],
            device_id=device_at(self.plane, *where),
            device_id_type=pl.DeviceIdType.MESH,
        )

    def sibling(self):
        return self.remote(
            self.source.at[:, :, 1 - self.core], self.total, 0, (self.y, self.x, 1 - self.core)
        )

    def start(self):
        self.sibling().start()

    def along(self, stage):
        return self.x_first == (stage == 0)

    def hops(self, stage):
        along_x = self.along(stage)
        size = self.plane[1] if along_x else self.plane[0]
        base = 1 if stage == 0 else self.plane[1] if self.x_first else self.plane[0]
        for k in range(1, size):
            if along_x:
                place = lax.rem(self.x + k, size)
                where = (self.y, place, self.core)
                view = (
                    self.total.at[:, place] if stage == 0 else self.total.at[self.y, place]
                )
            else:
                place = lax.rem(self.y + k, size)
                where = (place, self.x, self.core)
                view = self.total.at[place] if stage == 0 else self.total.at[place, self.x]
            yield k, self.remote(view, self.lands[stage].at[k - 1], base + k - 1, where)

    def send(self, stage):
        for _, copy in self.hops(stage):
            copy.start()

    def pair_sum(self):
        if self.local is not None:
            self.local.wait()
        self.sibling().wait_recv()
        count = self.plane[0] * self.plane[1]
        for b in range(count):
            y, x = b // self.plane[1], b % self.plane[1]
            own = self.own[y, x] if self.local is not None else self.source[y, x, self.core]
            self.total[y, x] = (self.total[y, x].astype(F32) + own.astype(F32)).astype(BF)

    def take(self, stage):
        land = self.lands[stage]
        for k, copy in self.hops(stage):
            copy.wait_recv()
        if stage == 0:
            for other in range(self.plane[0] if self.x_first else self.plane[1]):
                where = (other, self.x) if self.x_first else (self.y, other)
                summed = self.total[where].astype(F32)
                for k in range(land.shape[0]):
                    summed = summed + land[k, other].astype(F32)
                self.total[where] = summed.astype(BF)
            return None
        summed = self.total[self.y, self.x].astype(F32)
        for k in range(land.shape[0]):
            summed = summed + land[k].astype(F32)
        return summed

    def crossed_view(self):
        return self.total.at[:, self.x] if self.x_first else self.total.at[self.y]

    def finish(self, parts=(0, 1, 2)):
        if 0 in parts:
            self.sibling().wait_send()
        for stage in range(2):
            if stage + 1 in parts:
                for _, copy in self.hops(stage):
                    copy.wait_send()


def early_experts(count, local):
    return 2 if count <= 4 and local >= 4 else 0


def late_sums(count):
    return count <= 4


def forward_kernel(
    dims,
    lengths,
    tokens,
    cot,
    routes,
    gain_one,
    gain_two,
    cos_ref,
    sin_ref,
    router,
    query_hbm,
    keyval_hbm,
    out_hbm,
    gate_up_hbm,
    down_hbm,
    y_out,
    hidden_out,
    moe_out,
    queries_out,
    keyval_out,
    mixture_out,
    grad_gu_out,
    grad_dn_out,
    late_out,
    early_gu_out,
    early_dn_out,
    wide,
    narrow,
    normed,
    queries,
    keyval,
    mixture,
    hidden,
    named,
    gates,
    gate_lanes,
    gate_terms,
    router_pad,
    rows_all,
    cot_all,
    acts,
    d_proj,
    w_out,
    w_gu,
    w_dn,
    out_parts,
    out_land,
    in_parts,
    in_land,
    own_sum,
    moe_sum,
    kv_sems,
    rows_sems,
    cot_sems,
    out_sems,
    in_sems,
    load_sems,
    store_sems,
    free_sems,
    lent_sems,
    flat_queries,
    lent_queries,
    lent_mixture,
    *early_scratch,
):
    micros, rows, count, local, ff, model, late, early_count, plane = dims
    seq_len = count * rows
    kv = keyval.shape[2] // 2
    chunks = kv // LANES
    z = lax.axis_index("expert")
    row_base = z * rows
    split = -(-model // seq_len)
    piece = model // split
    back = wide
    bias = gate_terms.at[:, 0:rows]
    scores = wide.at[:, 0 : 4 * rows]
    probs = d_proj.at[micros * local - 1, :, 0 : 4 * rows]
    tile = 512

    loads = []

    def load(src, dst):
        copy = pltpu.make_async_copy(src, dst, load_sems.at[len(loads)])
        copy.start()
        loads.append(copy)
        return copy

    early = []
    for index, weight in enumerate((query_hbm, keyval_hbm)):
        early.append(
            [
                load(
                    weight.at[pl.ds(k * piece, piece), :],
                    d_proj.at[index * split + k, pl.ds(0, piece), :],
                )
                for k in range(split)
            ]
        )
    load_out = load(out_hbm, w_out)
    load_gu = load(gate_up_hbm, w_gu)
    load_dn = load(down_hbm, w_dn)

    line_barrier(count, plane if early_count else None)

    lender, last_z = count - 2, count - 1
    pieces = [(p, PIECES) for p in range(PIECES)]
    gather_kv = [
        [
            Gather(keyval, m, rows, count - 1, kv_sems.at[m, p], down=False, piece=pieces[p])
            for p in range(PIECES)
        ]
        for m in range(micros)
    ]

    def lent_copy(kind, m):
        own = rows_at(jnp.int32(last_z), rows)
        earlier = pl.ds(0, last_z * rows)
        src, dst, target = (
            (flat_queries.at[m], flat_queries.at[m], lender),
            (keyval.at[m, own, :], keyval.at[m, own, :], lender),
            (lent_mixture.at[m], mixture.at[m], last_z),
            (keyval.at[m, earlier, :], keyval.at[m, earlier, :], last_z),
        )[kind]
        copy = pltpu.make_async_remote_copy(
            src_ref=src,
            dst_ref=dst,
            send_sem=lent_sems.at[0, m, kind],
            recv_sem=lent_sems.at[1, m, kind],
            device_id={"expert": jnp.int32(target)},
            device_id_type=pl.DeviceIdType.MESH,
        )
        return copy, z == (last_z if target == lender else lender), z == target

    def lent_start(kind, m):
        copy, sends, _ = lent_copy(kind, m)

        @pl.when(sends)
        def _():
            copy.start()

    def lent_wait(kind, m):
        copy, _, receives = lent_copy(kind, m)

        @pl.when(receives)
        def _():
            copy.wait_recv()

    def lent_finish(kind, m):
        copy, sends, _ = lent_copy(kind, m)

        @pl.when(sends)
        def _():
            copy.wait_send()
    gather_rows = [
        [
            Gather(rows_all, m, rows, count, rows_sems.at[m, p], piece=pieces[p])
            for p in range(PIECES)
        ]
        for m in range(micros)
    ]
    gather_cot = [[Gather(cot_all, m, rows, count, cot_sems.at[m, 0])] for m in range(micros)]
    reduce_out = [
        [Reduce(out_parts, out_land, rows, count, out_sems.at[m, 0])] for m in range(micros)
    ]
    reduce_in = [
        [
            Reduce(in_parts, in_land, rows, count, in_sems.at[m, p], piece=pieces[p])
            for p in range(PIECES)
        ]
        for m in range(micros)
    ]

    for m in range(micros):
        cot_all[m, rows_at(z, rows), :] = cot[m, 0]

    both = micros * rows

    def norm():
        for m in range(micros):
            x_rows = tokens[m, 0].astype(F32)
            normed[m * rows : (m + 1) * rows, :] = (
                x_rows * rms_scale(x_rows) * gain_one[...]
            ).astype(BF)

    cos = cos_ref[rows_at(z, rows), :]
    sin = sin_ref[rows_at(z, rows), :]

    def project(index):
        for copy in early[index]:
            copy.wait()
        total = None
        for k in range(split):
            part = nn(
                normed[:, k * piece : (k + 1) * piece], d_proj[index * split + k, 0:piece, :]
            )
            total = part if total is None else total + part
        wide[0:both, :] = total

    def keys_values():
        project(1)
        for m in range(micros):
            span = slice(m * rows, (m + 1) * rows)
            for c in range(chunks):
                lanes = slice(c * LANES, (c + 1) * LANES)
                keyval[m, rows_at(z, rows), lanes] = rope(wide[span, lanes], cos, sin).astype(BF)
            keyval[m, rows_at(z, rows), kv:] = wide[span, kv:].astype(BF)

    def first_queries():
        project(0)
        for m in range(micros):
            span = slice(m * rows, (m + 1) * rows)
            for i in range(chunks):
                pair = [
                    rope(wide[span, c * LANES : (c + 1) * LANES], cos, sin)
                    for c in (2 * i, 2 * i + 1)
                ]
                pair = [(chunk.astype(BF) * ATTENTION_SCALE).astype(BF) for chunk in pair]

                @pl.when(z == last_z)
                def _(m=m, i=i, pair=pair):
                    for c, chunk in zip((2 * i, 2 * i + 1), pair):
                        flat_queries[m, :, c * LANES : (c + 1) * LANES] = chunk

                pair = [chunk.astype(F32) for chunk in pair]
                for k, block in enumerate(stack_heads(*pair)):
                    queries[m, i, k * rows : (k + 1) * rows, :] = block.astype(BF)
            for b in range(count):

                @pl.when(jnp.logical_and(b > z, z < lender))
                def _(m=m, b=b):
                    keyval[m, b * rows : (b + 1) * rows, :] = jnp.zeros((rows, 2 * kv), BF)

            live = lax.broadcasted_iota(jnp.int32, (seq_len, LANES), 0) < lengths[0, m]
            named[m] = jnp.where(live, named_lanes(routes[m, 0]), 0.0)
        router_pad[...] = jnp.zeros(router_pad.shape, BF)
        router_pad[0 : router.shape[0], :] = router[...]

    def attend_rows(m, stacked, mixed_rows, first_row):
        score_bias(bias, first_row, lengths[0, m])

        def chunk_step(i, carry):
            key_lanes = rows_at(i, LANES)
            value_lanes = pl.ds(pl.multiple_of(kv + i * LANES, LANES), LANES)
            scores[...] = nt(keyval[m, :, key_lanes], stacked[i])
            for k in range(4):
                span = slice(k * rows, (k + 1) * rows)
                probs[:, span] = softmax_columns(scores[:, span] + bias[...]).astype(BF)
            mixed = tn(probs[...], keyval[m, :, value_lanes])
            for c, part in enumerate(unstack_heads(mixed, rows)):
                lanes = pl.ds(pl.multiple_of((2 * i + c) * LANES, LANES), LANES)
                mixed_rows[:, lanes] = part.astype(BF)
            return carry

        lax.fori_loop(0, chunks, chunk_step, 0)

    def lend(m):
        @pl.when(z == lender)
        def _():
            for i in range(chunks):
                pair = [
                    flat_queries[m, :, c * LANES : (c + 1) * LANES].astype(F32)
                    for c in (2 * i, 2 * i + 1)
                ]
                for k, block in enumerate(stack_heads(*pair)):
                    lent_queries[i, k * rows : (k + 1) * rows, :] = block.astype(BF)
            attend_rows(m, lent_queries, lent_mixture.at[m], last_z * rows)

    def attend(m):
        @pl.when(z < last_z)
        def _():
            attend_rows(m, queries.at[m], mixture.at[m], row_base)

    def hidden_rows(m):
        if m == 0:
            load_out.wait()
        live = (row_base + lax.broadcasted_iota(jnp.int32, (rows, 1), 0)) < lengths[0, m]
        rows_hidden = tokens[m, 0].astype(F32) + jnp.where(
            live, nn(mixture[m], w_out[...]), 0.0
        )
        hidden[m] = rows_hidden
        rows_all[m, rows_at(z, rows), :] = (
            rows_hidden * rms_scale(rows_hidden) * gain_two[...]
        ).astype(BF)

    def gate_rows(m):
        if m == 0:
            load_gu.wait()
            load_dn.wait()
        logits = nt(rows_all[m], router_pad[...])
        on = named[m] > 0.0
        masked = jnp.where(on, logits, NEG_FILL)
        raised = jnp.where(on, jnp.exp(masked - jnp.max(masked, -1, keepdims=True)), 0.0)
        total = jnp.sum(raised, -1, keepdims=True)
        gate = raised / jnp.where(total > 0.0, total, 1.0)
        for j in range(local):
            gate_lanes[j] = jnp.broadcast_to(column(gate, z * local + j), gate.shape)

    def column(block, expert):
        return jnp.sum(
            jnp.where(lane_ids(block.shape[0]) == expert, block, 0.0), -1, keepdims=True
        )

    blocks = [slice(c, c + LANES) for c in range(0, ff, LANES)]

    def expert_forward(m, j):
        wide[...] = nn(rows_all[m], w_gu[j].reshape(model, 2 * ff))

        def strip_step(strip, carry):
            where = rows_at(strip, STRIP)
            gate = gate_lanes[j, where, :]
            for c, lanes in enumerate(blocks):
                front, up = wide[where, lanes], wide[where, ff + c * LANES : ff + (c + 1) * LANES]
                value = front * sigmoid(front) * up * gate
                acts[m, where, j * ff + c * LANES : j * ff + (c + 1) * LANES] = value.astype(BF)
            d_proj[m * local + j, where, :] = wide[where, :].astype(BF)
            return carry

        lax.fori_loop(0, seq_len // STRIP, strip_step, 0)

    def expert_backward(m, j):
        expert = z * local + j
        narrow[...] = nt(cot_all[m], w_dn[j].reshape(ff, model))

        def strip_step(strip, carry):
            where = rows_at(strip, STRIP)
            gate = gate_lanes[j, where, :]
            terms = None
            for c, lanes in enumerate(blocks):
                up_lanes = slice(ff + c * LANES, ff + (c + 1) * LANES)
                front = d_proj[m * local + j, where, lanes].astype(F32)
                up = d_proj[m * local + j, where, up_lanes].astype(F32)
                d_act = narrow[where, lanes]
                sig = sigmoid(front)
                silu = front * sig
                term = d_act * silu
                terms = term * up if terms is None else terms + term * up
                d_proj[m * local + j, where, up_lanes] = (term * gate).astype(BF)
                d_proj[m * local + j, where, lanes] = (
                    d_act * gate * up * (sig + silu * (1.0 - sig))
                ).astype(BF)
            gate_terms[where, :] = terms
            return carry

        lax.fori_loop(0, seq_len // STRIP, strip_step, 0)
        d_gate = jnp.sum(gate_terms[...], -1, keepdims=True)
        mine = lane_ids(seq_len) == expert
        if j == 0:
            gates[...] = jnp.where(mine, d_gate, 0.0)
        else:
            gates[...] = jnp.where(mine, d_gate, gates[...])
        if j == local - 1:
            in_parts[:, model:] = (gates[...] * named[m]).astype(BF)
        for r in range(0, seq_len, tile):
            span = slice(r, r + tile)
            part = nt(d_proj[m * local + j, span, :], w_gu[j].reshape(model, 2 * ff))
            if j == 0:
                back[span, :] = part
            elif j < local - 1:
                back[span, :] += part
            else:
                in_parts[span, 0:model] = (back[span, :] + part).astype(BF)

    def weight_grads(j):
        for part_of in range(4):
            lanes = slice(part_of * ff // 2, (part_of + 1) * ff // 2)
            total = None
            for m in range(micros):
                part = tn(rows_all[m], d_proj[m * local + j, :, lanes])
                total = part if total is None else total + part
            w_gu[j, :, :, :, :, lanes] = total.astype(BF).reshape(
                w_gu.shape[1:5] + (ff // 2,)
            )
        total = None
        for m in range(micros):
            part = tn(acts[m, :, j * ff : (j + 1) * ff], cot_all[m])
            total = part if total is None else total + part
        w_dn[j] = total.astype(BF).reshape(w_dn.shape[1:])

    def out_rows(m):
        for r in range(0, seq_len, tile):
            out_parts[r : r + tile, :] = nn(
                acts[m, r : r + tile, :], w_dn[...].reshape(local * ff, model)
            ).astype(BF)

    stores = []

    def store(src, dst):
        copy = pltpu.make_async_copy(src, dst, store_sems.at[len(stores)])
        copy.start()
        stores.append(copy)

    early_items = []
    if early_count:
        gu_sum, gu_land, dn_sum, dn_land, gu_sems, dn_sems = early_scratch
        for j in range(early_count):
            for source, total, land, sems in (
                (w_gu, gu_sum, gu_land, gu_sems), (w_dn, dn_sum, dn_land, dn_sems)
            ):
                early_items.append(
                    PlaneReduce(
                        plane, source.at[j], None, total.at[j], land.at[j], None, j % 2 == 0,
                        sems.at[j],
                    )
                )

    def grad(j):
        weight_grads(j)
        if j < early_count:
            for item in early_items[2 * j : 2 * j + 2]:
                item.start()
        else:
            store(w_gu.at[j], grad_gu_out.at[j])
            store(w_dn.at[j], grad_dn_out.at[j])

    def early_paired(number):
        early_items[number].pair_sum()
        early_items[number].send(0)

    def early_crossed(number):
        early_items[number].take(0)

    def finish_out(m):
        reduce_out[m][0].total(own_sum)
        y_out[m, 0] = (hidden[m] + own_sum[...]).astype(BF)
        reduce_out[m][0].finish()
        if not late:
            free_landing(0, m)

    def finish_in(m):
        for part in reduce_in[m]:
            part.total(moe_sum.at[m, part.inside])
            part.finish()
        free_landing(1, m)

    def free_landing(kind, m):
        if m < micros - 1:
            for p in range((1, PIECES)[kind]):
                for way, target, on in ((0, z - 1, z > 0), (1, z + 1, z < count - 1)):

                    @pl.when(on)
                    def _(p=p, way=way, target=target):
                        pl.semaphore_signal(
                            free_sems.at[kind, p, way], inc=1, device_id={"expert": target},
                            device_id_type=pl.DeviceIdType.MESH,
                        )

    def reduce_slot(kind, m, p, way, slot):
        if m > 0 and slot == 0:

            @pl.when(z < count - 1 if way == 0 else z > 0)
            def _():
                pl.semaphore_wait(free_sems.at[kind, p, way], 1)

        (reduce_out, reduce_in)[kind][m][p].slot(way, slot)

    steps, last = count - 1, local - 1
    work, before, services = {}, [], []
    work[DO_NORM,], work[DO_KV,], work[DO_QUERY,] = norm, keys_values, first_queries
    chain = [(DO_NORM,), (DO_KV,), (DO_QUERY,)]
    for m in range(micros):
        for name, function in ((DO_LEND, lend), (DO_ATTEND, attend), (DO_REST, hidden_rows)):
            work[name, m] = functools.partial(function, m)
            chain.append((name, m))
    for m in range(micros):
        work[DO_GATE, m] = functools.partial(gate_rows, m)
        work[DO_OUT, m] = functools.partial(out_rows, m)
        chain.append((DO_GATE, m))
        for name, function in ((DO_FWD, expert_forward), (DO_BWD, expert_backward)):
            for j in range(local):
                work[name, m, j] = functools.partial(function, m, j)
                chain.append((name, m, j))
            if name == DO_FWD:
                chain.append((DO_OUT, m))
    for j in range(local):
        work[DO_GRAD, j] = functools.partial(grad, j)
        chain.append((DO_GRAD, j))
    before += chained(*chain)
    for m in range(micros):
        for name, gathers, after, ahead in (
            (ON_K, gather_kv[m], (DO_KV,), (DO_LEND, m)),
            (ON_N, gather_rows[m], (DO_REST, m), (DO_GATE, m)),
            (ON_C, gather_cot[m], None, (DO_BWD, m, 0)),
        ):
            for p, gather in enumerate(gathers):
                for way in gather.ways:
                    items = [(ON_S, name, m, p, way)]
                    work[items[0]] = functools.partial(gather.start, way, 0)
                    for step in range(gather.count - 1):
                        items.append((ON_H, name, m, p, way, step))
                        work[items[-1]] = functools.partial(gather.hop, way, step)
                    services += items
                    before += chained(*([after] if after else []), *items, ahead)
        for kind, after, ahead in (
            (0, (DO_QUERY,), (DO_LEND, m)),
            (1, (DO_KV,), (DO_LEND, m)),
            (2, (DO_LEND, m), (DO_REST, m)),
            (3, (ON_H, ON_K, m, 0, 0, count - 3), None),
        ):
            if kind == 3 and m == micros - 1:
                continue
            items = [(ON_T, kind, m), (ON_W, kind, m)]
            work[items[0]] = functools.partial(lent_start, kind, m)
            work[items[1]] = functools.partial(lent_wait, kind, m)
            services += items
            before += chained(after, *items, *([ahead] if ahead else []))
        if m < micros - 1:
            before.append(((ON_H, ON_K, m, PIECES - 1, 0, count - 3), (ON_T, 3, m)))
        for name, parts, after in (
            (ON_O, reduce_out[m], (DO_OUT, m)), (ON_D, reduce_in[m], (DO_BWD, m, last))
        ):
            if name == ON_O and m > 0 and late:
                continue
            for p in range(len(parts)):
                for way in range(2):
                    items = [(ON_L, name, m, p, way, t) for t in range(count)]
                    for t, item in enumerate(items):
                        work[item] = functools.partial(
                            reduce_slot, int(name == ON_D), m, p, way, t
                        )
                    services += items
                    before += chained(after, *items)
                    if m < micros - 1:
                        ahead = (DO_BWD, m + 1, last) if name == ON_D else (DO_OUT, m + 1)
                        before.append((items[-1], ahead))
    for number in range(len(early_items)):
        items = [(ON_P, ON_E, number), (ON_X, ON_E, number)]
        work[items[0]] = functools.partial(early_paired, number)
        work[items[1]] = functools.partial(early_crossed, number)
        services += items
        before += chained((DO_GRAD, number // 2), *items)
    orders = [order for order in FORWARD_ORDER if set(order) == set(work)]
    if len(orders) != len(FORWARD_ORDER):
        orders = [natural_order(chain, services, before)]

    def serve(items, done):
        for item in items:
            work[item]()
            done.add(item)
            if item[0] == ON_L and item[5] == count - 1:
                ends = [other for other in work if other[:3] == item[:3] and other[5] == count - 1]
                if done.issuperset(ends):
                    (finish_out if item[1] == ON_O else finish_in)(item[2])

    splits, dones = [], [set() for _ in orders]
    for order in orders:
        runs = [[]]
        for item in order:
            if item in chain:
                runs.append([])
            else:
                runs[-1].append(item)
        splits.append(runs)
    for number in range(len(chain) + 1):
        for part, runs in enumerate(splits):

            @pl.when(z * len(orders) // count == part)
            def _(part=part, runs=runs):
                serve(runs[number], dones[part])

        if number < len(chain):
            item = chain[number]
            work[item]()
            if item == (DO_OUT, micros - 1) and late:
                store(out_parts, late_out)
            if item == (DO_REST, micros - 1):
                for src, dst in (
                    (hidden, hidden_out), (queries, queries_out), (mixture, mixture_out)
                ):
                    store(src, dst)
    for number, item in enumerate(early_items):
        out = early_gu_out if number % 2 == 0 else early_dn_out
        store(item.crossed_view(), out.at[number // 2])
    store(keyval, keyval_out)
    store(moe_sum, moe_out)
    for gathers in gather_kv + gather_rows + gather_cot:
        for item in gathers:
            item.finish()
    for m in range(micros):
        for kind in range(4 if m < micros - 1 else 3):
            lent_finish(kind, m)
    for item in early_items:
        item.finish((0, 1))
    for copy in stores:
        copy.wait()


def forward_call(
    count, devices, tokens, lengths, routes, gain_one, w_query, w_keyval, w_out, gain_two, w_router,
    gate_up, down, cot,
):
    micros, _, rows, model = tokens.shape
    local, ff = gate_up.shape[0], down.shape[1]
    seq_len = routes.shape[2]
    kv = w_keyval.shape[1] // 2
    chunks = kv // LANES
    heads = w_query.shape[1]
    steps = count - 1
    split = -(-model // seq_len)
    cos, sin = rope_constants(seq_len)
    vmem = pl.BlockSpec(memory_space=pltpu.VMEM)
    smem = pl.BlockSpec(memory_space=pltpu.SMEM)
    hbm = pl.BlockSpec(memory_space=pl.ANY)
    dma = pltpu.SemaphoreType.DMA
    wide_in = model + LANES
    plane = plane_of(devices)
    early = early_experts(count, local)
    gu_shape = (local,) + plane + (2, model // devices, 2 * ff)
    dn_shape = (local,) + plane + (2, ff // devices, model)
    out_shape = (
        jax.ShapeDtypeStruct((micros, 1, rows, model), BF),
        jax.ShapeDtypeStruct((micros, rows, model), F32),
        jax.ShapeDtypeStruct((micros, rows, wide_in), F32),
        jax.ShapeDtypeStruct((micros, chunks, 4 * rows, LANES), BF),
        jax.ShapeDtypeStruct((micros, seq_len, 2 * kv), BF),
        jax.ShapeDtypeStruct((micros, rows, heads), BF),
        jax.ShapeDtypeStruct(gu_shape, BF),
        jax.ShapeDtypeStruct(dn_shape, BF),
        jax.ShapeDtypeStruct((seq_len, model), BF),
        jax.ShapeDtypeStruct((max(early, 1), plane[0]) + gu_shape[4:], BF),
        jax.ShapeDtypeStruct((max(early, 1), plane[0]) + dn_shape[4:], BF),
    )
    scratch = [
        pltpu.VMEM((seq_len, model), F32),
        pltpu.VMEM((seq_len, ff), F32),
        pltpu.VMEM((micros * rows, model), BF),
        pltpu.VMEM((micros, chunks, 4 * rows, LANES), BF),
        pltpu.VMEM((micros, seq_len, 2 * kv), BF),
        pltpu.VMEM((micros, rows, heads), BF),
        pltpu.VMEM((micros, rows, model), F32),
        pltpu.VMEM((micros, seq_len, LANES), F32),
        pltpu.VMEM((seq_len, LANES), F32),
        pltpu.VMEM((local, seq_len, LANES), F32),
        pltpu.VMEM((seq_len, LANES), F32),
        pltpu.VMEM((LANES, model), BF),
        pltpu.VMEM((micros, seq_len, model), BF),
        pltpu.VMEM((micros, seq_len, model), BF),
        pltpu.VMEM((micros, seq_len, local * ff), BF),
        pltpu.VMEM((micros * local, seq_len, 2 * ff), BF),
        pltpu.VMEM(w_out.shape, BF),
        pltpu.VMEM(gu_shape, BF),
        pltpu.VMEM(dn_shape, BF),
        pltpu.VMEM((seq_len, model), BF),
        pltpu.VMEM((count + 1, rows, model), BF),
        pltpu.VMEM((seq_len, wide_in), BF),
        pltpu.VMEM((count + 1, rows, wide_in), BF),
        pltpu.VMEM((rows, model), F32),
        pltpu.VMEM((micros, rows, wide_in), F32),
    ] + [dma((micros, PIECES, 2, 2, steps))] * 5 + [dma((2 * split + 3,)), dma((2 * local + 6,))]
    scratch += [pltpu.SemaphoreType.REGULAR((2, PIECES, 2)), dma((2, micros, 4))]
    scratch += [
        pltpu.VMEM((micros, rows, heads), BF),
        pltpu.VMEM((chunks, 4 * rows, LANES), BF),
        pltpu.VMEM((micros, rows, heads), BF),
    ]
    if early:
        for shape in (gu_shape, dn_shape):
            scratch.append(pltpu.VMEM((early,) + plane + shape[4:], BF))
            scratch.append(pltpu.VMEM((early, plane[1] - 1, plane[0]) + shape[4:], BF))
        scratch += [dma((early, 2, plane[0] + plane[1] - 1))] * 2
    dims = (micros, rows, count, local, ff, model, late_sums(count), early, plane)
    return pl.pallas_call(
        functools.partial(forward_kernel, dims),
        out_shape=out_shape,
        in_specs=[smem] + [vmem] * 8 + [hbm] * 5,
        out_specs=(vmem,) + (hbm,) * 10,
        scratch_shapes=scratch,
        name="layer_forward",
        compiler_params=pltpu.CompilerParams(
            collective_id=0, has_side_effects=True, vmem_limit_bytes=VMEM_LIMIT
        ),
    )(
        lengths.T, tokens, cot, jnp.swapaxes(routes, 2, 3), gain_one.reshape(1, -1),
        gain_two.reshape(1, -1), jnp.asarray(cos), jnp.asarray(sin), w_router.T, w_query, w_keyval, w_out,
        gate_up.reshape(gu_shape), down.reshape(dn_shape),
    )


class LineReduce:
    def __init__(self, parts, land, rows, count, sems):
        self.parts, self.land, self.rows, self.count, self.sems = parts, land, rows, count, sems
        self.group = max(rows, GROUP)

    def span(self, z):
        if self.group == self.rows:
            return rows_at(z, self.rows)
        return pl.ds(pl.multiple_of(z * self.rows // self.group * self.group, self.group), self.group)

    def hops(self):
        z = lax.axis_index("expert")
        for k in range(1, self.count):
            target = lax.rem(z + k, self.count)
            yield k, pltpu.make_async_remote_copy(
                src_ref=self.parts.at[self.span(target), :],
                dst_ref=self.land.at[k - 1],
                send_sem=self.sems.at[0, k - 1],
                recv_sem=self.sems.at[1, k - 1],
                device_id={"expert": target},
                device_id_type=pl.DeviceIdType.MESH,
            )

    def start(self):
        for _, copy in self.hops():
            copy.start()

    def total(self):
        for _, copy in self.hops():
            copy.wait_recv()
        summed = self.parts[self.span(lax.axis_index("expert")), :].astype(F32)
        for k in range(self.count - 1):
            summed = summed + self.land[k].astype(F32)
        return summed

    def finish(self):
        for _, copy in self.hops():
            copy.wait_send()


def full_barrier(plane, count):
    z = lax.axis_index("expert")
    barrier = pltpu.get_barrier_semaphore()
    greeted = plane_partners(plane)
    greeted += [{"expert": lax.rem(z + k, count)} for k in range(1, count)]
    for device in greeted:
        pl.semaphore_signal(barrier, inc=1, device_id=device, device_id_type=pl.DeviceIdType.MESH)
    pl.semaphore_wait(barrier, len(greeted))


def backward_kernel(
    dims,
    plane,
    lengths,
    tokens,
    cot,
    routes,
    gain_one,
    gain_two,
    cos_ref,
    sin_ref,
    router,
    moe_hbm,
    hidden_hbm,
    queries_hbm,
    keyval_hbm_rows,
    mixture_hbm,
    y_hbm,
    query_hbm,
    keyval_hbm,
    out_hbm,
    grad_gu,
    grad_dn,
    late_parts,
    early_gu,
    early_dn,
    y_result,
    input_result,
    gu_result,
    dn_result,
    dense_out,
    small_out,
    y_out,
    input_grad,
    gu_out,
    dn_out,
    moe,
    hidden,
    queries,
    keyval,
    mixture,
    w_query,
    w_keyval,
    w_out,
    router_pad,
    normed,
    normed2,
    d_attn,
    d_mix,
    d_keyval,
    d_logits,
    wide,
    gains,
    bias,
    scores,
    d_probs,
    probs,
    d_scores,
    stacked,
    kv_parts,
    kv_land,
    gu_own,
    gu_sum,
    gu_land_a,
    gu_land_b,
    dn_own,
    dn_sum,
    dn_land_a,
    dn_land_b,
    grads,
    grads_sum,
    grads_land_a,
    grads_land_b,
    grads_line,
    grads_line_land,
    small,
    small_sum,
    small_land_a,
    small_land_b,
    small_line,
    small_line_land,
    gu_sems,
    dn_sems,
    grads_sems,
    small_sems,
    line_sems,
    kv_sems,
    load_sems,
    own_sems,
    out_sems,
    store_sems,
    earlier_sems,
    *late_scratch,
):
    micros, rows, count, local, ff, model, late, early_count = dims
    seq_len = count * rows
    kv = keyval.shape[2] // 2
    chunks = kv // LANES
    both = micros * rows
    d_query = d_mix
    z = lax.axis_index("expert")
    row_base = z * rows
    block = small_line.shape[0] // count
    core = lax.rem(lax.axis_index("dp"), 2)

    loads = []
    for number, (src, dst) in enumerate(
        (
            (moe_hbm, moe), (hidden_hbm, hidden), (out_hbm, w_out), (queries_hbm, queries),
            (keyval_hbm_rows.at[0 : micros - 1], keyval.at[0 : micros - 1]),
            (mixture_hbm, mixture), (query_hbm, w_query),
            (keyval_hbm, w_keyval), (y_hbm, y_out),
        )
    ):
        loads.append(pltpu.make_async_copy(src, dst, load_sems.at[number]))
        loads[-1].start()
    tail, top = micros - 1, (count - 1) * rows
    own_load = pltpu.make_async_copy(
        keyval_hbm_rows.at[tail, top:, :], keyval.at[tail, top:, :], load_sems.at[10]
    )
    own_load.start()
    earlier_load = pltpu.make_async_copy(
        keyval_hbm_rows.at[tail, 0:top, :], keyval.at[tail, 0:top, :], load_sems.at[11]
    )

    @pl.when(z < count - 1)
    def _():
        earlier_load.start()

    earlier = pltpu.make_async_remote_copy(
        src_ref=keyval.at[tail, 0:top, :],
        dst_ref=keyval.at[tail, 0:top, :],
        send_sem=earlier_sems.at[0],
        recv_sem=earlier_sems.at[1],
        device_id={"expert": jnp.int32(count - 1)},
        device_id_type=pl.DeviceIdType.MESH,
    )

    def earlier_start():
        @pl.when(z < count - 1)
        def _():
            earlier_load.wait()

        @pl.when(z == count - 2)
        def _():
            earlier.start()

    def earlier_wait():
        own_load.wait()

        @pl.when(z == count - 1)
        def _():
            earlier.wait_recv()

    stores = []

    def store(src, dst):
        stores.append(pltpu.make_async_copy(src, dst, store_sems.at[len(stores)]))
        stores[-1].start()

    def loaded(*numbers):
        for number in numbers:
            loads[number].wait()

    full_barrier(plane, count)

    experts = []
    for j in range(local):
        for kind, (source, early, own, total, land_a, land_b, sems) in enumerate(
            (
                (grad_gu, early_gu, gu_own, gu_sum, gu_land_a, gu_land_b, gu_sems),
                (grad_dn, early_dn, dn_own, dn_sum, dn_land_a, dn_land_b, dn_sems),
            )
        ):
            slot = (j - early_count) % 2
            item = PlaneReduce(
                plane, source.at[j], own.at[slot], total.at[j], land_a.at[j], land_b.at[j],
                j % 2 == 0, sems.at[j],
            )
            if j < early_count:
                view, into = early.at[j], item.crossed_view()
            else:
                view, into = source.at[j, :, :, core], own.at[slot]
                item.start()
            item.local = pltpu.make_async_copy(view, into, own_sems.at[2 * j + kind])
            if j < early_count + 2:
                item.local.start()
            experts.append(item)
    dense = [
        PlaneReduce(
            plane, grads.at[k], None, grads_sum.at[k], grads_land_a.at[k], grads_land_b.at[k],
            k % 2 == 0, grads_sems.at[k],
        )
        for k in range(6)
    ]
    dense.append(
        PlaneReduce(
            plane, small, None, small_sum, small_land_a, small_land_b, True, small_sems
        )
    )
    lines = [
        LineReduce(grads_line.at[k], grads_line_land.at[k], block, count, line_sems.at[k])
        for k in range(6)
    ] + [LineReduce(small_line, small_line_land, block, count, line_sems.at[6])]
    reduce_kv = [
        Reduce(kv_parts.at[m], kv_land.at[m], rows, count, kv_sems.at[m], up=False)
        for m in range(micros)
    ]

    def paired(item):
        item.pair_sum()
        item.send(0)

    def crossed(item):
        item.take(0)
        item.send(1)

    def expert_paired(number):
        paired(experts[number])
        if 2 * early_count + 4 <= number + 4 < len(experts):
            experts[number + 4].local.start()

    def early_crossed(number):
        experts[number].local.wait()
        experts[number].send(1)

    def expert_done(number):
        out, result = (gu_out, gu_result) if number % 2 == 0 else (dn_out, dn_result)
        out[number // 2] = experts[number].take(1)
        store(out.at[number // 2], result.at[number // 2])

    def dense_done(number):
        ref = grads_line.at[number] if number < 6 else small_line
        ref[...] = dense[number].take(1).astype(BF)
        lines[number].start()

    def line_done(number):
        if number < 6:
            half = model // 2
            dense_out[number // 2, :, (number % 2) * half : (number % 2 + 1) * half] = lines[
                number
            ].total()
        else:
            small_out[...] = lines[number].total().T[:, 0 : small_out.shape[1]]

    def put_grads(number, left, right):
        half = model // 2
        shape = grads.shape[1:]
        for k in range(2):
            value = tn(left, right[:, k * half : (k + 1) * half])
            grads[2 * number + k] = value.astype(BF).reshape(shape)
            dense[2 * number + k].start()

    router_pad[...] = jnp.zeros(router_pad.shape, BF)
    router_pad[0 : router.shape[0], :] = router[...]
    gains[...] = jnp.zeros(gains.shape, F32)

    def norm_back(d_rows, inputs, scale, gain, row):
        scaled = d_rows * gain
        gains[row : row + 1, :] += jnp.sum(d_rows * inputs * scale, 0, keepdims=True)
        return scale * (
            scaled - inputs * scale * scale * jnp.mean(scaled * inputs, -1, keepdims=True)
        )

    def live_rows(m):
        return (row_base + lax.broadcasted_iota(jnp.int32, (rows, 1), 0)) < lengths[0, m]

    router_lanes = router.shape[0]

    def router_back(m):
        if m == 0:
            loaded(0, 1)
        span = slice(m * rows, (m + 1) * rows)
        x_rows = tokens[m, 0].astype(F32)
        normed[span, :] = (x_rows * rms_scale(x_rows) * gain_one[...]).astype(BF)
        v = hidden[m]
        scale = rms_scale(v)
        normed2[span, :] = (v * scale * gain_two[...]).astype(BF)
        logits = nt(normed2[span, :], router_pad[...])
        live = live_rows(m)
        on = jnp.where(live, named_lanes(routes[m, 0, :, rows_at(z, rows)]), 0.0) > 0.0
        masked = jnp.where(on, logits, NEG_FILL)
        raised = jnp.where(on, jnp.exp(masked - jnp.max(masked, -1, keepdims=True)), 0.0)
        total = jnp.sum(raised, -1, keepdims=True)
        gate = raised / jnp.where(total > 0.0, total, 1.0)
        d_gate = moe[m, :, model:]
        d_logits[span, :] = (
            gate * (d_gate - jnp.sum(gate * d_gate, -1, keepdims=True))
        ).astype(BF)
        d_rows = moe[m, :, 0:model] + nn(d_logits[span, :], router_pad[...])
        grown = cot[m, 0].astype(F32) + norm_back(
            d_rows, v, scale, gain_two[...], router_lanes + 1
        )
        input_grad[m, 0] = grown
        d_attn[span, :] = jnp.where(live, grown, 0.0).astype(BF)

    def mixture_back(m):
        if m == 0:
            loaded(2)
        span = slice(m * rows, (m + 1) * rows)
        d_mix[span, :] = nt(d_attn[span, :], w_out[...]).astype(BF)

    def grad_out():
        loaded(5)
        put_grads(2, mixture[...].reshape(both, mixture.shape[2]), d_attn[...])

    cos = cos_ref[rows_at(z, rows), :]
    sin = sin_ref[rows_at(z, rows), :]

    def attend_back(m, i):
        if m == 0 and i == 0:
            loaded(3, 4)
        span = slice(m * rows, (m + 1) * rows)
        lanes = slice(i * LANES, (i + 1) * LANES)
        value_lanes = slice(kv + i * LANES, kv + (i + 1) * LANES)
        if i == 0:
            score_bias(bias, row_base, lengths[0, m])
        pair = [d_mix[span, c * LANES : (c + 1) * LANES].astype(F32) for c in (2 * i, 2 * i + 1)]
        for k, rows_of in enumerate(stack_heads(*pair)):
            stacked[k * rows : (k + 1) * rows, :] = rows_of.astype(BF)
        scores[...] = nt(keyval[m, :, lanes], queries[m, i])
        d_probs[...] = nt(keyval[m, :, value_lanes], stacked[...])
        for k in range(4):
            where = slice(k * rows, (k + 1) * rows)
            prob = softmax_columns(scores[:, where] + bias[...])
            d_prob = d_probs[:, where]
            delta = jnp.sum(prob * d_prob, 0, keepdims=True)
            d_scores[:, where] = (prob * (d_prob - delta)).astype(BF)
            probs[:, where] = prob.astype(BF)
        turned = tn(d_scores[...], keyval[m, :, lanes]) * ATTENTION_SCALE
        for c, chunk in zip((2 * i, 2 * i + 1), unstack_heads(turned, rows)):
            d_query[span, c * LANES : (c + 1) * LANES] = rope(chunk, cos, -sin).astype(BF)
        kv_parts[m, :, lanes] = nn(d_scores[...], queries[m, i]).astype(BF)
        kv_parts[m, :, value_lanes] = nn(probs[...], stacked[...]).astype(BF)

    def grad_query():
        put_grads(0, normed[...], d_query[...])

    def query_back():
        loaded(6)
        wide[...] = nt(d_query[...], w_query[...])

    def keyval_total():
        for m in range(micros):
            span = slice(m * rows, (m + 1) * rows)
            key_own = d_probs.at[0:rows, 0:kv]
            value_own = d_probs.at[rows : 2 * rows, 0:kv]
            reduce_kv[m].total(key_own, slice(0, kv))
            reduce_kv[m].total(value_own, slice(kv, 2 * kv))
            for c in range(chunks):
                lanes = slice(c * LANES, (c + 1) * LANES)
                d_keyval[span, lanes] = rope(key_own[:, lanes], cos, -sin).astype(BF)
            d_keyval[span, kv:] = value_own[...].astype(BF)

    def grad_keyval():
        put_grads(1, normed[...], d_keyval[...])

    def keyval_back():
        loaded(7)
        wide[...] += nt(d_keyval[...], w_keyval[...])

    def input_back():
        for m in range(micros):
            span = slice(m * rows, (m + 1) * rows)
            x_rows = tokens[m, 0].astype(F32)
            input_grad[m, 0] += norm_back(
                wide[span, :], x_rows, rms_scale(x_rows), gain_one[...], router_lanes
            )
        store(input_grad, input_result)

    def grad_small():
        small_value = tn(normed2[...], d_logits[...]) + gains[...].T
        small[...] = small_value.astype(BF).reshape(small.shape)
        dense[6].start()

    if late:
        out_parts, out_land, out_own = late_scratch
        late_load = pltpu.make_async_copy(late_parts, out_parts, load_sems.at[9])
        late_load.start()
        reduce_out = Reduce(out_parts, out_land, rows, count, out_sems)

    arrived = []

    def out_slot(way, slot):
        if not arrived:
            late_load.wait()
            arrived.append(True)
        reduce_out.slot(way, slot)

    def finish_out():
        reduce_out.total(out_own)
        loaded(8)
        y_out[micros - 1, 0] = (hidden[micros - 1] + out_own[...]).astype(BF)
        reduce_out.finish()

    work, before, services = {}, [], []
    chain = []
    for m in range(micros):
        chain += [(DO_ROUTER, m), (DO_MIXTURE, m)]
        work[DO_ROUTER, m] = functools.partial(router_back, m)
        work[DO_MIXTURE, m] = functools.partial(mixture_back, m)
        for i in range(chunks):
            chain.append((DO_ATTEND, m, i))
            work[chain[-1]] = functools.partial(attend_back, m, i)
    for name, function in (
        (DO_GRAD_OUT, grad_out),
        (DO_GRAD_QUERY, grad_query), (DO_QUERY, query_back), (DO_TOTAL, keyval_total),
        (DO_GRAD_KEYVAL, grad_keyval), (DO_KEYVAL, keyval_back), (DO_INPUT, input_back),
        (DO_SMALL, grad_small),
    ):
        chain.append((name,))
        work[name,] = function
    before += chained(*chain)
    work[ON_T,], work[ON_W,] = earlier_start, earlier_wait
    services += [(ON_T,), (ON_W,)]
    before += chained((ON_T,), (ON_W,), (DO_ATTEND, micros - 1, 0))
    for m in range(micros):
        items = [(ON_L, ON_K, m, 1, t) for t in range(count)]
        for t, item in enumerate(items):
            work[item] = functools.partial(reduce_kv[m].slot, 1, t)
        services += items
        before += chained((DO_ATTEND, m, chunks - 1), *items, (DO_TOTAL,))
    if late:
        for way in range(2):
            items = [(ON_L, ON_O, way, t) for t in range(count)]
            for t, item in enumerate(items):
                work[item] = functools.partial(out_slot, way, t)
            services += items
            before += chained(*items)
    for number in range(len(experts)):
        items = [(stage, ON_E, number) for stage in (ON_P, ON_X, ON_D)]
        work[items[1]] = functools.partial(crossed, experts[number])
        work[items[2]] = functools.partial(expert_done, number)
        if number < 2 * early_count:
            items = items[1:]
            work[items[0]] = functools.partial(early_crossed, number)
        else:
            work[items[0]] = functools.partial(expert_paired, number)
            if number >= 2 * early_count + 4:
                before.append(((ON_P, ON_E, number - 4), items[0]))
        services += items
        before += chained(*items)
    for number, source in enumerate(
        (DO_GRAD_QUERY, DO_GRAD_QUERY, DO_GRAD_KEYVAL, DO_GRAD_KEYVAL, DO_GRAD_OUT, DO_GRAD_OUT, DO_SMALL)
    ):
        items = [(stage, ON_G, number) for stage in (ON_P, ON_X, ON_D, ON_Z)]
        work[items[0]] = functools.partial(paired, dense[number])
        work[items[1]] = functools.partial(crossed, dense[number])
        work[items[2]] = functools.partial(dense_done, number)
        work[items[3]] = functools.partial(line_done, number)
        services += items
        before += chained((source,), *items)
    services.sort(key=lambda item: (ON_T, ON_W, ON_L, ON_P, ON_X, ON_D, ON_Z).index(item[0]))
    order = [item for item in BACKWARD_ORDER if item in work]
    if set(order) != set(work):
        order = natural_order(chain, services, before)
    done = set()
    for item in order:
        work[item]()
        done.add(item)
        if item[:2] == (ON_L, ON_O) and item[3] == count - 1 and (ON_L, ON_O, 1 - item[2], count - 1) in done:
            finish_out()
    if not late:
        loaded(8)
    store(y_out, y_result)
    for number, item in enumerate(experts):
        item.finish((2,) if number < 2 * early_count else (0, 1, 2))
    for item in dense + lines + reduce_kv:
        item.finish()

    @pl.when(z == count - 2)
    def _():
        earlier.wait_send()

    for copy in stores:
        copy.wait()


def backward_call(
    count, devices, tokens, lengths, routes, gain_one, w_query, w_keyval, w_out, gain_two,
    w_router, cot, local, ff, y_first, hidden, moe, queries, keyval, mixture, grad_gu, grad_dn, late_parts,
    early_gu, early_dn,
):
    micros, _, rows, model = tokens.shape
    seq_len = routes.shape[2]
    kv = w_keyval.shape[1] // 2
    heads = w_query.shape[1]
    plane = plane_of(devices)
    block = model // devices // count
    group = max(block, GROUP)
    line = count * block
    half = model // 2
    both = micros * rows
    cos, sin = rope_constants(seq_len)
    gu_rows, dn_rows = model // devices, ff // devices
    vmem = pl.BlockSpec(memory_space=pltpu.VMEM)
    smem = pl.BlockSpec(memory_space=pltpu.SMEM)
    hbm = pl.BlockSpec(memory_space=pl.ANY)
    dma = pltpu.SemaphoreType.DMA
    hops = plane[0] + plane[1] - 1

    def reduce_scratch(lead, block_rows, width):
        lead = tuple(lead)
        return [
            pltpu.VMEM(lead + plane + (block_rows, width), BF),
            pltpu.VMEM(lead + (plane[1] - 1, plane[0], block_rows, width), BF),
            pltpu.VMEM(lead + (plane[0] - 1, block_rows, width), BF),
        ]

    wide_bf = pltpu.VMEM((both, model), BF)
    late = late_sums(count)
    out_shape = (
        jax.ShapeDtypeStruct((micros, 1, rows, model), BF),
        jax.ShapeDtypeStruct((micros, 1, rows, model), F32),
        jax.ShapeDtypeStruct((local, gu_rows, 2 * ff), F32),
        jax.ShapeDtypeStruct((local, dn_rows, model), F32),
        jax.ShapeDtypeStruct((3, group, model), F32),
        jax.ShapeDtypeStruct((LANES, group), F32),
    )
    scratch = (
        [pltpu.VMEM(v.shape, v.dtype) for v in out_shape[:4]]
        + [pltpu.VMEM(v.shape, v.dtype) for v in (moe, hidden, queries, keyval, mixture)]
        + [pltpu.VMEM(w.shape, BF) for w in (w_query, w_keyval, w_out)]
        + [pltpu.VMEM((LANES, model), BF)]
        + [wide_bf, wide_bf, wide_bf, pltpu.VMEM((both, heads), BF)]
        + [pltpu.VMEM((both, 2 * kv), BF), pltpu.VMEM((both, LANES), BF)]
        + [pltpu.VMEM((both, model), F32)]
        + [pltpu.VMEM((LANES, model), F32)]
        + [pltpu.VMEM((seq_len, rows), F32)]
        + [pltpu.VMEM((seq_len, 4 * rows), F32)] * 2
        + [pltpu.VMEM((seq_len, 4 * rows), BF)] * 2
        + [pltpu.VMEM((4 * rows, LANES), BF)]
        + [pltpu.VMEM((micros, seq_len, 2 * kv), BF)]
        + [pltpu.VMEM((micros, count - 1, rows, 2 * kv), BF)]
        + [pltpu.VMEM((2,) + plane + (gu_rows, 2 * ff), BF)]
        + reduce_scratch((local,), gu_rows, 2 * ff)
        + [pltpu.VMEM((2,) + plane + (dn_rows, model), BF)]
        + reduce_scratch((local,), dn_rows, model)
        + [pltpu.VMEM((6,) + plane + (2, line, half), BF)]
        + reduce_scratch((6,), line, half)
        + [pltpu.VMEM((6, line, half), BF), pltpu.VMEM((6, count - 1, group, half), BF)]
        + [pltpu.VMEM(plane + (2, line, LANES), BF)]
        + reduce_scratch((), line, LANES)
        + [pltpu.VMEM((line, LANES), BF), pltpu.VMEM((count - 1, group, LANES), BF)]
        + [dma((local, 2, hops)), dma((local, 2, hops)), dma((6, 2, hops)), dma((2, hops))]
        + [dma((7, 2, count - 1)), dma((micros, 2, 2, count - 1)), dma((12,)), dma((2 * local,))]
        + [dma((2, 2, count - 1)), dma((2 * local + 2,)), dma((2,))]
    )
    if late:
        scratch += [
            pltpu.VMEM((seq_len, model), BF),
            pltpu.VMEM((count + 1, rows, model), BF),
            pltpu.VMEM((rows, model), F32),
        ]
    dims = (micros, rows, count, local, ff, model, late, early_experts(count, local))
    return pl.pallas_call(
        functools.partial(backward_kernel, dims, plane),
        out_shape=out_shape,
        in_specs=[smem] + [vmem] * 8 + [hbm] * 14,
        out_specs=(hbm,) * 4 + (vmem,) * 2,
        scratch_shapes=scratch,
        name="layer_backward",
        compiler_params=pltpu.CompilerParams(
            collective_id=1, has_side_effects=True, vmem_limit_bytes=VMEM_LIMIT
        ),
    )(
        lengths.T, tokens, cot, jnp.swapaxes(routes, 2, 3), gain_one.reshape(1, -1),
        gain_two.reshape(1, -1), jnp.asarray(cos), jnp.asarray(sin), w_router.T, moe, hidden,
        queries, keyval, mixture, y_first,
        w_query, w_keyval, w_out,
        grad_gu.reshape((local,) + plane + (2, gu_rows, 2 * ff)),
        grad_dn.reshape((local,) + plane + (2, dn_rows, model)),
        late_parts,
        early_gu,
        early_dn,
    )


def finish_kernel(*refs):
    *arrays, dense, small = refs[:6]
    outs, stages, sems = refs[6:16], refs[16:23], refs[23]
    pairs = list(zip(arrays, outs)) + [(dense.at[k], outs[4 + k]) for k in range(3)]
    inward = [
        pltpu.make_async_copy(src, stage, sems.at[0, k])
        for k, ((src, _), stage) in enumerate(zip(pairs, stages))
    ]
    outward = [
        pltpu.make_async_copy(stage, dst, sems.at[1, k])
        for k, ((_, dst), stage) in enumerate(zip(pairs, stages))
    ]
    for copy in inward:
        copy.start()
    router, gain_one, gain_two = outs[7:]
    lanes = router.shape[0]
    router[...] = small[0:lanes, :]
    gain_one[...] = small[lanes : lanes + 1, :]
    gain_two[...] = small[lanes + 1 : lanes + 2, :]
    for arrived, leaving in zip(inward, outward):
        arrived.wait()
        leaving.start()
    for copy in outward:
        copy.wait()


def finish_call(arrays, dense, small, experts):
    hbm = pl.BlockSpec(memory_space=pl.ANY)
    vmem = pl.BlockSpec(memory_space=pltpu.VMEM)
    shapes = [jax.ShapeDtypeStruct(v.shape, v.dtype) for v in arrays]
    shapes += [jax.ShapeDtypeStruct(dense.shape[1:], F32)] * 3
    shapes += [jax.ShapeDtypeStruct((n, small.shape[1]), F32) for n in (experts, 1, 1)]
    return pl.pallas_call(
        finish_kernel,
        out_shape=tuple(shapes),
        in_specs=[hbm] * 5 + [vmem],
        out_specs=(hbm,) * 7 + (vmem,) * 3,
        scratch_shapes=[pltpu.VMEM(v.shape, v.dtype) for v in shapes[:7]]
        + [pltpu.SemaphoreType.DMA((2, 7))],
        name="layer_results",
    )(*arrays, dense, small)


def on_device(
    tokens, lengths, routes, attn_gain, w_query, w_keyval, w_out, ffn_gain, w_router,
    expert_gate_up, expert_down, cotangent,
):
    count = lax.axis_size("expert")
    devices = lax.axis_size("dp")
    model = tokens.shape[3]
    experts = w_router.shape[1]
    local, ff = expert_gate_up.shape[0], expert_down.shape[1]
    y, hidden, moe, queries, keyval, mixture, grad_gu, grad_dn, *partial = forward_call(
        count, devices, tokens, lengths, routes, attn_gain, w_query, w_keyval, w_out, ffn_gain, w_router,
        expert_gate_up, expert_down, cotangent,
    )
    y, input_grad, gu, dn, dense, small = backward_call(
        count, devices, tokens, lengths, routes, attn_gain, w_query, w_keyval, w_out, ffn_gain,
        w_router, cotangent, local, ff, y, hidden, moe, queries, keyval, mixture, grad_gu,
        grad_dn, *partial,
    )
    block = model // devices // count
    if dense.shape[1] != block:
        first = lax.rem(lax.axis_index("expert") * block, dense.shape[1])
        dense = lax.dynamic_slice_in_dim(dense, first, block, 1)
        small = lax.dynamic_slice_in_dim(small, first, block, 1)
    *whole, router, gain_one, gain_two = finish_call(
        (y, input_grad, gu, dn), dense, small, experts
    )
    return (
        whole[0], whole[1], gain_one[0], whole[4], whole[5], whole[6], gain_two[0], router.T,
        whole[2], whole[3],
    )


def solution(mesh):
    placed = (
        P(None, "dp", "expert", None), P(None, "dp"), P(None, "dp", None, None), P(), P(), P(), P(),
        P(), P(), P("expert", None, None), P("expert", None, None), P(None, "dp", "expert", None),
    )
    return jax.shard_map(
        on_device,
        mesh=mesh,
        in_specs=placed,
        out_specs=(
            P(None, "dp", "expert", None), P(None, "dp", "expert", None), P(("dp", "expert")),
            P(("dp", "expert"), None), P(("dp", "expert"), None), P(("dp", "expert"), None),
            P(("dp", "expert")), P(("dp", "expert"), None), P("expert", "dp", None),
            P("expert", "dp", None),
        ),
        check_vma=False,
    )
```
